32 devices in a mesh: blk: 16 (over z, y, core), rep: 2 (over x).
Axes of the slice: x: 2, y: 2, z: 4, core: 2. Of those that a mesh axis runs over, the one named last changes fastest.
Arguments:
- query_ids: int32 [2, 32, 128], P('rep', 'blk'), may hold values from 0 to 30591
- passage_ids: int32 [2, 32, 512], P('rep', 'blk'), may hold values from 0 to 30591
- query_lengths: int32 [2, 32], P('rep', 'blk'), may hold values from 32 to 128, as said below
- passage_lengths: int32 [2, 32], P('rep', 'blk'), may hold values from 64 to 512, as said below
- positive: int32 [2, 32], P('rep', 'blk'), may hold values from -1 to 31, as said below
- prefix_lengths: int32 [6], replicated, may hold values from 8 to 256, as said below
- prefix_weights: float32 [6], replicated, may hold values from 0.5 to 2
- owners: int32 [269], replicated, may hold values from 0 to 271, as said below
- weights: float32 [272, 128, 256], P('blk'), may hold values from -0.375 to 0.375
- first_moments: float32 [272, 128, 256], P('blk'), may hold values from -5.722046e-06 to 5.722046e-06
- second_moments: float32 [272, 128, 256], P('blk'), may hold values from 1.1344825e-14 to 4.53793e-14
- vectors: float32 [16, 256], replicated, may hold values from -0.5 to 1.5
- vector_first: float32 [16, 256], replicated, may hold values from -1.9073486e-05 to 1.9073486e-05
- vector_second: float32 [16, 256], replicated, may hold values from 1.4935193e-12 to 4.7792617e-11
Outputs:
- new_weights: float32 [272, 128, 256], P('blk')
- new_first: float32 [272, 128, 256], P('blk')
- new_second: float32 [272, 128, 256], P('blk')
- new_vectors: float32 [16, 256], replicated
- new_vector_first: float32 [16, 256], replicated
- new_vector_second: float32 [16, 256], replicated
- loss_sum: float32 [], replicated
- valid_count: float32 [], replicated
- clip_norm: float32 [], replicated
The draws below stay inside these ranges and needn't reach their ends.
Inputs may be any that keep to these rules, and one draw needn't show every extreme that they name: `query_lengths`: at least 32; each rep group has a query of length 128. `passage_lengths`: at least 64; each rep group has a passage of length 512. `positive`: indices within a rep group are distinct; the last query of each group counts. `prefix_lengths`: rising multiples of 8, the last equal to 256. `owners`: distinct slots; slot s lies on index s // 17 of blk; some index of blk holds 17 blocks.
All inputs are finite; a program needn't handle non-finite values.
Results may differ from the reference program's by a relative error of at most 0.029.
Values may be sent and summed in bfloat16 or wider, within the bound.
No kernel may reach another device: no remote copies, remote signals or barrier semaphores. Data moves between devices by JAX's collectives and lax.ppermute only.
A program may use at most 320 MiB of HBM per device.

```python
import math
import jax
import jax.numpy as jnp
import numpy as np
from jax import lax

D = 256
HEADS = 4
FF = 1024
VOCAB = 30592
LAYERS = 1
QLEN = 128
PLEN = 512
PAIRS_DEV = 2
NPRE = 6
UROWS = 128
STEP = 7
PAIRS_BLK = 32
UNITS = 269
SLOTS = 17
NVEC = 16
N_BLK = 16
N_REP = 2


def ragged(seed_key, longest, shortest):
    drawn = jax.random.randint(seed_key, (N_REP, PAIRS_BLK), shortest, longest + 1)
    chosen = jax.random.randint(jax.random.fold_in(seed_key, 1), (N_REP, 1), 0, PAIRS_BLK)
    return jnp.where(jnp.arange(PAIRS_BLK)[None, :] == chosen, longest, drawn).astype(jnp.int32)


def draw_query_lengths(key, part):
    key = jax.random.fold_in(key, 11)
    return ragged(key, QLEN, max(QLEN // 4, 1))


def draw_passage_lengths(key, part):
    key = jax.random.fold_in(key, 12)
    return ragged(key, PLEN, max(PLEN // 8, 1))


def draw_positive(key, part):
    key = jax.random.fold_in(key, 13)
    orders = jax.vmap(lambda row_key: jax.random.permutation(row_key, PAIRS_BLK))(jax.random.split(key, N_REP))
    chance = jax.random.randint(jax.random.fold_in(key, 1), (N_REP, PAIRS_BLK), 0, 1000)
    places = jnp.arange(PAIRS_BLK)
    threshold = 300 + 600 * places // max(PAIRS_BLK - 1, 1)
    counted = (chance < threshold[None, :]) | (places[None, :] == PAIRS_BLK - 1)
    return jnp.where(counted, orders, -1).astype(jnp.int32)


def draw_prefix_lengths(key, part):
    key = jax.random.fold_in(key, 14)
    picked = jax.random.permutation(key, D // 8 - 1)[:NPRE - 1]
    return jnp.concatenate([jnp.sort((picked + 1) * 8), jnp.full((1,), D)]).astype(jnp.int32)


def draw_owners(key, part):
    key = jax.random.fold_in(key, 15)
    total_slots = N_BLK * SLOTS
    shuffled = jax.random.permutation(key, total_slots)
    busiest = jax.random.randint(jax.random.fold_in(key, 1), (), 0, N_BLK)
    scores = shuffled - total_slots * (jnp.arange(total_slots) // SLOTS == busiest).astype(jnp.int32)
    return jnp.argsort(scores)[:UNITS].astype(jnp.int32)


def draw_vectors(key, part):
    key = jax.random.fold_in(key, 16)
    noise = jnp.clip(0.1 * jax.random.normal(key, (NVEC, D), jnp.float32), -0.5, 0.5)
    rows_all = jnp.arange(NVEC)
    within = (rows_all - 4) % (8 + FF // D)
    gain_rows = (rows_all == 1) | (rows_all >= 4) & ((within == 4) | (within == 6))
    return jnp.where(gain_rows[:, None], 1.0 + noise, noise).astype(jnp.float32)


def with_ends(array, stream_key, least, high):
    longest = array.shape.index(max(array.shape))
    spots = []
    for shift in (0, 1):
        where = [jax.random.randint(jax.random.fold_in(stream_key, axis), (), 0, length) for axis, length in enumerate(array.shape)]
        where[longest] = (where[longest] + shift) % array.shape[longest]
        spots.append(tuple(where))
    return array.at[spots[0]].set(least).at[spots[1]].set(high)


def steps_of(stream_key, shape, cuts, smallest, high):
    def one(position, parts):
        draws = jax.random.uniform(jax.random.fold_in(jax.random.fold_in(stream_key, 6), position), (parts,), jnp.float32, smallest / len(cuts), high / len(cuts))
        return jnp.repeat(jnp.exp(draws), shape[position] // parts).reshape((-1,) + (1,) * (len(shape) - position - 1))

    factor_of = one(*cuts[0])
    for cut in cuts[1:]:
        factor_of = factor_of * one(*cut)
    return factor_of


def rank_table(amount, skew):
    weights = [(1 << 20) // math.isqrt(rank ** skew) + 1 for rank in range(1, amount + 1)]
    scale = 1 + sum(weights) // (1 << 30)
    return np.cumsum(np.array([max(1, weight // scale) for weight in weights]))


def ranked(rng, extent, number_of, slope):
    listing = rank_table(number_of, slope)
    ticket = jax.random.randint(jax.random.fold_in(rng, 1), extent, 0, int(listing[number_of - 1]))
    rank = jnp.searchsorted(jnp.asarray(listing, jnp.int32), ticket, side="right")
    return jax.random.permutation(jax.random.fold_in(rng, 2), number_of)[rank].astype(jnp.int32)


def normal_values(stream_key, extent, scale, most, shards=(), held_as=jnp.bfloat16):
    gain = steps_of(stream_key, extent, shards, -0.22, 0.18) if shards else 1.0
    values = jax.random.normal(stream_key, extent, jnp.float32) * scale * gain
    return jnp.minimum(jnp.maximum(values, -most), most).astype(held_as)


def setup_inputs(seed: int = 0) -> dict:
    key_list = jax.random.split(jax.random.key(seed), 15)
    query_ids = with_ends(ranked(key_list[0], (N_REP, PAIRS_BLK, QLEN), VOCAB, 2), jax.random.fold_in(key_list[0], 3), 0, VOCAB - 1).astype(jnp.int32)
    passage_ids = with_ends(ranked(key_list[1], (N_REP, PAIRS_BLK, PLEN), VOCAB, 2), jax.random.fold_in(key_list[1], 3), 0, VOCAB - 1).astype(jnp.int32)
    query_lengths = draw_query_lengths(jax.random.fold_in(key_list[14], 71), 0)
    passage_lengths = draw_passage_lengths(jax.random.fold_in(key_list[14], 71), 0)
    positive = draw_positive(jax.random.fold_in(key_list[14], 71), 0)
    prefix_lengths = draw_prefix_lengths(jax.random.fold_in(key_list[14], 71), 0)
    prefix_weights = jnp.clip(jnp.exp(jax.random.uniform(key_list[6], (NPRE,), jnp.float32, math.log(0.5), math.log(2.0))), 0.5, 2.0)
    owners = draw_owners(jax.random.fold_in(key_list[14], 71), 0)
    weights = normal_values(key_list[8], (N_BLK * SLOTS, UROWS, D), D ** -0.5, 0.375, ((0, 16),), jnp.float32)
    first_moments = normal_values(key_list[9], (N_BLK * SLOTS, UROWS, D), (0.0011 / (UNITS * UROWS * D) ** 0.5), 5.7220458984375e-06, ((0, 16),), jnp.float32)
    second_moments = jnp.clip(jnp.exp(math.log(4.5379298870039733e-14) - 1.3862944 * jax.random.uniform(key_list[10], (N_BLK * SLOTS, UROWS, D), jnp.float32) ** steps_of(key_list[10], (N_BLK * SLOTS, UROWS, D), ((0, 16),), -0.2, 0.2)), 1.1344824717509933e-14, 4.5379298870039733e-14)
    vectors = draw_vectors(jax.random.fold_in(key_list[14], 71), 0)
    vector_first = normal_values(key_list[12], (NVEC, D), (0.004 / (UNITS * UROWS * D) ** 0.5), 1.9073486328125e-05, (), jnp.float32)
    vector_second = jnp.clip(jnp.exp(jax.random.uniform(key_list[13], (NVEC, D), jnp.float32, math.log(1.493519283940481e-12), math.log(4.779261708609539e-11))), 1.493519283940481e-12, 4.779261708609539e-11)
    return dict(query_ids=query_ids, passage_ids=passage_ids, query_lengths=query_lengths, passage_lengths=passage_lengths, positive=positive, prefix_lengths=prefix_lengths, prefix_weights=prefix_weights, owners=owners, weights=weights, first_moments=first_moments, second_moments=second_moments, vectors=vectors, vector_first=vector_first, vector_second=vector_second)


TEMPER = 8.0
CLIP_AT = 0.01
RATE = 0.06
VECTOR_RATE = 0.8
BETA_ONE = 0.9
BETA_TWO = 0.999
DECAY = 0.01
EPSILON = 1e-08
NORM_EPS = 1e-06
HUGE = 1000000000.0
HIGHEST = lax.Precision.HIGHEST

@jax.custom_vjp
def low(v):
    return lax.optimization_barrier(v.astype(jnp.bfloat16)).astype(jnp.float32)

@jax.custom_vjp
def low_back(v):
    return v

def low_keep(v):
    return (low(v), None)

def low_pass(kept, grad):
    return (grad,)

def back_keep(v):
    return (v, None)

def back_low(kept, grad):
    return (low(grad),)
low.defvjp(low_keep, low_pass)
low_back.defvjp(back_keep, back_low)

def matmul(left_op, right_op):
    return jnp.dot(left_op, right_op, precision=HIGHEST)

def norm_rows(values_in, gain_row, shift_row):
    centred = values_in - lax.optimization_barrier(jnp.mean(values_in, -1, keepdims=True))
    inv_scale = lax.rsqrt(lax.optimization_barrier(jnp.mean(centred * centred, -1, keepdims=True)) + NORM_EPS)
    return centred * inv_scale * gain_row + shift_row

def layer(hidden_in, flat_rows, vectors, key_keep, layer_index):
    offset = VOCAB + PLEN + D + layer_index * (4 * D + 2 * FF)
    w_query = flat_rows[offset:offset + D]
    w_key = flat_rows[offset + D:offset + 2 * D]
    w_value = flat_rows[offset + 2 * D:offset + 3 * D]
    w_out = flat_rows[offset + 3 * D:offset + 4 * D]
    w_up = flat_rows[offset + 4 * D:offset + 4 * D + FF]
    w_down = flat_rows[offset + 4 * D + FF:offset + 4 * D + 2 * FF]
    row_base = 4 + layer_index * (8 + FF // D)
    vec_rows = vectors[row_base:row_base + 8 + FF // D]
    groups, seq_len = key_keep.shape
    head_size = D // HEADS
    head_shape = (groups, seq_len, HEADS, head_size)
    in_low = low(hidden_in)
    queries = low(low_back(matmul(in_low, w_query) + vec_rows[0]))
    key_rows = low(low_back(matmul(in_low, w_key)))
    value_rows = low(low_back(matmul(in_low, w_value) + vec_rows[1]))
    scores = jnp.einsum('glhd,gmhd->ghlm', queries.reshape(head_shape), key_rows.reshape(head_shape), precision=HIGHEST) * head_size ** (-0.5)
    scores = low_back(jnp.where(key_keep[:, None, None, :], scores, -HUGE))
    attn_probs = jax.nn.softmax(scores, -1)
    blended = jnp.einsum('ghlm,gmhd->glhd', low(attn_probs), value_rows.reshape(head_shape), precision=HIGHEST).reshape(groups, seq_len, D)
    blend_low = low(low_back(blended))
    summed = hidden_in + low_back(matmul(blend_low, w_out) + vec_rows[2])
    normal_one = norm_rows(summed, vec_rows[4], vec_rows[5])
    up_in = low_back(matmul(low(normal_one), w_up.T) + vec_rows[8:].reshape(FF))
    acted = low(jax.nn.gelu(up_in, approximate=False))
    second = normal_one + low_back(matmul(acted, w_down) + vec_rows[3])
    return norm_rows(second, vec_rows[6], vec_rows[7])

def embed_sequences(flat_rows, vectors, token_ids, lengths):
    groups, seq_len = token_ids.shape
    key_keep = jnp.arange(seq_len)[None, :] < lengths[:, None]
    embedded = flat_rows[token_ids] + flat_rows[VOCAB:VOCAB + seq_len][None] + vectors[0]
    hidden_now = norm_rows(embedded, vectors[1], vectors[2])
    for layer_index in range(LAYERS):
        hidden_now = layer(hidden_now, flat_rows, vectors, key_keep, layer_index)
    first_rows = low(hidden_now[:, 0])
    return jnp.tanh(matmul(first_rows, flat_rows[VOCAB + PLEN:VOCAB + PLEN + D]) + vectors[3])

def contrast(query_emb, passage_emb, positive, prefix_lengths, prefix_weights):
    prefix_masks = (jnp.arange(D)[None, :] < prefix_lengths[:, None]).astype(jnp.float32)
    prefix_scale = TEMPER * lax.rsqrt(prefix_lengths.astype(jnp.float32))
    masked = query_emb[None] * prefix_masks[:, None, :]
    logits = jnp.einsum('mpd,jd->mpj', masked, passage_emb, precision=HIGHEST) * prefix_scale[:, None, None]
    target = (jnp.arange(passage_emb.shape[0])[None, :] == positive[:, None]).astype(jnp.float32)
    running_totals = jax.nn.logsumexp(logits, -1) - lax.optimization_barrier(jnp.sum(logits * target[None], -1))
    per_query = lax.optimization_barrier(jnp.sum(prefix_weights[:, None] * running_totals, 0))
    return jnp.sum(jnp.where(positive >= 0, per_query, 0.0))

def total_loss(flat_rows, vectors, query_ids, passage_ids, query_lengths, passage_lengths, positive, prefix_lengths, prefix_weights):
    encoder = jax.checkpoint(lambda pieces: embed_sequences(flat_rows, vectors, pieces[0], pieces[1]))
    batches = N_REP * N_BLK
    query_pooled = lax.map(encoder, (query_ids.reshape(batches, PAIRS_DEV, QLEN), query_lengths.reshape(batches, PAIRS_DEV))).reshape(N_REP, PAIRS_BLK, D)
    passage_pooled = lax.map(encoder, (passage_ids.reshape(batches, PAIRS_DEV, PLEN), passage_lengths.reshape(batches, PAIRS_DEV))).reshape(N_REP, PAIRS_BLK, D)
    loss_total = jnp.zeros((), jnp.float32)
    for replica in range(N_REP):
        loss_total = loss_total + contrast(low(query_pooled[replica]), low(passage_pooled[replica]), positive[replica], prefix_lengths, prefix_weights)
    return loss_total

def adam_step(weight, moment_one, moment_two, gradient, step_rate, decay_rate):
    moment_one = BETA_ONE * moment_one + (1.0 - BETA_ONE) * gradient
    moment_two = BETA_TWO * moment_two + (1.0 - BETA_TWO) * gradient * gradient
    update = moment_one / (1.0 - BETA_ONE ** STEP) / (jnp.sqrt(moment_two / (1.0 - BETA_TWO ** STEP)) + EPSILON)
    return (weight - step_rate * (update + decay_rate * weight), moment_one, moment_two)

def reference(query_ids, passage_ids, query_lengths, passage_lengths, positive, prefix_lengths, prefix_weights, owners, weights, first_moments, second_moments, vectors, vector_first, vector_second):
    flat_rows = low(jnp.take(weights, owners, axis=0).reshape(-1, D))

    def objective(flat_in, vec_in):
        return total_loss(flat_in, vec_in, query_ids, passage_ids, query_lengths, passage_lengths, positive, prefix_lengths, prefix_weights)
    loss_sum, pull_back = jax.vjp(objective, flat_rows, vectors)
    valid_count = jnp.sum((positive >= 0).astype(jnp.float32))
    grad_flat, grad_vec = pull_back(1.0 / valid_count)
    buffer = jnp.zeros(weights.shape, jnp.float32).at[owners].set(grad_flat.reshape(-1, UROWS, D))
    clip_norm = jnp.sqrt(jnp.sum(buffer * buffer) + jnp.sum(grad_vec * grad_vec))
    factor = CLIP_AT / jnp.maximum(clip_norm, CLIP_AT)
    new_weight, new_first, new_second = adam_step(weights, first_moments, second_moments, buffer * factor, RATE, DECAY)
    owned_mask = jnp.any(jnp.arange(weights.shape[0])[:, None] == owners[None, :], 1)[:, None, None]
    new_weight = jnp.where(owned_mask, new_weight, weights)
    new_first = jnp.where(owned_mask, new_first, first_moments)
    new_second = jnp.where(owned_mask, new_second, second_moments)
    new_vec, new_vec_first, new_vec_second = adam_step(vectors, vector_first, vector_second, grad_vec * factor, VECTOR_RATE, 0.0)
    return (new_weight, new_first, new_second, new_vec, new_vec_first, new_vec_second, loss_sum, valid_count, clip_norm)
```

```python
from functools import partial

import jax
import jax.numpy as jnp
from jax import lax
from jax.experimental import pallas as pl
from jax.experimental.pallas import tpu as pltpu
from jax.sharding import PartitionSpec as P

D = 256
HEADS = 4
FF = 1024
VOCAB = 30592
LAYERS = 1
PLEN = 512
STEP = 7


TEMPER = 8.0
CLIP_AT = 0.01
RATE = 0.06
VECTOR_RATE = 0.8
BETA_ONE = 0.9
BETA_TWO = 0.999
DECAY = 0.01
EPSILON = 1e-08
NORM_EPS = 1e-06
HUGE = 1000000000.0
HIGHEST = lax.Precision.HIGHEST


def mult(left_op, right_op):
    return jnp.dot(left_op, right_op, preferred_element_type=jnp.float32)


def mult_tn(left_op, right_op):
    return lax.dot_general(
        left_op, right_op, (((0,), (0,)), ((), ())), preferred_element_type=jnp.float32
    )


def mult_nt(left_op, right_op):
    return lax.dot_general(
        left_op, right_op, (((1,), (1,)), ((), ())), preferred_element_type=jnp.float32
    )


def norm_rows(values_in, gain_row, shift_row):
    centred = values_in - jnp.mean(values_in, -1, keepdims=True)
    inv_scale = lax.rsqrt(jnp.mean(centred * centred, -1, keepdims=True) + NORM_EPS)
    normed = centred * inv_scale
    return (normed * gain_row + shift_row, normed, inv_scale)


def norm_back(incoming, normed, inv_scale, gain_row):
    dnormed = incoming * gain_row
    inner_part = (
        dnormed
        - jnp.mean(dnormed, -1, keepdims=True)
        - normed * jnp.mean(dnormed * normed, -1, keepdims=True)
    )
    return (inner_part * inv_scale, jnp.sum(incoming * normed, 0), jnp.sum(incoming, 0))


def layer_parts(flat_rows, vectors, layer_index):
    offset = VOCAB + PLEN + D + layer_index * (4 * D + 2 * FF)
    w_qkv = jnp.concatenate(
        [
            flat_rows[offset : offset + D],
            flat_rows[offset + D : offset + 2 * D],
            flat_rows[offset + 2 * D : offset + 3 * D],
        ],
        1,
    )
    w_out = flat_rows[offset + 3 * D : offset + 4 * D]
    w_up = flat_rows[offset + 4 * D : offset + 4 * D + FF]
    w_down = flat_rows[offset + 4 * D + FF : offset + 4 * D + 2 * FF]
    row_base = 4 + layer_index * (8 + FF // D)
    return ((w_qkv, w_out, w_up, w_down), vectors[row_base : row_base + 8 + FF // D])


def divide_into_heads(packed_buffer, column):
    return packed_buffer[:, column * D : (column + 1) * D].reshape(
        packed_buffer.shape[0], HEADS, D // HEADS
    )


def attend_probs(packed_buffer, key_keep):
    scores = jnp.einsum(
        "cnp,fnp->ncf",
        divide_into_heads(packed_buffer, 0),
        divide_into_heads(packed_buffer, 1),
        preferred_element_type=jnp.float32,
    ) * (D // HEADS) ** (-0.5)
    scores = jnp.where(key_keep[None, None, :], scores, -HUGE)
    return jax.nn.softmax(scores, -1)


def attend(pieces):
    packed_buffer, key_keep = pieces
    attn_probs = attend_probs(packed_buffer, key_keep)
    blended = jnp.einsum(
        "nbi,ins->bns",
        attn_probs.astype(jnp.bfloat16),
        divide_into_heads(packed_buffer, 2),
        preferred_element_type=jnp.float32,
    )
    return blended.reshape(packed_buffer.shape[0], D)


def attend_back(pieces):
    packed_buffer, key_keep, grad_out = pieces
    seq_len = packed_buffer.shape[0]
    head_scale = (D // HEADS) ** (-0.5)
    attn_probs = attend_probs(packed_buffer, key_keep)
    gradient_row_block = grad_out.reshape(seq_len, HEADS, D // HEADS)
    grad_values = jnp.einsum(
        "fxn,xfa->nfa",
        attn_probs.astype(jnp.bfloat16),
        gradient_row_block,
        preferred_element_type=jnp.float32,
    )
    grad_probs = jnp.einsum(
        "cnp,fnp->ncf",
        gradient_row_block,
        divide_into_heads(packed_buffer, 2),
        preferred_element_type=jnp.float32,
    )
    grad_scores = attn_probs * (grad_probs - jnp.sum(grad_probs * attn_probs, -1, keepdims=True))
    score_lowered = grad_scores.astype(jnp.bfloat16)
    grad_queries = (
        jnp.einsum(
            "nbi,ins->bns",
            score_lowered,
            divide_into_heads(packed_buffer, 1),
            preferred_element_type=jnp.float32,
        )
        * head_scale
    )
    grad_keys = (
        jnp.einsum(
            "fxn,xfa->nfa",
            score_lowered,
            divide_into_heads(packed_buffer, 0),
            preferred_element_type=jnp.float32,
        )
        * head_scale
    )
    return jnp.concatenate(
        [
            grad_queries.reshape(seq_len, D),
            grad_keys.reshape(seq_len, D),
            grad_values.reshape(seq_len, D),
        ],
        1,
    ).astype(jnp.bfloat16)


def layer_forward(hidden_in, weights_set, vec_rows, key_keep):
    w_qkv, w_out, w_up, w_down = weights_set
    groups, seq_len = key_keep.shape
    in_low = hidden_in.astype(jnp.bfloat16)
    bias_qkv = jnp.concatenate([vec_rows[0], jnp.zeros_like(vec_rows[0]), vec_rows[1]])
    packed_buffer = (mult(in_low, w_qkv) + bias_qkv).astype(jnp.bfloat16)
    blended = lax.map(attend, (packed_buffer.reshape(groups, seq_len, 3 * D), key_keep))
    blend_low = blended.reshape(groups * seq_len, D).astype(jnp.bfloat16)
    summed = hidden_in + mult(blend_low, w_out) + vec_rows[2]
    normal_one, normed_one, scale_one = norm_rows(summed, vec_rows[4], vec_rows[5])
    normal_low = normal_one.astype(jnp.bfloat16)
    up_in = mult_nt(normal_low, w_up) + vec_rows[8:].reshape(FF)
    acted = jax.nn.gelu(up_in, approximate=False).astype(jnp.bfloat16)
    second = normal_one + mult(acted, w_down) + vec_rows[3]
    result, normed_two, scale_two = norm_rows(second, vec_rows[6], vec_rows[7])
    return (
        result,
        (
            in_low,
            packed_buffer,
            blend_low,
            normed_one,
            scale_one,
            normal_low,
            up_in,
            acted,
            normed_two,
            scale_two,
        ),
    )


def layer_backward(grad_out, weights_set, vec_rows, key_keep, saved):
    w_qkv, w_out, w_up, w_down = weights_set
    (
        in_low,
        packed_buffer,
        blend_low,
        normed_one,
        scale_one,
        normal_low,
        up_in,
        acted,
        normed_two,
        scale_two,
    ) = saved
    groups, seq_len = key_keep.shape
    grad_second, grad_gain_two, grad_shift_two = norm_back(
        grad_out, normed_two, scale_two, vec_rows[6]
    )
    down_low = grad_second.astype(jnp.bfloat16)
    grad_down = mult_tn(acted, down_low)
    grad_acted = mult_nt(down_low, w_down)
    gelu_pull = jax.vjp(partial(jax.nn.gelu, approximate=False), up_in)[1]
    up_low = gelu_pull(grad_acted)[0].astype(jnp.bfloat16)
    grad_up = mult_tn(up_low, normal_low)
    grad_normal = grad_second + mult(up_low, w_up)
    grad_summed, gradient_first_gain, grad_shift_one = norm_back(
        grad_normal, normed_one, scale_one, vec_rows[4]
    )
    branch_low = grad_summed.astype(jnp.bfloat16)
    grad_wout = mult_tn(blend_low, branch_low)
    blend_grad = mult_nt(branch_low, w_out).astype(jnp.bfloat16)
    grad_packed = lax.map(
        attend_back,
        (
            packed_buffer.reshape(groups, seq_len, 3 * D),
            key_keep,
            blend_grad.reshape(groups, seq_len, D),
        ),
    ).reshape(groups * seq_len, 3 * D)
    grad_wqkv = mult_tn(in_low, grad_packed)
    grad_in = grad_summed + mult_nt(grad_packed, w_qkv)
    packed_sum = jnp.sum(grad_packed.astype(jnp.float32), 0)
    matrix_grads = jnp.concatenate(
        [
            grad_wqkv[:, :D],
            grad_wqkv[:, D : 2 * D],
            grad_wqkv[:, 2 * D :],
            grad_wout,
            grad_up,
            grad_down,
        ],
        0,
    )
    vector_grads = jnp.concatenate(
        [
            jnp.stack(
                [
                    packed_sum[:D],
                    packed_sum[2 * D :],
                    jnp.sum(branch_low.astype(jnp.float32), 0),
                    jnp.sum(down_low.astype(jnp.float32), 0),
                    gradient_first_gain,
                    grad_shift_one,
                    grad_gain_two,
                    grad_shift_two,
                ]
            ),
            jnp.sum(up_low.astype(jnp.float32), 0).reshape(FF // D, D),
        ],
        0,
    )
    return (grad_in, matrix_grads, vector_grads)


def embed_sequences(flat_rows, vectors, token_ids, lengths):
    groups, seq_len = token_ids.shape
    key_keep = jnp.arange(seq_len)[None, :] < lengths[:, None]
    table_rows = jnp.take(flat_rows, token_ids.reshape(-1), axis=0).astype(jnp.float32)
    places = flat_rows[VOCAB : VOCAB + seq_len].astype(jnp.float32)
    embedded = (table_rows.reshape(groups, seq_len, D) + places[None] + vectors[0]).reshape(
        groups * seq_len, D
    )
    hidden_now, normed_emb, scaled_embedding = norm_rows(embedded, vectors[1], vectors[2])
    weights_set, vec_rows = layer_parts(flat_rows, vectors, 0)
    hidden_now, saved = layer_forward(hidden_now, weights_set, vec_rows, key_keep)
    layer_saves = [saved]
    first_rows = hidden_now.reshape(groups, seq_len, D)[:, 0].astype(jnp.bfloat16)
    pooled = jnp.tanh(mult(first_rows, flat_rows[VOCAB + PLEN : VOCAB + PLEN + D]) + vectors[3])
    return (pooled, (normed_emb, scaled_embedding, layer_saves, first_rows))


def encode_back(grad_pooled, pooled, flat_rows, vectors, token_ids, lengths, encoder_kept):
    normed_emb, scaled_embedding, layer_saves, first_rows = encoder_kept
    groups, seq_len = token_ids.shape
    key_keep = jnp.arange(seq_len)[None, :] < lengths[:, None]
    w_pool = flat_rows[VOCAB + PLEN : VOCAB + PLEN + D].astype(jnp.float32)
    grad_pre = grad_pooled * (1.0 - pooled * pooled)
    grad_pool = jnp.dot(first_rows.astype(jnp.float32).T, grad_pre, precision=HIGHEST)
    grad_first = jnp.dot(grad_pre, w_pool.T, precision=HIGHEST)
    grad_hidden = (
        jnp.zeros((groups, seq_len, D), jnp.float32)
        .at[:, 0]
        .set(grad_first)
        .reshape(groups * seq_len, D)
    )
    matrices = []
    vector_parts = []
    for layer_index in reversed(range(LAYERS)):
        weights_set, vec_rows = layer_parts(flat_rows, vectors, layer_index)
        grad_hidden, matrix_grads, vector_grads = layer_backward(
            grad_hidden, weights_set, vec_rows, key_keep, layer_saves[layer_index]
        )
        matrices.insert(0, matrix_grads)
        vector_parts.insert(0, vector_grads)
    grad_embed, grad_gain, grad_shift = norm_back(
        grad_hidden, normed_emb, scaled_embedding, vectors[1]
    )
    grad_table = jnp.zeros((VOCAB, D), jnp.float32).at[token_ids.reshape(-1)].add(grad_embed)
    grad_places = (
        jnp.zeros((PLEN, D), jnp.float32)
        .at[:seq_len]
        .set(jnp.sum(grad_embed.reshape(groups, seq_len, D), 0))
    )
    flat_grad = jnp.concatenate([grad_table, grad_places, grad_pool] + matrices, 0)
    head_rows = jnp.stack([jnp.sum(grad_embed, 0), grad_gain, grad_shift, jnp.sum(grad_pre, 0)])
    return (flat_grad, jnp.concatenate([head_rows] + vector_parts, 0))


def adam_step(weight, moment_one, moment_two, gradient, step_rate, decay_rate):
    moment_one = BETA_ONE * moment_one + (1.0 - BETA_ONE) * gradient
    moment_two = BETA_TWO * moment_two + (1.0 - BETA_TWO) * gradient * gradient
    update = (
        moment_one
        / (1.0 - BETA_ONE**STEP)
        / (jnp.sqrt(moment_two / (1.0 - BETA_TWO**STEP)) + EPSILON)
    )
    return (weight - step_rate * (update + decay_rate * weight), moment_one, moment_two)


def local(
    query_ids,
    passage_ids,
    query_lengths,
    passage_lengths,
    positive,
    prefix_lengths,
    prefix_weights,
    owners,
    weights,
    first_moments,
    second_moments,
    vectors,
    vector_first,
    vector_second,
):
    slot_count, unit_rows = (weights.shape[0], weights.shape[1])
    gathered = lax.all_gather(weights.astype(jnp.bfloat16), "blk", axis=0, tiled=True)
    flat_rows = jnp.take(gathered, owners, axis=0).reshape(-1, D)
    query_pooled, query_kept = embed_sequences(flat_rows, vectors, query_ids[0], query_lengths[0])
    passage_pooled, passage_kept = embed_sequences(
        flat_rows, vectors, passage_ids[0], passage_lengths[0]
    )
    all_passages = lax.all_gather(passage_pooled.astype(jnp.bfloat16), "blk", axis=0, tiled=True)
    prefix_masks = (jnp.arange(D)[None, :] < prefix_lengths[:, None]).astype(jnp.float32)
    prefix_scale = TEMPER * lax.rsqrt(prefix_lengths.astype(jnp.float32))
    queries = query_pooled.astype(jnp.bfloat16).astype(jnp.float32)
    passages = all_passages.astype(jnp.float32)
    masked = queries[None] * prefix_masks[:, None, :]
    logits = (
        jnp.einsum("mpd,jd->mpj", masked, passages, precision=HIGHEST) * prefix_scale[:, None, None]
    )
    counted = positive[0] >= 0
    target = (jnp.arange(passages.shape[0])[None, :] == positive[0][:, None]).astype(jnp.float32)
    running_totals = jax.nn.logsumexp(logits, -1) - jnp.sum(logits * target[None], -1)
    per_query = jnp.sum(prefix_weights[:, None] * running_totals, 0)
    loss_part = jnp.sum(jnp.where(counted, per_query, 0.0))
    count_part = jnp.sum(counted.astype(jnp.float32))
    count_total, loss_total = lax.psum((count_part, loss_part), ("blk", "rep"))
    row_factor = (prefix_weights * prefix_scale / count_total)[:, None, None] * counted.astype(
        jnp.float32
    )[None, :, None]
    grad_logits = (jax.nn.softmax(logits, -1) - target[None]) * row_factor
    grad_query = jnp.sum(
        jnp.einsum("mpj,jd->mpd", grad_logits, passages, precision=HIGHEST)
        * prefix_masks[:, None, :],
        0,
    )
    grad_passage = lax.psum_scatter(
        jnp.einsum("mpj,mpd->jd", grad_logits, masked, precision=HIGHEST),
        "blk",
        scatter_dimension=0,
        tiled=True,
    )
    flat_query, vec_query = encode_back(
        grad_query, query_pooled, flat_rows, vectors, query_ids[0], query_lengths[0], query_kept
    )
    flat_pass, vec_pass = encode_back(
        grad_passage,
        passage_pooled,
        flat_rows,
        vectors,
        passage_ids[0],
        passage_lengths[0],
        passage_kept,
    )
    vec_total = lax.psum(vec_query + vec_pass, ("blk", "rep"))
    buffer = (
        jnp.zeros((lax.axis_size("blk") * slot_count, unit_rows, D), jnp.float32)
        .at[owners]
        .set((flat_query + flat_pass).reshape(-1, unit_rows, D))
    )
    vec_square = jnp.sum(vec_total * vec_total)
    reduced = lax.psum_scatter(buffer, "blk", scatter_dimension=0, tiled=True)
    reduced = lax.psum(reduced, "rep")
    square_sum = lax.psum(jnp.sum(reduced * reduced), "blk")
    old_weight, old_first, old_second = (weights, first_moments, second_moments)
    slot_ids = lax.axis_index("blk") * slot_count + jnp.arange(slot_count)
    owned_mask = jnp.any(slot_ids[:, None] == owners[None, :], 1)[:, None, None]
    grad_norm = jnp.sqrt(square_sum + vec_square)
    factor = CLIP_AT / jnp.maximum(grad_norm, CLIP_AT)
    new_weight, new_first, new_second = adam_step(
        old_weight, old_first, old_second, reduced * factor, RATE, DECAY
    )
    new_weight = jnp.where(owned_mask, new_weight, old_weight)
    new_first = jnp.where(owned_mask, new_first, old_first)
    new_second = jnp.where(owned_mask, new_second, old_second)
    new_vec, new_vec_first, new_vec_second = adam_step(
        vectors, vector_first, vector_second, vec_total * factor, VECTOR_RATE, 0.0
    )
    return (
        new_weight,
        new_first,
        new_second,
        new_vec,
        new_vec_first,
        new_vec_second,
        loss_total,
        count_total,
        grad_norm,
    )


F32 = jnp.float32
BF16 = jnp.bfloat16
I32 = jnp.int32
UNIT = 128
TABLE_BLOCKS = VOCAB // UNIT
PLACE_BLOCKS = PLEN // UNIT
DENSE = PLACE_BLOCKS + (D + 4 * D + 2 * FF) // UNIT
HALF = 64
QROWS = 128
TOKENS = 2 * QROWS + 2 * PLEN
STARTS = (0, QROWS, 2 * QROWS, 2 * QROWS + PLEN)
UNITS_L = 12
L_ROWS = 4 * UNITS_L
NEVER = -1e30
PARAMS = pltpu.CompilerParams(vmem_limit_bytes=56 << 20)

AT_POOL = PLEN
AT_Q = AT_POOL + D
AT_K = AT_Q + D
AT_V = AT_K + D
AT_O = AT_V + D
AT_UP = AT_O + D
AT_DOWN = AT_UP + FF

TAB_PLACE, TAB_OWNER, TAB_UNIT, TAB_SLOT, TAB_KIND, TAB_FLAG = 0, 32, 64, 96, 128, 160
TAB_SIZE = 256

KIND_TABLE, KIND_PLACE, KIND_DENSE = 1, 2, 8

vmem = pl.BlockSpec(memory_space=pltpu.VMEM)
smem = pl.BlockSpec(memory_space=pltpu.SMEM)
hbm = pl.BlockSpec(memory_space=pl.ANY)


def iota(shape, axis):
    return lax.broadcasted_iota(I32, shape, axis)


def dot_nn(a, b):
    return lax.dot_general(a, b, (((1,), (0,)), ((), ())), preferred_element_type=F32)


def dot_nt(a, b):
    return lax.dot_general(a, b, (((1,), (1,)), ((), ())), preferred_element_type=F32)


def dot_tn(a, b):
    return lax.dot_general(a, b, (((0,), (0,)), ((), ())), preferred_element_type=F32)


def split(a):
    high = a.astype(BF16)
    return high, (a - high.astype(F32)).astype(BF16)


def fine(dot, a, b):
    high, low = split(a)
    rows = a.shape[0]
    both = dot(jnp.concatenate([high, low], 0), b)
    return both[:rows] + both[rows:]


def to_column(row):
    return jnp.broadcast_to(row, (128, 128)).T[:, :1]


def token_facts(query_lengths, passage_lengths):
    lane = iota((1, TOKENS), 1)
    sequence = (
        (lane >= STARTS[1]).astype(I32)
        + (lane >= STARTS[2]).astype(I32)
        + (lane >= STARTS[3]).astype(I32)
    )
    ends = [
        STARTS[0] + query_lengths[0, 0],
        STARTS[1] + query_lengths[0, 1],
        STARTS[2] + passage_lengths[0, 0],
        STARTS[3] + passage_lengths[0, 1],
    ]
    end = jnp.where(
        sequence == 0,
        ends[0],
        jnp.where(sequence == 1, ends[1], jnp.where(sequence == 2, ends[2], ends[3])),
    )
    return sequence, lane < end


def prepare_kernel(slots, cap, owners, me, weights, dense_out, tab, counts, units, block, sems):
    n_units = owners.shape[0]
    n_blk = counts.shape[0]

    def clear(i, c):
        counts[i] = 0
        units[i] = 0
        return c

    lax.fori_loop(0, n_blk, clear, 0)

    def wipe(i, c):
        tab[i] = 0
        return c

    lax.fori_loop(0, TAB_SIZE, wipe, 0)
    mine = me[0]
    base = n_units - DENSE

    def place(b, c):
        slot = owners[base + b]
        owner = slot // slots
        inside = slot - owner * slots
        rank = counts[owner]
        counts[owner] = rank + 1
        tab[TAB_PLACE + b] = owner * cap + jnp.minimum(rank, cap - 1)
        tab[TAB_OWNER + b] = owner
        tab[TAB_SLOT + b] = inside
        tab[TAB_FLAG] = jnp.maximum(tab[TAB_FLAG], (rank >= cap).astype(I32))

        @pl.when((owner == mine) & (rank < cap))
        def _():
            pltpu.make_async_copy(weights.at[inside], block.at[rank], sems.at[rank]).start()

        return c

    lax.fori_loop(0, DENSE, place, 0)
    have = counts[mine]
    for c in range(cap):

        @pl.when(c < have)
        def _():
            pltpu.make_async_copy(weights.at[0], block.at[c], sems.at[c]).wait()
            dense_out[c] = block[c].astype(BF16)

        @pl.when(c >= have)
        def _():
            dense_out[c] = jnp.zeros((UNIT, D), BF16)


def prepare(owners, me, weights, n_blk, cap):
    slots = weights.shape[0]
    return pl.pallas_call(
        partial(prepare_kernel, slots, cap),
        out_shape=(
            jax.ShapeDtypeStruct((cap, UNIT, D), BF16),
            jax.ShapeDtypeStruct((TAB_SIZE,), I32),
        ),
        in_specs=[smem, smem, hbm],
        out_specs=(vmem, smem),
        scratch_shapes=[
            pltpu.SMEM((n_blk,), I32),
            pltpu.SMEM((n_blk,), I32),
            pltpu.VMEM((cap, UNIT, D), F32),
            pltpu.SemaphoreType.DMA((cap,)),
        ],
        compiler_params=PARAMS,
        name="prepare",
    )(owners, me, weights)


def request_kernel(
    slots, n_blk, cap, owners, tab_in, me, positive, query_lengths, passage_lengths, owner_row,
    query_ids, passage_ids, message, where_row, tab, ids, units,
):
    n_rep = 2
    n_dest = n_blk * n_rep
    mine = me[0]
    n_units = owners.shape[0]

    def copy(i, c):
        tab[i] = tab_in[i]
        return c

    lax.fori_loop(0, TAB_SIZE, copy, 0)

    def clear(i, c):
        units[i] = 0
        return c

    lax.fori_loop(0, n_blk, clear, 0)

    def kind(b, c):
        inside = owners[b] - mine * slots

        @pl.when((inside >= 0) & (inside < slots))
        def _():
            tab[TAB_KIND + inside] = jnp.where(
                b < TABLE_BLOCKS,
                KIND_TABLE,
                jnp.where(
                    b < TABLE_BLOCKS + PLACE_BLOCKS, KIND_PLACE + b - TABLE_BLOCKS, KIND_DENSE
                ),
            )

        return c

    lax.fori_loop(0, n_units, kind, 0)
    for b in range(PLACE_BLOCKS, DENSE):
        owner = tab_in[TAB_OWNER + b]
        used = units[owner]
        need = 2 if AT_K <= b * UNIT < AT_O else 1
        units[owner] = used + need
        tab[TAB_UNIT + b] = jnp.minimum(used, UNITS_L - need)
        tab[TAB_FLAG] = jnp.maximum(tab[TAB_FLAG], (used + need > UNITS_L).astype(I32))

    ids[:, 0:QROWS] = query_ids[0:1]
    ids[:, QROWS : 2 * QROWS] = query_ids[1:2]
    ids[:, STARTS[2] : STARTS[3]] = passage_ids[0:1]
    ids[:, STARTS[3] :] = passage_ids[1:2]
    token = ids[...]
    _, live = token_facts(query_lengths, passage_lengths)
    lane = iota((1, TOKENS), 1)
    block = token // UNIT
    slot = jnp.zeros((1, TOKENS), I32)
    table_rows = -(-TABLE_BLOCKS // 128) * 128
    for at in range(0, table_rows, 128):
        column = to_column(owner_row[:, at : at + 128])
        hit = (iota((128, TOKENS), 0) + at) == block
        slot = slot + jnp.sum(jnp.where(hit, column, 0), 0, keepdims=True)
    owner = jnp.zeros((1, TOKENS), I32)
    for k in range(1, n_blk):
        owner = owner + (slot >= k * slots).astype(I32)
    inside = slot - owner * slots
    row = token - block * UNIT
    upper = (row >= HALF).astype(I32)
    dest = owner * n_rep + upper
    local_row = inside * HALF + row - upper * HALF
    token = jnp.where(live, token, -1)
    first_at = jnp.full((128, TOKENS), TOKENS, I32)
    for at in range(0, TOKENS, 128):
        column = to_column(token[:, at : at + 128])
        same = column == token
        first_at = jnp.minimum(first_at, jnp.where(same, iota((128, TOKENS), 0) + at, TOKENS))
    first_at = jnp.min(first_at, 0, keepdims=True)
    first = live & (first_at == lane)
    chosen = ((iota((n_dest, TOKENS), 0) == dest) & first).astype(F32)
    chosen_low = chosen.astype(BF16)
    seen = jnp.zeros((n_dest, TOKENS), F32)
    for at in range(0, TOKENS, 128):
        earlier = ((iota((128, TOKENS), 0) + at) < first_at).astype(F32).astype(BF16)
        seen = seen + dot_nn(chosen_low[:, at : at + 128], earlier)
    rank = jnp.sum(
        jnp.where(iota((n_dest, TOKENS), 0) == dest, seen, 0.0), 0, keepdims=True
    ).astype(I32)
    fits = live & (rank < cap)
    where_row[...] = jnp.where(fits, dest * cap + rank, -1)
    over = jnp.max((live & (rank >= cap)).astype(I32))
    code = local_row + 1
    high = code // 32
    low = code - high * 32
    spread = (iota((128, TOKENS), 0) == rank).astype(F32).astype(BF16)
    sent_high = dot_nt((chosen * high.astype(F32)).astype(BF16), spread)
    sent_low = dot_nt((chosen * low.astype(F32)).astype(BF16), spread)
    request = sent_high.astype(I32) * 32 + sent_low.astype(I32) - 1
    flag = jnp.maximum(over, tab[TAB_FLAG])
    column_of = iota((n_dest, 128), 1)
    out = jnp.where(column_of < cap, request, 0)
    out = jnp.where(column_of == 124, positive[0, 0], out)
    out = jnp.where(column_of == 125, positive[0, 1], out)
    message[...] = jnp.where(column_of == 126, flag, out)


def request(owners, tab, me, positive, query_lengths, passage_lengths, query_ids, passage_ids, slots, n_blk, cap):
    n_dest = 2 * n_blk
    table_rows = -(-TABLE_BLOCKS // 128) * 128
    owner_row = owners[:table_rows].reshape(1, table_rows)
    return pl.pallas_call(
        partial(request_kernel, slots, n_blk, cap),
        out_shape=(
            jax.ShapeDtypeStruct((n_dest, 128), I32),
            jax.ShapeDtypeStruct((1, TOKENS), I32),
            jax.ShapeDtypeStruct((TAB_SIZE,), I32),
        ),
        in_specs=[smem, smem, smem, smem, smem, smem, vmem, vmem, vmem],
        out_specs=(vmem, vmem, smem),
        scratch_shapes=[pltpu.VMEM((1, TOKENS), I32), pltpu.SMEM((n_blk,), I32)],
        compiler_params=PARAMS,
        name="request",
    )(owners, tab, me, positive, query_lengths, passage_lengths, owner_row, query_ids, passage_ids)


def fetch_kernel(slots, cap, me, message, weights, rows_out, held, table, hot, sem):
    n_dest = message.shape[0]
    half = me[1]
    copy = pltpu.make_async_copy(weights.at[:, pl.ds(half * HALF, HALF), :], held, sem)
    copy.start()
    wide = table.shape[0]
    rows = message[...]
    pad = -n_dest % 128
    if pad:
        rows = jnp.concatenate([rows, jnp.zeros((pad, 128), I32)], 0)
    columns = rows.T
    for s in range(n_dest):
        hot[s * cap : (s + 1) * cap] = (
            (iota((cap, wide), 1) == columns[:cap, s : s + 1]).astype(F32).astype(BF16)
        )
    copy.wait()
    filled = slots * HALF
    table[:filled] = held[...].reshape(filled, D).astype(BF16)
    if wide > filled:
        table[filled:] = jnp.zeros((wide - filled, D), BF16)
    rows_out[...] = dot_nn(hot[...], table[...]).astype(BF16)


def fetch(me, message, weights, cap):
    slots = weights.shape[0]
    n_dest = message.shape[0]
    wide = -(-slots * HALF // 128) * 128
    return pl.pallas_call(
        partial(fetch_kernel, slots, cap),
        out_shape=jax.ShapeDtypeStruct((n_dest * cap, D), BF16),
        in_specs=[smem, vmem, hbm],
        out_specs=vmem,
        scratch_shapes=[
            pltpu.VMEM((slots, HALF, D), F32),
            pltpu.VMEM((wide, D), BF16),
            pltpu.VMEM((n_dest * cap, wide), BF16),
            pltpu.SemaphoreType.DMA,
        ],
        compiler_params=PARAMS,
        name="fetch",
    )(me, message, weights)


ST_POOLED, ST_C, ST_N2, ST_N1, ST_H, ST_O, ST_Q, ST_X0 = range(0, 64, 8)
ST_KQ, ST_B, ST_U, ST_A, ST_I1, ST_I2 = 64, 96, 128, 160, 192, 200
ST_ROWS = 208


def start_matrices(tab, gathered, matrices, sems, first=0):
    for b in range(first, DENSE):
        pltpu.make_async_copy(
            gathered.at[tab[TAB_PLACE + b]], matrices.at[pl.ds(b * UNIT, UNIT)], sems.at[b]
        ).start()


def wait_matrices(gathered, matrices, sems, first=0):
    for b in range(first, DENSE):
        pltpu.make_async_copy(
            gathered.at[0], matrices.at[pl.ds(b * UNIT, UNIT)], sems.at[b]
        ).wait()


def forward_kernel(
    tab, query_lengths, passage_lengths, positive, rows, where_row, vectors, gathered,
    emb_out, low_out, normed_out, scale_out, probs_out, state, matrices, embedded, sems,
):
    start_matrices(tab, gathered, matrices, sems)
    taken = rows.shape[0]
    for at in range(0, TOKENS, 128):
        column = to_column(where_row[:, at : at + 128])
        hot = (iota((128, taken), 1) == column).astype(F32).astype(BF16)
        embedded[at : at + 128] = dot_nn(hot, rows[...])
    wait_matrices(gathered, matrices, sems)
    shift = vectors[0:1]
    for start, length in zip(STARTS, (QROWS, QROWS, PLEN, PLEN)):
        e = embedded[start : start + length] + matrices[:length].astype(F32) + shift
        centred = e - jnp.mean(e, -1, keepdims=True)
        scale = lax.rsqrt(jnp.mean(centred * centred, -1, keepdims=True) + NORM_EPS)
        normed = centred * scale
        normed_out[start : start + length] = normed
        scale_out[start : start + length] = jnp.broadcast_to(scale, (length, 128))
        x = normed * vectors[1:2] + vectors[2:3]
        embedded[start : start + length] = x
        low_out[start : start + length] = x.astype(BF16)
    x0 = jnp.concatenate(
        [embedded[s : s + 1] for s in STARTS] + [jnp.zeros((4, D), F32)], 0
    )
    x0_low = x0.astype(BF16)
    q = (dot_nn(x0_low, matrices[AT_Q:AT_K]) + vectors[4:5]).astype(BF16)
    head_of = iota((8, D), 1) // HALF
    q_heads = jnp.concatenate(
        [jnp.where(head_of == h, q.astype(F32), 0.0) for h in range(HEADS)], 0
    ).astype(BF16)
    kq = dot_nt(q_heads, matrices[AT_K:AT_V]) * (D // HEADS) ** (-0.5)
    low = low_out[...]
    scores = fine(dot_nt, kq, low)
    sequence, live = token_facts(query_lengths, passage_lengths)
    valid = ((iota((32, TOKENS), 0) & 7) == sequence) & live
    scores = jnp.where(valid, scores, NEVER)
    top = jnp.max(scores, -1, keepdims=True)
    weight = jnp.where(valid, jnp.exp(scores - top), 0.0)
    total = jnp.sum(weight, -1, keepdims=True)
    probs = weight / jnp.where(total > 0.0, total, 1.0)
    probs_out[...] = probs
    mixed = dot_nn(probs.astype(BF16), low)
    valued = fine(dot_nn, mixed, matrices[AT_V:AT_O])
    blended = jnp.zeros((8, D), F32)
    for h in range(HEADS):
        blended = blended + jnp.where(head_of == h, valued[8 * h : 8 * h + 8], 0.0)
    real = iota((8, D), 0) < 4
    blended = jnp.where(real, blended + vectors[5:6], 0.0).astype(BF16)
    summed = x0 + dot_nn(blended, matrices[AT_O:AT_UP]) + vectors[6:7]
    h0, n1, i1 = norm_rows(summed, vectors[8:9], vectors[9:10])
    h_low = h0.astype(BF16)
    bias_up = jnp.concatenate([vectors[12 + i : 13 + i] for i in range(FF // D)], 1)
    u = dot_nt(h_low, matrices[AT_UP:AT_DOWN]) + bias_up
    a = (0.5 * u * (1.0 + lax.erf(u * (0.5**0.5)))).astype(BF16)
    second = h0 + dot_nn(a, matrices[AT_DOWN:]) + vectors[7:8]
    x, n2, i2 = norm_rows(second, vectors[10:11], vectors[11:12])
    c = x.astype(BF16)
    pooled = jnp.tanh(dot_nn(c, matrices[AT_POOL:AT_Q]) + vectors[3:4])
    row8 = iota((8, 128), 0)
    sent = jnp.concatenate(
        [
            jnp.where(real, pooled, 0.0),
            jnp.where(
                row8 == 0,
                positive[0, 0].astype(F32),
                jnp.where(row8 == 1, positive[0, 1].astype(F32), -1.0),
            ),
        ],
        1,
    )
    n_blk = emb_out.shape[0] // 8
    emb_out[...] = jnp.concatenate([sent] * n_blk, 0).astype(BF16)
    state[ST_POOLED : ST_POOLED + 8] = pooled
    state[ST_C : ST_C + 8] = c.astype(F32)
    state[ST_N2 : ST_N2 + 8] = n2
    state[ST_N1 : ST_N1 + 8] = n1
    state[ST_H : ST_H + 8] = h_low.astype(F32)
    state[ST_O : ST_O + 8] = blended.astype(F32)
    state[ST_Q : ST_Q + 8] = q.astype(F32)
    state[ST_X0 : ST_X0 + 8] = x0_low.astype(F32)
    state[ST_KQ : ST_KQ + 32] = kq
    state[ST_B : ST_B + 32] = mixed
    for i in range(FF // D):
        state[ST_U + 8 * i : ST_U + 8 * i + 8] = u[:, i * D : (i + 1) * D]
        state[ST_A + 8 * i : ST_A + 8 * i + 8] = a[:, i * D : (i + 1) * D].astype(F32)
    state[ST_I1 : ST_I1 + 8] = jnp.broadcast_to(i1, (8, D))
    state[ST_I2 : ST_I2 + 8] = jnp.broadcast_to(i2, (8, D))


def forward(tab, query_lengths, passage_lengths, positive, rows, where_row, vectors, gathered, n_blk):
    return pl.pallas_call(
        forward_kernel,
        out_shape=(
            jax.ShapeDtypeStruct((n_blk * 8, D + 128), BF16),
            jax.ShapeDtypeStruct((TOKENS, D), BF16),
            jax.ShapeDtypeStruct((TOKENS, D), F32),
            jax.ShapeDtypeStruct((TOKENS, 128), F32),
            jax.ShapeDtypeStruct((32, TOKENS), F32),
            jax.ShapeDtypeStruct((ST_ROWS, D), F32),
        ),
        in_specs=[smem, smem, smem, smem, vmem, vmem, vmem, hbm],
        out_specs=(vmem,) * 6,
        scratch_shapes=[
            pltpu.VMEM((DENSE * UNIT, D), BF16),
            pltpu.VMEM((TOKENS, D), F32),
            pltpu.SemaphoreType.DMA((DENSE,)),
        ],
        compiler_params=PARAMS,
        name="forward",
    )(tab, query_lengths, passage_lengths, positive, rows, where_row, vectors, gathered)


def place_rows(n_dest):
    return max(PLEN // n_dest, 16)


def payload_rows(n_dest, cap):
    at_place = 2 * cap
    at_left = at_place + 2 * place_rows(n_dest)
    at_right = at_left + L_ROWS
    return at_place, at_left, at_right, at_right + 32


def backward_kernel(
    cap, tab, me, prefix_lengths, prefix_weights, emb, message, where_row, low_in, normed, scale,
    probs_in, state, vectors, gathered, payload, loss_out, count_out,
    matrices, received, grad_emb, dx, left, sems,
):
    start_matrices(tab, gathered, matrices, sems, PLACE_BLOCKS)
    n_blk = emb.shape[0] // 8
    n_dest = 2 * n_blk
    for i in range(3):
        received[i * n_blk * 8 : (i + 1) * n_blk * 8] = emb[:, 128 * i : 128 * i + 128].astype(F32)

    def every(k):
        return jnp.concatenate(
            [received[pl.ds(i * n_blk * 8 + k, n_blk, stride=8), :] for i in range(3)], 1
        )

    queries = jnp.concatenate([every(0), every(1)], 0)
    passages = jnp.concatenate([every(2), every(3)], 0)[:, :D].astype(BF16)
    wanted = queries[:, D : D + 1].astype(I32)
    queries = queries[:, :D]
    query_low = queries.astype(BF16)
    size = 2 * n_blk
    counted = wanted >= 0
    counted_f = counted.astype(F32)
    column = iota((size, size), 1)
    target = (column == (wanted & 1) * n_blk + wanted // 2) & counted
    marks = message[...]
    lane = iota(marks.shape, 1)
    count = jnp.sum((((lane == 124) | (lane == 125)) & (marks >= 0)).astype(F32))
    count_out[0, 0] = count
    feature = iota((1, D), 1)
    losses = jnp.zeros((size, 1), F32)
    d_queries = jnp.zeros((size, D), F32)
    d_passages = jnp.zeros((size, D), F32)
    for k in range(prefix_lengths.shape[0]):
        mask = (feature < prefix_lengths[k]).astype(F32)
        prefix = jnp.full((1, 1), prefix_lengths[k], I32).astype(F32)
        temper = TEMPER * lax.rsqrt(prefix)
        logits = dot_nt((queries * mask).astype(BF16), passages) * temper
        top = jnp.max(logits, -1, keepdims=True)
        weight = jnp.exp(logits - top)
        total = jnp.sum(weight, -1, keepdims=True)
        hit = jnp.sum(jnp.where(target, logits, 0.0), -1, keepdims=True)
        losses = losses + prefix_weights[k] * (top + jnp.log(total) - hit)
        factor = counted_f * (prefix_weights[k] / count) * temper
        grad = (weight / total - target.astype(F32)) * factor
        high, lower = split(grad)
        d_queries = d_queries + mask * (dot_nn(high, passages) + dot_nn(lower, passages))
        d_passages = d_passages + mask * (dot_tn(high, query_low) + dot_tn(lower, query_low))
    loss_out[0, 0] = jnp.sum(losses * counted_f)
    grad_emb[:size] = d_queries
    grad_emb[size : 2 * size] = d_passages
    grad_pooled = jnp.concatenate(
        [grad_emb[pl.ds(me[0] + i * n_blk, 1), :] for i in range(4)]
        + [jnp.zeros((4, D), F32)],
        0,
    )
    wait_matrices(gathered, matrices, sems, PLACE_BLOCKS)

    def kept_rows(at, rows=8):
        return state[at : at + rows]

    pooled = kept_rows(ST_POOLED)
    d_pre = grad_pooled * (1.0 - pooled * pooled)
    d_c = fine(dot_nt, d_pre, matrices[AT_POOL:AT_Q])
    n2 = kept_rows(ST_N2)
    d_second, d_g2, d_s2 = norm_back(d_c, n2, kept_rows(ST_I2), vectors[10:11])
    down_low = d_second.astype(BF16)
    d_a = dot_nt(down_low, matrices[AT_DOWN:])
    u = jnp.concatenate([kept_rows(ST_U + 8 * i) for i in range(FF // D)], 1)
    slope = 0.5 * (1.0 + lax.erf(u * (0.5**0.5))) + u * jnp.exp(-0.5 * u * u) * (
        0.3989422804014327
    )
    up_low = (d_a * slope).astype(BF16)
    d_h = d_second + dot_nn(up_low, matrices[AT_UP:AT_DOWN])
    d_summed, d_g1, d_s1 = norm_back(d_h, kept_rows(ST_N1), kept_rows(ST_I1), vectors[8:9])
    branch_low = d_summed.astype(BF16)
    d_o = dot_nt(branch_low, matrices[AT_O:AT_UP]).astype(BF16)
    head_of = iota((8, D), 1) // HALF
    o_heads = jnp.concatenate(
        [jnp.where(head_of == h, d_o.astype(F32), 0.0) for h in range(HEADS)], 0
    ).astype(BF16)
    vo = dot_nt(o_heads, matrices[AT_V:AT_O])
    low = low_in[...]
    probs = probs_in[...]
    d_probs = fine(dot_nt, vo, low)
    d_scores = probs * (d_probs - jnp.sum(d_probs * probs, -1, keepdims=True))
    score_low = d_scores.astype(BF16)
    mixed_score = dot_nn(score_low, low)
    keyed = fine(dot_nn, mixed_score, matrices[AT_K:AT_V])
    d_q = jnp.zeros((8, D), F32)
    for h in range(HEADS):
        d_q = d_q + jnp.where(head_of == h, keyed[8 * h : 8 * h + 8], 0.0)
    d_q_low = (d_q * (D // HEADS) ** (-0.5)).astype(BF16)
    d_x0 = d_summed + dot_nt(d_q_low, matrices[AT_Q:AT_K])
    kq = kept_rows(ST_KQ, 32)
    vo_high, vo_low = split(vo)
    kq_high, kq_low = split(kq)
    probs_low = probs.astype(BF16)
    dx[...] = dot_tn(
        jnp.concatenate([probs_low, score_low, probs_low, score_low], 0),
        jnp.concatenate([vo_high, kq_high, vo_low, kq_low], 0),
    )
    for i, start in enumerate(STARTS):
        dx[start : start + 1] = dx[start : start + 1] + d_x0[i : i + 1]
    d_gain = jnp.zeros((1, D), F32)
    d_shift = jnp.zeros((1, D), F32)
    d_type = jnp.zeros((1, D), F32)
    for start in range(0, TOKENS, 256):
        incoming = dx[start : start + 256]
        n = normed[start : start + 256]
        d_gain = d_gain + jnp.sum(incoming * n, 0, keepdims=True)
        d_shift = d_shift + jnp.sum(incoming, 0, keepdims=True)
        dn = incoming * vectors[1:2]
        inner = (
            dn - jnp.mean(dn, -1, keepdims=True) - n * jnp.mean(dn * n, -1, keepdims=True)
        )
        de = inner * scale[start : start + 256, :1]
        d_type = d_type + jnp.sum(de, 0, keepdims=True)
        dx[start : start + 256] = de
    de_low = dx[...].astype(BF16)
    at_place, at_left, at_right, n_rows = payload_rows(n_dest, cap)
    per = max(128 // cap, 1)
    step = per * cap
    for at in range(0, n_dest * cap, step):
        hot = ((iota((step, TOKENS), 0) + at) == where_row[...]).astype(F32).astype(BF16)
        summed = dot_nn(hot, de_low).astype(BF16)
        for i in range(per):
            d = at // cap + i
            if d < n_dest:
                payload[d, :cap] = summed[i * cap : (i + 1) * cap, :128]
                payload[d, cap : 2 * cap] = summed[i * cap : (i + 1) * cap, 128:]
    spots = dx[STARTS[2] : STARTS[3]] + dx[STARTS[3] :]
    dx[STARTS[2] : STARTS[3]] = spots
    dx[STARTS[2] : STARTS[2] + QROWS] = (
        dx[STARTS[2] : STARTS[2] + QROWS] + dx[:QROWS] + dx[QROWS : 2 * QROWS]
    )
    pr = place_rows(n_dest)
    share = PLEN // n_dest
    for d in range(n_dest):
        spot = dx[STARTS[2] + d * share : STARTS[2] + (d + 1) * share]
        if share < pr:
            spot = jnp.concatenate([spot, jnp.zeros((pr - share, D), F32)], 0)
        payload[d, at_place : at_place + pr] = spot[:, :128].astype(BF16)
        payload[d, at_place + pr : at_place + 2 * pr] = spot[:, 128:].astype(BF16)
    left[...] = jnp.zeros(left.shape, F32)
    up_f = up_low.astype(F32)

    def put(b, r, unit, values):
        spot = (tab[TAB_OWNER + b] * 2 + r) * L_ROWS + (tab[TAB_UNIT + b] + unit) * 4
        for i in range(4):
            left[pl.ds(spot + i, 1), :] = values[i : i + 1]

    for b in range(PLACE_BLOCKS, DENSE):
        at = b * UNIT
        if AT_K <= at < AT_O:
            heads = mixed_score if at < AT_V else kept_rows(ST_B, 32)
            off = (at - AT_K) % D
            for r in range(2):
                for j in range(2):
                    h = 2 * r + j
                    put(b, r, j, heads[8 * h : 8 * h + 4, off : off + UNIT])
            continue
        if at < AT_Q:
            values, off = kept_rows(ST_C), at - AT_POOL
        elif at < AT_K:
            values, off = kept_rows(ST_X0), at - AT_Q
        elif at < AT_UP:
            values, off = kept_rows(ST_O), at - AT_O
        elif at < AT_DOWN:
            values, off = up_f, at - AT_UP
        else:
            off = (at - AT_DOWN) % D
            values = kept_rows(ST_A + 8 * ((at - AT_DOWN) // D))
        for r in range(2):
            put(b, r, 0, values[:4, off : off + UNIT])
    d_vectors = jnp.concatenate(
        [
            d_type,
            d_gain,
            d_shift,
            jnp.sum(d_pre, 0, keepdims=True),
            jnp.sum(d_q_low.astype(F32), 0, keepdims=True),
            jnp.sum(d_o.astype(F32), 0, keepdims=True),
            jnp.sum(branch_low.astype(F32), 0, keepdims=True),
            jnp.sum(down_low.astype(F32), 0, keepdims=True),
            d_g1[None],
            d_s1[None],
            d_g2[None],
            d_s2[None],
        ]
        + [
            jnp.sum(up_f[:, i * D : (i + 1) * D], 0, keepdims=True) for i in range(FF // D)
        ],
        0,
    )
    scaled_q = kept_rows(ST_Q) * (D // HEADS) ** (-0.5)
    right = jnp.concatenate(
        [
            v.astype(F32)[:4]
            for v in (d_pre, d_q_low, scaled_q, d_o, branch_low, kept_rows(ST_H), down_low)
        ],
        0,
    )
    for d in range(n_dest):
        payload[d, at_left:at_right] = left[d * L_ROWS : (d + 1) * L_ROWS].astype(BF16)
        r = d % 2
        if d < 32:
            share_vec = d_vectors[d // 2 : d // 2 + 1, r * 128 : (r + 1) * 128]
        else:
            share_vec = jnp.zeros((1, 128), F32)
        payload[d, at_right:n_rows] = jnp.concatenate(
            [right[:, r * 128 : (r + 1) * 128], share_vec, jnp.zeros((3, 128), F32)], 0
        ).astype(BF16)


def backward(tab, me, prefix_lengths, prefix_weights, emb, message, where_row, low, normed, scale, probs, state, vectors, gathered, cap):
    n_dest = message.shape[0]
    n_rows = payload_rows(n_dest, cap)[-1]
    return pl.pallas_call(
        partial(backward_kernel, cap),
        out_shape=(
            jax.ShapeDtypeStruct((n_dest, n_rows, 128), BF16),
            jax.ShapeDtypeStruct((1, 1), F32),
            jax.ShapeDtypeStruct((1, 1), F32),
        ),
        in_specs=[smem] * 4 + [vmem] * 9 + [hbm],
        out_specs=(vmem, smem, smem),
        scratch_shapes=[
            pltpu.VMEM((DENSE * UNIT, D), BF16),
            pltpu.VMEM((emb.shape[0] * 3, 128), F32),
            pltpu.VMEM((emb.shape[0], D), F32),
            pltpu.VMEM((TOKENS, D), F32),
            pltpu.VMEM((n_dest * L_ROWS, 128), F32),
            pltpu.SemaphoreType.DMA((DENSE,)),
        ],
        compiler_params=PARAMS,
        name="backward",
    )(tab, me, prefix_lengths, prefix_weights, emb, message, where_row, low, normed, scale, probs, state, vectors, gathered)


def reduce_kernel(slots, cap, tab, me, loss, asked, payload, reduced, news, total, row_grads, left, right):
    n_dest = payload.shape[0]
    at_place, at_left, at_right, n_rows = payload_rows(n_dest, cap)
    for d in range(n_dest):
        row_grads[d * cap : (d + 1) * cap, :128] = payload[d, :cap]
        row_grads[d * cap : (d + 1) * cap, 128:] = payload[d, cap : 2 * cap]
        left[d * L_ROWS : (d + 1) * L_ROWS] = payload[d, at_left:at_right].astype(F32)
        right[d * 32 : (d + 1) * 32] = payload[d, at_right:n_rows].astype(F32)
    grads = row_grads[...]
    filled = slots * HALF
    for at in range(0, filled, 64):
        hot = ((iota((64, n_dest * cap), 0) + at) == asked[...]).astype(F32).astype(BF16)
        total[at : at + 64] = dot_nn(hot, grads)
    mine = me[0]
    odd = me[1]
    column = iota((n_dest * 4, 128), 1)

    def rows_of(ref, start, stride):
        return jnp.concatenate(
            [ref[pl.ds(start + q, n_dest, stride=stride), :] for q in range(4)], 0
        ).astype(BF16)

    for b in range(PLACE_BLOCKS, DENSE):
        at = b * UNIT
        if at < AT_Q:
            m = 0
        elif at < AT_UP:
            m = 1 + (at - AT_Q) // D
        elif at < AT_DOWN:
            m = 5
        else:
            m = 6

        @pl.when(tab[TAB_OWNER + b] == mine)
        def _():
            unit = tab[TAB_UNIT + b] * 4
            pull = rows_of(right, m * 4, 32)
            if AT_K <= at < AT_O:
                grad = dot_tn(
                    rows_of(left, unit, L_ROWS), jnp.where(column < HALF, pull, 0).astype(BF16)
                ) + dot_tn(
                    rows_of(left, unit + 4, L_ROWS),
                    jnp.where(column < HALF, 0, pull).astype(BF16),
                )
            else:
                grad = dot_tn(rows_of(left, unit, L_ROWS), pull)
            spot = pl.multiple_of(tab[TAB_SLOT + b] * HALF, HALF)
            total[pl.ds(spot, HALF), :128] = grad[:HALF]
            total[pl.ds(spot, HALF), 128:] = grad[HALF:]

    pr = place_rows(n_dest)
    spots_low = jnp.zeros((pr, 128), F32)
    spots_high = jnp.zeros((pr, 128), F32)
    for d in range(n_dest):
        spots_low = spots_low + payload[d, at_place : at_place + pr].astype(F32)
        spots_high = spots_high + payload[d, at_place + pr : at_place + 2 * pr].astype(F32)
    spots = jnp.concatenate([spots_low, spots_high], 1)
    vector = jnp.sum(right[pl.ds(28, n_dest, stride=32), :], 0, keepdims=True)
    summed = total[...]
    reduced[...] = summed.astype(BF16).reshape(reduced.shape)
    square = jnp.sum(summed * summed) + jnp.sum(spots * spots) + jnp.sum(vector * vector)
    row16 = iota((pr, 128), 0)

    def parts(v):
        first = v.astype(BF16).astype(F32)
        second = (v - first).astype(BF16).astype(F32)
        return first, second, v - first - second

    extra = jnp.zeros((pr, 128), F32)
    for i, part in enumerate(
        parts(vector)
        + parts(jnp.full((1, 128), square, F32))
        + parts(jnp.full((1, 128), loss[0, 0], F32))
    ):
        extra = jnp.where(row16 == i, part, extra)
    block = jnp.concatenate([spots, extra], 1).astype(BF16)
    for d in range(n_dest):
        news[d * pr : (d + 1) * pr] = block


def reduce(tab, me, loss, asked, payload, slots, cap):
    n_dest = payload.shape[0]
    pr = place_rows(n_dest)
    return pl.pallas_call(
        partial(reduce_kernel, slots, cap),
        out_shape=(
            jax.ShapeDtypeStruct((slots, HALF, D), BF16),
            jax.ShapeDtypeStruct((n_dest * pr, D + 128), BF16),
        ),
        in_specs=[smem, smem, smem, vmem, vmem],
        out_specs=(vmem, vmem),
        scratch_shapes=[
            pltpu.VMEM((slots * HALF, D), F32),
            pltpu.VMEM((n_dest * cap, D), BF16),
            pltpu.VMEM((n_dest * L_ROWS, 128), F32),
            pltpu.VMEM((n_dest * 32, 128), F32),
        ],
        compiler_params=PARAMS,
        name="reduce",
    )(tab, me, loss, asked, payload)


def update_kernel(
    pr, tab, me, news, places, own, other, weight, first, second, vectors, vector_first,
    vector_second, weight_out, first_out, second_out, vectors_out, vector_first_out,
    vector_second_out, loss_out, norm_out, factor_ref,
):
    i = pl.program_id(0)
    n_dest = news.shape[0] // pr

    def strip(row):
        return news[pl.ds(row, n_dest, stride=pr), D:]

    @pl.when(i == 0)
    def _():
        extra = news[...][:, D:].astype(F32).reshape(n_dest, pr, 128)
        sums = jnp.sum(extra[:, 3:6, :], 0)
        square = jnp.sum(sums, 0, keepdims=True)
        norm = jnp.sqrt(square)
        factor = CLIP_AT / jnp.maximum(norm, CLIP_AT)
        factor_ref[...] = jnp.broadcast_to(factor, (8, 128))
        norm_out[0, 0] = norm[0, 0]
        loss = jnp.sum(extra[0:2, 6:9, :], 0)
        loss = jnp.sum(loss, 0, keepdims=True)
        loss_out[0, 0] = loss[0, 0]
        pieces = jnp.sum(extra[:32, 0:3, :], 1)
        pairs = pieces.reshape(16, 2, 128)
        grad = jnp.concatenate([pairs[:, 0], pairs[:, 1]], 1) * factor[0, 0]
        v, m1, m2 = adam_step(
            vectors[...], vector_first[...], vector_second[...], grad, VECTOR_RATE, 0.0
        )
        vectors_out[...] = v
        vector_first_out[...] = m1
        vector_second_out[...] = m2

    kind = tab[TAB_KIND + i]
    flip = me[1] == 0
    mine = own[0].astype(F32)
    theirs = other[0].astype(F32)
    lower = jnp.where(flip, mine, theirs)
    upper = jnp.where(flip, theirs, mine)

    def step(grad):
        w, m1, m2 = adam_step(
            weight[0], first[0], second[0], grad * factor_ref[0:1, 0:1], RATE, DECAY
        )
        weight_out[0] = w
        first_out[0] = m1
        second_out[0] = m2

    @pl.when(kind == 0)
    def _():
        weight_out[0] = weight[0]
        first_out[0] = first[0]
        second_out[0] = second[0]

    @pl.when(kind == KIND_TABLE)
    def _():
        step(jnp.concatenate([lower, upper], 0))

    @pl.when(kind == KIND_DENSE)
    def _():
        step(
            jnp.concatenate(
                [
                    jnp.concatenate([lower[:, :128], lower[:, 128:]], 0),
                    jnp.concatenate([upper[:, :128], upper[:, 128:]], 0),
                ],
                1,
            )
        )

    @pl.when((kind >= KIND_PLACE) & (kind < KIND_DENSE))
    def _():
        spot = pl.multiple_of((kind - KIND_PLACE) * UNIT, UNIT)
        step(places[pl.ds(spot, UNIT), :D].astype(F32))


def update(tab, me, news, own, other, weights, first, second, vectors, vector_first, vector_second, pr):
    slots = weights.shape[0]
    n_dest = news.shape[0] // pr
    share = PLEN // n_dest
    places = news
    if share < pr:
        places = news.reshape(n_dest, pr, -1)[:, :share].reshape(PLEN, -1)
    slot = pl.BlockSpec((1, UNIT, D), lambda i: (i, 0, 0))
    half = pl.BlockSpec((1, HALF, D), lambda i: (i, 0, 0))
    whole = lambda a: pl.BlockSpec(a.shape, lambda i: (0,) * a.ndim)
    big = jax.ShapeDtypeStruct(weights.shape, F32)
    small = jax.ShapeDtypeStruct(vectors.shape, F32)
    one = jax.ShapeDtypeStruct((1, 1), F32)
    return pl.pallas_call(
        partial(update_kernel, pr),
        grid=(slots,),
        out_shape=(big, big, big, small, small, small, one, one),
        in_specs=[smem, smem, whole(news), whole(places), half, half, slot, slot, slot]
        + [whole(vectors)] * 3,
        out_specs=(slot, slot, slot) + (whole(vectors),) * 3 + (smem, smem),
        scratch_shapes=[pltpu.VMEM((8, 128), F32)],
        compiler_params=PARAMS,
        name="update",
    )(tab, me, news, places, own, other, weights, first, second, vectors, vector_first, vector_second)


def quick(
    query_ids, passage_ids, query_lengths, passage_lengths, positive, prefix_lengths,
    prefix_weights, owners, weights, first_moments, second_moments, vectors, vector_first,
    vector_second,
):
    slots = weights.shape[0]
    n_blk = lax.axis_size("blk")
    everyone = ("blk", "rep")
    cap = 48 if n_blk <= 16 else 16
    dense_cap = min(7, slots)
    me = jnp.stack([lax.axis_index("blk"), lax.axis_index("rep")]).astype(I32)

    def exchange(a, axes):
        return lax.all_to_all(a, axes, 0, 0, tiled=True)

    dense, tab = prepare(owners, me, weights, n_blk, dense_cap)
    gathered = lax.all_gather(dense, "blk", axis=0, tiled=True)
    message, where_row, tab = request(
        owners, tab, me, positive, query_lengths, passage_lengths, query_ids[0], passage_ids[0],
        slots, n_blk, cap,
    )
    message = exchange(message, everyone)
    rows = exchange(fetch(me, message, weights, cap), everyone)
    emb, low, normed, scale, probs, state = forward(
        tab, query_lengths, passage_lengths, positive, rows, where_row, vectors, gathered, n_blk
    )
    emb = exchange(emb, "blk")
    payload, loss, count = backward(
        tab, me, prefix_lengths, prefix_weights, emb, message, where_row, low, normed, scale,
        probs, state, vectors, gathered, cap,
    )
    payload = exchange(payload, everyone)
    asked = message[:, :cap].reshape(1, -1)
    own, news = reduce(tab, me, loss, asked, payload, slots, cap)
    other = lax.ppermute(own, "rep", [(0, 1), (1, 0)])
    news = exchange(news, everyone)
    overflow = jnp.max(message[:, 126]) > 0

    def roomy():
        return local(
            query_ids, passage_ids, query_lengths, passage_lengths, positive, prefix_lengths,
            prefix_weights, owners, weights, first_moments, second_moments, vectors, vector_first,
            vector_second,
        )

    def usual():
        *outs, loss_sum, norm = update(
            tab, me, news, own, other, weights, first_moments, second_moments, vectors,
            vector_first, vector_second, place_rows(2 * n_blk),
        )
        return (*outs, loss_sum.reshape(()), count.reshape(()), norm.reshape(()))

    return lax.cond(overflow, roomy, usual)


def solution(mesh):
    in_specs = (
        P("rep", "blk", None),
        P("rep", "blk", None),
        P("rep", "blk"),
        P("rep", "blk"),
        P("rep", "blk"),
        P(),
        P(),
        P(),
        P("blk", None, None),
        P("blk", None, None),
        P("blk", None, None),
        P(),
        P(),
        P(),
    )
    out_specs = (
        P("blk", None, None),
        P("blk", None, None),
        P("blk", None, None),
        P(),
        P(),
        P(),
        P(),
        P(),
        P(),
    )
    return jax.shard_map(quick, mesh=mesh, in_specs=in_specs, out_specs=out_specs, check_vma=False)
```

```python
from functools import partial

import jax
import jax.numpy as jnp
from jax import lax
from jax.experimental import pallas as pl
from jax.experimental.pallas import tpu as pltpu
from jax.sharding import PartitionSpec as P

D = 256
HEADS = 4
FF = 1024
VOCAB = 30592
LAYERS = 1
PLEN = 512
STEP = 7


TEMPER = 8.0
CLIP_AT = 0.01
RATE = 0.06
VECTOR_RATE = 0.8
BETA_ONE = 0.9
BETA_TWO = 0.999
DECAY = 0.01
EPSILON = 1e-08
NORM_EPS = 1e-06
HUGE = 1000000000.0
HIGHEST = lax.Precision.HIGHEST


def mult(left_op, right_op):
    return jnp.dot(left_op, right_op, preferred_element_type=jnp.float32)


def mult_tn(left_op, right_op):
    return lax.dot_general(
        left_op, right_op, (((0,), (0,)), ((), ())), preferred_element_type=jnp.float32
    )


def mult_nt(left_op, right_op):
    return lax.dot_general(
        left_op, right_op, (((1,), (1,)), ((), ())), preferred_element_type=jnp.float32
    )


def norm_rows(values_in, gain_row, shift_row):
    centred = values_in - jnp.mean(values_in, -1, keepdims=True)
    inv_scale = lax.rsqrt(jnp.mean(centred * centred, -1, keepdims=True) + NORM_EPS)
    normed = centred * inv_scale
    return (normed * gain_row + shift_row, normed, inv_scale)


def norm_back(incoming, normed, inv_scale, gain_row):
    dnormed = incoming * gain_row
    inner_part = (
        dnormed
        - jnp.mean(dnormed, -1, keepdims=True)
        - normed * jnp.mean(dnormed * normed, -1, keepdims=True)
    )
    return (inner_part * inv_scale, jnp.sum(incoming * normed, 0), jnp.sum(incoming, 0))


def layer_parts(flat_rows, vectors, layer_index):
    offset = VOCAB + PLEN + D + layer_index * (4 * D + 2 * FF)
    w_qkv = jnp.concatenate(
        [
            flat_rows[offset : offset + D],
            flat_rows[offset + D : offset + 2 * D],
            flat_rows[offset + 2 * D : offset + 3 * D],
        ],
        1,
    )
    w_out = flat_rows[offset + 3 * D : offset + 4 * D]
    w_up = flat_rows[offset + 4 * D : offset + 4 * D + FF]
    w_down = flat_rows[offset + 4 * D + FF : offset + 4 * D + 2 * FF]
    row_base = 4 + layer_index * (8 + FF // D)
    return ((w_qkv, w_out, w_up, w_down), vectors[row_base : row_base + 8 + FF // D])


def divide_into_heads(packed_buffer, column):
    return packed_buffer[:, column * D : (column + 1) * D].reshape(
        packed_buffer.shape[0], HEADS, D // HEADS
    )


def attend_probs(packed_buffer, key_keep):
    scores = jnp.einsum(
        "cnp,fnp->ncf",
        divide_into_heads(packed_buffer, 0),
        divide_into_heads(packed_buffer, 1),
        preferred_element_type=jnp.float32,
    ) * (D // HEADS) ** (-0.5)
    scores = jnp.where(key_keep[None, None, :], scores, -HUGE)
    return jax.nn.softmax(scores, -1)


def attend(pieces):
    packed_buffer, key_keep = pieces
    attn_probs = attend_probs(packed_buffer, key_keep)
    blended = jnp.einsum(
        "nbi,ins->bns",
        attn_probs.astype(jnp.bfloat16),
        divide_into_heads(packed_buffer, 2),
        preferred_element_type=jnp.float32,
    )
    return blended.reshape(packed_buffer.shape[0], D)


def attend_back(pieces):
    packed_buffer, key_keep, grad_out = pieces
    seq_len = packed_buffer.shape[0]
    head_scale = (D // HEADS) ** (-0.5)
    attn_probs = attend_probs(packed_buffer, key_keep)
    gradient_row_block = grad_out.reshape(seq_len, HEADS, D // HEADS)
    grad_values = jnp.einsum(
        "fxn,xfa->nfa",
        attn_probs.astype(jnp.bfloat16),
        gradient_row_block,
        preferred_element_type=jnp.float32,
    )
    grad_probs = jnp.einsum(
        "cnp,fnp->ncf",
        gradient_row_block,
        divide_into_heads(packed_buffer, 2),
        preferred_element_type=jnp.float32,
    )
    grad_scores = attn_probs * (grad_probs - jnp.sum(grad_probs * attn_probs, -1, keepdims=True))
    score_lowered = grad_scores.astype(jnp.bfloat16)
    grad_queries = (
        jnp.einsum(
            "nbi,ins->bns",
            score_lowered,
            divide_into_heads(packed_buffer, 1),
            preferred_element_type=jnp.float32,
        )
        * head_scale
    )
    grad_keys = (
        jnp.einsum(
            "fxn,xfa->nfa",
            score_lowered,
            divide_into_heads(packed_buffer, 0),
            preferred_element_type=jnp.float32,
        )
        * head_scale
    )
    return jnp.concatenate(
        [
            grad_queries.reshape(seq_len, D),
            grad_keys.reshape(seq_len, D),
            grad_values.reshape(seq_len, D),
        ],
        1,
    ).astype(jnp.bfloat16)


def layer_forward(hidden_in, weights_set, vec_rows, key_keep):
    w_qkv, w_out, w_up, w_down = weights_set
    groups, seq_len = key_keep.shape
    in_low = hidden_in.astype(jnp.bfloat16)
    bias_qkv = jnp.concatenate([vec_rows[0], jnp.zeros_like(vec_rows[0]), vec_rows[1]])
    packed_buffer = (mult(in_low, w_qkv) + bias_qkv).astype(jnp.bfloat16)
    blended = lax.map(attend, (packed_buffer.reshape(groups, seq_len, 3 * D), key_keep))
    blend_low = blended.reshape(groups * seq_len, D).astype(jnp.bfloat16)
    summed = hidden_in + mult(blend_low, w_out) + vec_rows[2]
    normal_one, normed_one, scale_one = norm_rows(summed, vec_rows[4], vec_rows[5])
    normal_low = normal_one.astype(jnp.bfloat16)
    up_in = mult_nt(normal_low, w_up) + vec_rows[8:].reshape(FF)
    acted = jax.nn.gelu(up_in, approximate=False).astype(jnp.bfloat16)
    second = normal_one + mult(acted, w_down) + vec_rows[3]
    result, normed_two, scale_two = norm_rows(second, vec_rows[6], vec_rows[7])
    return (
        result,
        (
            in_low,
            packed_buffer,
            blend_low,
            normed_one,
            scale_one,
            normal_low,
            up_in,
            acted,
            normed_two,
            scale_two,
        ),
    )


def layer_backward(grad_out, weights_set, vec_rows, key_keep, saved):
    w_qkv, w_out, w_up, w_down = weights_set
    (
        in_low,
        packed_buffer,
        blend_low,
        normed_one,
        scale_one,
        normal_low,
        up_in,
        acted,
        normed_two,
        scale_two,
    ) = saved
    groups, seq_len = key_keep.shape
    grad_second, grad_gain_two, grad_shift_two = norm_back(
        grad_out, normed_two, scale_two, vec_rows[6]
    )
    down_low = grad_second.astype(jnp.bfloat16)
    grad_down = mult_tn(acted, down_low)
    grad_acted = mult_nt(down_low, w_down)
    gelu_pull = jax.vjp(partial(jax.nn.gelu, approximate=False), up_in)[1]
    up_low = gelu_pull(grad_acted)[0].astype(jnp.bfloat16)
    grad_up = mult_tn(up_low, normal_low)
    grad_normal = grad_second + mult(up_low, w_up)
    grad_summed, gradient_first_gain, grad_shift_one = norm_back(
        grad_normal, normed_one, scale_one, vec_rows[4]
    )
    branch_low = grad_summed.astype(jnp.bfloat16)
    grad_wout = mult_tn(blend_low, branch_low)
    blend_grad = mult_nt(branch_low, w_out).astype(jnp.bfloat16)
    grad_packed = lax.map(
        attend_back,
        (
            packed_buffer.reshape(groups, seq_len, 3 * D),
            key_keep,
            blend_grad.reshape(groups, seq_len, D),
        ),
    ).reshape(groups * seq_len, 3 * D)
    grad_wqkv = mult_tn(in_low, grad_packed)
    grad_in = grad_summed + mult_nt(grad_packed, w_qkv)
    packed_sum = jnp.sum(grad_packed.astype(jnp.float32), 0)
    matrix_grads = jnp.concatenate(
        [
            grad_wqkv[:, :D],
            grad_wqkv[:, D : 2 * D],
            grad_wqkv[:, 2 * D :],
            grad_wout,
            grad_up,
            grad_down,
        ],
        0,
    )
    vector_grads = jnp.concatenate(
        [
            jnp.stack(
                [
                    packed_sum[:D],
                    packed_sum[2 * D :],
                    jnp.sum(branch_low.astype(jnp.float32), 0),
                    jnp.sum(down_low.astype(jnp.float32), 0),
                    gradient_first_gain,
                    grad_shift_one,
                    grad_gain_two,
                    grad_shift_two,
                ]
            ),
            jnp.sum(up_low.astype(jnp.float32), 0).reshape(FF // D, D),
        ],
        0,
    )
    return (grad_in, matrix_grads, vector_grads)


def embed_sequences(flat_rows, vectors, token_ids, lengths):
    groups, seq_len = token_ids.shape
    key_keep = jnp.arange(seq_len)[None, :] < lengths[:, None]
    table_rows = jnp.take(flat_rows, token_ids.reshape(-1), axis=0).astype(jnp.float32)
    places = flat_rows[VOCAB : VOCAB + seq_len].astype(jnp.float32)
    embedded = (table_rows.reshape(groups, seq_len, D) + places[None] + vectors[0]).reshape(
        groups * seq_len, D
    )
    hidden_now, normed_emb, scaled_embedding = norm_rows(embedded, vectors[1], vectors[2])
    weights_set, vec_rows = layer_parts(flat_rows, vectors, 0)
    hidden_now, saved = layer_forward(hidden_now, weights_set, vec_rows, key_keep)
    layer_saves = [saved]
    first_rows = hidden_now.reshape(groups, seq_len, D)[:, 0].astype(jnp.bfloat16)
    pooled = jnp.tanh(mult(first_rows, flat_rows[VOCAB + PLEN : VOCAB + PLEN + D]) + vectors[3])
    return (pooled, (normed_emb, scaled_embedding, layer_saves, first_rows))


def encode_back(grad_pooled, pooled, flat_rows, vectors, token_ids, lengths, encoder_kept):
    normed_emb, scaled_embedding, layer_saves, first_rows = encoder_kept
    groups, seq_len = token_ids.shape
    key_keep = jnp.arange(seq_len)[None, :] < lengths[:, None]
    w_pool = flat_rows[VOCAB + PLEN : VOCAB + PLEN + D].astype(jnp.float32)
    grad_pre = grad_pooled * (1.0 - pooled * pooled)
    grad_pool = jnp.dot(first_rows.astype(jnp.float32).T, grad_pre, precision=HIGHEST)
    grad_first = jnp.dot(grad_pre, w_pool.T, precision=HIGHEST)
    grad_hidden = (
        jnp.zeros((groups, seq_len, D), jnp.float32)
        .at[:, 0]
        .set(grad_first)
        .reshape(groups * seq_len, D)
    )
    matrices = []
    vector_parts = []
    for layer_index in reversed(range(LAYERS)):
        weights_set, vec_rows = layer_parts(flat_rows, vectors, layer_index)
        grad_hidden, matrix_grads, vector_grads = layer_backward(
            grad_hidden, weights_set, vec_rows, key_keep, layer_saves[layer_index]
        )
        matrices.insert(0, matrix_grads)
        vector_parts.insert(0, vector_grads)
    grad_embed, grad_gain, grad_shift = norm_back(
        grad_hidden, normed_emb, scaled_embedding, vectors[1]
    )
    grad_table = jnp.zeros((VOCAB, D), jnp.float32).at[token_ids.reshape(-1)].add(grad_embed)
    grad_places = (
        jnp.zeros((PLEN, D), jnp.float32)
        .at[:seq_len]
        .set(jnp.sum(grad_embed.reshape(groups, seq_len, D), 0))
    )
    flat_grad = jnp.concatenate([grad_table, grad_places, grad_pool] + matrices, 0)
    head_rows = jnp.stack([jnp.sum(grad_embed, 0), grad_gain, grad_shift, jnp.sum(grad_pre, 0)])
    return (flat_grad, jnp.concatenate([head_rows] + vector_parts, 0))


def adam_step(weight, moment_one, moment_two, gradient, step_rate, decay_rate):
    moment_one = BETA_ONE * moment_one + (1.0 - BETA_ONE) * gradient
    moment_two = BETA_TWO * moment_two + (1.0 - BETA_TWO) * gradient * gradient
    update = (
        moment_one
        / (1.0 - BETA_ONE**STEP)
        / (jnp.sqrt(moment_two / (1.0 - BETA_TWO**STEP)) + EPSILON)
    )
    return (weight - step_rate * (update + decay_rate * weight), moment_one, moment_two)


def gather_all(values, axes):
    count = lax.axis_size(axes)
    copies = jnp.broadcast_to(values[None], (count,) + values.shape)
    return lax.all_to_all(copies, axes, 0, 0, tiled=True).reshape((-1,) + values.shape[1:])


def sum_all(values, axes):
    count = lax.axis_size(axes)
    copies = jnp.broadcast_to(values[None], (count,) + values.shape)
    return jnp.sum(lax.all_to_all(copies, axes, 0, 0, tiled=True), 0)


def sum_share(values, axes):
    count = lax.axis_size(axes)
    parts = lax.all_to_all(values, axes, 0, 0, tiled=True)
    return jnp.sum(parts.reshape((count, -1) + values.shape[1:]), 0)


def local(
    query_ids,
    passage_ids,
    query_lengths,
    passage_lengths,
    positive,
    prefix_lengths,
    prefix_weights,
    owners,
    weights,
    first_moments,
    second_moments,
    vectors,
    vector_first,
    vector_second,
):
    slot_count, unit_rows = (weights.shape[0], weights.shape[1])
    gathered = gather_all(weights.astype(jnp.bfloat16), "blk")
    flat_rows = jnp.take(gathered, owners, axis=0).reshape(-1, D)
    query_pooled, query_kept = embed_sequences(flat_rows, vectors, query_ids[0], query_lengths[0])
    passage_pooled, passage_kept = embed_sequences(
        flat_rows, vectors, passage_ids[0], passage_lengths[0]
    )
    all_passages = gather_all(passage_pooled.astype(jnp.bfloat16), "blk")
    prefix_masks = (jnp.arange(D)[None, :] < prefix_lengths[:, None]).astype(jnp.float32)
    prefix_scale = TEMPER * lax.rsqrt(prefix_lengths.astype(jnp.float32))
    queries = query_pooled.astype(jnp.bfloat16).astype(jnp.float32)
    passages = all_passages.astype(jnp.float32)
    masked = queries[None] * prefix_masks[:, None, :]
    logits = (
        jnp.einsum("mpd,jd->mpj", masked, passages, precision=HIGHEST) * prefix_scale[:, None, None]
    )
    counted = positive[0] >= 0
    target = (jnp.arange(passages.shape[0])[None, :] == positive[0][:, None]).astype(jnp.float32)
    running_totals = jax.nn.logsumexp(logits, -1) - jnp.sum(logits * target[None], -1)
    per_query = jnp.sum(prefix_weights[:, None] * running_totals, 0)
    loss_part = jnp.sum(jnp.where(counted, per_query, 0.0))
    count_part = jnp.sum(counted.astype(jnp.float32))
    count_total, loss_total = sum_all(jnp.stack([count_part, loss_part]), ("blk", "rep"))
    row_factor = (prefix_weights * prefix_scale / count_total)[:, None, None] * counted.astype(
        jnp.float32
    )[None, :, None]
    grad_logits = (jax.nn.softmax(logits, -1) - target[None]) * row_factor
    grad_query = jnp.sum(
        jnp.einsum("mpj,jd->mpd", grad_logits, passages, precision=HIGHEST)
        * prefix_masks[:, None, :],
        0,
    )
    grad_passage = sum_share(
        jnp.einsum("mpj,mpd->jd", grad_logits, masked, precision=HIGHEST), "blk"
    )
    flat_query, vec_query = encode_back(
        grad_query, query_pooled, flat_rows, vectors, query_ids[0], query_lengths[0], query_kept
    )
    flat_pass, vec_pass = encode_back(
        grad_passage,
        passage_pooled,
        flat_rows,
        vectors,
        passage_ids[0],
        passage_lengths[0],
        passage_kept,
    )
    vec_total = sum_all(vec_query + vec_pass, ("blk", "rep"))
    buffer = (
        jnp.zeros((lax.axis_size("blk") * slot_count, unit_rows, D), jnp.float32)
        .at[owners]
        .set((flat_query + flat_pass).reshape(-1, unit_rows, D))
    )
    vec_square = jnp.sum(vec_total * vec_total)
    reduced = sum_share(buffer, "blk")
    reduced = sum_all(reduced, "rep")
    square_sum = sum_all(jnp.sum(reduced * reduced)[None], "blk")[0]
    old_weight, old_first, old_second = (weights, first_moments, second_moments)
    slot_ids = lax.axis_index("blk") * slot_count + jnp.arange(slot_count)
    owned_mask = jnp.any(slot_ids[:, None] == owners[None, :], 1)[:, None, None]
    grad_norm = jnp.sqrt(square_sum + vec_square)
    factor = CLIP_AT / jnp.maximum(grad_norm, CLIP_AT)
    new_weight, new_first, new_second = adam_step(
        old_weight, old_first, old_second, reduced * factor, RATE, DECAY
    )
    new_weight = jnp.where(owned_mask, new_weight, old_weight)
    new_first = jnp.where(owned_mask, new_first, old_first)
    new_second = jnp.where(owned_mask, new_second, old_second)
    new_vec, new_vec_first, new_vec_second = adam_step(
        vectors, vector_first, vector_second, vec_total * factor, VECTOR_RATE, 0.0
    )
    return (
        new_weight,
        new_first,
        new_second,
        new_vec,
        new_vec_first,
        new_vec_second,
        loss_total,
        count_total,
        grad_norm,
    )


F32 = jnp.float32
BF16 = jnp.bfloat16
I32 = jnp.int32
UNIT = 128
TABLE_BLOCKS = VOCAB // UNIT
PLACE_BLOCKS = PLEN // UNIT
DENSE = PLACE_BLOCKS + (D + 4 * D + 2 * FF) // UNIT
HALF = 64
QROWS = 128
TOKENS = 2 * QROWS + 2 * PLEN
STARTS = (0, QROWS, 2 * QROWS, 2 * QROWS + PLEN)
UNITS_L = 12
L_ROWS = 4 * UNITS_L
NEVER = -1e30


def params(n_blk, small):
    return pltpu.CompilerParams(vmem_limit_bytes=(small if n_blk <= 16 else 58) << 20)


AT_POOL = PLEN
AT_Q = AT_POOL + D
AT_K = AT_Q + D
AT_V = AT_K + D
AT_O = AT_V + D
AT_UP = AT_O + D
AT_DOWN = AT_UP + FF

TAB_OWNER, TAB_RANK, TAB_SLOT, TAB_UNIT, TAB_KIND, TAB_ORDER = range(6)
PIECE = 16
PIECES = 16
DENSE_CAP = 8
CLASS = DENSE // 2
HELD = DENSE_CAP // 2
AT_ASKED = DENSE_CAP // 4 * PIECE
MESSAGE_ROWS = AT_ASKED + 16

KIND_TABLE, KIND_PLACE, KIND_DENSE = 1, 2, 8

vmem = pl.BlockSpec(memory_space=pltpu.VMEM)
smem = pl.BlockSpec(memory_space=pltpu.SMEM)
hbm = pl.BlockSpec(memory_space=pl.ANY)


def iota(shape, axis):
    return lax.broadcasted_iota(I32, shape, axis)


def dot_nn(a, b):
    return lax.dot_general(a, b, (((1,), (0,)), ((), ())), preferred_element_type=F32)


def dot_nt(a, b):
    return lax.dot_general(a, b, (((1,), (1,)), ((), ())), preferred_element_type=F32)


def dot_tn(a, b):
    return lax.dot_general(a, b, (((0,), (0,)), ((), ())), preferred_element_type=F32)


def split(a):
    high = a.astype(BF16)
    return high, (a - high.astype(F32)).astype(BF16)


def fine(dot, a, b):
    high, low = split(a)
    rows = a.shape[0]
    both = dot(jnp.concatenate([high, low], 0), b)
    return both[:rows] + both[rows:]


def to_column(row):
    return jnp.broadcast_to(row, (128, 128)).T[:, :1]


def token_facts(query_lengths, passage_lengths):
    lane = iota((1, TOKENS), 1)
    sequence = (
        (lane >= STARTS[1]).astype(I32)
        + (lane >= STARTS[2]).astype(I32)
        + (lane >= STARTS[3]).astype(I32)
    )
    ends = [
        STARTS[0] + query_lengths[0, 0],
        STARTS[1] + query_lengths[0, 1],
        STARTS[2] + passage_lengths[0, 0],
        STARTS[3] + passage_lengths[0, 1],
    ]
    end = jnp.where(
        sequence == 0,
        ends[0],
        jnp.where(sequence == 1, ends[1], jnp.where(sequence == 2, ends[2], ends[3])),
    )
    return sequence, lane < end


def across(values, n_blk, step):
    pairs = [(i, i // PIECES * PIECES + step(i % PIECES)) for i in range(n_blk)]
    return lax.ppermute(values, "blk", pairs)


def along_z(mine, n_blk):
    return jnp.stack(
        [mine] + [across(mine, n_blk, lambda i, k=k: (i + 4 * k) % PIECES) for k in (1, 2, 3)]
    )


def spread(first, n_blk):
    arrays = [first, lax.ppermute(first, "rep", [(0, 1), (1, 0)])]
    arrays = arrays + [across(a, n_blk, lambda i: i ^ 2) for a in arrays]
    return arrays + [across(a, n_blk, lambda i: i ^ 1) for a in arrays]


def piece_copies(me, gathered, matrices, sems):
    copies = []
    for part, array in enumerate(gathered):
        low = (me[0] % 4) ^ (part & 2) ^ (part // 4)
        odd = me[1] ^ (part % 2)
        for k in range(4):
            p = low + (me[0] % PIECES // 4 * 4 + 4 * (4 - k)) % PIECES
            row = pl.multiple_of((p % 8) * PIECE, PIECE)
            lane = pl.multiple_of((p // 8) * 128, 128)
            copies.append(
                pltpu.make_async_copy(
                    array.at[k],
                    matrices.at[:, odd, pl.ds(row, PIECE), pl.ds(lane, 128)],
                    sems.at[4 * part + k],
                )
            )
    return copies


def rows_at(matrices, tab, start, stop):
    blocks = []
    for b in range(start // UNIT, stop // UNIT):
        order = tab[b, TAB_ORDER]
        blocks.append(matrices[order // 2, order % 2])
    return jnp.concatenate(blocks, 0)


def owner_of(slot, slots, n_blk):
    owner = jnp.zeros(slot.shape, I32)
    for k in range(1, n_blk):
        owner = owner + (slot >= k * slots).astype(I32)
    return owner


def request_kernel(
    slots, n_blk, cap, owners, me, positive, query_lengths, passage_lengths, owner_line,
    query_ids, passage_ids, weights, message, where_row, tab, ids, owner_row, loaded, sems,
):
    n_rep = 2
    n_dest = n_blk * n_rep
    n_units = owners.shape[0]
    start = me[0] * slots

    def take(b, carry):
        before, have = carry
        slot = owners[n_units - DENSE + b]
        inside = slot - start
        mine = (inside >= 0) & (inside < slots)

        @pl.when(mine & (have // 2 % 2 == me[1]) & (have < DENSE_CAP))
        def _():
            spot = have // 4 * 2 + have % 2
            pltpu.make_async_copy(weights.at[inside], loaded.at[spot], sems.at[spot]).start()

        return before + (slot < start).astype(I32), have + mine.astype(I32)

    before, have = lax.fori_loop(0, DENSE, take, (0, 0))
    owner_row[...] = jnp.full(owner_row.shape, -1, I32)
    owner_row[:, :n_units] = owner_line[...]
    every_slot = owner_row[...]
    wide = every_slot.shape[1]
    base = n_units - DENSE
    low = base // 128 * 128
    rolled = pltpu.roll(every_slot[:, low:], wide - low - (base - low), 1)[:, :128]
    dense_owner = owner_of(rolled, slots, n_blk)
    owner_column = to_column(dense_owner)[:32]
    slot_column = to_column(rolled)[:32]
    block_row = iota((32, 128), 1)
    block_column = iota((32, 128), 0)
    same = (owner_column == dense_owner) & (block_row < block_column) & (block_row < DENSE)
    rank = jnp.sum(same.astype(I32), 1, keepdims=True)
    at = block_row * UNIT
    need = jnp.where(block_row < PLACE_BLOCKS, 0, jnp.where((at >= AT_K) & (at < AT_O), 2, 1))
    unit = jnp.sum(jnp.where(same, need, 0), 1, keepdims=True)
    lower = (dense_owner < owner_column) & (block_row < DENSE)
    order = rank + jnp.sum(lower.astype(I32), 1, keepdims=True)
    crowded = jnp.max(((rank >= DENSE_CAP) & (iota((32, 1), 0) < DENSE)).astype(I32))
    which = iota((32, wide), 1)
    code = jnp.where(
        which < TABLE_BLOCKS,
        KIND_TABLE,
        jnp.where(
            which < TABLE_BLOCKS + PLACE_BLOCKS, KIND_PLACE + which - TABLE_BLOCKS, KIND_DENSE
        ),
    )
    here = (every_slot == me[0] * slots + iota((32, wide), 0)) & (which < n_units)
    kind = jnp.sum(jnp.where(here, code, 0), 1, keepdims=True)
    entry = block_row
    tab[...] = jnp.where(
        entry == TAB_OWNER,
        owner_column,
        jnp.where(
            entry == TAB_RANK,
            jnp.minimum(rank, DENSE_CAP - 1),
            jnp.where(
                entry == TAB_SLOT,
                slot_column - owner_column * slots,
                jnp.where(
                    entry == TAB_UNIT,
                    jnp.minimum(unit, UNITS_L - 2),
                    jnp.where(entry == TAB_KIND, kind, jnp.minimum(order, DENSE - 1)),
                ),
            ),
        ),
    )

    ids[:, 0:QROWS] = query_ids[0:1]
    ids[:, QROWS : 2 * QROWS] = query_ids[1:2]
    ids[:, STARTS[2] : STARTS[3]] = passage_ids[0:1]
    ids[:, STARTS[3] :] = passage_ids[1:2]
    token = ids[...]
    _, live = token_facts(query_lengths, passage_lengths)
    lane = iota((1, TOKENS), 1)
    block = token // UNIT
    slot = jnp.zeros((1, TOKENS), I32)
    table_rows = -(-TABLE_BLOCKS // 128) * 128
    for at in range(0, table_rows, 128):
        column = to_column(owner_row[:, at : at + 128])
        hit = (iota((128, TOKENS), 0) + at) == block
        slot = slot + jnp.sum(jnp.where(hit, column, 0), 0, keepdims=True)
    owner = owner_of(slot, slots, n_blk)
    inside = slot - owner * slots
    row = token - block * UNIT
    upper = (row >= HALF).astype(I32)
    dest = owner * n_rep + upper
    local_row = inside * HALF + row - upper * HALF
    token = jnp.where(live, token, -1)
    first_at = jnp.full((128, TOKENS), TOKENS, I32)
    for at in range(0, TOKENS, 128):
        column = to_column(token[:, at : at + 128])
        same = column == token
        first_at = jnp.minimum(first_at, jnp.where(same, iota((128, TOKENS), 0) + at, TOKENS))
    first_at = jnp.min(first_at, 0, keepdims=True)
    first = live & (first_at == lane)
    chosen = ((iota((n_dest, TOKENS), 0) == dest) & first).astype(F32)
    chosen_low = chosen.astype(BF16)
    seen = jnp.zeros((n_dest, TOKENS), F32)
    for at in range(0, TOKENS, 128):
        earlier = ((iota((128, TOKENS), 0) + at) < first_at).astype(F32).astype(BF16)
        seen = seen + dot_nn(chosen_low[:, at : at + 128], earlier)
    rank = jnp.sum(
        jnp.where(iota((n_dest, TOKENS), 0) == dest, seen, 0.0), 0, keepdims=True
    ).astype(I32)
    fits = live & (rank < cap)
    where_row[...] = jnp.where(fits, dest * cap + rank, -1)
    over = jnp.max((live & (rank >= cap)).astype(I32))
    code = local_row + 1
    high = code // 32
    low = code - high * 32
    spread = (iota((128, TOKENS), 0) == rank).astype(F32).astype(BF16)
    sent_high = dot_nt((chosen * high.astype(F32)).astype(BF16), spread)
    sent_low = dot_nt((chosen * low.astype(F32)).astype(BF16), spread)
    flag = jnp.maximum(over, crowded)
    column_of = iota((1, 128), 1)
    marks = jnp.where(
        column_of == 0,
        positive[0, 0],
        jnp.where(column_of == 1, positive[0, 1], jnp.where(column_of == 2, flag, 0)),
    ).astype(F32)
    row16 = iota((16, 128), 0)
    for d in range(n_dest):
        asked = jnp.where(
            row16 == 0,
            sent_high[d : d + 1],
            jnp.where(row16 == 1, sent_low[d : d + 1], jnp.where(row16 == 2, marks, 0.0)),
        )
        message[d, AT_ASKED:] = asked.astype(BF16)
    for spot in range(HELD):
        present = spot // 2 * 4 + 2 * me[1] + spot % 2 < have

        @pl.when(present)
        def _():
            pltpu.make_async_copy(weights.at[0], loaded.at[spot], sems.at[spot]).wait()

        @pl.when(jnp.logical_not(present))
        def _():
            loaded[spot] = jnp.zeros((UNIT, D), F32)

    for odd in range(2):
        for c in range(DENSE_CAP // 4):
            whole = loaded[2 * c + (odd + before) % 2].astype(BF16)
            for s in range(n_blk):
                p = s % PIECES
                message[2 * s + odd, PIECE * c : PIECE * (c + 1)] = whole[
                    PIECE * (p % 8) : PIECE * (p % 8 + 1), 128 * (p // 8) : 128 * (p // 8 + 1)
                ]


def request(owners, me, positive, query_lengths, passage_lengths, query_ids, passage_ids, weights, n_blk, cap):
    slots = weights.shape[0]
    n_dest = 2 * n_blk
    n_units = owners.shape[0]
    owner_row = owners.reshape(1, n_units)
    return pl.pallas_call(
        partial(request_kernel, slots, n_blk, cap),
        out_shape=(
            jax.ShapeDtypeStruct((n_dest, MESSAGE_ROWS, 128), BF16),
            jax.ShapeDtypeStruct((1, TOKENS), I32),
            jax.ShapeDtypeStruct((32, 128), I32),
        ),
        in_specs=[smem] * 5 + [vmem] * 3 + [hbm],
        out_specs=(vmem, vmem, vmem),
        scratch_shapes=[
            pltpu.VMEM((1, TOKENS), I32),
            pltpu.VMEM((1, -(-n_units // 128) * 128), I32),
            pltpu.VMEM((HELD, UNIT, D), F32),
            pltpu.SemaphoreType.DMA((HELD,)),
        ],
        compiler_params=params(n_blk, 12),
        name="request",
    )(owners, me, positive, query_lengths, passage_lengths, owner_row, query_ids, passage_ids, weights)


def collect_kernel(tab, me, message, mine_out):
    for b in range(DENSE):
        order = tab[b, TAB_ORDER]
        rank = tab[b, TAB_RANK]

        @pl.when(order % 2 == me[1])
        def _():
            spot = pl.multiple_of(rank // 4 * PIECE, PIECE)
            sender = 2 * tab[b, TAB_OWNER] + rank // 2 % 2
            mine_out[order // 2] = message[sender, pl.ds(spot, PIECE), :]


def collect(tab, me, message):
    return pl.pallas_call(
        collect_kernel,
        out_shape=jax.ShapeDtypeStruct((CLASS, PIECE, 128), BF16),
        in_specs=[smem, smem, vmem],
        out_specs=vmem,
        compiler_params=params(message.shape[0] // 2, 2),
        name="collect",
    )(tab, me, message)


def fetch_kernel(slots, cap, me, message, weights, rows_out, asked_out, held, table, hot, sem):
    n_dest = message.shape[0]
    copy = pltpu.make_async_copy(weights.at[:, pl.ds(me[1] * HALF, HALF), :], held, sem)
    copy.start()
    column_of = iota((1, 128), 1)
    for s in range(n_dest):
        part = message[s, AT_ASKED:].astype(F32)
        wanted = part[0:1] * 32.0 + part[1:2] - 1.0
        marks = part[2:3]
        row = jnp.where(column_of < cap, wanted, 0.0)
        for i in range(3):
            row = jnp.where(column_of == 124 + i, marks[:, i : i + 1], row)
        asked_out[s : s + 1] = row.astype(I32)
    wide = table.shape[0]
    rows = asked_out[...]
    pad = -n_dest % 128
    if pad:
        rows = jnp.concatenate([rows, jnp.zeros((pad, 128), I32)], 0)
    columns = rows.T
    for s in range(n_dest):
        hot[s * cap : (s + 1) * cap] = (
            (iota((cap, wide), 1) == columns[:cap, s : s + 1]).astype(F32).astype(BF16)
        )
    copy.wait()
    filled = slots * HALF
    table[:filled] = held[...].reshape(filled, D).astype(BF16)
    if wide > filled:
        table[filled:] = jnp.zeros((wide - filled, D), BF16)
    rows_out[...] = dot_nn(hot[...], table[...]).astype(BF16)


def fetch(me, message, weights, cap):
    slots = weights.shape[0]
    n_dest = message.shape[0]
    wide = -(-slots * HALF // 128) * 128
    return pl.pallas_call(
        partial(fetch_kernel, slots, cap),
        out_shape=(
            jax.ShapeDtypeStruct((n_dest * cap, D), BF16),
            jax.ShapeDtypeStruct((n_dest, 128), I32),
        ),
        in_specs=[smem, vmem, hbm],
        out_specs=(vmem, vmem),
        scratch_shapes=[
            pltpu.VMEM((slots, HALF, D), F32),
            pltpu.VMEM((wide, D), BF16),
            pltpu.VMEM((n_dest * cap, wide), BF16),
            pltpu.SemaphoreType.DMA,
        ],
        compiler_params=params(n_dest // 2, 16),
        name="fetch",
    )(me, message, weights)


ST_POOLED, ST_C, ST_N2, ST_N1, ST_H, ST_O, ST_Q, ST_X0 = range(0, 64, 8)
ST_KQ, ST_B, ST_U, ST_A, ST_I1, ST_I2 = 64, 96, 128, 160, 192, 200
ST_ROWS = 208


def forward_kernel(
    tab, me, query_lengths, passage_lengths, positive, rows, where_row, vectors, g0, g1, g2, g3,
    g4, g5, g6, g7, emb_out, low_out, normed_out, scale_out, probs_out, state, matrices, embedded,
    sems,
):
    copies = piece_copies(me, (g0, g1, g2, g3, g4, g5, g6, g7), matrices, sems)
    for copy in copies:
        copy.start()
    taken = rows.shape[0]
    for at in range(0, TOKENS, 128):
        column = to_column(where_row[:, at : at + 128])
        hot = (iota((128, taken), 1) == column).astype(F32).astype(BF16)
        embedded[at : at + 128] = dot_nn(hot, rows[...])
    for copy in copies:
        copy.wait()
    shift = vectors[0:1]
    for start, length in zip(STARTS, (QROWS, QROWS, PLEN, PLEN)):
        e = embedded[start : start + length] + rows_at(matrices, tab, 0, length).astype(F32) + shift
        centred = e - jnp.mean(e, -1, keepdims=True)
        scale = lax.rsqrt(jnp.mean(centred * centred, -1, keepdims=True) + NORM_EPS)
        normed = centred * scale
        normed_out[start : start + length] = normed
        scale_out[start : start + length] = jnp.broadcast_to(scale, (length, 128))
        x = normed * vectors[1:2] + vectors[2:3]
        embedded[start : start + length] = x
        low_out[start : start + length] = x.astype(BF16)
    x0 = jnp.concatenate(
        [embedded[s : s + 1] for s in STARTS] + [jnp.zeros((4, D), F32)], 0
    )
    x0_low = x0.astype(BF16)
    q = (dot_nn(x0_low, rows_at(matrices, tab, AT_Q, AT_K)) + vectors[4:5]).astype(BF16)
    head_of = iota((8, D), 1) // HALF
    q_heads = jnp.concatenate(
        [jnp.where(head_of == h, q.astype(F32), 0.0) for h in range(HEADS)], 0
    ).astype(BF16)
    kq = dot_nt(q_heads, rows_at(matrices, tab, AT_K, AT_V)) * (D // HEADS) ** (-0.5)
    low = low_out[...]
    scores = fine(dot_nt, kq, low)
    sequence, live = token_facts(query_lengths, passage_lengths)
    valid = ((iota((32, TOKENS), 0) & 7) == sequence) & live
    scores = jnp.where(valid, scores, NEVER)
    top = jnp.max(scores, -1, keepdims=True)
    weight = jnp.where(valid, jnp.exp(scores - top), 0.0)
    total = jnp.sum(weight, -1, keepdims=True)
    probs = weight / jnp.where(total > 0.0, total, 1.0)
    probs_out[...] = probs
    mixed = dot_nn(probs.astype(BF16), low)
    valued = fine(dot_nn, mixed, rows_at(matrices, tab, AT_V, AT_O))
    blended = jnp.zeros((8, D), F32)
    for h in range(HEADS):
        blended = blended + jnp.where(head_of == h, valued[8 * h : 8 * h + 8], 0.0)
    real = iota((8, D), 0) < 4
    blended = jnp.where(real, blended + vectors[5:6], 0.0).astype(BF16)
    summed = x0 + dot_nn(blended, rows_at(matrices, tab, AT_O, AT_UP)) + vectors[6:7]
    h0, n1, i1 = norm_rows(summed, vectors[8:9], vectors[9:10])
    h_low = h0.astype(BF16)
    bias_up = jnp.concatenate([vectors[12 + i : 13 + i] for i in range(FF // D)], 1)
    u = dot_nt(h_low, rows_at(matrices, tab, AT_UP, AT_DOWN)) + bias_up
    a = (0.5 * u * (1.0 + lax.erf(u * (0.5**0.5)))).astype(BF16)
    second = h0 + dot_nn(a, rows_at(matrices, tab, AT_DOWN, DENSE * UNIT)) + vectors[7:8]
    x, n2, i2 = norm_rows(second, vectors[10:11], vectors[11:12])
    c = x.astype(BF16)
    pooled = jnp.tanh(dot_nn(c, rows_at(matrices, tab, AT_POOL, AT_Q)) + vectors[3:4])
    row8 = iota((8, 128), 0)
    sent = jnp.concatenate(
        [
            jnp.where(real, pooled, 0.0),
            jnp.where(
                row8 == 0,
                positive[0, 0].astype(F32),
                jnp.where(row8 == 1, positive[0, 1].astype(F32), -1.0),
            ),
        ],
        1,
    )
    n_blk = emb_out.shape[0] // 8
    emb_out[...] = jnp.concatenate([sent] * n_blk, 0).astype(BF16)
    state[ST_POOLED : ST_POOLED + 8] = pooled
    state[ST_C : ST_C + 8] = c.astype(F32)
    state[ST_N2 : ST_N2 + 8] = n2
    state[ST_N1 : ST_N1 + 8] = n1
    state[ST_H : ST_H + 8] = h_low.astype(F32)
    state[ST_O : ST_O + 8] = blended.astype(F32)
    state[ST_Q : ST_Q + 8] = q.astype(F32)
    state[ST_X0 : ST_X0 + 8] = x0_low.astype(F32)
    state[ST_KQ : ST_KQ + 32] = kq
    state[ST_B : ST_B + 32] = mixed
    for i in range(FF // D):
        state[ST_U + 8 * i : ST_U + 8 * i + 8] = u[:, i * D : (i + 1) * D]
        state[ST_A + 8 * i : ST_A + 8 * i + 8] = a[:, i * D : (i + 1) * D].astype(F32)
    state[ST_I1 : ST_I1 + 8] = jnp.broadcast_to(i1, (8, D))
    state[ST_I2 : ST_I2 + 8] = jnp.broadcast_to(i2, (8, D))


def forward(tab, me, query_lengths, passage_lengths, positive, rows, where_row, vectors, gathered, n_blk):
    return pl.pallas_call(
        forward_kernel,
        out_shape=(
            jax.ShapeDtypeStruct((n_blk * 8, D + 128), BF16),
            jax.ShapeDtypeStruct((TOKENS, D), BF16),
            jax.ShapeDtypeStruct((TOKENS, D), F32),
            jax.ShapeDtypeStruct((TOKENS, 128), F32),
            jax.ShapeDtypeStruct((32, TOKENS), F32),
            jax.ShapeDtypeStruct((ST_ROWS, D), F32),
            jax.ShapeDtypeStruct((CLASS, 2, UNIT, D), BF16),
        ),
        in_specs=[smem] * 5 + [vmem] * 3 + [hbm] * 8,
        out_specs=(vmem,) * 7,
        scratch_shapes=[
            pltpu.VMEM((TOKENS, D), F32),
            pltpu.SemaphoreType.DMA((2 * PIECES,)),
        ],
        compiler_params=params(n_blk, 12),
        name="forward",
    )(
        tab, me, query_lengths, passage_lengths, positive, rows, where_row, vectors,
        *[pltpu.with_memory_space_constraint(a, pltpu.HBM) for a in gathered],
    )


def place_rows(n_dest):
    return max(PLEN // n_dest, 16)


def payload_rows(n_dest, cap):
    at_place = 2 * cap
    at_left = at_place + 2 * place_rows(n_dest)
    at_right = at_left + L_ROWS
    return at_place, at_left, at_right, at_right + 32


def backward_kernel(
    cap, tab, me, prefix_lengths, prefix_weights, emb, message, where_row, low_in, normed, scale,
    probs_in, state, vectors, matrices, payload, loss_out, count_out,
    received, grad_emb, dx, left,
):
    n_blk = emb.shape[0] // 8
    n_dest = 2 * n_blk
    for i in range(3):
        received[i * n_blk * 8 : (i + 1) * n_blk * 8] = emb[:, 128 * i : 128 * i + 128].astype(F32)

    def every(k):
        return jnp.concatenate(
            [received[pl.ds(i * n_blk * 8 + k, n_blk, stride=8), :] for i in range(3)], 1
        )

    queries = jnp.concatenate([every(0), every(1)], 0)
    passages = jnp.concatenate([every(2), every(3)], 0)[:, :D].astype(BF16)
    wanted = queries[:, D : D + 1].astype(I32)
    queries = queries[:, :D]
    query_low = queries.astype(BF16)
    size = 2 * n_blk
    counted = wanted >= 0
    counted_f = counted.astype(F32)
    column = iota((size, size), 1)
    target = (column == (wanted & 1) * n_blk + wanted // 2) & counted
    marks = message[...]
    lane = iota(marks.shape, 1)
    count = jnp.sum((((lane == 124) | (lane == 125)) & (marks >= 0)).astype(F32))
    count_out[0, 0] = count
    feature = iota((1, D), 1)
    losses = jnp.zeros((size, 1), F32)
    d_queries = jnp.zeros((size, D), F32)
    d_passages = jnp.zeros((size, D), F32)
    for k in range(prefix_lengths.shape[0]):
        mask = (feature < prefix_lengths[k]).astype(F32)
        prefix = jnp.full((1, 1), prefix_lengths[k], I32).astype(F32)
        temper = TEMPER * lax.rsqrt(prefix)
        logits = dot_nt((queries * mask).astype(BF16), passages) * temper
        top = jnp.max(logits, -1, keepdims=True)
        weight = jnp.exp(logits - top)
        total = jnp.sum(weight, -1, keepdims=True)
        hit = jnp.sum(jnp.where(target, logits, 0.0), -1, keepdims=True)
        losses = losses + prefix_weights[k] * (top + jnp.log(total) - hit)
        factor = counted_f * (prefix_weights[k] / count) * temper
        grad = (weight / total - target.astype(F32)) * factor
        high, lower = split(grad)
        d_queries = d_queries + mask * (dot_nn(high, passages) + dot_nn(lower, passages))
        d_passages = d_passages + mask * (dot_tn(high, query_low) + dot_tn(lower, query_low))
    loss_out[0, 0] = jnp.sum(losses * counted_f)
    grad_emb[:size] = d_queries
    grad_emb[size : 2 * size] = d_passages
    grad_pooled = jnp.concatenate(
        [grad_emb[pl.ds(me[0] + i * n_blk, 1), :] for i in range(4)]
        + [jnp.zeros((4, D), F32)],
        0,
    )

    def kept_rows(at, rows=8):
        return state[at : at + rows]

    pooled = kept_rows(ST_POOLED)
    d_pre = grad_pooled * (1.0 - pooled * pooled)
    d_c = fine(dot_nt, d_pre, rows_at(matrices, tab, AT_POOL, AT_Q))
    n2 = kept_rows(ST_N2)
    d_second, d_g2, d_s2 = norm_back(d_c, n2, kept_rows(ST_I2), vectors[10:11])
    down_low = d_second.astype(BF16)
    d_a = dot_nt(down_low, rows_at(matrices, tab, AT_DOWN, DENSE * UNIT))
    u = jnp.concatenate([kept_rows(ST_U + 8 * i) for i in range(FF // D)], 1)
    slope = 0.5 * (1.0 + lax.erf(u * (0.5**0.5))) + u * jnp.exp(-0.5 * u * u) * (
        0.3989422804014327
    )
    up_low = (d_a * slope).astype(BF16)
    d_h = d_second + dot_nn(up_low, rows_at(matrices, tab, AT_UP, AT_DOWN))
    d_summed, d_g1, d_s1 = norm_back(d_h, kept_rows(ST_N1), kept_rows(ST_I1), vectors[8:9])
    branch_low = d_summed.astype(BF16)
    d_o = dot_nt(branch_low, rows_at(matrices, tab, AT_O, AT_UP)).astype(BF16)
    head_of = iota((8, D), 1) // HALF
    o_heads = jnp.concatenate(
        [jnp.where(head_of == h, d_o.astype(F32), 0.0) for h in range(HEADS)], 0
    ).astype(BF16)
    vo = dot_nt(o_heads, rows_at(matrices, tab, AT_V, AT_O))
    low = low_in[...]
    probs = probs_in[...]
    d_probs = fine(dot_nt, vo, low)
    d_scores = probs * (d_probs - jnp.sum(d_probs * probs, -1, keepdims=True))
    score_low = d_scores.astype(BF16)
    mixed_score = dot_nn(score_low, low)
    keyed = fine(dot_nn, mixed_score, rows_at(matrices, tab, AT_K, AT_V))
    d_q = jnp.zeros((8, D), F32)
    for h in range(HEADS):
        d_q = d_q + jnp.where(head_of == h, keyed[8 * h : 8 * h + 8], 0.0)
    d_q_low = (d_q * (D // HEADS) ** (-0.5)).astype(BF16)
    d_x0 = d_summed + dot_nt(d_q_low, rows_at(matrices, tab, AT_Q, AT_K))
    kq = kept_rows(ST_KQ, 32)
    vo_high, vo_low = split(vo)
    kq_high, kq_low = split(kq)
    probs_low = probs.astype(BF16)
    dx[...] = dot_tn(
        jnp.concatenate([probs_low, score_low, probs_low, score_low], 0),
        jnp.concatenate([vo_high, kq_high, vo_low, kq_low], 0),
    )
    for i, start in enumerate(STARTS):
        dx[start : start + 1] = dx[start : start + 1] + d_x0[i : i + 1]
    d_gain = jnp.zeros((1, D), F32)
    d_shift = jnp.zeros((1, D), F32)
    d_type = jnp.zeros((1, D), F32)
    for start in range(0, TOKENS, 256):
        incoming = dx[start : start + 256]
        n = normed[start : start + 256]
        d_gain = d_gain + jnp.sum(incoming * n, 0, keepdims=True)
        d_shift = d_shift + jnp.sum(incoming, 0, keepdims=True)
        dn = incoming * vectors[1:2]
        inner = (
            dn - jnp.mean(dn, -1, keepdims=True) - n * jnp.mean(dn * n, -1, keepdims=True)
        )
        de = inner * scale[start : start + 256, :1]
        d_type = d_type + jnp.sum(de, 0, keepdims=True)
        dx[start : start + 256] = de
    de_low = dx[...].astype(BF16)
    at_place, at_left, at_right, n_rows = payload_rows(n_dest, cap)
    per = max(128 // cap, 1)
    step = per * cap
    for at in range(0, n_dest * cap, step):
        hot = ((iota((step, TOKENS), 0) + at) == where_row[...]).astype(F32).astype(BF16)
        summed = dot_nn(hot, de_low).astype(BF16)
        for i in range(per):
            d = at // cap + i
            if d < n_dest:
                payload[d, :cap] = summed[i * cap : (i + 1) * cap, :128]
                payload[d, cap : 2 * cap] = summed[i * cap : (i + 1) * cap, 128:]
    spots = dx[STARTS[2] : STARTS[3]] + dx[STARTS[3] :]
    dx[STARTS[2] : STARTS[3]] = spots
    dx[STARTS[2] : STARTS[2] + QROWS] = (
        dx[STARTS[2] : STARTS[2] + QROWS] + dx[:QROWS] + dx[QROWS : 2 * QROWS]
    )
    pr = place_rows(n_dest)
    share = PLEN // n_dest
    for d in range(n_dest):
        spot = dx[STARTS[2] + d * share : STARTS[2] + (d + 1) * share]
        if share < pr:
            spot = jnp.concatenate([spot, jnp.zeros((pr - share, D), F32)], 0)
        payload[d, at_place : at_place + pr] = spot[:, :128].astype(BF16)
        payload[d, at_place + pr : at_place + 2 * pr] = spot[:, 128:].astype(BF16)
    left[...] = jnp.zeros(left.shape, F32)
    up_f = up_low.astype(F32)

    def put(b, r, unit, values):
        spot = (tab[b, TAB_OWNER] * 2 + r) * L_ROWS + (tab[b, TAB_UNIT] + unit) * 4
        for i in range(4):
            left[pl.ds(spot + i, 1), :] = values[i : i + 1]

    for b in range(PLACE_BLOCKS, DENSE):
        at = b * UNIT
        if AT_K <= at < AT_O:
            heads = mixed_score if at < AT_V else kept_rows(ST_B, 32)
            off = (at - AT_K) % D
            for r in range(2):
                for j in range(2):
                    h = 2 * r + j
                    put(b, r, j, heads[8 * h : 8 * h + 4, off : off + UNIT])
            continue
        if at < AT_Q:
            values, off = kept_rows(ST_C), at - AT_POOL
        elif at < AT_K:
            values, off = kept_rows(ST_X0), at - AT_Q
        elif at < AT_UP:
            values, off = kept_rows(ST_O), at - AT_O
        elif at < AT_DOWN:
            values, off = up_f, at - AT_UP
        else:
            off = (at - AT_DOWN) % D
            values = kept_rows(ST_A + 8 * ((at - AT_DOWN) // D))
        for r in range(2):
            put(b, r, 0, values[:4, off : off + UNIT])
    d_vectors = jnp.concatenate(
        [
            d_type,
            d_gain,
            d_shift,
            jnp.sum(d_pre, 0, keepdims=True),
            jnp.sum(d_q_low.astype(F32), 0, keepdims=True),
            jnp.sum(d_o.astype(F32), 0, keepdims=True),
            jnp.sum(branch_low.astype(F32), 0, keepdims=True),
            jnp.sum(down_low.astype(F32), 0, keepdims=True),
            d_g1[None],
            d_s1[None],
            d_g2[None],
            d_s2[None],
        ]
        + [
            jnp.sum(up_f[:, i * D : (i + 1) * D], 0, keepdims=True) for i in range(FF // D)
        ],
        0,
    )
    scaled_q = kept_rows(ST_Q) * (D // HEADS) ** (-0.5)
    right = jnp.concatenate(
        [
            v.astype(F32)[:4]
            for v in (d_pre, d_q_low, scaled_q, d_o, branch_low, kept_rows(ST_H), down_low)
        ],
        0,
    )
    for d in range(n_dest):
        payload[d, at_left:at_right] = left[d * L_ROWS : (d + 1) * L_ROWS].astype(BF16)
        r = d % 2
        if d < 32:
            share_vec = d_vectors[d // 2 : d // 2 + 1, r * 128 : (r + 1) * 128]
        else:
            share_vec = jnp.zeros((1, 128), F32)
        payload[d, at_right:n_rows] = jnp.concatenate(
            [right[:, r * 128 : (r + 1) * 128], share_vec, jnp.zeros((3, 128), F32)], 0
        ).astype(BF16)


def backward(tab, me, prefix_lengths, prefix_weights, emb, message, where_row, low, normed, scale, probs, state, vectors, matrices, cap):
    n_dest = message.shape[0]
    n_rows = payload_rows(n_dest, cap)[-1]
    return pl.pallas_call(
        partial(backward_kernel, cap),
        out_shape=(
            jax.ShapeDtypeStruct((n_dest, n_rows, 128), BF16),
            jax.ShapeDtypeStruct((1, 1), F32),
            jax.ShapeDtypeStruct((1, 1), F32),
        ),
        in_specs=[smem] * 4 + [vmem] * 10,
        out_specs=(vmem, smem, smem),
        scratch_shapes=[
            pltpu.VMEM((emb.shape[0] * 3, 128), F32),
            pltpu.VMEM((emb.shape[0], D), F32),
            pltpu.VMEM((TOKENS, D), F32),
            pltpu.VMEM((n_dest * L_ROWS, 128), F32),
        ],
        compiler_params=params(n_dest // 2, 16),
        name="backward",
    )(tab, me, prefix_lengths, prefix_weights, emb, message, where_row, low, normed, scale, probs, state, vectors, matrices)


def reduce_kernel(slots, cap, tab, me, loss, asked, payload, reduced, news, total, row_grads, left, right):
    n_dest = payload.shape[0]
    at_place, at_left, at_right, n_rows = payload_rows(n_dest, cap)
    for d in range(n_dest):
        row_grads[d * cap : (d + 1) * cap, :128] = payload[d, :cap]
        row_grads[d * cap : (d + 1) * cap, 128:] = payload[d, cap : 2 * cap]
        left[d * L_ROWS : (d + 1) * L_ROWS] = payload[d, at_left:at_right].astype(F32)
        right[d * 32 : (d + 1) * 32] = payload[d, at_right:n_rows].astype(F32)
    grads = row_grads[...]
    filled = slots * HALF
    for at in range(0, filled, 64):
        hot = ((iota((64, n_dest * cap), 0) + at) == asked[...]).astype(F32).astype(BF16)
        total[at : at + 64] = dot_nn(hot, grads)
    mine = me[0]
    odd = me[1]
    column = iota((n_dest * 4, 128), 1)

    def rows_of(ref, start, stride):
        return jnp.concatenate(
            [ref[pl.ds(start + q, n_dest, stride=stride), :] for q in range(4)], 0
        ).astype(BF16)

    for b in range(PLACE_BLOCKS, DENSE):
        at = b * UNIT
        if at < AT_Q:
            m = 0
        elif at < AT_UP:
            m = 1 + (at - AT_Q) // D
        elif at < AT_DOWN:
            m = 5
        else:
            m = 6

        @pl.when(tab[b, TAB_OWNER] == mine)
        def _():
            unit = tab[b, TAB_UNIT] * 4
            pull = rows_of(right, m * 4, 32)
            if AT_K <= at < AT_O:
                grad = dot_tn(
                    rows_of(left, unit, L_ROWS), jnp.where(column < HALF, pull, 0).astype(BF16)
                ) + dot_tn(
                    rows_of(left, unit + 4, L_ROWS),
                    jnp.where(column < HALF, 0, pull).astype(BF16),
                )
            else:
                grad = dot_tn(rows_of(left, unit, L_ROWS), pull)
            spot = pl.multiple_of(tab[b, TAB_SLOT] * HALF, HALF)
            total[pl.ds(spot, HALF), :128] = grad[:HALF]
            total[pl.ds(spot, HALF), 128:] = grad[HALF:]

    pr = place_rows(n_dest)
    spots_low = jnp.zeros((pr, 128), F32)
    spots_high = jnp.zeros((pr, 128), F32)
    for d in range(n_dest):
        spots_low = spots_low + payload[d, at_place : at_place + pr].astype(F32)
        spots_high = spots_high + payload[d, at_place + pr : at_place + 2 * pr].astype(F32)
    spots = jnp.concatenate([spots_low, spots_high], 1)
    vector = jnp.sum(right[pl.ds(28, n_dest, stride=32), :], 0, keepdims=True)
    summed = total[...]
    reduced[...] = summed.astype(BF16).reshape(reduced.shape)
    square = jnp.sum(summed * summed) + jnp.sum(spots * spots) + jnp.sum(vector * vector)
    row16 = iota((pr, 128), 0)

    def parts(v):
        first = v.astype(BF16).astype(F32)
        second = (v - first).astype(BF16).astype(F32)
        return first, second, v - first - second

    extra = jnp.zeros((pr, 128), F32)
    for i, part in enumerate(
        parts(vector)
        + parts(jnp.full((1, 128), square, F32))
        + parts(jnp.full((1, 128), loss[0, 0], F32))
    ):
        extra = jnp.where(row16 == i, part, extra)
    block = jnp.concatenate([spots, extra], 1).astype(BF16)
    for d in range(n_dest):
        news[d * pr : (d + 1) * pr] = block


def reduce(tab, me, loss, asked, payload, slots, cap):
    n_dest = payload.shape[0]
    pr = place_rows(n_dest)
    return pl.pallas_call(
        partial(reduce_kernel, slots, cap),
        out_shape=(
            jax.ShapeDtypeStruct((slots, HALF, D), BF16),
            jax.ShapeDtypeStruct((n_dest * pr, D + 128), BF16),
        ),
        in_specs=[smem, smem, smem, vmem, vmem],
        out_specs=(vmem, vmem),
        scratch_shapes=[
            pltpu.VMEM((slots * HALF, D), F32),
            pltpu.VMEM((n_dest * cap, D), BF16),
            pltpu.VMEM((n_dest * L_ROWS, 128), F32),
            pltpu.VMEM((n_dest * 32, 128), F32),
        ],
        compiler_params=params(n_dest // 2, 16),
        name="reduce",
    )(tab, me, loss, asked, payload)


RING = 4


def update_kernel(
    pr, tab, me, news, places, own, other, weight, first, second, vectors, vector_first,
    vector_second, weight_out, first_out, second_out, vectors_out, vector_first_out,
    vector_second_out, loss_out, norm_out, grad, held, done, in_sems, sems,
):
    n_dest = news.shape[0] // pr
    slots = weight.shape[0]

    def in_copies(i):
        return [
            pltpu.make_async_copy(a.at[i], held.at[k, i], in_sems.at[k, i])
            for k, a in enumerate((weight, first, second))
        ]

    def fetch_one(i, c):
        for copy in in_copies(i):
            copy.start()
        return c

    lax.fori_loop(0, slots, fetch_one, 0)
    extra = news[:, D:].astype(F32).reshape(n_dest, pr, 128)
    square = jnp.sum(jnp.sum(extra[:, 3:6, :], 0), 0, keepdims=True)
    norm = jnp.sqrt(square)
    factor = CLIP_AT / jnp.maximum(norm, CLIP_AT)
    norm_out[0, 0] = norm[0, 0]
    loss = jnp.sum(jnp.sum(extra[0:2, 6:9, :], 0), 0, keepdims=True)
    loss_out[0, 0] = loss[0, 0]
    pairs = jnp.sum(extra[:32, 0:3, :], 1).reshape(16, 2, 128)
    vector_grad = jnp.concatenate([pairs[:, 0], pairs[:, 1]], 1) * factor[:, :1]
    v, m1, m2 = adam_step(
        vectors[...], vector_first[...], vector_second[...], vector_grad, VECTOR_RATE, 0.0
    )
    vectors_out[...] = v
    vector_first_out[...] = m1
    vector_second_out[...] = m2
    flip = me[1] == 0
    scale = jnp.broadcast_to(jnp.concatenate([factor, factor], 1), (UNIT, D))
    first_scale = -RATE / (1.0 - BETA_ONE**STEP)
    second_scale = 1.0 / (1.0 - BETA_TWO**STEP)

    def out_copies(i, b):
        return [
            pltpu.make_async_copy(done.at[b, k], out.at[i], sems.at[b, k])
            for k, out in enumerate((weight_out, first_out, second_out))
        ]

    def one(i, c):
        kind = tab[i, TAB_KIND]
        b = lax.rem(i, RING)
        mine = own[i].astype(F32)
        theirs = other[i].astype(F32)
        lower = jnp.where(flip, mine, theirs)
        upper = jnp.where(flip, theirs, mine)

        @pl.when(kind == KIND_TABLE)
        def _():
            grad[:HALF] = lower
            grad[HALF:] = upper

        @pl.when(kind == KIND_DENSE)
        def _():
            grad[:HALF, :128] = lower[:, :128]
            grad[HALF:, :128] = lower[:, 128:]
            grad[:HALF, 128:] = upper[:, :128]
            grad[HALF:, 128:] = upper[:, 128:]

        @pl.when((kind >= KIND_PLACE) & (kind < KIND_DENSE))
        def _():
            spot = pl.multiple_of((kind - KIND_PLACE) * UNIT, UNIT)
            grad[...] = places[pl.ds(spot, UNIT), :D].astype(F32)

        @pl.when(i >= RING)
        def _():
            for copy in out_copies(i - RING, b):
                copy.wait()

        for copy in in_copies(i):
            copy.wait()

        @pl.when(kind == 0)
        def _():
            for k in range(3):
                done[b, k] = held[k, i]

        @pl.when(kind > 0)
        def _():
            g = grad[...] * scale
            m1 = BETA_ONE * held[1, i] + (1.0 - BETA_ONE) * g
            m2 = BETA_TWO * held[2, i] + (1.0 - BETA_TWO) * (g * g)
            root = jnp.sqrt(m2 * second_scale) + EPSILON
            done[b, 0] = held[0, i] * (1.0 - RATE * DECAY) + (m1 * first_scale) / root
            done[b, 1] = m1
            done[b, 2] = m2

        for copy in out_copies(i, b):
            copy.start()
        return c

    lax.fori_loop(0, slots, one, 0)
    for i in range(max(slots - RING, 0), slots):
        for copy in out_copies(i, i % RING):
            copy.wait()


def update(tab, me, news, own, other, weights, first, second, vectors, vector_first, vector_second, pr):
    n_dest = news.shape[0] // pr
    share = PLEN // n_dest
    places = news
    if share < pr:
        places = news.reshape(n_dest, pr, -1)[:, :share].reshape(PLEN, -1)
    big = jax.ShapeDtypeStruct(weights.shape, F32)
    small = jax.ShapeDtypeStruct(vectors.shape, F32)
    one = jax.ShapeDtypeStruct((1, 1), F32)
    return pl.pallas_call(
        partial(update_kernel, pr),
        out_shape=(big, big, big, small, small, small, one, one),
        in_specs=[smem, smem] + [vmem] * 4 + [hbm] * 3 + [vmem] * 3,
        out_specs=(hbm, hbm, hbm, vmem, vmem, vmem, smem, smem),
        scratch_shapes=[
            pltpu.VMEM((UNIT, D), F32),
            pltpu.VMEM((3,) + weights.shape, F32),
            pltpu.VMEM((RING, 3, UNIT, D), F32),
            pltpu.SemaphoreType.DMA((3, weights.shape[0])),
            pltpu.SemaphoreType.DMA((RING, 3)),
        ],
        compiler_params=params(n_dest // 2, 14),
        name="update",
    )(tab, me, news, places, own, other, weights, first, second, vectors, vector_first, vector_second)


def quick(
    query_ids, passage_ids, query_lengths, passage_lengths, positive, prefix_lengths,
    prefix_weights, owners, weights, first_moments, second_moments, vectors, vector_first,
    vector_second,
):
    slots = weights.shape[0]
    n_blk = lax.axis_size("blk")
    everyone = ("blk", "rep")
    cap = 48 if n_blk <= 16 else 16
    me = jnp.stack([lax.axis_index("blk"), lax.axis_index("rep")]).astype(I32)

    def exchange(a, axes):
        return lax.all_to_all(a, axes, 0, 0, tiled=True)

    message, where_row, tab = request(
        owners, me, positive, query_lengths, passage_lengths, query_ids[0], passage_ids[0],
        weights, n_blk, cap,
    )
    message = exchange(message, everyone)
    first = along_z(collect(tab, me, message), n_blk)
    rows, message = fetch(me, message, weights, cap)
    rows, first = lax.optimization_barrier((rows, first))
    rows = exchange(rows, everyone)
    gathered = spread(first, n_blk)
    emb, low, normed, scale, probs, state, matrices = forward(
        tab, me, query_lengths, passage_lengths, positive, rows, where_row, vectors, gathered, n_blk
    )
    emb = exchange(emb, "blk")
    payload, loss, count = backward(
        tab, me, prefix_lengths, prefix_weights, emb, message, where_row, low, normed, scale,
        probs, state, vectors, matrices, cap,
    )
    payload = exchange(payload, everyone)
    asked = message[:, :cap].reshape(1, -1)
    own, news = reduce(tab, me, loss, asked, payload, slots, cap)
    other = lax.ppermute(own, "rep", [(0, 1), (1, 0)])
    news = exchange(news, everyone)
    *outs, loss_sum, norm = update(
        tab, me, news, own, other, weights, first_moments, second_moments, vectors, vector_first,
        vector_second, place_rows(2 * n_blk),
    )

    def general(carry):
        return 0, local(
            query_ids, passage_ids, query_lengths, passage_lengths, positive, prefix_lengths,
            prefix_weights, owners, weights, first_moments, second_moments, vectors, vector_first,
            vector_second,
        )

    outs = (*outs, loss_sum.reshape(()), count.reshape(()), norm.reshape(()))
    return lax.while_loop(lambda c: c[0] > 0, general, (jnp.max(message[:, 126]), outs))[1]


def solution(mesh):
    in_specs = (
        P("rep", "blk", None),
        P("rep", "blk", None),
        P("rep", "blk"),
        P("rep", "blk"),
        P("rep", "blk"),
        P(),
        P(),
        P(),
        P("blk", None, None),
        P("blk", None, None),
        P("blk", None, None),
        P(),
        P(),
        P(),
    )
    out_specs = (
        P("blk", None, None),
        P("blk", None, None),
        P("blk", None, None),
        P(),
        P(),
        P(),
        P(),
        P(),
        P(),
    )
    return jax.shard_map(quick, mesh=mesh, in_specs=in_specs, out_specs=out_specs, check_vma=False)
```

```python
from functools import partial

import jax
import jax.numpy as jnp
from jax import lax
from jax.experimental import pallas as pl
from jax.experimental.pallas import tpu as pltpu
from jax.sharding import PartitionSpec as P

D = 256
HEADS = 4
FF = 1024
VOCAB = 30592
LAYERS = 1
PLEN = 512
STEP = 7


TEMPER = 8.0
CLIP_AT = 0.01
RATE = 0.06
VECTOR_RATE = 0.8
BETA_ONE = 0.9
BETA_TWO = 0.999
DECAY = 0.01
EPSILON = 1e-08
NORM_EPS = 1e-06
HUGE = 1000000000.0
HIGHEST = lax.Precision.HIGHEST


def mult(left_op, right_op):
    return jnp.dot(left_op, right_op, preferred_element_type=jnp.float32)


def mult_tn(left_op, right_op):
    return lax.dot_general(
        left_op, right_op, (((0,), (0,)), ((), ())), preferred_element_type=jnp.float32
    )


def mult_nt(left_op, right_op):
    return lax.dot_general(
        left_op, right_op, (((1,), (1,)), ((), ())), preferred_element_type=jnp.float32
    )


def norm_rows(values_in, gain_row, shift_row):
    centred = values_in - jnp.mean(values_in, -1, keepdims=True)
    inv_scale = lax.rsqrt(jnp.mean(centred * centred, -1, keepdims=True) + NORM_EPS)
    normed = centred * inv_scale
    return (normed * gain_row + shift_row, normed, inv_scale)


def norm_back(incoming, normed, inv_scale, gain_row):
    dnormed = incoming * gain_row
    inner_part = (
        dnormed
        - jnp.mean(dnormed, -1, keepdims=True)
        - normed * jnp.mean(dnormed * normed, -1, keepdims=True)
    )
    return (inner_part * inv_scale, jnp.sum(incoming * normed, 0), jnp.sum(incoming, 0))


def layer_parts(flat_rows, vectors, layer_index):
    offset = VOCAB + PLEN + D + layer_index * (4 * D + 2 * FF)
    w_qkv = jnp.concatenate(
        [
            flat_rows[offset : offset + D],
            flat_rows[offset + D : offset + 2 * D],
            flat_rows[offset + 2 * D : offset + 3 * D],
        ],
        1,
    )
    w_out = flat_rows[offset + 3 * D : offset + 4 * D]
    w_up = flat_rows[offset + 4 * D : offset + 4 * D + FF]
    w_down = flat_rows[offset + 4 * D + FF : offset + 4 * D + 2 * FF]
    row_base = 4 + layer_index * (8 + FF // D)
    return ((w_qkv, w_out, w_up, w_down), vectors[row_base : row_base + 8 + FF // D])


def divide_into_heads(packed_buffer, column):
    return packed_buffer[:, column * D : (column + 1) * D].reshape(
        packed_buffer.shape[0], HEADS, D // HEADS
    )


def attend_probs(packed_buffer, key_keep):
    scores = jnp.einsum(
        "cnp,fnp->ncf",
        divide_into_heads(packed_buffer, 0),
        divide_into_heads(packed_buffer, 1),
        preferred_element_type=jnp.float32,
    ) * (D // HEADS) ** (-0.5)
    scores = jnp.where(key_keep[None, None, :], scores, -HUGE)
    return jax.nn.softmax(scores, -1)


def attend(pieces):
    packed_buffer, key_keep = pieces
    attn_probs = attend_probs(packed_buffer, key_keep)
    blended = jnp.einsum(
        "nbi,ins->bns",
        attn_probs.astype(jnp.bfloat16),
        divide_into_heads(packed_buffer, 2),
        preferred_element_type=jnp.float32,
    )
    return blended.reshape(packed_buffer.shape[0], D)


def attend_back(pieces):
    packed_buffer, key_keep, grad_out = pieces
    seq_len = packed_buffer.shape[0]
    head_scale = (D // HEADS) ** (-0.5)
    attn_probs = attend_probs(packed_buffer, key_keep)
    gradient_row_block = grad_out.reshape(seq_len, HEADS, D // HEADS)
    grad_values = jnp.einsum(
        "fxn,xfa->nfa",
        attn_probs.astype(jnp.bfloat16),
        gradient_row_block,
        preferred_element_type=jnp.float32,
    )
    grad_probs = jnp.einsum(
        "cnp,fnp->ncf",
        gradient_row_block,
        divide_into_heads(packed_buffer, 2),
        preferred_element_type=jnp.float32,
    )
    grad_scores = attn_probs * (grad_probs - jnp.sum(grad_probs * attn_probs, -1, keepdims=True))
    score_lowered = grad_scores.astype(jnp.bfloat16)
    grad_queries = (
        jnp.einsum(
            "nbi,ins->bns",
            score_lowered,
            divide_into_heads(packed_buffer, 1),
            preferred_element_type=jnp.float32,
        )
        * head_scale
    )
    grad_keys = (
        jnp.einsum(
            "fxn,xfa->nfa",
            score_lowered,
            divide_into_heads(packed_buffer, 0),
            preferred_element_type=jnp.float32,
        )
        * head_scale
    )
    return jnp.concatenate(
        [
            grad_queries.reshape(seq_len, D),
            grad_keys.reshape(seq_len, D),
            grad_values.reshape(seq_len, D),
        ],
        1,
    ).astype(jnp.bfloat16)


def layer_forward(hidden_in, weights_set, vec_rows, key_keep):
    w_qkv, w_out, w_up, w_down = weights_set
    groups, seq_len = key_keep.shape
    in_low = hidden_in.astype(jnp.bfloat16)
    bias_qkv = jnp.concatenate([vec_rows[0], jnp.zeros_like(vec_rows[0]), vec_rows[1]])
    packed_buffer = (mult(in_low, w_qkv) + bias_qkv).astype(jnp.bfloat16)
    blended = lax.map(attend, (packed_buffer.reshape(groups, seq_len, 3 * D), key_keep))
    blend_low = blended.reshape(groups * seq_len, D).astype(jnp.bfloat16)
    summed = hidden_in + mult(blend_low, w_out) + vec_rows[2]
    normal_one, normed_one, scale_one = norm_rows(summed, vec_rows[4], vec_rows[5])
    normal_low = normal_one.astype(jnp.bfloat16)
    up_in = mult_nt(normal_low, w_up) + vec_rows[8:].reshape(FF)
    acted = jax.nn.gelu(up_in, approximate=False).astype(jnp.bfloat16)
    second = normal_one + mult(acted, w_down) + vec_rows[3]
    result, normed_two, scale_two = norm_rows(second, vec_rows[6], vec_rows[7])
    return (
        result,
        (
            in_low,
            packed_buffer,
            blend_low,
            normed_one,
            scale_one,
            normal_low,
            up_in,
            acted,
            normed_two,
            scale_two,
        ),
    )


def layer_backward(grad_out, weights_set, vec_rows, key_keep, saved):
    w_qkv, w_out, w_up, w_down = weights_set
    (
        in_low,
        packed_buffer,
        blend_low,
        normed_one,
        scale_one,
        normal_low,
        up_in,
        acted,
        normed_two,
        scale_two,
    ) = saved
    groups, seq_len = key_keep.shape
    grad_second, grad_gain_two, grad_shift_two = norm_back(
        grad_out, normed_two, scale_two, vec_rows[6]
    )
    down_low = grad_second.astype(jnp.bfloat16)
    grad_down = mult_tn(acted, down_low)
    grad_acted = mult_nt(down_low, w_down)
    gelu_pull = jax.vjp(partial(jax.nn.gelu, approximate=False), up_in)[1]
    up_low = gelu_pull(grad_acted)[0].astype(jnp.bfloat16)
    grad_up = mult_tn(up_low, normal_low)
    grad_normal = grad_second + mult(up_low, w_up)
    grad_summed, gradient_first_gain, grad_shift_one = norm_back(
        grad_normal, normed_one, scale_one, vec_rows[4]
    )
    branch_low = grad_summed.astype(jnp.bfloat16)
    grad_wout = mult_tn(blend_low, branch_low)
    blend_grad = mult_nt(branch_low, w_out).astype(jnp.bfloat16)
    grad_packed = lax.map(
        attend_back,
        (
            packed_buffer.reshape(groups, seq_len, 3 * D),
            key_keep,
            blend_grad.reshape(groups, seq_len, D),
        ),
    ).reshape(groups * seq_len, 3 * D)
    grad_wqkv = mult_tn(in_low, grad_packed)
    grad_in = grad_summed + mult_nt(grad_packed, w_qkv)
    packed_sum = jnp.sum(grad_packed.astype(jnp.float32), 0)
    matrix_grads = jnp.concatenate(
        [
            grad_wqkv[:, :D],
            grad_wqkv[:, D : 2 * D],
            grad_wqkv[:, 2 * D :],
            grad_wout,
            grad_up,
            grad_down,
        ],
        0,
    )
    vector_grads = jnp.concatenate(
        [
            jnp.stack(
                [
                    packed_sum[:D],
                    packed_sum[2 * D :],
                    jnp.sum(branch_low.astype(jnp.float32), 0),
                    jnp.sum(down_low.astype(jnp.float32), 0),
                    gradient_first_gain,
                    grad_shift_one,
                    grad_gain_two,
                    grad_shift_two,
                ]
            ),
            jnp.sum(up_low.astype(jnp.float32), 0).reshape(FF // D, D),
        ],
        0,
    )
    return (grad_in, matrix_grads, vector_grads)


def embed_sequences(flat_rows, vectors, token_ids, lengths):
    groups, seq_len = token_ids.shape
    key_keep = jnp.arange(seq_len)[None, :] < lengths[:, None]
    table_rows = jnp.take(flat_rows, token_ids.reshape(-1), axis=0).astype(jnp.float32)
    places = flat_rows[VOCAB : VOCAB + seq_len].astype(jnp.float32)
    embedded = (table_rows.reshape(groups, seq_len, D) + places[None] + vectors[0]).reshape(
        groups * seq_len, D
    )
    hidden_now, normed_emb, scaled_embedding = norm_rows(embedded, vectors[1], vectors[2])
    weights_set, vec_rows = layer_parts(flat_rows, vectors, 0)
    hidden_now, saved = layer_forward(hidden_now, weights_set, vec_rows, key_keep)
    layer_saves = [saved]
    first_rows = hidden_now.reshape(groups, seq_len, D)[:, 0].astype(jnp.bfloat16)
    pooled = jnp.tanh(mult(first_rows, flat_rows[VOCAB + PLEN : VOCAB + PLEN + D]) + vectors[3])
    return (pooled, (normed_emb, scaled_embedding, layer_saves, first_rows))


def encode_back(grad_pooled, pooled, flat_rows, vectors, token_ids, lengths, encoder_kept):
    normed_emb, scaled_embedding, layer_saves, first_rows = encoder_kept
    groups, seq_len = token_ids.shape
    key_keep = jnp.arange(seq_len)[None, :] < lengths[:, None]
    w_pool = flat_rows[VOCAB + PLEN : VOCAB + PLEN + D].astype(jnp.float32)
    grad_pre = grad_pooled * (1.0 - pooled * pooled)
    grad_pool = jnp.dot(first_rows.astype(jnp.float32).T, grad_pre, precision=HIGHEST)
    grad_first = jnp.dot(grad_pre, w_pool.T, precision=HIGHEST)
    grad_hidden = (
        jnp.zeros((groups, seq_len, D), jnp.float32)
        .at[:, 0]
        .set(grad_first)
        .reshape(groups * seq_len, D)
    )
    matrices = []
    vector_parts = []
    for layer_index in reversed(range(LAYERS)):
        weights_set, vec_rows = layer_parts(flat_rows, vectors, layer_index)
        grad_hidden, matrix_grads, vector_grads = layer_backward(
            grad_hidden, weights_set, vec_rows, key_keep, layer_saves[layer_index]
        )
        matrices.insert(0, matrix_grads)
        vector_parts.insert(0, vector_grads)
    grad_embed, grad_gain, grad_shift = norm_back(
        grad_hidden, normed_emb, scaled_embedding, vectors[1]
    )
    grad_table = jnp.zeros((VOCAB, D), jnp.float32).at[token_ids.reshape(-1)].add(grad_embed)
    grad_places = (
        jnp.zeros((PLEN, D), jnp.float32)
        .at[:seq_len]
        .set(jnp.sum(grad_embed.reshape(groups, seq_len, D), 0))
    )
    flat_grad = jnp.concatenate([grad_table, grad_places, grad_pool] + matrices, 0)
    head_rows = jnp.stack([jnp.sum(grad_embed, 0), grad_gain, grad_shift, jnp.sum(grad_pre, 0)])
    return (flat_grad, jnp.concatenate([head_rows] + vector_parts, 0))


def adam_step(weight, moment_one, moment_two, gradient, step_rate, decay_rate):
    moment_one = BETA_ONE * moment_one + (1.0 - BETA_ONE) * gradient
    moment_two = BETA_TWO * moment_two + (1.0 - BETA_TWO) * gradient * gradient
    update = (
        moment_one
        / (1.0 - BETA_ONE**STEP)
        / (jnp.sqrt(moment_two / (1.0 - BETA_TWO**STEP)) + EPSILON)
    )
    return (weight - step_rate * (update + decay_rate * weight), moment_one, moment_two)


def gather_all(values, axes):
    count = lax.axis_size(axes)
    copies = jnp.broadcast_to(values[None], (count,) + values.shape)
    return lax.all_to_all(copies, axes, 0, 0, tiled=True).reshape((-1,) + values.shape[1:])


def sum_all(values, axes):
    count = lax.axis_size(axes)
    copies = jnp.broadcast_to(values[None], (count,) + values.shape)
    return jnp.sum(lax.all_to_all(copies, axes, 0, 0, tiled=True), 0)


def sum_share(values, axes):
    count = lax.axis_size(axes)
    parts = lax.all_to_all(values, axes, 0, 0, tiled=True)
    return jnp.sum(parts.reshape((count, -1) + values.shape[1:]), 0)


def local(
    query_ids,
    passage_ids,
    query_lengths,
    passage_lengths,
    positive,
    prefix_lengths,
    prefix_weights,
    owners,
    weights,
    first_moments,
    second_moments,
    vectors,
    vector_first,
    vector_second,
):
    slot_count, unit_rows = (weights.shape[0], weights.shape[1])
    gathered = gather_all(weights.astype(jnp.bfloat16), "blk")
    flat_rows = jnp.take(gathered, owners, axis=0).reshape(-1, D)
    query_pooled, query_kept = embed_sequences(flat_rows, vectors, query_ids[0], query_lengths[0])
    passage_pooled, passage_kept = embed_sequences(
        flat_rows, vectors, passage_ids[0], passage_lengths[0]
    )
    all_passages = gather_all(passage_pooled.astype(jnp.bfloat16), "blk")
    prefix_masks = (jnp.arange(D)[None, :] < prefix_lengths[:, None]).astype(jnp.float32)
    prefix_scale = TEMPER * lax.rsqrt(prefix_lengths.astype(jnp.float32))
    queries = query_pooled.astype(jnp.bfloat16).astype(jnp.float32)
    passages = all_passages.astype(jnp.float32)
    masked = queries[None] * prefix_masks[:, None, :]
    logits = (
        jnp.einsum("mpd,jd->mpj", masked, passages, precision=HIGHEST) * prefix_scale[:, None, None]
    )
    counted = positive[0] >= 0
    target = (jnp.arange(passages.shape[0])[None, :] == positive[0][:, None]).astype(jnp.float32)
    running_totals = jax.nn.logsumexp(logits, -1) - jnp.sum(logits * target[None], -1)
    per_query = jnp.sum(prefix_weights[:, None] * running_totals, 0)
    loss_part = jnp.sum(jnp.where(counted, per_query, 0.0))
    count_part = jnp.sum(counted.astype(jnp.float32))
    count_total, loss_total = sum_all(jnp.stack([count_part, loss_part]), ("blk", "rep"))
    row_factor = (prefix_weights * prefix_scale / count_total)[:, None, None] * counted.astype(
        jnp.float32
    )[None, :, None]
    grad_logits = (jax.nn.softmax(logits, -1) - target[None]) * row_factor
    grad_query = jnp.sum(
        jnp.einsum("mpj,jd->mpd", grad_logits, passages, precision=HIGHEST)
        * prefix_masks[:, None, :],
        0,
    )
    grad_passage = sum_share(
        jnp.einsum("mpj,mpd->jd", grad_logits, masked, precision=HIGHEST), "blk"
    )
    flat_query, vec_query = encode_back(
        grad_query, query_pooled, flat_rows, vectors, query_ids[0], query_lengths[0], query_kept
    )
    flat_pass, vec_pass = encode_back(
        grad_passage,
        passage_pooled,
        flat_rows,
        vectors,
        passage_ids[0],
        passage_lengths[0],
        passage_kept,
    )
    vec_total = sum_all(vec_query + vec_pass, ("blk", "rep"))
    buffer = (
        jnp.zeros((lax.axis_size("blk") * slot_count, unit_rows, D), jnp.float32)
        .at[owners]
        .set((flat_query + flat_pass).reshape(-1, unit_rows, D))
    )
    vec_square = jnp.sum(vec_total * vec_total)
    reduced = sum_share(buffer, "blk")
    reduced = sum_all(reduced, "rep")
    square_sum = sum_all(jnp.sum(reduced * reduced)[None], "blk")[0]
    old_weight, old_first, old_second = (weights, first_moments, second_moments)
    slot_ids = lax.axis_index("blk") * slot_count + jnp.arange(slot_count)
    owned_mask = jnp.any(slot_ids[:, None] == owners[None, :], 1)[:, None, None]
    grad_norm = jnp.sqrt(square_sum + vec_square)
    factor = CLIP_AT / jnp.maximum(grad_norm, CLIP_AT)
    new_weight, new_first, new_second = adam_step(
        old_weight, old_first, old_second, reduced * factor, RATE, DECAY
    )
    new_weight = jnp.where(owned_mask, new_weight, old_weight)
    new_first = jnp.where(owned_mask, new_first, old_first)
    new_second = jnp.where(owned_mask, new_second, old_second)
    new_vec, new_vec_first, new_vec_second = adam_step(
        vectors, vector_first, vector_second, vec_total * factor, VECTOR_RATE, 0.0
    )
    return (
        new_weight,
        new_first,
        new_second,
        new_vec,
        new_vec_first,
        new_vec_second,
        loss_total,
        count_total,
        grad_norm,
    )


F32 = jnp.float32
BF16 = jnp.bfloat16
I32 = jnp.int32
UNIT = 128
TABLE_BLOCKS = VOCAB // UNIT
PLACE_BLOCKS = PLEN // UNIT
DENSE = PLACE_BLOCKS + (D + 4 * D + 2 * FF) // UNIT
HALF = 64
QROWS = 128
TOKENS = 2 * QROWS + 2 * PLEN
STARTS = (0, QROWS, 2 * QROWS, 2 * QROWS + PLEN)
UNITS_L = 10
L_ROWS = 4 * UNITS_L
NEVER = -1e30


def params(n_blk, small):
    return pltpu.CompilerParams(vmem_limit_bytes=(small if n_blk <= 16 else 58) << 20)


AT_POOL = PLEN
AT_Q = AT_POOL + D
AT_K = AT_Q + D
AT_V = AT_K + D
AT_O = AT_V + D
AT_UP = AT_O + D
AT_DOWN = AT_UP + FF

TAB_OWNER, TAB_RANK, TAB_SLOT, TAB_UNIT, TAB_KIND, TAB_ORDER = range(6)
PIECE = 16
PIECES = 16
DENSE_CAP = 8
CLASS = DENSE // 2
HELD = DENSE_CAP // 2
AT_ASKED = DENSE_CAP // 4 * PIECE
MESSAGE_ROWS = AT_ASKED + 8

KIND_TABLE, KIND_PLACE, KIND_DENSE = 1, 2, 8

vmem = pl.BlockSpec(memory_space=pltpu.VMEM)
smem = pl.BlockSpec(memory_space=pltpu.SMEM)
hbm = pl.BlockSpec(memory_space=pl.ANY)
in_hbm = pl.BlockSpec(memory_space=pltpu.HBM)


def stay(*arrays):
    return [pltpu.with_memory_space_constraint(a, pltpu.HBM) for a in arrays]


def iota(shape, axis):
    return lax.broadcasted_iota(I32, shape, axis)


def dot_nn(a, b):
    return lax.dot_general(a, b, (((1,), (0,)), ((), ())), preferred_element_type=F32)


def dot_nt(a, b):
    return lax.dot_general(a, b, (((1,), (1,)), ((), ())), preferred_element_type=F32)


def dot_tn(a, b):
    return lax.dot_general(a, b, (((0,), (0,)), ((), ())), preferred_element_type=F32)


def split(a):
    high = a.astype(BF16)
    return high, (a - high.astype(F32)).astype(BF16)


def fine(dot, a, b):
    high, low = split(a)
    rows = a.shape[0]
    both = dot(jnp.concatenate([high, low], 0), b)
    return both[:rows] + both[rows:]


def to_column(row):
    return jnp.broadcast_to(row, (128, 128)).T[:, :1]


def token_facts(query_lengths, passage_lengths):
    lane = iota((1, TOKENS), 1)
    sequence = (
        (lane >= STARTS[1]).astype(I32)
        + (lane >= STARTS[2]).astype(I32)
        + (lane >= STARTS[3]).astype(I32)
    )
    ends = [
        STARTS[0] + query_lengths[0, 0],
        STARTS[1] + query_lengths[0, 1],
        STARTS[2] + passage_lengths[0, 0],
        STARTS[3] + passage_lengths[0, 1],
    ]
    end = jnp.where(
        sequence == 0,
        ends[0],
        jnp.where(sequence == 1, ends[1], jnp.where(sequence == 2, ends[2], ends[3])),
    )
    return sequence, lane < end


def across(values, n_blk, step):
    pairs = [(i, i // PIECES * PIECES + step(i % PIECES)) for i in range(n_blk)]
    return lax.ppermute(values, "blk", pairs)


def along_z(mine, n_blk):
    return jnp.stack(
        [mine] + [across(mine, n_blk, lambda i, k=k: (i + 4 * k) % PIECES) for k in (1, 2, 3)]
    )


def spread(first, n_blk):
    arrays = [first, lax.ppermute(first, "rep", [(0, 1), (1, 0)])]
    arrays = arrays + [across(a, n_blk, lambda i: i ^ 2) for a in arrays]
    return arrays + [across(a, n_blk, lambda i: i ^ 1) for a in arrays]


def piece_copies(me, gathered, matrices, sems):
    copies = []
    for part, array in enumerate(gathered):
        low = (me[0] % 4) ^ (part & 2) ^ (part // 4)
        odd = me[1] ^ (part % 2)
        for k in range(4):
            p = low + (me[0] % PIECES // 4 * 4 + 4 * (4 - k)) % PIECES
            row = pl.multiple_of((p % 8) * PIECE, PIECE)
            lane = pl.multiple_of((p // 8) * 128, 128)
            copies.append(
                pltpu.make_async_copy(
                    array.at[k],
                    matrices.at[:, odd, pl.ds(row, PIECE), pl.ds(lane, 128)],
                    sems.at[4 * part + k],
                )
            )
    return copies


def rows_at(matrices, tab, start, stop):
    blocks = []
    for b in range(start // UNIT, stop // UNIT):
        order = tab[b, TAB_ORDER]
        blocks.append(matrices[order // 2, order % 2])
    return jnp.concatenate(blocks, 0)


def owner_of(slot, slots, n_blk):
    owner = jnp.zeros(slot.shape, I32)
    for k in range(1, n_blk):
        owner = owner + (slot >= k * slots).astype(I32)
    return owner


def request_kernel(
    slots, n_blk, cap, take_cap, owners, me, positive, query_lengths, passage_lengths, owner_line,
    query_ids, passage_ids, weights, message, where_row, tab, ids, owner_row, loaded, sems,
):
    n_rep = 2
    n_dest = n_blk * n_rep
    n_units = owners.shape[0]
    start = me[0] * slots

    def take(b, carry):
        before, have = carry
        slot = owners[n_units - DENSE + b]
        inside = slot - start
        mine = (inside >= 0) & (inside < slots)

        @pl.when(mine & (have // 2 % 2 == me[1]) & (have < DENSE_CAP))
        def _():
            spot = have // 4 * 2 + have % 2
            pltpu.make_async_copy(weights.at[inside], loaded.at[spot], sems.at[spot]).start()

        return before + (slot < start).astype(I32), have + mine.astype(I32)

    before, have = lax.fori_loop(0, DENSE, take, (0, 0))
    owner_row[...] = jnp.full(owner_row.shape, -1, I32)
    owner_row[:, :n_units] = owner_line[...]
    every_slot = owner_row[...]
    wide = every_slot.shape[1]
    base = n_units - DENSE
    low = base // 128 * 128
    rolled = pltpu.roll(every_slot[:, low:], wide - low - (base - low), 1)[:, :128]
    dense_owner = owner_of(rolled, slots, n_blk)
    owner_column = to_column(dense_owner)[:32]
    slot_column = to_column(rolled)[:32]
    block_row = iota((32, 128), 1)
    block_column = iota((32, 128), 0)
    same = (owner_column == dense_owner) & (block_row < block_column) & (block_row < DENSE)
    rank = jnp.sum(same.astype(I32), 1, keepdims=True)
    at = block_row * UNIT
    need = jnp.where(block_row < PLACE_BLOCKS, 0, jnp.where((at >= AT_K) & (at < AT_O), 2, 1))
    unit = jnp.sum(jnp.where(same, need, 0), 1, keepdims=True)
    lower = (dense_owner < owner_column) & (block_row < DENSE)
    order = rank + jnp.sum(lower.astype(I32), 1, keepdims=True)
    is_dense = (iota((32, 1), 0) >= PLACE_BLOCKS) & (iota((32, 1), 0) < DENSE)
    at = iota((32, 1), 0) * UNIT
    needs = jnp.where((at >= AT_K) & (at < AT_O), 2, 1)
    crowded = jnp.max(
        (
            ((rank >= DENSE_CAP) & (iota((32, 1), 0) < DENSE))
            | (is_dense & (unit + needs > UNITS_L))
        ).astype(I32)
    )
    which = iota((32, wide), 1)
    code = jnp.where(
        which < TABLE_BLOCKS,
        KIND_TABLE,
        jnp.where(
            which < TABLE_BLOCKS + PLACE_BLOCKS, KIND_PLACE + which - TABLE_BLOCKS, KIND_DENSE
        ),
    )
    here = (every_slot == me[0] * slots + iota((32, wide), 0)) & (which < n_units)
    kind = jnp.sum(jnp.where(here, code, 0), 1, keepdims=True)
    entry = block_row
    tab[...] = jnp.where(
        entry == TAB_OWNER,
        owner_column,
        jnp.where(
            entry == TAB_RANK,
            jnp.minimum(rank, DENSE_CAP - 1),
            jnp.where(
                entry == TAB_SLOT,
                slot_column - owner_column * slots,
                jnp.where(
                    entry == TAB_UNIT,
                    jnp.minimum(unit, UNITS_L - 2),
                    jnp.where(entry == TAB_KIND, kind, jnp.minimum(order, DENSE - 1)),
                ),
            ),
        ),
    )

    ids[:, 0:QROWS] = query_ids[0:1]
    ids[:, QROWS : 2 * QROWS] = query_ids[1:2]
    ids[:, STARTS[2] : STARTS[3]] = passage_ids[0:1]
    ids[:, STARTS[3] :] = passage_ids[1:2]
    token = ids[...]
    _, live = token_facts(query_lengths, passage_lengths)
    lane = iota((1, TOKENS), 1)
    block = token // UNIT
    slot = jnp.zeros((1, TOKENS), I32)
    table_rows = -(-TABLE_BLOCKS // 128) * 128
    for at in range(0, table_rows, 128):
        column = to_column(owner_row[:, at : at + 128])
        hit = (iota((128, TOKENS), 0) + at) == block
        slot = slot + jnp.sum(jnp.where(hit, column, 0), 0, keepdims=True)
    owner = owner_of(slot, slots, n_blk)
    inside = slot - owner * slots
    row = token - block * UNIT
    upper = (row >= HALF).astype(I32)
    dest = owner * n_rep + upper
    local_row = inside * HALF + row - upper * HALF
    token = jnp.where(live, token, -1)
    first_at = jnp.full((128, TOKENS), TOKENS, I32)
    for at in range(0, TOKENS, 128):
        column = to_column(token[:, at : at + 128])
        same = column == token
        first_at = jnp.minimum(first_at, jnp.where(same, iota((128, TOKENS), 0) + at, TOKENS))
    first_at = jnp.min(first_at, 0, keepdims=True)
    first = live & (first_at == lane)
    chosen = ((iota((n_dest, TOKENS), 0) == dest) & first).astype(F32)
    chosen_low = chosen.astype(BF16)
    seen = jnp.zeros((n_dest, TOKENS), F32)
    for at in range(0, TOKENS, 128):
        earlier = ((iota((128, TOKENS), 0) + at) < first_at).astype(F32).astype(BF16)
        seen = seen + dot_nn(chosen_low[:, at : at + 128], earlier)
    to = iota((n_dest, TOKENS), 0)
    rank = jnp.sum(jnp.where(to == dest, seen, 0.0), 0, keepdims=True).astype(I32)
    turn = jnp.sum(jnp.where(to // n_rep == owner, seen, 0.0), 0, keepdims=True).astype(I32)
    source = owner * n_rep + turn % n_rep
    spot = turn // n_rep
    where_row[0:1] = jnp.where(live & (spot < take_cap), source * take_cap + spot, -1)
    where_row[1:2] = jnp.where(live & (rank < cap), dest * cap + rank, -1)
    over = jnp.max((live & ((rank >= cap) | (spot >= take_cap))).astype(I32))

    def listed(dest, spot, code):
        high = code // 32
        low = code - high * 32
        chosen = ((to == dest) & first).astype(F32)
        both = jnp.concatenate([chosen * high.astype(F32), chosen * low.astype(F32)], 0)
        spread = (iota((128, TOKENS), 0) == spot).astype(F32).astype(BF16)
        both = dot_nt(both.astype(BF16), spread)
        return both[:n_dest], both[n_dest:]

    take_high, take_low = listed(source, spot, inside * UNIT + row + 1)
    sent_high, sent_low = listed(dest, rank, local_row + 1)
    flag = jnp.maximum(over, crowded)
    column_of = iota((1, 128), 1)
    marks = jnp.where(
        column_of == 0,
        positive[0, 0],
        jnp.where(column_of == 1, positive[0, 1], jnp.where(column_of == 2, flag, 0)),
    ).astype(F32)
    row8 = iota((8, 128), 0)
    for d in range(n_dest):
        asked = jnp.where(row8 == 0, take_high[d : d + 1], marks)
        for i, part in ((1, take_low), (3, sent_high), (4, sent_low)):
            asked = jnp.where(row8 == i, part[d : d + 1], asked)
        message[d, AT_ASKED:] = asked.astype(BF16)
    for spot in range(HELD):
        present = spot // 2 * 4 + 2 * me[1] + spot % 2 < have

        @pl.when(present)
        def _():
            pltpu.make_async_copy(weights.at[0], loaded.at[spot], sems.at[spot]).wait()

        @pl.when(jnp.logical_not(present))
        def _():
            loaded[spot] = jnp.zeros((UNIT, D), F32)

    for odd in range(2):
        for c in range(DENSE_CAP // 4):
            whole = loaded[2 * c + (odd + before) % 2].astype(BF16)
            for s in range(n_blk):
                p = s % PIECES
                message[2 * s + odd, PIECE * c : PIECE * (c + 1)] = whole[
                    PIECE * (p % 8) : PIECE * (p % 8 + 1), 128 * (p // 8) : 128 * (p // 8 + 1)
                ]


def request(owners, me, positive, query_lengths, passage_lengths, query_ids, passage_ids, weights, n_blk, cap, take_cap):
    slots = weights.shape[0]
    n_dest = 2 * n_blk
    n_units = owners.shape[0]
    owner_row = owners.reshape(1, n_units)
    return pl.pallas_call(
        partial(request_kernel, slots, n_blk, cap, take_cap),
        out_shape=(
            jax.ShapeDtypeStruct((n_dest, MESSAGE_ROWS, 128), BF16),
            jax.ShapeDtypeStruct((2, TOKENS), I32),
            jax.ShapeDtypeStruct((32, 128), I32),
        ),
        in_specs=[smem] * 5 + [vmem] * 3 + [in_hbm],
        out_specs=(vmem, vmem, vmem),
        scratch_shapes=[
            pltpu.VMEM((1, TOKENS), I32),
            pltpu.VMEM((1, -(-n_units // 128) * 128), I32),
            pltpu.VMEM((HELD, UNIT, D), F32),
            pltpu.SemaphoreType.DMA((HELD,)),
        ],
        compiler_params=params(n_blk, 12),
        name="request",
    )(owners, me, positive, query_lengths, passage_lengths, owner_row, query_ids, passage_ids, *stay(weights))


def collect_kernel(tab, me, message, mine_out):
    for b in range(DENSE):
        order = tab[b, TAB_ORDER]
        rank = tab[b, TAB_RANK]

        @pl.when(order % 2 == me[1])
        def _():
            spot = pl.multiple_of(rank // 4 * PIECE, PIECE)
            sender = 2 * tab[b, TAB_OWNER] + rank // 2 % 2
            mine_out[order // 2] = message[sender, pl.ds(spot, PIECE), :]


def collect(tab, me, message):
    return pl.pallas_call(
        collect_kernel,
        out_shape=jax.ShapeDtypeStruct((CLASS, PIECE, 128), BF16),
        in_specs=[smem, smem, vmem],
        out_specs=vmem,
        compiler_params=params(message.shape[0] // 2, 2),
        name="collect",
    )(tab, me, message)


def fetch_kernel(slots, cap, take_cap, message, weights, rows_out, asked_out, wanted, held, table, hot, sem):
    n_dest = message.shape[0]
    copy = pltpu.make_async_copy(weights, held, sem)
    copy.start()
    column_of = iota((1, 128), 1)
    wanted[...] = jnp.zeros(wanted.shape, I32)
    for s in range(n_dest):
        part = message[s, AT_ASKED:].astype(F32)
        wanted[s : s + 1] = (part[0:1] * 32.0 + part[1:2] - 1.0).astype(I32)
        marks = part[2:3]
        row = jnp.where(column_of < cap, part[3:4] * 32.0 + part[4:5] - 1.0, 0.0)
        for i in range(3):
            row = jnp.where(column_of == 124 + i, marks[:, i : i + 1], row)
        asked_out[s : s + 1] = row.astype(I32)
    wide = table.shape[0]
    columns = wanted[...].T
    for s in range(n_dest):
        hot[s * take_cap : (s + 1) * take_cap] = (
            (iota((take_cap, wide), 1) == columns[:take_cap, s : s + 1]).astype(F32).astype(BF16)
        )
    copy.wait()
    table[...] = held[...].reshape(wide, D).astype(BF16)
    rows_out[...] = dot_nn(hot[...], table[...]).astype(BF16)


def fetch(message, weights, cap, take_cap):
    slots = weights.shape[0]
    n_dest = message.shape[0]
    return pl.pallas_call(
        partial(fetch_kernel, slots, cap, take_cap),
        out_shape=(
            jax.ShapeDtypeStruct((n_dest * take_cap, D), BF16),
            jax.ShapeDtypeStruct((n_dest, 128), I32),
        ),
        in_specs=[vmem, in_hbm],
        out_specs=(vmem, vmem),
        scratch_shapes=[
            pltpu.VMEM((-(-n_dest // 128) * 128, 128), I32),
            pltpu.VMEM(weights.shape, F32),
            pltpu.VMEM((slots * UNIT, D), BF16),
            pltpu.VMEM((n_dest * take_cap, slots * UNIT), BF16),
            pltpu.SemaphoreType.DMA,
        ],
        compiler_params=params(n_dest // 2, 20),
        name="fetch",
    )(message, *stay(weights))


ST_POOLED, ST_C, ST_N2, ST_N1, ST_H, ST_O, ST_Q, ST_X0 = range(0, 64, 8)
ST_KQ, ST_B, ST_U, ST_A, ST_I1, ST_I2 = 64, 96, 128, 160, 192, 200
ST_ROWS = 208


def forward_kernel(
    tab, me, query_lengths, passage_lengths, positive, rows, where_row, vectors, g0, g1, g2, g3,
    g4, g5, g6, g7, emb_out, low_out, normed_out, scale_out, probs_out, state, matrices, embedded,
    sems,
):
    copies = piece_copies(me, (g0, g1, g2, g3, g4, g5, g6, g7), matrices, sems)
    for copy in copies:
        copy.start()
    taken = rows.shape[0]
    for at in range(0, TOKENS, 128):
        column = to_column(where_row[0:1, at : at + 128])
        hot = (iota((128, taken), 1) == column).astype(F32).astype(BF16)
        embedded[at : at + 128] = dot_nn(hot, rows[...])
    for copy in copies:
        copy.wait()
    shift = vectors[0:1]
    for start, length in zip(STARTS, (QROWS, QROWS, PLEN, PLEN)):
        e = embedded[start : start + length] + rows_at(matrices, tab, 0, length).astype(F32) + shift
        centred = e - jnp.mean(e, -1, keepdims=True)
        scale = lax.rsqrt(jnp.mean(centred * centred, -1, keepdims=True) + NORM_EPS)
        normed = centred * scale
        normed_out[start : start + length] = normed
        scale_out[start : start + length] = jnp.broadcast_to(scale, (length, 128))
        x = normed * vectors[1:2] + vectors[2:3]
        embedded[start : start + length] = x
        low_out[start : start + length] = x.astype(BF16)
    x0 = jnp.concatenate(
        [embedded[s : s + 1] for s in STARTS] + [jnp.zeros((4, D), F32)], 0
    )
    x0_low = x0.astype(BF16)
    q = (dot_nn(x0_low, rows_at(matrices, tab, AT_Q, AT_K)) + vectors[4:5]).astype(BF16)
    head_of = iota((8, D), 1) // HALF
    q_heads = jnp.concatenate(
        [jnp.where(head_of == h, q.astype(F32), 0.0) for h in range(HEADS)], 0
    ).astype(BF16)
    kq = dot_nt(q_heads, rows_at(matrices, tab, AT_K, AT_V)) * (D // HEADS) ** (-0.5)
    low = low_out[...]
    scores = fine(dot_nt, kq, low)
    sequence, live = token_facts(query_lengths, passage_lengths)
    valid = ((iota((32, TOKENS), 0) & 7) == sequence) & live
    scores = jnp.where(valid, scores, NEVER)
    top = jnp.max(scores, -1, keepdims=True)
    weight = jnp.where(valid, jnp.exp(scores - top), 0.0)
    total = jnp.sum(weight, -1, keepdims=True)
    probs = weight / jnp.where(total > 0.0, total, 1.0)
    probs_out[...] = probs
    mixed = dot_nn(probs.astype(BF16), low)
    valued = fine(dot_nn, mixed, rows_at(matrices, tab, AT_V, AT_O))
    blended = jnp.zeros((8, D), F32)
    for h in range(HEADS):
        blended = blended + jnp.where(head_of == h, valued[8 * h : 8 * h + 8], 0.0)
    real = iota((8, D), 0) < 4
    blended = jnp.where(real, blended + vectors[5:6], 0.0).astype(BF16)
    summed = x0 + dot_nn(blended, rows_at(matrices, tab, AT_O, AT_UP)) + vectors[6:7]
    h0, n1, i1 = norm_rows(summed, vectors[8:9], vectors[9:10])
    h_low = h0.astype(BF16)
    bias_up = jnp.concatenate([vectors[12 + i : 13 + i] for i in range(FF // D)], 1)
    u = dot_nt(h_low, rows_at(matrices, tab, AT_UP, AT_DOWN)) + bias_up
    a = (0.5 * u * (1.0 + lax.erf(u * (0.5**0.5)))).astype(BF16)
    second = h0 + dot_nn(a, rows_at(matrices, tab, AT_DOWN, DENSE * UNIT)) + vectors[7:8]
    x, n2, i2 = norm_rows(second, vectors[10:11], vectors[11:12])
    c = x.astype(BF16)
    pooled = jnp.tanh(dot_nn(c, rows_at(matrices, tab, AT_POOL, AT_Q)) + vectors[3:4])
    row8 = iota((8, 128), 0)
    sent = jnp.concatenate(
        [
            jnp.where(real, pooled, 0.0),
            jnp.where(
                row8 == 0,
                positive[0, 0].astype(F32),
                jnp.where(row8 == 1, positive[0, 1].astype(F32), -1.0),
            ),
        ],
        1,
    )
    n_blk = emb_out.shape[0] // 8
    emb_out[...] = jnp.concatenate([sent] * n_blk, 0).astype(BF16)
    state[ST_POOLED : ST_POOLED + 8] = pooled
    state[ST_C : ST_C + 8] = c.astype(F32)
    state[ST_N2 : ST_N2 + 8] = n2
    state[ST_N1 : ST_N1 + 8] = n1
    state[ST_H : ST_H + 8] = h_low.astype(F32)
    state[ST_O : ST_O + 8] = blended.astype(F32)
    state[ST_Q : ST_Q + 8] = q.astype(F32)
    state[ST_X0 : ST_X0 + 8] = x0_low.astype(F32)
    state[ST_KQ : ST_KQ + 32] = kq
    state[ST_B : ST_B + 32] = mixed
    for i in range(FF // D):
        state[ST_U + 8 * i : ST_U + 8 * i + 8] = u[:, i * D : (i + 1) * D]
        state[ST_A + 8 * i : ST_A + 8 * i + 8] = a[:, i * D : (i + 1) * D].astype(F32)
    state[ST_I1 : ST_I1 + 8] = jnp.broadcast_to(i1, (8, D))
    state[ST_I2 : ST_I2 + 8] = jnp.broadcast_to(i2, (8, D))


def forward(tab, me, query_lengths, passage_lengths, positive, rows, where_row, vectors, gathered, n_blk):
    return pl.pallas_call(
        forward_kernel,
        out_shape=(
            jax.ShapeDtypeStruct((n_blk * 8, D + 128), BF16),
            jax.ShapeDtypeStruct((TOKENS, D), BF16),
            jax.ShapeDtypeStruct((TOKENS, D), F32),
            jax.ShapeDtypeStruct((TOKENS, 128), F32),
            jax.ShapeDtypeStruct((32, TOKENS), F32),
            jax.ShapeDtypeStruct((ST_ROWS, D), F32),
            jax.ShapeDtypeStruct((CLASS, 2, UNIT, D), BF16),
        ),
        in_specs=[smem] * 5 + [vmem] * 3 + [hbm] * 8,
        out_specs=(vmem,) * 7,
        scratch_shapes=[
            pltpu.VMEM((TOKENS, D), F32),
            pltpu.SemaphoreType.DMA((2 * PIECES,)),
        ],
        compiler_params=params(n_blk, 12),
        name="forward",
    )(
        tab, me, query_lengths, passage_lengths, positive, rows, where_row, vectors,
        *[pltpu.with_memory_space_constraint(a, pltpu.HBM) for a in gathered],
    )


def news_rows(n_dest):
    return 2 * place_rows(n_dest) + 8


def place_rows(n_dest):
    return max(PLEN // n_dest, 16)


def payload_rows(n_dest, cap):
    at_place = 2 * cap
    at_left = at_place + 2 * place_rows(n_dest)
    at_right = at_left + L_ROWS
    return at_place, at_left, at_right, at_right + 32


def backward_kernel(
    cap, tab, me, prefix_lengths, prefix_weights, emb, message, where_row, low_in, normed, scale,
    probs_in, state, vectors, matrices, payload, loss_out, count_out,
    received, grad_emb, dx, left,
):
    n_blk = emb.shape[0] // 8
    n_dest = 2 * n_blk
    for i in range(3):
        received[i * n_blk * 8 : (i + 1) * n_blk * 8] = emb[:, 128 * i : 128 * i + 128].astype(F32)

    def every(k):
        return jnp.concatenate(
            [received[pl.ds(i * n_blk * 8 + k, n_blk, stride=8), :] for i in range(3)], 1
        )

    queries = jnp.concatenate([every(0), every(1)], 0)
    passages = jnp.concatenate([every(2), every(3)], 0)[:, :D].astype(BF16)
    wanted = queries[:, D : D + 1].astype(I32)
    queries = queries[:, :D]
    size = 2 * n_blk
    counted = wanted >= 0
    counted_f = counted.astype(F32)
    column = iota((size, size), 1)
    target = (column == (wanted & 1) * n_blk + wanted // 2) & counted
    marks = message[...]
    lane = iota(marks.shape, 1)
    count = jnp.sum((((lane == 124) | (lane == 125)) & (marks >= 0)).astype(F32))
    count_out[0, 0] = count
    n_pre = prefix_lengths.shape[0]
    prefix_of = iota((n_pre * size, 1), 0) // size
    prefix = jnp.zeros((n_pre * size, 1), I32)
    share = jnp.zeros((n_pre * size, 1), F32)
    for k in range(n_pre):
        prefix = jnp.where(prefix_of == k, prefix_lengths[k], prefix)
        share = jnp.where(prefix_of == k, prefix_weights[k], share)
    temper = TEMPER * lax.rsqrt(prefix.astype(F32))
    mask = iota((n_pre * size, D), 1) < prefix
    masked = jnp.where(mask, jnp.concatenate([queries] * n_pre, 0), 0.0).astype(BF16)
    logits = dot_nt(masked, passages) * temper
    targets = jnp.concatenate([target.astype(F32)] * n_pre, 0)
    counts = jnp.concatenate([counted_f] * n_pre, 0)
    top = jnp.max(logits, -1, keepdims=True)
    weight = jnp.exp(logits - top)
    total = jnp.sum(weight, -1, keepdims=True)
    hit = jnp.sum(logits * targets, -1, keepdims=True)
    losses = share * (top + jnp.log(total) - hit) * counts
    grad = (weight / total - targets) * (counts * (share / count) * temper)
    high, lower = split(grad)
    spread_queries = jnp.where(mask, dot_nn(high, passages) + dot_nn(lower, passages), 0.0)
    d_queries = spread_queries[:size]
    for k in range(1, n_pre):
        d_queries = d_queries + spread_queries[k * size : (k + 1) * size]
    d_passages = dot_tn(high, masked) + dot_tn(lower, masked)
    loss_out[0, 0] = jnp.sum(losses)
    grad_emb[:size] = d_queries
    grad_emb[size : 2 * size] = d_passages
    grad_pooled = jnp.concatenate(
        [grad_emb[pl.ds(me[0] + i * n_blk, 1), :] for i in range(4)]
        + [jnp.zeros((4, D), F32)],
        0,
    )

    def kept_rows(at, rows=8):
        return state[at : at + rows]

    pooled = kept_rows(ST_POOLED)
    d_pre = grad_pooled * (1.0 - pooled * pooled)
    d_c = fine(dot_nt, d_pre, rows_at(matrices, tab, AT_POOL, AT_Q))
    n2 = kept_rows(ST_N2)
    d_second, d_g2, d_s2 = norm_back(d_c, n2, kept_rows(ST_I2), vectors[10:11])
    down_low = d_second.astype(BF16)
    d_a = dot_nt(down_low, rows_at(matrices, tab, AT_DOWN, DENSE * UNIT))
    u = jnp.concatenate([kept_rows(ST_U + 8 * i) for i in range(FF // D)], 1)
    slope = 0.5 * (1.0 + lax.erf(u * (0.5**0.5))) + u * jnp.exp(-0.5 * u * u) * (
        0.3989422804014327
    )
    up_low = (d_a * slope).astype(BF16)
    d_h = d_second + dot_nn(up_low, rows_at(matrices, tab, AT_UP, AT_DOWN))
    d_summed, d_g1, d_s1 = norm_back(d_h, kept_rows(ST_N1), kept_rows(ST_I1), vectors[8:9])
    branch_low = d_summed.astype(BF16)
    d_o = dot_nt(branch_low, rows_at(matrices, tab, AT_O, AT_UP)).astype(BF16)
    head_of = iota((8, D), 1) // HALF
    o_heads = jnp.concatenate(
        [jnp.where(head_of == h, d_o.astype(F32), 0.0) for h in range(HEADS)], 0
    ).astype(BF16)
    vo = dot_nt(o_heads, rows_at(matrices, tab, AT_V, AT_O))
    low = low_in[...]
    probs = probs_in[...]
    d_probs = fine(dot_nt, vo, low)
    d_scores = probs * (d_probs - jnp.sum(d_probs * probs, -1, keepdims=True))
    score_low = d_scores.astype(BF16)
    mixed_score = dot_nn(score_low, low)
    keyed = fine(dot_nn, mixed_score, rows_at(matrices, tab, AT_K, AT_V))
    d_q = jnp.zeros((8, D), F32)
    for h in range(HEADS):
        d_q = d_q + jnp.where(head_of == h, keyed[8 * h : 8 * h + 8], 0.0)
    d_q_low = (d_q * (D // HEADS) ** (-0.5)).astype(BF16)
    d_x0 = d_summed + dot_nt(d_q_low, rows_at(matrices, tab, AT_Q, AT_K))
    kq = kept_rows(ST_KQ, 32)
    vo_high, vo_low = split(vo)
    kq_high, kq_low = split(kq)
    probs_low = probs.astype(BF16)
    dx[...] = dot_tn(
        jnp.concatenate([probs_low, score_low, probs_low, score_low], 0),
        jnp.concatenate([vo_high, kq_high, vo_low, kq_low], 0),
    )
    for i, start in enumerate(STARTS):
        dx[start : start + 1] = dx[start : start + 1] + d_x0[i : i + 1]
    d_gain = jnp.zeros((1, D), F32)
    d_shift = jnp.zeros((1, D), F32)
    d_type = jnp.zeros((1, D), F32)
    for start in range(0, TOKENS, 256):
        incoming = dx[start : start + 256]
        n = normed[start : start + 256]
        d_gain = d_gain + jnp.sum(incoming * n, 0, keepdims=True)
        d_shift = d_shift + jnp.sum(incoming, 0, keepdims=True)
        dn = incoming * vectors[1:2]
        inner = (
            dn - jnp.mean(dn, -1, keepdims=True) - n * jnp.mean(dn * n, -1, keepdims=True)
        )
        de = inner * scale[start : start + 256, :1]
        d_type = d_type + jnp.sum(de, 0, keepdims=True)
        dx[start : start + 256] = de
    de_low = dx[...].astype(BF16)
    at_place, at_left, at_right, n_rows = payload_rows(n_dest, cap)
    per = max(128 // cap, 1)
    step = per * cap
    for at in range(0, n_dest * cap, step):
        hot = ((iota((step, TOKENS), 0) + at) == where_row[1:2]).astype(F32).astype(BF16)
        summed = dot_nn(hot, de_low).astype(BF16)
        for i in range(per):
            d = at // cap + i
            if d < n_dest:
                payload[d, :cap] = summed[i * cap : (i + 1) * cap, :128]
                payload[d, cap : 2 * cap] = summed[i * cap : (i + 1) * cap, 128:]
    spots = dx[STARTS[2] : STARTS[3]] + dx[STARTS[3] :]
    dx[STARTS[2] : STARTS[3]] = spots
    dx[STARTS[2] : STARTS[2] + QROWS] = (
        dx[STARTS[2] : STARTS[2] + QROWS] + dx[:QROWS] + dx[QROWS : 2 * QROWS]
    )
    pr = place_rows(n_dest)
    share = PLEN // n_dest
    for d in range(n_dest):
        spot = dx[STARTS[2] + d * share : STARTS[2] + (d + 1) * share]
        if share < pr:
            spot = jnp.concatenate([spot, jnp.zeros((pr - share, D), F32)], 0)
        payload[d, at_place : at_place + pr] = spot[:, :128].astype(BF16)
        payload[d, at_place + pr : at_place + 2 * pr] = spot[:, 128:].astype(BF16)
    left[...] = jnp.zeros(left.shape, F32)
    up_f = up_low.astype(F32)

    def put(b, r, unit, values):
        spot = (tab[b, TAB_OWNER] * 2 + r) * L_ROWS + (tab[b, TAB_UNIT] + unit) * 4
        for i in range(4):
            left[pl.ds(spot + i, 1), :] = values[i : i + 1]

    for b in range(PLACE_BLOCKS, DENSE):
        at = b * UNIT
        if AT_K <= at < AT_O:
            heads = mixed_score if at < AT_V else kept_rows(ST_B, 32)
            off = (at - AT_K) % D
            for r in range(2):
                for j in range(2):
                    h = 2 * r + j
                    put(b, r, j, heads[8 * h : 8 * h + 4, off : off + UNIT])
            continue
        if at < AT_Q:
            values, off = kept_rows(ST_C), at - AT_POOL
        elif at < AT_K:
            values, off = kept_rows(ST_X0), at - AT_Q
        elif at < AT_UP:
            values, off = kept_rows(ST_O), at - AT_O
        elif at < AT_DOWN:
            values, off = up_f, at - AT_UP
        else:
            off = (at - AT_DOWN) % D
            values = kept_rows(ST_A + 8 * ((at - AT_DOWN) // D))
        for r in range(2):
            put(b, r, 0, values[:4, off : off + UNIT])
    d_vectors = jnp.concatenate(
        [
            d_type,
            d_gain,
            d_shift,
            jnp.sum(d_pre, 0, keepdims=True),
            jnp.sum(d_q_low.astype(F32), 0, keepdims=True),
            jnp.sum(d_o.astype(F32), 0, keepdims=True),
            jnp.sum(branch_low.astype(F32), 0, keepdims=True),
            jnp.sum(down_low.astype(F32), 0, keepdims=True),
            d_g1[None],
            d_s1[None],
            d_g2[None],
            d_s2[None],
        ]
        + [
            jnp.sum(up_f[:, i * D : (i + 1) * D], 0, keepdims=True) for i in range(FF // D)
        ],
        0,
    )
    scaled_q = kept_rows(ST_Q) * (D // HEADS) ** (-0.5)
    right = jnp.concatenate(
        [
            v.astype(F32)[:4]
            for v in (d_pre, d_q_low, scaled_q, d_o, branch_low, kept_rows(ST_H), down_low)
        ],
        0,
    )
    for d in range(n_dest):
        payload[d, at_left:at_right] = left[d * L_ROWS : (d + 1) * L_ROWS].astype(BF16)
        r = d % 2
        if d < 32:
            share_vec = d_vectors[d // 2 : d // 2 + 1, r * 128 : (r + 1) * 128]
        else:
            share_vec = jnp.zeros((1, 128), F32)
        payload[d, at_right:n_rows] = jnp.concatenate(
            [right[:, r * 128 : (r + 1) * 128], share_vec, jnp.zeros((3, 128), F32)], 0
        ).astype(BF16)


def backward(tab, me, prefix_lengths, prefix_weights, emb, message, where_row, low, normed, scale, probs, state, vectors, matrices, cap):
    n_dest = message.shape[0]
    n_rows = payload_rows(n_dest, cap)[-1]
    return pl.pallas_call(
        partial(backward_kernel, cap),
        out_shape=(
            jax.ShapeDtypeStruct((n_dest, n_rows, 128), BF16),
            jax.ShapeDtypeStruct((1, 1), F32),
            jax.ShapeDtypeStruct((1, 1), F32),
        ),
        in_specs=[smem] * 4 + [vmem] * 10,
        out_specs=(vmem, smem, smem),
        scratch_shapes=[
            pltpu.VMEM((emb.shape[0] * 3, 128), F32),
            pltpu.VMEM((emb.shape[0], D), F32),
            pltpu.VMEM((TOKENS, D), F32),
            pltpu.VMEM((n_dest * L_ROWS, 128), F32),
        ],
        compiler_params=params(n_dest // 2, 16),
        name="backward",
    )(tab, me, prefix_lengths, prefix_weights, emb, message, where_row, low, normed, scale, probs, state, vectors, matrices)


def reduce_kernel(slots, cap, tab, me, loss, asked, payload, reduced, news, total, row_grads, left, right):
    n_dest = payload.shape[0]
    at_place, at_left, at_right, n_rows = payload_rows(n_dest, cap)
    for d in range(n_dest):
        row_grads[d * cap : (d + 1) * cap, :128] = payload[d, :cap]
        row_grads[d * cap : (d + 1) * cap, 128:] = payload[d, cap : 2 * cap]
        left[d * L_ROWS : (d + 1) * L_ROWS] = payload[d, at_left:at_right].astype(F32)
        right[d * 32 : (d + 1) * 32] = payload[d, at_right:n_rows].astype(F32)
    grads = row_grads[...]
    filled = slots * HALF
    for at in range(0, filled, 64):
        hot = ((iota((64, n_dest * cap), 0) + at) == asked[...]).astype(F32).astype(BF16)
        total[at : at + 64] = dot_nn(hot, grads)
    mine = me[0]
    odd = me[1]
    column = iota((n_dest * 4, 128), 1)

    def rows_of(ref, start, stride):
        return jnp.concatenate(
            [ref[pl.ds(start + q, n_dest, stride=stride), :] for q in range(4)], 0
        ).astype(BF16)

    for b in range(PLACE_BLOCKS, DENSE):
        at = b * UNIT
        if at < AT_Q:
            m = 0
        elif at < AT_UP:
            m = 1 + (at - AT_Q) // D
        elif at < AT_DOWN:
            m = 5
        else:
            m = 6

        @pl.when(tab[b, TAB_OWNER] == mine)
        def _():
            unit = tab[b, TAB_UNIT] * 4
            pull = rows_of(right, m * 4, 32)
            if AT_K <= at < AT_O:
                grad = dot_tn(
                    rows_of(left, unit, L_ROWS), jnp.where(column < HALF, pull, 0).astype(BF16)
                ) + dot_tn(
                    rows_of(left, unit + 4, L_ROWS),
                    jnp.where(column < HALF, 0, pull).astype(BF16),
                )
            else:
                grad = dot_tn(rows_of(left, unit, L_ROWS), pull)
            spot = pl.multiple_of(tab[b, TAB_SLOT] * HALF, HALF)
            total[pl.ds(spot, HALF), :128] = grad[:HALF]
            total[pl.ds(spot, HALF), 128:] = grad[HALF:]

    pr = place_rows(n_dest)
    spots_low = jnp.zeros((pr, 128), F32)
    spots_high = jnp.zeros((pr, 128), F32)
    for d in range(n_dest):
        spots_low = spots_low + payload[d, at_place : at_place + pr].astype(F32)
        spots_high = spots_high + payload[d, at_place + pr : at_place + 2 * pr].astype(F32)
    spots = jnp.concatenate([spots_low, spots_high], 1)
    vector = jnp.sum(right[pl.ds(28, n_dest, stride=32), :], 0, keepdims=True)
    summed = total[...]
    reduced[...] = summed.astype(BF16).reshape(reduced.shape)
    square = jnp.sum(summed * summed) + jnp.sum(spots * spots) + jnp.sum(vector * vector)
    row8 = iota((8, 128), 0)

    def parts(v):
        first = v.astype(BF16).astype(F32)
        second = (v - first).astype(BF16).astype(F32)
        return first, second, v - first - second

    extra = jnp.where(row8 == 0, vector, 0.0)
    for i, part in enumerate(
        parts(jnp.full((1, 128), square, F32)) + parts(jnp.full((1, 128), loss[0, 0], F32))
    ):
        extra = jnp.where(row8 == 1 + i, part, extra)
    block = jnp.concatenate([spots[:, :128], spots[:, 128:], extra], 0).astype(BF16)
    for d in range(n_dest):
        news[d] = block


def reduce(tab, me, loss, asked, payload, slots, cap):
    n_dest = payload.shape[0]
    pr = place_rows(n_dest)
    return pl.pallas_call(
        partial(reduce_kernel, slots, cap),
        out_shape=(
            jax.ShapeDtypeStruct((slots, HALF, D), BF16),
            jax.ShapeDtypeStruct((n_dest, news_rows(n_dest), 128), BF16),
        ),
        in_specs=[smem, smem, smem, vmem, vmem],
        out_specs=(vmem, vmem),
        scratch_shapes=[
            pltpu.VMEM((slots * HALF, D), F32),
            pltpu.VMEM((n_dest * cap, D), BF16),
            pltpu.VMEM((n_dest * L_ROWS, 128), F32),
            pltpu.VMEM((n_dest * 32, 128), F32),
        ],
        compiler_params=params(n_dest // 2, 16),
        name="reduce",
    )(tab, me, loss, asked, payload)


def update_slots(tab, half, rest, grads, places, scale, arrays, outs, held, in_sems, out_sems):
    slots = held.shape[1]
    first_scale = -RATE / (1.0 - BETA_ONE**STEP)
    second_scale = 1.0 / (1.0 - BETA_TWO**STEP)
    rows = (pl.ds(pl.multiple_of(half * HALF, HALF), HALF), slice(None))
    columns = (slice(None), pl.ds(pl.multiple_of(half * 128, 128), 128))
    whole = (slice(None), slice(None))

    def each(i, action):
        kind = tab[i, TAB_KIND]

        def other():
            pl.when(kind == KIND_DENSE)(lambda: action(KIND_DENSE, columns))
            if rest:
                pl.when(kind != KIND_DENSE)(lambda: action(KIND_PLACE, whole))

        lax.cond(kind == KIND_TABLE, lambda: action(KIND_TABLE, rows), other)

    def loop(act):
        def body(i, c):
            each(i, partial(act, i))
            return c

        lax.fori_loop(0, slots, body, 0)

    def in_copies(i, region):
        return [
            pltpu.make_async_copy(a.at[(i,) + region], held.at[(k, i) + region], in_sems.at[k, i])
            for k, a in enumerate(arrays)
        ]

    def out_copies(i, region):
        return [
            pltpu.make_async_copy(held.at[(k, i) + region], out.at[(i,) + region], out_sems.at[k, i])
            for k, out in enumerate(outs)
        ]

    def start(i, case, region):
        for copy in in_copies(i, region):
            copy.start()

    def step(i, region, g):
        g = g * scale[: g.shape[0], : g.shape[1]]
        m1 = BETA_ONE * held[(1, i) + region] + (1.0 - BETA_ONE) * g
        m2 = BETA_TWO * held[(2, i) + region] + (1.0 - BETA_TWO) * (g * g)
        root = jnp.sqrt(m2 * second_scale) + EPSILON
        held[(0, i) + region] = (
            held[(0, i) + region] * (1.0 - RATE * DECAY) + (m1 * first_scale) / root
        )
        held[(1, i) + region] = m1
        held[(2, i) + region] = m2

    def act(i, case, region):
        for copy in in_copies(i, region):
            copy.wait()
        if case == KIND_TABLE:
            step(i, region, grads[i].astype(F32))
        elif case == KIND_DENSE:
            g = grads[i].astype(F32)
            step(i, region, jnp.concatenate([g[:, :128], g[:, 128:]], 0))
        else:

            @pl.when(tab[i, TAB_KIND] > 0)
            def _():
                spot = pl.multiple_of((tab[i, TAB_KIND] - KIND_PLACE) * UNIT, UNIT)
                step(i, region, places[pl.ds(spot, UNIT), :])

        for copy in out_copies(i, region):
            copy.start()

    def finish(i, case, region):
        for copy in out_copies(i, region):
            copy.wait()

    loop(start)
    yield
    loop(act)
    loop(finish)
    yield


def update_kernel(
    tab, me, news, own, weight, first, second, vectors, vector_first, vector_second,
    weight_out, first_out, second_out, vectors_out, vector_first_out, vector_second_out, loss_out,
    norm_out, factor_out, places, held, in_sems, out_sems,
):
    n_dest = news.shape[0]
    pr = place_rows(n_dest)
    share = PLEN // n_dest
    scale = factor_out
    steps = update_slots(
        tab, me[1], True, own, places, scale, (weight, first, second),
        (weight_out, first_out, second_out), held, in_sems, out_sems,
    )
    next(steps)
    extras = []
    for d in range(n_dest):
        part = news[d].astype(F32)
        places[d * share : (d + 1) * share, :128] = part[:share]
        places[d * share : (d + 1) * share, 128:] = part[pr : pr + share]
        extras.append(part[2 * pr :])
    sums = extras[0]
    for extra in extras[1:]:
        sums = sums + extra
    square = sums[1:2] + sums[2:3] + sums[3:4]
    norm = jnp.sqrt(square)
    factor = CLIP_AT / jnp.maximum(norm, CLIP_AT)
    norm_out[0, 0] = norm[0, 0]
    losses = extras[0] + extras[1]
    loss = losses[4:5] + losses[5:6] + losses[6:7]
    loss_out[0, 0] = loss[0, 0]
    vector_grad = jnp.concatenate(
        [
            jnp.concatenate([extras[2 * i][0:1], extras[2 * i + 1][0:1]], 1)
            for i in range(vectors.shape[0])
        ],
        0,
    ) * jnp.concatenate([factor, factor], 1)
    v, m1, m2 = adam_step(
        vectors[...], vector_first[...], vector_second[...], vector_grad, VECTOR_RATE, 0.0
    )
    vectors_out[...] = v
    vector_first_out[...] = m1
    vector_second_out[...] = m2
    factor_out[...] = jnp.broadcast_to(jnp.concatenate([factor, factor], 1), (UNIT, D))
    next(steps)


def finish_kernel(
    tab, me, factor, other, weight, first, second, weight_in, first_in, second_in, weight_out,
    first_out, second_out, held, in_sems, out_sems,
):
    steps = update_slots(
        tab, 1 - me[1], False, other, None, factor, (weight, first, second),
        (weight_out, first_out, second_out), held, in_sems, out_sems,
    )
    next(steps)
    next(steps)


def update_scratch(shape):
    return [
        pltpu.VMEM((3,) + shape, F32),
        pltpu.SemaphoreType.DMA((3, shape[0])),
        pltpu.SemaphoreType.DMA((3, shape[0])),
    ]


def update(tab, me, news, own, weights, first, second, vectors, vector_first, vector_second):
    n_dest = news.shape[0]
    big = pltpu.HBM(weights.shape, F32)
    small = jax.ShapeDtypeStruct(vectors.shape, F32)
    one = jax.ShapeDtypeStruct((1, 1), F32)
    return pl.pallas_call(
        update_kernel,
        out_shape=(big, big, big, small, small, small, one, one, jax.ShapeDtypeStruct((UNIT, D), F32)),
        in_specs=[smem, smem] + [vmem] * 2 + [in_hbm] * 3 + [vmem] * 3,
        out_specs=(in_hbm, in_hbm, in_hbm, vmem, vmem, vmem, smem, smem, vmem),
        scratch_shapes=[pltpu.VMEM((PLEN, D), F32)] + update_scratch(weights.shape),
        compiler_params=params(n_dest // 2, 14),
        name="update",
    )(tab, me, news, own, *stay(weights, first, second), vectors, vector_first, vector_second)


def finish(tab, me, factor, other, weights, first, second, started, n_blk):
    big = pltpu.HBM(weights.shape, F32)
    return pl.pallas_call(
        finish_kernel,
        out_shape=(big, big, big),
        in_specs=[smem, smem, vmem, vmem] + [in_hbm] * 6,
        out_specs=(in_hbm, in_hbm, in_hbm),
        scratch_shapes=update_scratch(weights.shape),
        input_output_aliases={7: 0, 8: 1, 9: 2},
        compiler_params=params(n_blk, 14),
        name="finish",
    )(tab, me, factor, other, *stay(weights, first, second, *started))


def quick(
    query_ids, passage_ids, query_lengths, passage_lengths, positive, prefix_lengths,
    prefix_weights, owners, weights, first_moments, second_moments, vectors, vector_first,
    vector_second,
):
    slots = weights.shape[0]
    n_blk = lax.axis_size("blk")
    everyone = ("blk", "rep")
    cap = 48 if n_blk <= 16 else 16
    take_cap = 40 if n_blk <= 16 else 16
    me = jnp.stack([lax.axis_index("blk"), lax.axis_index("rep")]).astype(I32)

    def exchange(a, axes):
        return lax.all_to_all(a, axes, 0, 0, tiled=True)

    message, where_row, tab = request(
        owners, me, positive, query_lengths, passage_lengths, query_ids[0], passage_ids[0],
        weights, n_blk, cap, take_cap,
    )
    message = exchange(message, everyone)
    first = along_z(collect(tab, me, message), n_blk)
    rows, message = fetch(message, weights, cap, take_cap)
    rows, first = lax.optimization_barrier((rows, first))
    rows = exchange(rows, everyone)
    gathered = spread(first, n_blk)
    emb, low, normed, scale, probs, state, matrices = forward(
        tab, me, query_lengths, passage_lengths, positive, rows, where_row, vectors, gathered, n_blk
    )
    emb = exchange(emb, "blk")
    payload, loss, count = backward(
        tab, me, prefix_lengths, prefix_weights, emb, message, where_row, low, normed, scale,
        probs, state, vectors, matrices, cap,
    )
    payload = exchange(payload, everyone)
    asked = message[:, :cap].reshape(1, -1)
    own, news = reduce(tab, me, loss, asked, payload, slots, cap)
    other = lax.ppermute(own, "rep", [(0, 1), (1, 0)])
    news = exchange(news, everyone)
    *outs, loss_sum, norm, factor = update(
        tab, me, news, own, weights, first_moments, second_moments, vectors, vector_first,
        vector_second,
    )
    outs[:3] = finish(
        tab, me, factor, other, weights, first_moments, second_moments, outs[:3], n_blk
    )

    def general(carry):
        return 0, local(
            query_ids, passage_ids, query_lengths, passage_lengths, positive, prefix_lengths,
            prefix_weights, owners, weights, first_moments, second_moments, vectors, vector_first,
            vector_second,
        )

    outs = (*outs, loss_sum.reshape(()), count.reshape(()), norm.reshape(()))
    return lax.while_loop(lambda c: c[0] > 0, general, (jnp.max(message[:, 126]), outs))[1]


def solution(mesh):
    in_specs = (
        P("rep", "blk", None),
        P("rep", "blk", None),
        P("rep", "blk"),
        P("rep", "blk"),
        P("rep", "blk"),
        P(),
        P(),
        P(),
        P("blk", None, None),
        P("blk", None, None),
        P("blk", None, None),
        P(),
        P(),
        P(),
    )
    out_specs = (
        P("blk", None, None),
        P("blk", None, None),
        P("blk", None, None),
        P(),
        P(),
        P(),
        P(),
        P(),
        P(),
    )
    return jax.shard_map(quick, mesh=mesh, in_specs=in_specs, out_specs=out_specs, check_vma=False)
```

```python
from functools import partial

import jax
import jax.numpy as jnp
from jax import lax
from jax.experimental import pallas as pl
from jax.experimental.pallas import tpu as pltpu
from jax.sharding import PartitionSpec as P

D = 256
HEADS = 4
FF = 1024
VOCAB = 30592
LAYERS = 1
PLEN = 512
STEP = 7


TEMPER = 8.0
CLIP_AT = 0.01
RATE = 0.06
VECTOR_RATE = 0.8
BETA_ONE = 0.9
BETA_TWO = 0.999
DECAY = 0.01
EPSILON = 1e-08
NORM_EPS = 1e-06
HUGE = 1000000000.0
HIGHEST = lax.Precision.HIGHEST


def mult(left_op, right_op):
    return jnp.dot(left_op, right_op, preferred_element_type=jnp.float32)


def mult_tn(left_op, right_op):
    return lax.dot_general(
        left_op, right_op, (((0,), (0,)), ((), ())), preferred_element_type=jnp.float32
    )


def mult_nt(left_op, right_op):
    return lax.dot_general(
        left_op, right_op, (((1,), (1,)), ((), ())), preferred_element_type=jnp.float32
    )


def norm_rows(values_in, gain_row, shift_row):
    centred = values_in - jnp.mean(values_in, -1, keepdims=True)
    inv_scale = lax.rsqrt(jnp.mean(centred * centred, -1, keepdims=True) + NORM_EPS)
    normed = centred * inv_scale
    return (normed * gain_row + shift_row, normed, inv_scale)


def norm_back(incoming, normed, inv_scale, gain_row):
    dnormed = incoming * gain_row
    inner_part = (
        dnormed
        - jnp.mean(dnormed, -1, keepdims=True)
        - normed * jnp.mean(dnormed * normed, -1, keepdims=True)
    )
    return (inner_part * inv_scale, jnp.sum(incoming * normed, 0), jnp.sum(incoming, 0))


def layer_parts(flat_rows, vectors, layer_index):
    offset = VOCAB + PLEN + D + layer_index * (4 * D + 2 * FF)
    w_qkv = jnp.concatenate(
        [
            flat_rows[offset : offset + D],
            flat_rows[offset + D : offset + 2 * D],
            flat_rows[offset + 2 * D : offset + 3 * D],
        ],
        1,
    )
    w_out = flat_rows[offset + 3 * D : offset + 4 * D]
    w_up = flat_rows[offset + 4 * D : offset + 4 * D + FF]
    w_down = flat_rows[offset + 4 * D + FF : offset + 4 * D + 2 * FF]
    row_base = 4 + layer_index * (8 + FF // D)
    return ((w_qkv, w_out, w_up, w_down), vectors[row_base : row_base + 8 + FF // D])


def divide_into_heads(packed_buffer, column):
    return packed_buffer[:, column * D : (column + 1) * D].reshape(
        packed_buffer.shape[0], HEADS, D // HEADS
    )


def attend_probs(packed_buffer, key_keep):
    scores = jnp.einsum(
        "cnp,fnp->ncf",
        divide_into_heads(packed_buffer, 0),
        divide_into_heads(packed_buffer, 1),
        preferred_element_type=jnp.float32,
    ) * (D // HEADS) ** (-0.5)
    scores = jnp.where(key_keep[None, None, :], scores, -HUGE)
    return jax.nn.softmax(scores, -1)


def attend(pieces):
    packed_buffer, key_keep = pieces
    attn_probs = attend_probs(packed_buffer, key_keep)
    blended = jnp.einsum(
        "nbi,ins->bns",
        attn_probs.astype(jnp.bfloat16),
        divide_into_heads(packed_buffer, 2),
        preferred_element_type=jnp.float32,
    )
    return blended.reshape(packed_buffer.shape[0], D)


def attend_back(pieces):
    packed_buffer, key_keep, grad_out = pieces
    seq_len = packed_buffer.shape[0]
    head_scale = (D // HEADS) ** (-0.5)
    attn_probs = attend_probs(packed_buffer, key_keep)
    gradient_row_block = grad_out.reshape(seq_len, HEADS, D // HEADS)
    grad_values = jnp.einsum(
        "fxn,xfa->nfa",
        attn_probs.astype(jnp.bfloat16),
        gradient_row_block,
        preferred_element_type=jnp.float32,
    )
    grad_probs = jnp.einsum(
        "cnp,fnp->ncf",
        gradient_row_block,
        divide_into_heads(packed_buffer, 2),
        preferred_element_type=jnp.float32,
    )
    grad_scores = attn_probs * (grad_probs - jnp.sum(grad_probs * attn_probs, -1, keepdims=True))
    score_lowered = grad_scores.astype(jnp.bfloat16)
    grad_queries = (
        jnp.einsum(
            "nbi,ins->bns",
            score_lowered,
            divide_into_heads(packed_buffer, 1),
            preferred_element_type=jnp.float32,
        )
        * head_scale
    )
    grad_keys = (
        jnp.einsum(
            "fxn,xfa->nfa",
            score_lowered,
            divide_into_heads(packed_buffer, 0),
            preferred_element_type=jnp.float32,
        )
        * head_scale
    )
    return jnp.concatenate(
        [
            grad_queries.reshape(seq_len, D),
            grad_keys.reshape(seq_len, D),
            grad_values.reshape(seq_len, D),
        ],
        1,
    ).astype(jnp.bfloat16)


def layer_forward(hidden_in, weights_set, vec_rows, key_keep):
    w_qkv, w_out, w_up, w_down = weights_set
    groups, seq_len = key_keep.shape
    in_low = hidden_in.astype(jnp.bfloat16)
    bias_qkv = jnp.concatenate([vec_rows[0], jnp.zeros_like(vec_rows[0]), vec_rows[1]])
    packed_buffer = (mult(in_low, w_qkv) + bias_qkv).astype(jnp.bfloat16)
    blended = lax.map(attend, (packed_buffer.reshape(groups, seq_len, 3 * D), key_keep))
    blend_low = blended.reshape(groups * seq_len, D).astype(jnp.bfloat16)
    summed = hidden_in + mult(blend_low, w_out) + vec_rows[2]
    normal_one, normed_one, scale_one = norm_rows(summed, vec_rows[4], vec_rows[5])
    normal_low = normal_one.astype(jnp.bfloat16)
    up_in = mult_nt(normal_low, w_up) + vec_rows[8:].reshape(FF)
    acted = jax.nn.gelu(up_in, approximate=False).astype(jnp.bfloat16)
    second = normal_one + mult(acted, w_down) + vec_rows[3]
    result, normed_two, scale_two = norm_rows(second, vec_rows[6], vec_rows[7])
    return (
        result,
        (
            in_low,
            packed_buffer,
            blend_low,
            normed_one,
            scale_one,
            normal_low,
            up_in,
            acted,
            normed_two,
            scale_two,
        ),
    )


def layer_backward(grad_out, weights_set, vec_rows, key_keep, saved):
    w_qkv, w_out, w_up, w_down = weights_set
    (
        in_low,
        packed_buffer,
        blend_low,
        normed_one,
        scale_one,
        normal_low,
        up_in,
        acted,
        normed_two,
        scale_two,
    ) = saved
    groups, seq_len = key_keep.shape
    grad_second, grad_gain_two, grad_shift_two = norm_back(
        grad_out, normed_two, scale_two, vec_rows[6]
    )
    down_low = grad_second.astype(jnp.bfloat16)
    grad_down = mult_tn(acted, down_low)
    grad_acted = mult_nt(down_low, w_down)
    gelu_pull = jax.vjp(partial(jax.nn.gelu, approximate=False), up_in)[1]
    up_low = gelu_pull(grad_acted)[0].astype(jnp.bfloat16)
    grad_up = mult_tn(up_low, normal_low)
    grad_normal = grad_second + mult(up_low, w_up)
    grad_summed, gradient_first_gain, grad_shift_one = norm_back(
        grad_normal, normed_one, scale_one, vec_rows[4]
    )
    branch_low = grad_summed.astype(jnp.bfloat16)
    grad_wout = mult_tn(blend_low, branch_low)
    blend_grad = mult_nt(branch_low, w_out).astype(jnp.bfloat16)
    grad_packed = lax.map(
        attend_back,
        (
            packed_buffer.reshape(groups, seq_len, 3 * D),
            key_keep,
            blend_grad.reshape(groups, seq_len, D),
        ),
    ).reshape(groups * seq_len, 3 * D)
    grad_wqkv = mult_tn(in_low, grad_packed)
    grad_in = grad_summed + mult_nt(grad_packed, w_qkv)
    packed_sum = jnp.sum(grad_packed.astype(jnp.float32), 0)
    matrix_grads = jnp.concatenate(
        [
            grad_wqkv[:, :D],
            grad_wqkv[:, D : 2 * D],
            grad_wqkv[:, 2 * D :],
            grad_wout,
            grad_up,
            grad_down,
        ],
        0,
    )
    vector_grads = jnp.concatenate(
        [
            jnp.stack(
                [
                    packed_sum[:D],
                    packed_sum[2 * D :],
                    jnp.sum(branch_low.astype(jnp.float32), 0),
                    jnp.sum(down_low.astype(jnp.float32), 0),
                    gradient_first_gain,
                    grad_shift_one,
                    grad_gain_two,
                    grad_shift_two,
                ]
            ),
            jnp.sum(up_low.astype(jnp.float32), 0).reshape(FF // D, D),
        ],
        0,
    )
    return (grad_in, matrix_grads, vector_grads)


def embed_sequences(flat_rows, vectors, token_ids, lengths):
    groups, seq_len = token_ids.shape
    key_keep = jnp.arange(seq_len)[None, :] < lengths[:, None]
    table_rows = jnp.take(flat_rows, token_ids.reshape(-1), axis=0).astype(jnp.float32)
    places = flat_rows[VOCAB : VOCAB + seq_len].astype(jnp.float32)
    embedded = (table_rows.reshape(groups, seq_len, D) + places[None] + vectors[0]).reshape(
        groups * seq_len, D
    )
    hidden_now, normed_emb, scaled_embedding = norm_rows(embedded, vectors[1], vectors[2])
    weights_set, vec_rows = layer_parts(flat_rows, vectors, 0)
    hidden_now, saved = layer_forward(hidden_now, weights_set, vec_rows, key_keep)
    layer_saves = [saved]
    first_rows = hidden_now.reshape(groups, seq_len, D)[:, 0].astype(jnp.bfloat16)
    pooled = jnp.tanh(mult(first_rows, flat_rows[VOCAB + PLEN : VOCAB + PLEN + D]) + vectors[3])
    return (pooled, (normed_emb, scaled_embedding, layer_saves, first_rows))


def encode_back(grad_pooled, pooled, flat_rows, vectors, token_ids, lengths, encoder_kept):
    normed_emb, scaled_embedding, layer_saves, first_rows = encoder_kept
    groups, seq_len = token_ids.shape
    key_keep = jnp.arange(seq_len)[None, :] < lengths[:, None]
    w_pool = flat_rows[VOCAB + PLEN : VOCAB + PLEN + D].astype(jnp.float32)
    grad_pre = grad_pooled * (1.0 - pooled * pooled)
    grad_pool = jnp.dot(first_rows.astype(jnp.float32).T, grad_pre, precision=HIGHEST)
    grad_first = jnp.dot(grad_pre, w_pool.T, precision=HIGHEST)
    grad_hidden = (
        jnp.zeros((groups, seq_len, D), jnp.float32)
        .at[:, 0]
        .set(grad_first)
        .reshape(groups * seq_len, D)
    )
    matrices = []
    vector_parts = []
    for layer_index in reversed(range(LAYERS)):
        weights_set, vec_rows = layer_parts(flat_rows, vectors, layer_index)
        grad_hidden, matrix_grads, vector_grads = layer_backward(
            grad_hidden, weights_set, vec_rows, key_keep, layer_saves[layer_index]
        )
        matrices.insert(0, matrix_grads)
        vector_parts.insert(0, vector_grads)
    grad_embed, grad_gain, grad_shift = norm_back(
        grad_hidden, normed_emb, scaled_embedding, vectors[1]
    )
    grad_table = jnp.zeros((VOCAB, D), jnp.float32).at[token_ids.reshape(-1)].add(grad_embed)
    grad_places = (
        jnp.zeros((PLEN, D), jnp.float32)
        .at[:seq_len]
        .set(jnp.sum(grad_embed.reshape(groups, seq_len, D), 0))
    )
    flat_grad = jnp.concatenate([grad_table, grad_places, grad_pool] + matrices, 0)
    head_rows = jnp.stack([jnp.sum(grad_embed, 0), grad_gain, grad_shift, jnp.sum(grad_pre, 0)])
    return (flat_grad, jnp.concatenate([head_rows] + vector_parts, 0))


def adam_step(weight, moment_one, moment_two, gradient, step_rate, decay_rate):
    moment_one = BETA_ONE * moment_one + (1.0 - BETA_ONE) * gradient
    moment_two = BETA_TWO * moment_two + (1.0 - BETA_TWO) * gradient * gradient
    update = (
        moment_one
        / (1.0 - BETA_ONE**STEP)
        / (jnp.sqrt(moment_two / (1.0 - BETA_TWO**STEP)) + EPSILON)
    )
    return (weight - step_rate * (update + decay_rate * weight), moment_one, moment_two)


def gather_all(values, axes):
    count = lax.axis_size(axes)
    copies = jnp.broadcast_to(values[None], (count,) + values.shape)
    return lax.all_to_all(copies, axes, 0, 0, tiled=True).reshape((-1,) + values.shape[1:])


def sum_all(values, axes):
    count = lax.axis_size(axes)
    copies = jnp.broadcast_to(values[None], (count,) + values.shape)
    return jnp.sum(lax.all_to_all(copies, axes, 0, 0, tiled=True), 0)


def sum_share(values, axes):
    count = lax.axis_size(axes)
    parts = lax.all_to_all(values, axes, 0, 0, tiled=True)
    return jnp.sum(parts.reshape((count, -1) + values.shape[1:]), 0)


def local(
    query_ids,
    passage_ids,
    query_lengths,
    passage_lengths,
    positive,
    prefix_lengths,
    prefix_weights,
    owners,
    weights,
    first_moments,
    second_moments,
    vectors,
    vector_first,
    vector_second,
):
    slot_count, unit_rows = (weights.shape[0], weights.shape[1])
    gathered = gather_all(weights.astype(jnp.bfloat16), "blk")
    flat_rows = jnp.take(gathered, owners, axis=0).reshape(-1, D)
    query_pooled, query_kept = embed_sequences(flat_rows, vectors, query_ids[0], query_lengths[0])
    passage_pooled, passage_kept = embed_sequences(
        flat_rows, vectors, passage_ids[0], passage_lengths[0]
    )
    all_passages = gather_all(passage_pooled.astype(jnp.bfloat16), "blk")
    prefix_masks = (jnp.arange(D)[None, :] < prefix_lengths[:, None]).astype(jnp.float32)
    prefix_scale = TEMPER * lax.rsqrt(prefix_lengths.astype(jnp.float32))
    queries = query_pooled.astype(jnp.bfloat16).astype(jnp.float32)
    passages = all_passages.astype(jnp.float32)
    masked = queries[None] * prefix_masks[:, None, :]
    logits = (
        jnp.einsum("mpd,jd->mpj", masked, passages, precision=HIGHEST) * prefix_scale[:, None, None]
    )
    counted = positive[0] >= 0
    target = (jnp.arange(passages.shape[0])[None, :] == positive[0][:, None]).astype(jnp.float32)
    running_totals = jax.nn.logsumexp(logits, -1) - jnp.sum(logits * target[None], -1)
    per_query = jnp.sum(prefix_weights[:, None] * running_totals, 0)
    loss_part = jnp.sum(jnp.where(counted, per_query, 0.0))
    count_part = jnp.sum(counted.astype(jnp.float32))
    count_total, loss_total = sum_all(jnp.stack([count_part, loss_part]), ("blk", "rep"))
    row_factor = (prefix_weights * prefix_scale / count_total)[:, None, None] * counted.astype(
        jnp.float32
    )[None, :, None]
    grad_logits = (jax.nn.softmax(logits, -1) - target[None]) * row_factor
    grad_query = jnp.sum(
        jnp.einsum("mpj,jd->mpd", grad_logits, passages, precision=HIGHEST)
        * prefix_masks[:, None, :],
        0,
    )
    grad_passage = sum_share(
        jnp.einsum("mpj,mpd->jd", grad_logits, masked, precision=HIGHEST), "blk"
    )
    flat_query, vec_query = encode_back(
        grad_query, query_pooled, flat_rows, vectors, query_ids[0], query_lengths[0], query_kept
    )
    flat_pass, vec_pass = encode_back(
        grad_passage,
        passage_pooled,
        flat_rows,
        vectors,
        passage_ids[0],
        passage_lengths[0],
        passage_kept,
    )
    vec_total = sum_all(vec_query + vec_pass, ("blk", "rep"))
    buffer = (
        jnp.zeros((lax.axis_size("blk") * slot_count, unit_rows, D), jnp.float32)
        .at[owners]
        .set((flat_query + flat_pass).reshape(-1, unit_rows, D))
    )
    vec_square = jnp.sum(vec_total * vec_total)
    reduced = sum_share(buffer, "blk")
    reduced = sum_all(reduced, "rep")
    square_sum = sum_all(jnp.sum(reduced * reduced)[None], "blk")[0]
    old_weight, old_first, old_second = (weights, first_moments, second_moments)
    slot_ids = lax.axis_index("blk") * slot_count + jnp.arange(slot_count)
    owned_mask = jnp.any(slot_ids[:, None] == owners[None, :], 1)[:, None, None]
    grad_norm = jnp.sqrt(square_sum + vec_square)
    factor = CLIP_AT / jnp.maximum(grad_norm, CLIP_AT)
    new_weight, new_first, new_second = adam_step(
        old_weight, old_first, old_second, reduced * factor, RATE, DECAY
    )
    new_weight = jnp.where(owned_mask, new_weight, old_weight)
    new_first = jnp.where(owned_mask, new_first, old_first)
    new_second = jnp.where(owned_mask, new_second, old_second)
    new_vec, new_vec_first, new_vec_second = adam_step(
        vectors, vector_first, vector_second, vec_total * factor, VECTOR_RATE, 0.0
    )
    return (
        new_weight,
        new_first,
        new_second,
        new_vec,
        new_vec_first,
        new_vec_second,
        loss_total,
        count_total,
        grad_norm,
    )


F32 = jnp.float32
BF16 = jnp.bfloat16
I32 = jnp.int32
UNIT = 128
TABLE_BLOCKS = VOCAB // UNIT
PLACE_BLOCKS = PLEN // UNIT
DENSE = PLACE_BLOCKS + (D + 4 * D + 2 * FF) // UNIT
HALF = 64
QROWS = 128
TOKENS = 2 * QROWS + 2 * PLEN
STARTS = (0, QROWS, 2 * QROWS, 2 * QROWS + PLEN)
UNITS_L = 10
L_ROWS = 4 * UNITS_L
NEVER = -1e30


def params(n_blk, small):
    return pltpu.CompilerParams(vmem_limit_bytes=(small if n_blk <= 16 else 58) << 20)


AT_POOL = PLEN
AT_Q = AT_POOL + D
AT_K = AT_Q + D
AT_V = AT_K + D
AT_O = AT_V + D
AT_UP = AT_O + D
AT_DOWN = AT_UP + FF

TAB_OWNER, TAB_RANK, TAB_SLOT, TAB_UNIT, TAB_KIND, TAB_ORDER, TAB_SORTED, TAB_ENDS = range(8)
PIECE = 16
PIECES = 16
DENSE_CAP = 8
CLASS = DENSE // 2
HELD = DENSE_CAP // 2
AT_ASKED = DENSE_CAP // 4 * PIECE
MESSAGE_ROWS = AT_ASKED + 8

KIND_TABLE, KIND_PLACE, KIND_DENSE = 1, 2, 8

vmem = pl.BlockSpec(memory_space=pltpu.VMEM)
smem = pl.BlockSpec(memory_space=pltpu.SMEM)
hbm = pl.BlockSpec(memory_space=pl.ANY)
in_hbm = pl.BlockSpec(memory_space=pltpu.HBM)


def stay(*arrays):
    return [pltpu.with_memory_space_constraint(a, pltpu.HBM) for a in arrays]


def iota(shape, axis):
    return lax.broadcasted_iota(I32, shape, axis)


def dot_nn(a, b):
    return lax.dot_general(a, b, (((1,), (0,)), ((), ())), preferred_element_type=F32)


def dot_nt(a, b):
    return lax.dot_general(a, b, (((1,), (1,)), ((), ())), preferred_element_type=F32)


def dot_tn(a, b):
    return lax.dot_general(a, b, (((0,), (0,)), ((), ())), preferred_element_type=F32)


def split(a):
    high = a.astype(BF16)
    return high, (a - high.astype(F32)).astype(BF16)


def fine(dot, a, b):
    high, low = split(a)
    rows = a.shape[0]
    both = dot(jnp.concatenate([high, low], 0), b)
    return both[:rows] + both[rows:]


def to_column(row):
    return jnp.broadcast_to(row, (128, 128)).T[:, :1]


def token_facts(query_lengths, passage_lengths):
    lane = iota((1, TOKENS), 1)
    sequence = (
        (lane >= STARTS[1]).astype(I32)
        + (lane >= STARTS[2]).astype(I32)
        + (lane >= STARTS[3]).astype(I32)
    )
    ends = [
        STARTS[0] + query_lengths[0, 0],
        STARTS[1] + query_lengths[0, 1],
        STARTS[2] + passage_lengths[0, 0],
        STARTS[3] + passage_lengths[0, 1],
    ]
    end = jnp.where(
        sequence == 0,
        ends[0],
        jnp.where(sequence == 1, ends[1], jnp.where(sequence == 2, ends[2], ends[3])),
    )
    return sequence, lane < end


def across(values, n_blk, step):
    pairs = [(i, i // PIECES * PIECES + step(i % PIECES)) for i in range(n_blk)]
    return lax.ppermute(values, "blk", pairs)


def along_z(mine, n_blk):
    return jnp.stack(
        [mine] + [across(mine, n_blk, lambda i, k=k: (i + 4 * k) % PIECES) for k in (1, 2, 3)]
    )


def spread(first, n_blk):
    arrays = [first, lax.ppermute(first, "rep", [(0, 1), (1, 0)])]
    arrays = arrays + [across(a, n_blk, lambda i: i ^ 2) for a in arrays]
    return arrays + [across(a, n_blk, lambda i: i ^ 1) for a in arrays]


def piece_copies(me, gathered, matrices, sems):
    copies = []
    for part, array in enumerate(gathered):
        low = (me[0] % 4) ^ (part & 2) ^ (part // 4)
        odd = me[1] ^ (part % 2)
        for k in range(4):
            p = low + (me[0] % PIECES // 4 * 4 + 4 * (4 - k)) % PIECES
            row = pl.multiple_of((p % 8) * PIECE, PIECE)
            lane = pl.multiple_of((p // 8) * 128, 128)
            copies.append(
                pltpu.make_async_copy(
                    array.at[k],
                    matrices.at[:, odd, pl.ds(row, PIECE), pl.ds(lane, 128)],
                    sems.at[4 * part + k],
                )
            )
    return copies


def rows_at(matrices, tab, start, stop):
    blocks = []
    for b in range(start // UNIT, stop // UNIT):
        order = tab[b, TAB_ORDER]
        blocks.append(matrices[order // 2, order % 2])
    return jnp.concatenate(blocks, 0)


def owner_of(slot, slots, n_blk):
    owner = jnp.zeros(slot.shape, I32)
    for k in range(1, n_blk):
        owner = owner + (slot >= k * slots).astype(I32)
    return owner


def request_kernel(
    slots, n_blk, cap, take_cap, owners, me, positive, query_lengths, passage_lengths, owner_line,
    query_ids, passage_ids, weights, message, where_row, tab, ids, owner_row, loaded, sems,
):
    n_rep = 2
    n_dest = n_blk * n_rep
    n_units = owners.shape[0]
    start = me[0] * slots

    def take(b, carry):
        before, have = carry
        slot = owners[n_units - DENSE + b]
        inside = slot - start
        mine = (inside >= 0) & (inside < slots)

        @pl.when(mine & (have // 2 % 2 == me[1]) & (have < DENSE_CAP))
        def _():
            spot = have // 4 * 2 + have % 2
            pltpu.make_async_copy(weights.at[inside], loaded.at[spot], sems.at[spot]).start()

        return before + (slot < start).astype(I32), have + mine.astype(I32)

    before, have = lax.fori_loop(0, DENSE, take, (0, 0))
    owner_row[...] = jnp.full(owner_row.shape, -1, I32)
    owner_row[:, :n_units] = owner_line[...].reshape(1, n_units)
    every_slot = owner_row[...]
    wide = every_slot.shape[1]
    base = n_units - DENSE
    low = base // 128 * 128
    rolled = pltpu.roll(every_slot[:, low:], wide - low - (base - low), 1)[:, :128]
    dense_owner = owner_of(rolled, slots, n_blk)
    owner_column = to_column(dense_owner)[:32]
    slot_column = to_column(rolled)[:32]
    block_row = iota((32, 128), 1)
    block_column = iota((32, 128), 0)
    same = (owner_column == dense_owner) & (block_row < block_column) & (block_row < DENSE)
    rank = jnp.sum(same.astype(I32), 1, keepdims=True)
    at = block_row * UNIT
    need = jnp.where(block_row < PLACE_BLOCKS, 0, jnp.where((at >= AT_K) & (at < AT_O), 2, 1))
    unit = jnp.sum(jnp.where(same, need, 0), 1, keepdims=True)
    lower = (dense_owner < owner_column) & (block_row < DENSE)
    order = rank + jnp.sum(lower.astype(I32), 1, keepdims=True)
    is_dense = (iota((32, 1), 0) >= PLACE_BLOCKS) & (iota((32, 1), 0) < DENSE)
    at = iota((32, 1), 0) * UNIT
    needs = jnp.where((at >= AT_K) & (at < AT_O), 2, 1)
    crowded = jnp.max(
        (
            ((rank >= DENSE_CAP) & (iota((32, 1), 0) < DENSE))
            | (is_dense & (unit + needs > UNITS_L))
        ).astype(I32)
    )
    which = iota((32, wide), 1)
    code = jnp.where(
        which < TABLE_BLOCKS,
        KIND_TABLE,
        jnp.where(
            which < TABLE_BLOCKS + PLACE_BLOCKS, KIND_PLACE + which - TABLE_BLOCKS, KIND_DENSE
        ),
    )
    here = (every_slot == me[0] * slots + iota((32, wide), 0)) & (which < n_units)
    kind = jnp.sum(jnp.where(here, code, 0), 1, keepdims=True)
    sort = jnp.where(
        kind == KIND_TABLE,
        0,
        jnp.where(kind == KIND_DENSE, 1, jnp.where(kind >= KIND_PLACE, 2, 3)),
    )
    sort = jnp.where(iota((32, 1), 0) < slots, sort, 4)

    def to_row(column):
        wide = jnp.concatenate([column, jnp.full((96, 1), 5, I32)], 0)
        return jnp.broadcast_to(wide, (128, 128)).T[:1]

    sort_row = to_row(sort)
    ahead = (sort_row < sort) | ((sort_row == sort) & (block_row < block_column))
    place_row = to_row(jnp.sum(ahead.astype(I32), 1, keepdims=True))
    sorted_slot = jnp.sum(
        jnp.where((place_row == block_column) & (block_row < 32), block_row, 0), 1, keepdims=True
    )
    ends = jnp.sum((sort_row <= iota((32, 1), 0)).astype(I32), 1, keepdims=True)
    entry = block_row
    tab[...] = jnp.where(
        entry == TAB_OWNER,
        owner_column,
        jnp.where(
            entry == TAB_RANK,
            jnp.minimum(rank, DENSE_CAP - 1),
            jnp.where(
                entry == TAB_SLOT,
                slot_column - owner_column * slots,
                jnp.where(
                    entry == TAB_UNIT,
                    jnp.minimum(unit, UNITS_L - 2),
                    jnp.where(
                        entry == TAB_KIND,
                        kind,
                        jnp.where(
                            entry == TAB_ORDER,
                            jnp.minimum(order, DENSE - 1),
                            jnp.where(entry == TAB_SORTED, sorted_slot, ends),
                        ),
                    ),
                ),
            ),
        ),
    )

    ids[:, 0:QROWS] = query_ids[0:1]
    ids[:, QROWS : 2 * QROWS] = query_ids[1:2]
    ids[:, STARTS[2] : STARTS[3]] = passage_ids[0:1]
    ids[:, STARTS[3] :] = passage_ids[1:2]
    token = ids[...]
    _, live = token_facts(query_lengths, passage_lengths)
    lane = iota((1, TOKENS), 1)
    block = token // UNIT
    slot = jnp.zeros((1, TOKENS), I32)
    table_rows = -(-TABLE_BLOCKS // 128) * 128
    for at in range(0, table_rows, 128):
        column = to_column(owner_row[:, at : at + 128])
        hit = (iota((128, TOKENS), 0) + at) == block
        slot = slot + jnp.sum(jnp.where(hit, column, 0), 0, keepdims=True)
    owner = owner_of(slot, slots, n_blk)
    inside = slot - owner * slots
    row = token - block * UNIT
    upper = (row >= HALF).astype(I32)
    dest = owner * n_rep + upper
    local_row = inside * HALF + row - upper * HALF
    token = jnp.where(live, token, -1)
    first_at = []
    columns = [to_column(token[:, at : at + 128]) for at in range(0, TOKENS, 128)]
    for to_at in range(0, TOKENS, 128):
        best = jnp.full((128, 128), TOKENS, I32)
        for at in range(0, to_at + 128, 128):
            same = columns[at // 128] == token[:, to_at : to_at + 128]
            best = jnp.minimum(best, jnp.where(same, iota((128, 128), 0) + at, TOKENS))
        first_at.append(jnp.min(best, 0, keepdims=True))
    first_at = jnp.concatenate(first_at, 1)
    first = live & (first_at == lane)
    chosen = ((iota((n_dest, TOKENS), 0) == dest) & first).astype(F32)
    chosen_low = chosen.astype(BF16)
    seen = []
    for to_at in range(0, TOKENS, 256):
        above = to_at + 256
        earlier = iota((above, 256), 0) < first_at[:, to_at:above]
        seen.append(dot_nn(chosen_low[:, :above], earlier.astype(F32).astype(BF16)))
    seen = jnp.concatenate(seen, 1)
    to = iota((n_dest, TOKENS), 0)
    rank = jnp.sum(jnp.where(to == dest, seen, 0.0), 0, keepdims=True).astype(I32)
    turn = jnp.sum(jnp.where(to // n_rep == owner, seen, 0.0), 0, keepdims=True).astype(I32)
    source = owner * n_rep + me[1]
    where_row[0:1] = jnp.where(live & (turn < take_cap), owner * take_cap + turn, -1)
    where_row[1:2] = jnp.where(live & (rank < cap), dest * cap + rank, -1)
    over = jnp.max((live & ((rank >= cap) | (turn >= take_cap))).astype(I32))

    def listed(dest, spot, code):
        high = code // 32
        low = code - high * 32
        chosen = ((to == dest) & first).astype(F32)
        both = jnp.concatenate([chosen * high.astype(F32), chosen * low.astype(F32)], 0)
        spread = (iota((128, TOKENS), 0) == spot).astype(F32).astype(BF16)
        both = dot_nt(both.astype(BF16), spread)
        return both[:n_dest], both[n_dest:]

    take_high, take_low = listed(source, turn, inside * UNIT + row + 1)
    sent_high, sent_low = listed(dest, rank, local_row + 1)
    flag = jnp.maximum(over, crowded)
    column_of = iota((1, 128), 1)
    marks = jnp.where(
        column_of == 0,
        positive[0, 0],
        jnp.where(column_of == 1, positive[0, 1], jnp.where(column_of == 2, flag, 0)),
    ).astype(F32)
    row8 = iota((8, 128), 0)
    for d in range(n_dest):
        asked = jnp.where(row8 == 0, take_high[d : d + 1], marks)
        for i, part in ((1, take_low), (3, sent_high), (4, sent_low)):
            asked = jnp.where(row8 == i, part[d : d + 1], asked)
        message[d, AT_ASKED:] = asked.astype(BF16)
    for spot in range(HELD):
        present = spot // 2 * 4 + 2 * me[1] + spot % 2 < have

        @pl.when(present)
        def _():
            pltpu.make_async_copy(weights.at[0], loaded.at[spot], sems.at[spot]).wait()

        @pl.when(jnp.logical_not(present))
        def _():
            loaded[spot] = jnp.zeros((UNIT, D), F32)

    for odd in range(2):
        for c in range(DENSE_CAP // 4):
            whole = loaded[2 * c + (odd + before) % 2].astype(BF16)
            for s in range(n_blk):
                p = s % PIECES
                message[2 * s + odd, PIECE * c : PIECE * (c + 1)] = whole[
                    PIECE * (p % 8) : PIECE * (p % 8 + 1), 128 * (p // 8) : 128 * (p // 8 + 1)
                ]


def request(owners, me, positive, query_lengths, passage_lengths, query_ids, passage_ids, weights, n_blk, cap, take_cap):
    slots = weights.shape[0]
    n_dest = 2 * n_blk
    n_units = owners.shape[0]
    owner_row = owners
    return pl.pallas_call(
        partial(request_kernel, slots, n_blk, cap, take_cap),
        out_shape=(
            jax.ShapeDtypeStruct((n_dest, MESSAGE_ROWS, 128), BF16),
            jax.ShapeDtypeStruct((2, TOKENS), I32),
            jax.ShapeDtypeStruct((32, 128), I32),
        ),
        in_specs=[smem] * 5 + [vmem] * 3 + [in_hbm],
        out_specs=(vmem, vmem, vmem),
        scratch_shapes=[
            pltpu.VMEM((1, TOKENS), I32),
            pltpu.VMEM((1, -(-n_units // 128) * 128), I32),
            pltpu.VMEM((HELD, UNIT, D), F32),
            pltpu.SemaphoreType.DMA((HELD,)),
        ],
        compiler_params=params(n_blk, 12),
        name="request",
    )(owners, me, positive, query_lengths, passage_lengths, owner_row, query_ids, passage_ids, *stay(weights))


def collect_kernel(tab, me, message, mine_out):
    for b in range(DENSE):
        order = tab[b, TAB_ORDER]
        rank = tab[b, TAB_RANK]

        @pl.when(order % 2 == me[1])
        def _():
            spot = pl.multiple_of(rank // 4 * PIECE, PIECE)
            sender = 2 * tab[b, TAB_OWNER] + rank // 2 % 2
            mine_out[order // 2] = message[sender, pl.ds(spot, PIECE), :]


def collect(tab, me, message):
    return pl.pallas_call(
        collect_kernel,
        out_shape=jax.ShapeDtypeStruct((CLASS, PIECE, 128), BF16),
        in_specs=[smem, smem, vmem],
        out_specs=vmem,
        compiler_params=params(message.shape[0] // 2, 2),
        name="collect",
    )(tab, me, message)


def fetch_kernel(slots, cap, take_cap, me, message, weights, rows_out, asked_out, wanted, held, table, sem):
    n_dest = message.shape[0]
    copy = pltpu.make_async_copy(weights, held, sem)
    copy.start()
    column_of = iota((1, 128), 1)
    wanted[...] = jnp.zeros(wanted.shape, I32)
    for s in range(n_dest):
        part = message[s, AT_ASKED:].astype(F32)
        want = (part[0:1] * 32.0 + part[1:2] - 1.0).astype(I32)
        if s % 2 == 0:
            even = want
        else:
            wanted[s // 2 : s // 2 + 1] = jnp.where(me[1] == 0, even, want)
        marks = part[2:3]
        row = jnp.where(column_of < cap, part[3:4] * 32.0 + part[4:5] - 1.0, 0.0)
        for i in range(3):
            row = jnp.where(column_of == 124 + i, marks[:, i : i + 1], row)
        asked_out[s : s + 1] = row.astype(I32)
    wide = table.shape[0]
    columns = wanted[...].T
    copy.wait()
    table[...] = held[...].reshape(wide, D).astype(BF16)
    row_of = iota((take_cap, wide), 1)
    for at in range(0, n_dest // 2, 4):
        hot = jnp.concatenate(
            [
                (row_of == columns[:take_cap, s : s + 1]).astype(F32)
                for s in range(at, at + 4)
            ],
            0,
        ).astype(BF16)
        rows_out[at * take_cap : (at + 4) * take_cap] = dot_nn(hot, table[...]).astype(BF16)


def fetch(me, message, weights, cap, take_cap):
    slots = weights.shape[0]
    n_dest = message.shape[0]
    return pl.pallas_call(
        partial(fetch_kernel, slots, cap, take_cap),
        out_shape=(
            jax.ShapeDtypeStruct((n_dest // 2 * take_cap, D), BF16),
            jax.ShapeDtypeStruct((n_dest, 128), I32),
        ),
        in_specs=[smem, vmem, in_hbm],
        out_specs=(vmem, vmem),
        scratch_shapes=[
            pltpu.VMEM((-(-n_dest // 256) * 128, 128), I32),
            pltpu.VMEM(weights.shape, F32),
            pltpu.VMEM((slots * UNIT, D), BF16),
            pltpu.SemaphoreType.DMA,
        ],
        compiler_params=params(n_dest // 2, 20),
        name="fetch",
    )(me, message, *stay(weights))


ST_POOLED, ST_C, ST_N2, ST_N1, ST_H, ST_O, ST_Q, ST_X0 = range(0, 64, 8)
ST_KQ, ST_B, ST_U, ST_A, ST_I1, ST_I2 = 64, 96, 128, 160, 192, 200
ST_ROWS = 208


def forward_kernel(
    tab, me, query_lengths, passage_lengths, positive, rows, where_row, vectors, g0, g1, g2, g3,
    g4, g5, g6, g7, emb_out, low_out, normed_out, scale_out, probs_out, state, matrices, embedded,
    sems,
):
    copies = piece_copies(me, (g0, g1, g2, g3, g4, g5, g6, g7), matrices, sems)
    for copy in copies:
        copy.start()
    taken = rows.shape[0]
    for at in range(0, TOKENS, 256):
        column = jnp.concatenate(
            [to_column(where_row[0:1, i : i + 128]) for i in (at, at + 128)], 0
        )
        hot = (iota((256, taken), 1) == column).astype(F32).astype(BF16)
        embedded[at : at + 256] = dot_nn(hot, rows[...])
    for copy in copies:
        copy.wait()
    shift = vectors[0:1]
    for start, length in zip(STARTS, (QROWS, QROWS, PLEN, PLEN)):
        e = embedded[start : start + length] + rows_at(matrices, tab, 0, length).astype(F32) + shift
        centred = e - jnp.mean(e, -1, keepdims=True)
        scale = lax.rsqrt(jnp.mean(centred * centred, -1, keepdims=True) + NORM_EPS)
        normed = centred * scale
        normed_out[start : start + length] = normed
        scale_out[start : start + length] = jnp.broadcast_to(scale, (length, 128))
        x = normed * vectors[1:2] + vectors[2:3]
        embedded[start : start + length] = x
        low_out[start : start + length] = x.astype(BF16)
    x0 = jnp.concatenate(
        [embedded[s : s + 1] for s in STARTS] + [jnp.zeros((4, D), F32)], 0
    )
    x0_low = x0.astype(BF16)
    q = (dot_nn(x0_low, rows_at(matrices, tab, AT_Q, AT_K)) + vectors[4:5]).astype(BF16)
    head_of = iota((8, D), 1) // HALF
    q_heads = jnp.concatenate(
        [jnp.where(head_of == h, q.astype(F32), 0.0) for h in range(HEADS)], 0
    ).astype(BF16)
    kq = dot_nt(q_heads, rows_at(matrices, tab, AT_K, AT_V)) * (D // HEADS) ** (-0.5)
    low = low_out[...]
    scores = fine(dot_nt, kq, low)
    sequence, live = token_facts(query_lengths, passage_lengths)
    valid = ((iota((32, TOKENS), 0) & 7) == sequence) & live
    scores = jnp.where(valid, scores, NEVER)
    top = jnp.max(scores, -1, keepdims=True)
    weight = jnp.where(valid, jnp.exp(scores - top), 0.0)
    total = jnp.sum(weight, -1, keepdims=True)
    probs = weight / jnp.where(total > 0.0, total, 1.0)
    probs_out[...] = probs
    mixed = dot_nn(probs.astype(BF16), low)
    valued = fine(dot_nn, mixed, rows_at(matrices, tab, AT_V, AT_O))
    blended = jnp.zeros((8, D), F32)
    for h in range(HEADS):
        blended = blended + jnp.where(head_of == h, valued[8 * h : 8 * h + 8], 0.0)
    real = iota((8, D), 0) < 4
    blended = jnp.where(real, blended + vectors[5:6], 0.0).astype(BF16)
    summed = x0 + dot_nn(blended, rows_at(matrices, tab, AT_O, AT_UP)) + vectors[6:7]
    h0, n1, i1 = norm_rows(summed, vectors[8:9], vectors[9:10])
    h_low = h0.astype(BF16)
    bias_up = jnp.concatenate([vectors[12 + i : 13 + i] for i in range(FF // D)], 1)
    u = dot_nt(h_low, rows_at(matrices, tab, AT_UP, AT_DOWN)) + bias_up
    a = (0.5 * u * (1.0 + lax.erf(u * (0.5**0.5)))).astype(BF16)
    second = h0 + dot_nn(a, rows_at(matrices, tab, AT_DOWN, DENSE * UNIT)) + vectors[7:8]
    x, n2, i2 = norm_rows(second, vectors[10:11], vectors[11:12])
    c = x.astype(BF16)
    pooled = jnp.tanh(dot_nn(c, rows_at(matrices, tab, AT_POOL, AT_Q)) + vectors[3:4])
    row8 = iota((8, 128), 0)
    sent = jnp.concatenate(
        [
            jnp.where(real, pooled, 0.0),
            jnp.where(
                row8 == 0,
                positive[0, 0].astype(F32),
                jnp.where(row8 == 1, positive[0, 1].astype(F32), -1.0),
            ),
        ],
        1,
    )
    n_blk = emb_out.shape[0] // 8
    emb_out[...] = jnp.concatenate([sent] * n_blk, 0).astype(BF16)
    state[ST_POOLED : ST_POOLED + 8] = pooled
    state[ST_C : ST_C + 8] = c.astype(F32)
    state[ST_N2 : ST_N2 + 8] = n2
    state[ST_N1 : ST_N1 + 8] = n1
    state[ST_H : ST_H + 8] = h_low.astype(F32)
    state[ST_O : ST_O + 8] = blended.astype(F32)
    state[ST_Q : ST_Q + 8] = q.astype(F32)
    state[ST_X0 : ST_X0 + 8] = x0_low.astype(F32)
    state[ST_KQ : ST_KQ + 32] = kq
    state[ST_B : ST_B + 32] = mixed
    for i in range(FF // D):
        state[ST_U + 8 * i : ST_U + 8 * i + 8] = u[:, i * D : (i + 1) * D]
        state[ST_A + 8 * i : ST_A + 8 * i + 8] = a[:, i * D : (i + 1) * D].astype(F32)
    state[ST_I1 : ST_I1 + 8] = jnp.broadcast_to(i1, (8, D))
    state[ST_I2 : ST_I2 + 8] = jnp.broadcast_to(i2, (8, D))


def forward(tab, me, query_lengths, passage_lengths, positive, rows, where_row, vectors, gathered, n_blk):
    return pl.pallas_call(
        forward_kernel,
        out_shape=(
            jax.ShapeDtypeStruct((n_blk * 8, D + 128), BF16),
            jax.ShapeDtypeStruct((TOKENS, D), BF16),
            jax.ShapeDtypeStruct((TOKENS, D), F32),
            jax.ShapeDtypeStruct((TOKENS, 128), F32),
            jax.ShapeDtypeStruct((32, TOKENS), F32),
            jax.ShapeDtypeStruct((ST_ROWS, D), F32),
            jax.ShapeDtypeStruct((CLASS, 2, UNIT, D), BF16),
        ),
        in_specs=[smem] * 5 + [vmem] * 3 + [hbm] * 8,
        out_specs=(vmem,) * 7,
        scratch_shapes=[
            pltpu.VMEM((TOKENS, D), F32),
            pltpu.SemaphoreType.DMA((2 * PIECES,)),
        ],
        compiler_params=params(n_blk, 12),
        name="forward",
    )(
        tab, me, query_lengths, passage_lengths, positive, rows, where_row, vectors,
        *stay(*gathered[:4]), *gathered[4:],
    )


def news_rows(n_dest):
    return 2 * place_rows(n_dest) + 8


def place_rows(n_dest):
    return max(PLEN // n_dest, 16)


def payload_rows(n_dest, cap):
    at_place = 2 * cap
    at_left = at_place + 2 * place_rows(n_dest)
    at_right = at_left + L_ROWS
    return at_place, at_left, at_right, at_right + 32


def backward_kernel(
    cap, tab, me, prefix_lengths, prefix_weights, emb, message, where_row, low_in, normed, scale,
    probs_in, state, vectors, matrices, payload, loss_out, count_out,
    received, grad_emb, dx, left,
):
    n_blk = emb.shape[0] // 8
    n_dest = 2 * n_blk
    for i in range(3):
        received[i * n_blk * 8 : (i + 1) * n_blk * 8] = emb[:, 128 * i : 128 * i + 128].astype(F32)

    def every(k):
        return jnp.concatenate(
            [received[pl.ds(i * n_blk * 8 + k, n_blk, stride=8), :] for i in range(3)], 1
        )

    queries = jnp.concatenate([every(0), every(1)], 0)
    passages = jnp.concatenate([every(2), every(3)], 0)[:, :D].astype(BF16)
    wanted = queries[:, D : D + 1].astype(I32)
    queries = queries[:, :D]
    size = 2 * n_blk
    counted = wanted >= 0
    counted_f = counted.astype(F32)
    column = iota((size, size), 1)
    target = (column == (wanted & 1) * n_blk + wanted // 2) & counted
    marks = message[...]
    lane = iota(marks.shape, 1)
    count = jnp.sum((((lane == 124) | (lane == 125)) & (marks >= 0)).astype(F32))
    count_out[0, 0] = count
    n_pre = prefix_lengths.shape[0]
    prefix_of = iota((n_pre * size, 1), 0) // size
    prefix = jnp.zeros((n_pre * size, 1), I32)
    share = jnp.zeros((n_pre * size, 1), F32)
    for k in range(n_pre):
        prefix = jnp.where(prefix_of == k, prefix_lengths[k], prefix)
        share = jnp.where(prefix_of == k, prefix_weights[k], share)
    temper = TEMPER * lax.rsqrt(prefix.astype(F32))
    mask = iota((n_pre * size, D), 1) < prefix
    masked = jnp.where(mask, jnp.concatenate([queries] * n_pre, 0), 0.0).astype(BF16)
    logits = dot_nt(masked, passages) * temper
    targets = jnp.concatenate([target.astype(F32)] * n_pre, 0)
    counts = jnp.concatenate([counted_f] * n_pre, 0)
    top = jnp.max(logits, -1, keepdims=True)
    weight = jnp.exp(logits - top)
    total = jnp.sum(weight, -1, keepdims=True)
    hit = jnp.sum(logits * targets, -1, keepdims=True)
    losses = share * (top + jnp.log(total) - hit) * counts
    grad = (weight / total - targets) * (counts * (share / count) * temper)
    high, lower = split(grad)
    spread_queries = jnp.where(mask, dot_nn(high, passages) + dot_nn(lower, passages), 0.0)
    d_queries = spread_queries[:size]
    for k in range(1, n_pre):
        d_queries = d_queries + spread_queries[k * size : (k + 1) * size]
    d_passages = dot_tn(high, masked) + dot_tn(lower, masked)
    loss_out[0, 0] = jnp.sum(losses)
    grad_emb[:size] = d_queries
    grad_emb[size : 2 * size] = d_passages
    grad_pooled = jnp.concatenate(
        [grad_emb[pl.ds(me[0] + i * n_blk, 1), :] for i in range(4)]
        + [jnp.zeros((4, D), F32)],
        0,
    )

    def kept_rows(at, rows=8):
        return state[at : at + rows]

    pooled = kept_rows(ST_POOLED)
    d_pre = grad_pooled * (1.0 - pooled * pooled)
    d_c = fine(dot_nt, d_pre, rows_at(matrices, tab, AT_POOL, AT_Q))
    n2 = kept_rows(ST_N2)
    d_second, d_g2, d_s2 = norm_back(d_c, n2, kept_rows(ST_I2), vectors[10:11])
    down_low = d_second.astype(BF16)
    d_a = dot_nt(down_low, rows_at(matrices, tab, AT_DOWN, DENSE * UNIT))
    u = jnp.concatenate([kept_rows(ST_U + 8 * i) for i in range(FF // D)], 1)
    slope = 0.5 * (1.0 + lax.erf(u * (0.5**0.5))) + u * jnp.exp(-0.5 * u * u) * (
        0.3989422804014327
    )
    up_low = (d_a * slope).astype(BF16)
    d_h = d_second + dot_nn(up_low, rows_at(matrices, tab, AT_UP, AT_DOWN))
    d_summed, d_g1, d_s1 = norm_back(d_h, kept_rows(ST_N1), kept_rows(ST_I1), vectors[8:9])
    branch_low = d_summed.astype(BF16)
    d_o = dot_nt(branch_low, rows_at(matrices, tab, AT_O, AT_UP)).astype(BF16)
    head_of = iota((8, D), 1) // HALF
    o_heads = jnp.concatenate(
        [jnp.where(head_of == h, d_o.astype(F32), 0.0) for h in range(HEADS)], 0
    ).astype(BF16)
    vo = dot_nt(o_heads, rows_at(matrices, tab, AT_V, AT_O))
    low = low_in[...]
    probs = probs_in[...]
    d_probs = fine(dot_nt, vo, low)
    d_scores = probs * (d_probs - jnp.sum(d_probs * probs, -1, keepdims=True))
    score_low = d_scores.astype(BF16)
    mixed_score = dot_nn(score_low, low)
    keyed = fine(dot_nn, mixed_score, rows_at(matrices, tab, AT_K, AT_V))
    d_q = jnp.zeros((8, D), F32)
    for h in range(HEADS):
        d_q = d_q + jnp.where(head_of == h, keyed[8 * h : 8 * h + 8], 0.0)
    d_q_low = (d_q * (D // HEADS) ** (-0.5)).astype(BF16)
    d_x0 = d_summed + dot_nt(d_q_low, rows_at(matrices, tab, AT_Q, AT_K))
    kq = kept_rows(ST_KQ, 32)
    vo_high, vo_low = split(vo)
    kq_high, kq_low = split(kq)
    probs_low = probs.astype(BF16)
    dx[...] = dot_tn(
        jnp.concatenate([probs_low, score_low, probs_low, score_low], 0),
        jnp.concatenate([vo_high, kq_high, vo_low, kq_low], 0),
    )
    for i, start in enumerate(STARTS):
        dx[start : start + 1] = dx[start : start + 1] + d_x0[i : i + 1]
    d_gain = jnp.zeros((1, D), F32)
    d_shift = jnp.zeros((1, D), F32)
    d_type = jnp.zeros((1, D), F32)
    for start in range(0, TOKENS, 256):
        incoming = dx[start : start + 256]
        n = normed[start : start + 256]
        d_gain = d_gain + jnp.sum(incoming * n, 0, keepdims=True)
        d_shift = d_shift + jnp.sum(incoming, 0, keepdims=True)
        dn = incoming * vectors[1:2]
        inner = (
            dn - jnp.mean(dn, -1, keepdims=True) - n * jnp.mean(dn * n, -1, keepdims=True)
        )
        de = inner * scale[start : start + 256, :1]
        d_type = d_type + jnp.sum(de, 0, keepdims=True)
        dx[start : start + 256] = de
    de_low = dx[...].astype(BF16)
    at_place, at_left, at_right, n_rows = payload_rows(n_dest, cap)
    per = 8
    step = per * cap
    for at in range(0, n_dest * cap, step):
        hot = ((iota((step, TOKENS), 0) + at) == where_row[1:2]).astype(F32).astype(BF16)
        summed = dot_nn(hot, de_low).astype(BF16)
        for i in range(per):
            d = at // cap + i
            if d < n_dest:
                payload[d, :cap] = summed[i * cap : (i + 1) * cap, :128]
                payload[d, cap : 2 * cap] = summed[i * cap : (i + 1) * cap, 128:]
    spots = dx[STARTS[2] : STARTS[3]] + dx[STARTS[3] :]
    dx[STARTS[2] : STARTS[3]] = spots
    dx[STARTS[2] : STARTS[2] + QROWS] = (
        dx[STARTS[2] : STARTS[2] + QROWS] + dx[:QROWS] + dx[QROWS : 2 * QROWS]
    )
    pr = place_rows(n_dest)
    share = PLEN // n_dest
    for d in range(n_dest):
        spot = dx[STARTS[2] + d * share : STARTS[2] + (d + 1) * share]
        if share < pr:
            spot = jnp.concatenate([spot, jnp.zeros((pr - share, D), F32)], 0)
        payload[d, at_place : at_place + pr] = spot[:, :128].astype(BF16)
        payload[d, at_place + pr : at_place + 2 * pr] = spot[:, 128:].astype(BF16)
    left[...] = jnp.zeros(left.shape, F32)
    up_f = up_low.astype(F32)

    def put(b, r, unit, values):
        spot = (tab[b, TAB_OWNER] * 2 + r) * L_ROWS + (tab[b, TAB_UNIT] + unit) * 4
        for i in range(4):
            left[pl.ds(spot + i, 1), :] = values[i : i + 1]

    for b in range(PLACE_BLOCKS, DENSE):
        at = b * UNIT
        if AT_K <= at < AT_O:
            heads = mixed_score if at < AT_V else kept_rows(ST_B, 32)
            off = (at - AT_K) % D
            for r in range(2):
                for j in range(2):
                    h = 2 * r + j
                    put(b, r, j, heads[8 * h : 8 * h + 4, off : off + UNIT])
            continue
        if at < AT_Q:
            values, off = kept_rows(ST_C), at - AT_POOL
        elif at < AT_K:
            values, off = kept_rows(ST_X0), at - AT_Q
        elif at < AT_UP:
            values, off = kept_rows(ST_O), at - AT_O
        elif at < AT_DOWN:
            values, off = up_f, at - AT_UP
        else:
            off = (at - AT_DOWN) % D
            values = kept_rows(ST_A + 8 * ((at - AT_DOWN) // D))
        for r in range(2):
            put(b, r, 0, values[:4, off : off + UNIT])
    d_vectors = jnp.concatenate(
        [
            d_type,
            d_gain,
            d_shift,
            jnp.sum(d_pre, 0, keepdims=True),
            jnp.sum(d_q_low.astype(F32), 0, keepdims=True),
            jnp.sum(d_o.astype(F32), 0, keepdims=True),
            jnp.sum(branch_low.astype(F32), 0, keepdims=True),
            jnp.sum(down_low.astype(F32), 0, keepdims=True),
            d_g1[None],
            d_s1[None],
            d_g2[None],
            d_s2[None],
        ]
        + [
            jnp.sum(up_f[:, i * D : (i + 1) * D], 0, keepdims=True) for i in range(FF // D)
        ],
        0,
    )
    scaled_q = kept_rows(ST_Q) * (D // HEADS) ** (-0.5)
    right = jnp.concatenate(
        [
            v.astype(F32)[:4]
            for v in (d_pre, d_q_low, scaled_q, d_o, branch_low, kept_rows(ST_H), down_low)
        ],
        0,
    )
    for d in range(n_dest):
        payload[d, at_left:at_right] = left[d * L_ROWS : (d + 1) * L_ROWS].astype(BF16)
        r = d % 2
        if d < 32:
            share_vec = d_vectors[d // 2 : d // 2 + 1, r * 128 : (r + 1) * 128]
        else:
            share_vec = jnp.zeros((1, 128), F32)
        payload[d, at_right:n_rows] = jnp.concatenate(
            [right[:, r * 128 : (r + 1) * 128], share_vec, jnp.zeros((3, 128), F32)], 0
        ).astype(BF16)


def backward(tab, me, prefix_lengths, prefix_weights, emb, message, where_row, low, normed, scale, probs, state, vectors, matrices, cap):
    n_dest = message.shape[0]
    n_rows = payload_rows(n_dest, cap)[-1]
    return pl.pallas_call(
        partial(backward_kernel, cap),
        out_shape=(
            jax.ShapeDtypeStruct((n_dest, n_rows, 128), BF16),
            jax.ShapeDtypeStruct((1, 1), F32),
            jax.ShapeDtypeStruct((1, 1), F32),
        ),
        in_specs=[smem] * 4 + [vmem] * 10,
        out_specs=(vmem, smem, smem),
        scratch_shapes=[
            pltpu.VMEM((emb.shape[0] * 3, 128), F32),
            pltpu.VMEM((emb.shape[0], D), F32),
            pltpu.VMEM((TOKENS, D), F32),
            pltpu.VMEM((n_dest * L_ROWS, 128), F32),
        ],
        compiler_params=params(n_dest // 2, 16),
        name="backward",
    )(tab, me, prefix_lengths, prefix_weights, emb, message, where_row, low, normed, scale, probs, state, vectors, matrices)


def reduce_kernel(slots, cap, tab, me, loss, asked, payload, reduced, news, total, row_grads, left, right):
    n_dest = payload.shape[0]
    at_place, at_left, at_right, n_rows = payload_rows(n_dest, cap)
    for d in range(n_dest):
        row_grads[d * cap : (d + 1) * cap, :128] = payload[d, :cap]
        row_grads[d * cap : (d + 1) * cap, 128:] = payload[d, cap : 2 * cap]
        left[d * L_ROWS : (d + 1) * L_ROWS] = payload[d, at_left:at_right].astype(F32)
        right[d * 32 : (d + 1) * 32] = payload[d, at_right:n_rows].astype(F32)
    grads = row_grads[...]
    filled = slots * HALF
    chunk = filled // 4
    for at in range(0, filled, chunk):
        hot = ((iota((chunk, n_dest * cap), 0) + at) == asked[...]).astype(F32).astype(BF16)
        total[at : at + chunk] = dot_nn(hot, grads)
    mine = me[0]
    odd = me[1]
    column = iota((n_dest * 4, 128), 1)

    def rows_of(ref, start, stride):
        return jnp.concatenate(
            [ref[pl.ds(start + q, n_dest, stride=stride), :] for q in range(4)], 0
        ).astype(BF16)

    for b in range(PLACE_BLOCKS, DENSE):
        at = b * UNIT
        if at < AT_Q:
            m = 0
        elif at < AT_UP:
            m = 1 + (at - AT_Q) // D
        elif at < AT_DOWN:
            m = 5
        else:
            m = 6

        @pl.when(tab[b, TAB_OWNER] == mine)
        def _():
            unit = tab[b, TAB_UNIT] * 4
            pull = rows_of(right, m * 4, 32)
            if AT_K <= at < AT_O:
                grad = dot_tn(
                    rows_of(left, unit, L_ROWS), jnp.where(column < HALF, pull, 0).astype(BF16)
                ) + dot_tn(
                    rows_of(left, unit + 4, L_ROWS),
                    jnp.where(column < HALF, 0, pull).astype(BF16),
                )
            else:
                grad = dot_tn(rows_of(left, unit, L_ROWS), pull)
            spot = pl.multiple_of(tab[b, TAB_SLOT] * HALF, HALF)
            total[pl.ds(spot, HALF), :128] = grad[:HALF]
            total[pl.ds(spot, HALF), 128:] = grad[HALF:]

    pr = place_rows(n_dest)
    spots_low = jnp.zeros((pr, 128), F32)
    spots_high = jnp.zeros((pr, 128), F32)
    for d in range(n_dest):
        spots_low = spots_low + payload[d, at_place : at_place + pr].astype(F32)
        spots_high = spots_high + payload[d, at_place + pr : at_place + 2 * pr].astype(F32)
    spots = jnp.concatenate([spots_low, spots_high], 1)
    vector = jnp.sum(right[pl.ds(28, n_dest, stride=32), :], 0, keepdims=True)
    summed = total[...]
    reduced[...] = summed.astype(BF16).reshape(reduced.shape)
    square = jnp.sum(summed * summed) + jnp.sum(spots * spots) + jnp.sum(vector * vector)
    row8 = iota((8, 128), 0)

    def parts(v):
        first = v.astype(BF16).astype(F32)
        second = (v - first).astype(BF16).astype(F32)
        return first, second, v - first - second

    extra = jnp.where(row8 == 0, vector, 0.0)
    for i, part in enumerate(
        parts(jnp.full((1, 128), square, F32)) + parts(jnp.full((1, 128), loss[0, 0], F32))
    ):
        extra = jnp.where(row8 == 1 + i, part, extra)
    block = jnp.concatenate([spots[:, :128], spots[:, 128:], extra], 0).astype(BF16)
    for d in range(n_dest):
        news[d] = block


def reduce(tab, me, loss, asked, payload, slots, cap):
    n_dest = payload.shape[0]
    pr = place_rows(n_dest)
    return pl.pallas_call(
        partial(reduce_kernel, slots, cap),
        out_shape=(
            jax.ShapeDtypeStruct((slots, HALF, D), BF16),
            jax.ShapeDtypeStruct((n_dest, news_rows(n_dest), 128), BF16),
        ),
        in_specs=[smem, smem, smem, vmem, vmem],
        out_specs=(vmem, vmem),
        scratch_shapes=[
            pltpu.VMEM((slots * HALF, D), F32),
            pltpu.VMEM((n_dest * cap, D), BF16),
            pltpu.VMEM((n_dest * L_ROWS, 128), F32),
            pltpu.VMEM((n_dest * 32, 128), F32),
        ],
        compiler_params=params(n_dest // 2, 16),
        name="reduce",
    )(tab, me, loss, asked, payload)


def update_slots(tab, half, rest, grads, places, scale, arrays, outs, held, in_sems, out_sems):
    first_scale = -RATE / (1.0 - BETA_ONE**STEP)
    second_scale = 1.0 / (1.0 - BETA_TWO**STEP)
    rows = (pl.ds(pl.multiple_of(half * HALF, HALF), HALF), slice(None))
    columns = (slice(None), pl.ds(pl.multiple_of(half * 128, 128), 128))
    whole = (slice(None), slice(None))
    ends = [tab[k, TAB_ENDS] for k in range(4)]
    spans = [(KIND_TABLE, 0, ends[0], rows), (KIND_DENSE, ends[0], ends[1], columns)]
    if rest:
        spans += [(KIND_PLACE, ends[1], ends[2], whole), (0, ends[2], ends[3], whole)]

    def loop(action):
        for case, start, stop, region in spans:

            def body(j, c):
                action(tab[j, TAB_SORTED], case, region)
                return c

            lax.fori_loop(start, stop, body, 0)

    def in_copies(i, region):
        return [
            pltpu.make_async_copy(a.at[(i,) + region], held.at[(k, i) + region], in_sems.at[k, i])
            for k, a in enumerate(arrays)
        ]

    def out_copies(i, region):
        return [
            pltpu.make_async_copy(held.at[(k, i) + region], out.at[(i,) + region], out_sems.at[k, i])
            for k, out in enumerate(outs)
        ]

    def start(i, case, region):
        for copy in in_copies(i, region):
            copy.start()

    def step(i, region, g):
        g = g * scale[: g.shape[0], : g.shape[1]]
        m1 = BETA_ONE * held[(1, i) + region] + (1.0 - BETA_ONE) * g
        m2 = BETA_TWO * held[(2, i) + region] + (1.0 - BETA_TWO) * (g * g)
        root = jnp.sqrt(m2 * second_scale) + EPSILON
        held[(0, i) + region] = (
            held[(0, i) + region] * (1.0 - RATE * DECAY) + (m1 * first_scale) / root
        )
        held[(1, i) + region] = m1
        held[(2, i) + region] = m2

    def act(i, case, region):
        for copy in in_copies(i, region):
            copy.wait()
        if case == KIND_TABLE:
            step(i, region, grads[i].astype(F32))
        elif case == KIND_DENSE:
            g = grads[i].astype(F32)
            step(i, region, jnp.concatenate([g[:, :128], g[:, 128:]], 0))
        elif case == KIND_PLACE:
            spot = pl.multiple_of((tab[i, TAB_KIND] - KIND_PLACE) * UNIT, UNIT)
            step(i, region, places[pl.ds(spot, UNIT), :])

        for copy in out_copies(i, region):
            copy.start()

    def finish(i, case, region):
        for copy in out_copies(i, region):
            copy.wait()

    loop(start)
    yield
    loop(act)
    loop(finish)
    yield


def update_kernel(
    tab, me, news, own, weight, first, second, vectors, vector_first, vector_second,
    weight_out, first_out, second_out, vectors_out, vector_first_out, vector_second_out, loss_out,
    norm_out, factor_out, places, held, in_sems, out_sems,
):
    n_dest = news.shape[0]
    pr = place_rows(n_dest)
    share = PLEN // n_dest
    scale = factor_out
    steps = update_slots(
        tab, me[1], True, own, places, scale, (weight, first, second),
        (weight_out, first_out, second_out), held, in_sems, out_sems,
    )
    next(steps)
    extras = []
    for d in range(n_dest):
        part = news[d].astype(F32)
        places[d * share : (d + 1) * share, :128] = part[:share]
        places[d * share : (d + 1) * share, 128:] = part[pr : pr + share]
        extras.append(part[2 * pr :])
    sums = extras[0]
    for extra in extras[1:]:
        sums = sums + extra
    square = sums[1:2] + sums[2:3] + sums[3:4]
    norm = jnp.sqrt(square)
    factor = CLIP_AT / jnp.maximum(norm, CLIP_AT)
    norm_out[0, 0] = norm[0, 0]
    losses = extras[0] + extras[1]
    loss = losses[4:5] + losses[5:6] + losses[6:7]
    loss_out[0, 0] = loss[0, 0]
    vector_grad = jnp.concatenate(
        [
            jnp.concatenate([extras[2 * i][0:1], extras[2 * i + 1][0:1]], 1)
            for i in range(vectors.shape[0])
        ],
        0,
    ) * jnp.concatenate([factor, factor], 1)
    v, m1, m2 = adam_step(
        vectors[...], vector_first[...], vector_second[...], vector_grad, VECTOR_RATE, 0.0
    )
    vectors_out[...] = v
    vector_first_out[...] = m1
    vector_second_out[...] = m2
    factor_out[...] = jnp.broadcast_to(jnp.concatenate([factor, factor], 1), (UNIT, D))
    next(steps)


def finish_kernel(
    tab, me, factor, other, weight, first, second, weight_in, first_in, second_in, weight_out,
    first_out, second_out, held, in_sems, out_sems,
):
    steps = update_slots(
        tab, 1 - me[1], False, other, None, factor, (weight, first, second),
        (weight_out, first_out, second_out), held, in_sems, out_sems,
    )
    next(steps)
    next(steps)


def update_scratch(shape):
    return [
        pltpu.VMEM((3,) + shape, F32),
        pltpu.SemaphoreType.DMA((3, shape[0])),
        pltpu.SemaphoreType.DMA((3, shape[0])),
    ]


def update(tab, me, news, own, weights, first, second, vectors, vector_first, vector_second):
    n_dest = news.shape[0]
    big = pltpu.HBM(weights.shape, F32)
    small = jax.ShapeDtypeStruct(vectors.shape, F32)
    one = jax.ShapeDtypeStruct((1, 1), F32)
    return pl.pallas_call(
        update_kernel,
        out_shape=(big, big, big, small, small, small, one, one, jax.ShapeDtypeStruct((UNIT, D), F32)),
        in_specs=[smem, smem] + [vmem] * 2 + [in_hbm] * 3 + [vmem] * 3,
        out_specs=(in_hbm, in_hbm, in_hbm, vmem, vmem, vmem, smem, smem, vmem),
        scratch_shapes=[pltpu.VMEM((PLEN, D), F32)] + update_scratch(weights.shape),
        compiler_params=params(n_dest // 2, 14),
        name="update",
    )(tab, me, news, own, *stay(weights, first, second), vectors, vector_first, vector_second)


def finish(tab, me, factor, other, weights, first, second, started, n_blk):
    big = pltpu.HBM(weights.shape, F32)
    return pl.pallas_call(
        finish_kernel,
        out_shape=(big, big, big),
        in_specs=[smem, smem, vmem, vmem] + [in_hbm] * 6,
        out_specs=(in_hbm, in_hbm, in_hbm),
        scratch_shapes=update_scratch(weights.shape),
        input_output_aliases={7: 0, 8: 1, 9: 2},
        compiler_params=params(n_blk, 14),
        name="finish",
    )(tab, me, factor, other, *stay(weights, first, second, *started))


def quick(
    query_ids, passage_ids, query_lengths, passage_lengths, positive, prefix_lengths,
    prefix_weights, owners, weights, first_moments, second_moments, vectors, vector_first,
    vector_second,
):
    slots = weights.shape[0]
    n_blk = lax.axis_size("blk")
    everyone = ("blk", "rep")
    cap = 48 if n_blk <= 16 else 16
    take_cap = 80 if n_blk <= 16 else 32
    me = jnp.stack([lax.axis_index("blk"), lax.axis_index("rep")]).astype(I32)

    def exchange(a, axes):
        return lax.all_to_all(a, axes, 0, 0, tiled=True)

    message, where_row, tab = request(
        owners, me, positive, query_lengths, passage_lengths, query_ids[0], passage_ids[0],
        weights, n_blk, cap, take_cap,
    )
    message = exchange(message, everyone)
    first = along_z(collect(tab, me, message), n_blk)
    rows, message = fetch(me, message, weights, cap, take_cap)
    rows, first = lax.optimization_barrier((rows, first))
    rows = exchange(rows, "blk")
    gathered = spread(first, n_blk)
    emb, low, normed, scale, probs, state, matrices = forward(
        tab, me, query_lengths, passage_lengths, positive, rows, where_row, vectors, gathered, n_blk
    )
    emb = exchange(emb, "blk")
    payload, loss, count = backward(
        tab, me, prefix_lengths, prefix_weights, emb, message, where_row, low, normed, scale,
        probs, state, vectors, matrices, cap,
    )
    payload = exchange(payload, everyone)
    asked = message[:, :cap].reshape(1, -1)
    own, news = reduce(tab, me, loss, asked, payload, slots, cap)
    other = lax.ppermute(own, "rep", [(0, 1), (1, 0)])
    news = exchange(news, everyone)
    *outs, loss_sum, norm, factor = update(
        tab, me, news, own, weights, first_moments, second_moments, vectors, vector_first,
        vector_second,
    )
    outs[:3] = finish(
        tab, me, factor, other, weights, first_moments, second_moments, outs[:3], n_blk
    )

    def general(carry):
        return 0, local(
            query_ids, passage_ids, query_lengths, passage_lengths, positive, prefix_lengths,
            prefix_weights, owners, weights, first_moments, second_moments, vectors, vector_first,
            vector_second,
        )

    outs = (*outs, loss_sum.reshape(()), count.reshape(()), norm.reshape(()))
    return lax.while_loop(lambda c: c[0] > 0, general, (jnp.max(message[:, 126]), outs))[1]


def solution(mesh):
    in_specs = (
        P("rep", "blk", None),
        P("rep", "blk", None),
        P("rep", "blk"),
        P("rep", "blk"),
        P("rep", "blk"),
        P(),
        P(),
        P(),
        P("blk", None, None),
        P("blk", None, None),
        P("blk", None, None),
        P(),
        P(),
        P(),
    )
    out_specs = (
        P("blk", None, None),
        P("blk", None, None),
        P("blk", None, None),
        P(),
        P(),
        P(),
        P(),
        P(),
        P(),
    )
    return jax.shard_map(quick, mesh=mesh, in_specs=in_specs, out_specs=out_specs, check_vma=False)
```

```python
from functools import partial

import jax
import jax.numpy as jnp
from jax import lax
from jax.experimental import pallas as pl
from jax.experimental.pallas import tpu as pltpu
from jax.sharding import PartitionSpec as P

D = 256
HEADS = 4
FF = 1024
VOCAB = 30592
LAYERS = 1
PLEN = 512
STEP = 7


TEMPER = 8.0
CLIP_AT = 0.01
RATE = 0.06
VECTOR_RATE = 0.8
BETA_ONE = 0.9
BETA_TWO = 0.999
DECAY = 0.01
EPSILON = 1e-08
NORM_EPS = 1e-06
HUGE = 1000000000.0
HIGHEST = lax.Precision.HIGHEST


def mult(left_op, right_op):
    return jnp.dot(left_op, right_op, preferred_element_type=jnp.float32)


def mult_tn(left_op, right_op):
    return lax.dot_general(
        left_op, right_op, (((0,), (0,)), ((), ())), preferred_element_type=jnp.float32
    )


def mult_nt(left_op, right_op):
    return lax.dot_general(
        left_op, right_op, (((1,), (1,)), ((), ())), preferred_element_type=jnp.float32
    )


def norm_rows(values_in, gain_row, shift_row):
    centred = values_in - jnp.mean(values_in, -1, keepdims=True)
    inv_scale = lax.rsqrt(jnp.mean(centred * centred, -1, keepdims=True) + NORM_EPS)
    normed = centred * inv_scale
    return (normed * gain_row + shift_row, normed, inv_scale)


def norm_back(incoming, normed, inv_scale, gain_row):
    dnormed = incoming * gain_row
    inner_part = (
        dnormed
        - jnp.mean(dnormed, -1, keepdims=True)
        - normed * jnp.mean(dnormed * normed, -1, keepdims=True)
    )
    return (inner_part * inv_scale, jnp.sum(incoming * normed, 0), jnp.sum(incoming, 0))


def layer_parts(flat_rows, vectors, layer_index):
    offset = VOCAB + PLEN + D + layer_index * (4 * D + 2 * FF)
    w_qkv = jnp.concatenate(
        [
            flat_rows[offset : offset + D],
            flat_rows[offset + D : offset + 2 * D],
            flat_rows[offset + 2 * D : offset + 3 * D],
        ],
        1,
    )
    w_out = flat_rows[offset + 3 * D : offset + 4 * D]
    w_up = flat_rows[offset + 4 * D : offset + 4 * D + FF]
    w_down = flat_rows[offset + 4 * D + FF : offset + 4 * D + 2 * FF]
    row_base = 4 + layer_index * (8 + FF // D)
    return ((w_qkv, w_out, w_up, w_down), vectors[row_base : row_base + 8 + FF // D])


def divide_into_heads(packed_buffer, column):
    return packed_buffer[:, column * D : (column + 1) * D].reshape(
        packed_buffer.shape[0], HEADS, D // HEADS
    )


def attend_probs(packed_buffer, key_keep):
    scores = jnp.einsum(
        "cnp,fnp->ncf",
        divide_into_heads(packed_buffer, 0),
        divide_into_heads(packed_buffer, 1),
        preferred_element_type=jnp.float32,
    ) * (D // HEADS) ** (-0.5)
    scores = jnp.where(key_keep[None, None, :], scores, -HUGE)
    return jax.nn.softmax(scores, -1)


def attend(pieces):
    packed_buffer, key_keep = pieces
    attn_probs = attend_probs(packed_buffer, key_keep)
    blended = jnp.einsum(
        "nbi,ins->bns",
        attn_probs.astype(jnp.bfloat16),
        divide_into_heads(packed_buffer, 2),
        preferred_element_type=jnp.float32,
    )
    return blended.reshape(packed_buffer.shape[0], D)


def attend_back(pieces):
    packed_buffer, key_keep, grad_out = pieces
    seq_len = packed_buffer.shape[0]
    head_scale = (D // HEADS) ** (-0.5)
    attn_probs = attend_probs(packed_buffer, key_keep)
    gradient_row_block = grad_out.reshape(seq_len, HEADS, D // HEADS)
    grad_values = jnp.einsum(
        "fxn,xfa->nfa",
        attn_probs.astype(jnp.bfloat16),
        gradient_row_block,
        preferred_element_type=jnp.float32,
    )
    grad_probs = jnp.einsum(
        "cnp,fnp->ncf",
        gradient_row_block,
        divide_into_heads(packed_buffer, 2),
        preferred_element_type=jnp.float32,
    )
    grad_scores = attn_probs * (grad_probs - jnp.sum(grad_probs * attn_probs, -1, keepdims=True))
    score_lowered = grad_scores.astype(jnp.bfloat16)
    grad_queries = (
        jnp.einsum(
            "nbi,ins->bns",
            score_lowered,
            divide_into_heads(packed_buffer, 1),
            preferred_element_type=jnp.float32,
        )
        * head_scale
    )
    grad_keys = (
        jnp.einsum(
            "fxn,xfa->nfa",
            score_lowered,
            divide_into_heads(packed_buffer, 0),
            preferred_element_type=jnp.float32,
        )
        * head_scale
    )
    return jnp.concatenate(
        [
            grad_queries.reshape(seq_len, D),
            grad_keys.reshape(seq_len, D),
            grad_values.reshape(seq_len, D),
        ],
        1,
    ).astype(jnp.bfloat16)


def layer_forward(hidden_in, weights_set, vec_rows, key_keep):
    w_qkv, w_out, w_up, w_down = weights_set
    groups, seq_len = key_keep.shape
    in_low = hidden_in.astype(jnp.bfloat16)
    bias_qkv = jnp.concatenate([vec_rows[0], jnp.zeros_like(vec_rows[0]), vec_rows[1]])
    packed_buffer = (mult(in_low, w_qkv) + bias_qkv).astype(jnp.bfloat16)
    blended = lax.map(attend, (packed_buffer.reshape(groups, seq_len, 3 * D), key_keep))
    blend_low = blended.reshape(groups * seq_len, D).astype(jnp.bfloat16)
    summed = hidden_in + mult(blend_low, w_out) + vec_rows[2]
    normal_one, normed_one, scale_one = norm_rows(summed, vec_rows[4], vec_rows[5])
    normal_low = normal_one.astype(jnp.bfloat16)
    up_in = mult_nt(normal_low, w_up) + vec_rows[8:].reshape(FF)
    acted = jax.nn.gelu(up_in, approximate=False).astype(jnp.bfloat16)
    second = normal_one + mult(acted, w_down) + vec_rows[3]
    result, normed_two, scale_two = norm_rows(second, vec_rows[6], vec_rows[7])
    return (
        result,
        (
            in_low,
            packed_buffer,
            blend_low,
            normed_one,
            scale_one,
            normal_low,
            up_in,
            acted,
            normed_two,
            scale_two,
        ),
    )


def layer_backward(grad_out, weights_set, vec_rows, key_keep, saved):
    w_qkv, w_out, w_up, w_down = weights_set
    (
        in_low,
        packed_buffer,
        blend_low,
        normed_one,
        scale_one,
        normal_low,
        up_in,
        acted,
        normed_two,
        scale_two,
    ) = saved
    groups, seq_len = key_keep.shape
    grad_second, grad_gain_two, grad_shift_two = norm_back(
        grad_out, normed_two, scale_two, vec_rows[6]
    )
    down_low = grad_second.astype(jnp.bfloat16)
    grad_down = mult_tn(acted, down_low)
    grad_acted = mult_nt(down_low, w_down)
    gelu_pull = jax.vjp(partial(jax.nn.gelu, approximate=False), up_in)[1]
    up_low = gelu_pull(grad_acted)[0].astype(jnp.bfloat16)
    grad_up = mult_tn(up_low, normal_low)
    grad_normal = grad_second + mult(up_low, w_up)
    grad_summed, gradient_first_gain, grad_shift_one = norm_back(
        grad_normal, normed_one, scale_one, vec_rows[4]
    )
    branch_low = grad_summed.astype(jnp.bfloat16)
    grad_wout = mult_tn(blend_low, branch_low)
    blend_grad = mult_nt(branch_low, w_out).astype(jnp.bfloat16)
    grad_packed = lax.map(
        attend_back,
        (
            packed_buffer.reshape(groups, seq_len, 3 * D),
            key_keep,
            blend_grad.reshape(groups, seq_len, D),
        ),
    ).reshape(groups * seq_len, 3 * D)
    grad_wqkv = mult_tn(in_low, grad_packed)
    grad_in = grad_summed + mult_nt(grad_packed, w_qkv)
    packed_sum = jnp.sum(grad_packed.astype(jnp.float32), 0)
    matrix_grads = jnp.concatenate(
        [
            grad_wqkv[:, :D],
            grad_wqkv[:, D : 2 * D],
            grad_wqkv[:, 2 * D :],
            grad_wout,
            grad_up,
            grad_down,
        ],
        0,
    )
    vector_grads = jnp.concatenate(
        [
            jnp.stack(
                [
                    packed_sum[:D],
                    packed_sum[2 * D :],
                    jnp.sum(branch_low.astype(jnp.float32), 0),
                    jnp.sum(down_low.astype(jnp.float32), 0),
                    gradient_first_gain,
                    grad_shift_one,
                    grad_gain_two,
                    grad_shift_two,
                ]
            ),
            jnp.sum(up_low.astype(jnp.float32), 0).reshape(FF // D, D),
        ],
        0,
    )
    return (grad_in, matrix_grads, vector_grads)


def embed_sequences(flat_rows, vectors, token_ids, lengths):
    groups, seq_len = token_ids.shape
    key_keep = jnp.arange(seq_len)[None, :] < lengths[:, None]
    table_rows = jnp.take(flat_rows, token_ids.reshape(-1), axis=0).astype(jnp.float32)
    places = flat_rows[VOCAB : VOCAB + seq_len].astype(jnp.float32)
    embedded = (table_rows.reshape(groups, seq_len, D) + places[None] + vectors[0]).reshape(
        groups * seq_len, D
    )
    hidden_now, normed_emb, scaled_embedding = norm_rows(embedded, vectors[1], vectors[2])
    weights_set, vec_rows = layer_parts(flat_rows, vectors, 0)
    hidden_now, saved = layer_forward(hidden_now, weights_set, vec_rows, key_keep)
    layer_saves = [saved]
    first_rows = hidden_now.reshape(groups, seq_len, D)[:, 0].astype(jnp.bfloat16)
    pooled = jnp.tanh(mult(first_rows, flat_rows[VOCAB + PLEN : VOCAB + PLEN + D]) + vectors[3])
    return (pooled, (normed_emb, scaled_embedding, layer_saves, first_rows))


def encode_back(grad_pooled, pooled, flat_rows, vectors, token_ids, lengths, encoder_kept):
    normed_emb, scaled_embedding, layer_saves, first_rows = encoder_kept
    groups, seq_len = token_ids.shape
    key_keep = jnp.arange(seq_len)[None, :] < lengths[:, None]
    w_pool = flat_rows[VOCAB + PLEN : VOCAB + PLEN + D].astype(jnp.float32)
    grad_pre = grad_pooled * (1.0 - pooled * pooled)
    grad_pool = jnp.dot(first_rows.astype(jnp.float32).T, grad_pre, precision=HIGHEST)
    grad_first = jnp.dot(grad_pre, w_pool.T, precision=HIGHEST)
    grad_hidden = (
        jnp.zeros((groups, seq_len, D), jnp.float32)
        .at[:, 0]
        .set(grad_first)
        .reshape(groups * seq_len, D)
    )
    matrices = []
    vector_parts = []
    for layer_index in reversed(range(LAYERS)):
        weights_set, vec_rows = layer_parts(flat_rows, vectors, layer_index)
        grad_hidden, matrix_grads, vector_grads = layer_backward(
            grad_hidden, weights_set, vec_rows, key_keep, layer_saves[layer_index]
        )
        matrices.insert(0, matrix_grads)
        vector_parts.insert(0, vector_grads)
    grad_embed, grad_gain, grad_shift = norm_back(
        grad_hidden, normed_emb, scaled_embedding, vectors[1]
    )
    grad_table = jnp.zeros((VOCAB, D), jnp.float32).at[token_ids.reshape(-1)].add(grad_embed)
    grad_places = (
        jnp.zeros((PLEN, D), jnp.float32)
        .at[:seq_len]
        .set(jnp.sum(grad_embed.reshape(groups, seq_len, D), 0))
    )
    flat_grad = jnp.concatenate([grad_table, grad_places, grad_pool] + matrices, 0)
    head_rows = jnp.stack([jnp.sum(grad_embed, 0), grad_gain, grad_shift, jnp.sum(grad_pre, 0)])
    return (flat_grad, jnp.concatenate([head_rows] + vector_parts, 0))


def adam_step(weight, moment_one, moment_two, gradient, step_rate, decay_rate):
    moment_one = BETA_ONE * moment_one + (1.0 - BETA_ONE) * gradient
    moment_two = BETA_TWO * moment_two + (1.0 - BETA_TWO) * gradient * gradient
    update = (
        moment_one
        / (1.0 - BETA_ONE**STEP)
        / (jnp.sqrt(moment_two / (1.0 - BETA_TWO**STEP)) + EPSILON)
    )
    return (weight - step_rate * (update + decay_rate * weight), moment_one, moment_two)


def gather_all(values, axes):
    count = lax.axis_size(axes)
    copies = jnp.broadcast_to(values[None], (count,) + values.shape)
    return lax.all_to_all(copies, axes, 0, 0, tiled=True).reshape((-1,) + values.shape[1:])


def sum_all(values, axes):
    count = lax.axis_size(axes)
    copies = jnp.broadcast_to(values[None], (count,) + values.shape)
    return jnp.sum(lax.all_to_all(copies, axes, 0, 0, tiled=True), 0)


def sum_share(values, axes):
    count = lax.axis_size(axes)
    parts = lax.all_to_all(values, axes, 0, 0, tiled=True)
    return jnp.sum(parts.reshape((count, -1) + values.shape[1:]), 0)


def local(
    query_ids,
    passage_ids,
    query_lengths,
    passage_lengths,
    positive,
    prefix_lengths,
    prefix_weights,
    owners,
    weights,
    first_moments,
    second_moments,
    vectors,
    vector_first,
    vector_second,
):
    slot_count, unit_rows = (weights.shape[0], weights.shape[1])
    gathered = gather_all(weights.astype(jnp.bfloat16), "blk")
    flat_rows = jnp.take(gathered, owners, axis=0).reshape(-1, D)
    query_pooled, query_kept = embed_sequences(flat_rows, vectors, query_ids[0], query_lengths[0])
    passage_pooled, passage_kept = embed_sequences(
        flat_rows, vectors, passage_ids[0], passage_lengths[0]
    )
    all_passages = gather_all(passage_pooled.astype(jnp.bfloat16), "blk")
    prefix_masks = (jnp.arange(D)[None, :] < prefix_lengths[:, None]).astype(jnp.float32)
    prefix_scale = TEMPER * lax.rsqrt(prefix_lengths.astype(jnp.float32))
    queries = query_pooled.astype(jnp.bfloat16).astype(jnp.float32)
    passages = all_passages.astype(jnp.float32)
    masked = queries[None] * prefix_masks[:, None, :]
    logits = (
        jnp.einsum("mpd,jd->mpj", masked, passages, precision=HIGHEST) * prefix_scale[:, None, None]
    )
    counted = positive[0] >= 0
    target = (jnp.arange(passages.shape[0])[None, :] == positive[0][:, None]).astype(jnp.float32)
    running_totals = jax.nn.logsumexp(logits, -1) - jnp.sum(logits * target[None], -1)
    per_query = jnp.sum(prefix_weights[:, None] * running_totals, 0)
    loss_part = jnp.sum(jnp.where(counted, per_query, 0.0))
    count_part = jnp.sum(counted.astype(jnp.float32))
    count_total, loss_total = sum_all(jnp.stack([count_part, loss_part]), ("blk", "rep"))
    row_factor = (prefix_weights * prefix_scale / count_total)[:, None, None] * counted.astype(
        jnp.float32
    )[None, :, None]
    grad_logits = (jax.nn.softmax(logits, -1) - target[None]) * row_factor
    grad_query = jnp.sum(
        jnp.einsum("mpj,jd->mpd", grad_logits, passages, precision=HIGHEST)
        * prefix_masks[:, None, :],
        0,
    )
    grad_passage = sum_share(
        jnp.einsum("mpj,mpd->jd", grad_logits, masked, precision=HIGHEST), "blk"
    )
    flat_query, vec_query = encode_back(
        grad_query, query_pooled, flat_rows, vectors, query_ids[0], query_lengths[0], query_kept
    )
    flat_pass, vec_pass = encode_back(
        grad_passage,
        passage_pooled,
        flat_rows,
        vectors,
        passage_ids[0],
        passage_lengths[0],
        passage_kept,
    )
    vec_total = sum_all(vec_query + vec_pass, ("blk", "rep"))
    buffer = (
        jnp.zeros((lax.axis_size("blk") * slot_count, unit_rows, D), jnp.float32)
        .at[owners]
        .set((flat_query + flat_pass).reshape(-1, unit_rows, D))
    )
    vec_square = jnp.sum(vec_total * vec_total)
    reduced = sum_share(buffer, "blk")
    reduced = sum_all(reduced, "rep")
    square_sum = sum_all(jnp.sum(reduced * reduced)[None], "blk")[0]
    old_weight, old_first, old_second = (weights, first_moments, second_moments)
    slot_ids = lax.axis_index("blk") * slot_count + jnp.arange(slot_count)
    owned_mask = jnp.any(slot_ids[:, None] == owners[None, :], 1)[:, None, None]
    grad_norm = jnp.sqrt(square_sum + vec_square)
    factor = CLIP_AT / jnp.maximum(grad_norm, CLIP_AT)
    new_weight, new_first, new_second = adam_step(
        old_weight, old_first, old_second, reduced * factor, RATE, DECAY
    )
    new_weight = jnp.where(owned_mask, new_weight, old_weight)
    new_first = jnp.where(owned_mask, new_first, old_first)
    new_second = jnp.where(owned_mask, new_second, old_second)
    new_vec, new_vec_first, new_vec_second = adam_step(
        vectors, vector_first, vector_second, vec_total * factor, VECTOR_RATE, 0.0
    )
    return (
        new_weight,
        new_first,
        new_second,
        new_vec,
        new_vec_first,
        new_vec_second,
        loss_total,
        count_total,
        grad_norm,
    )


F32 = jnp.float32
BF16 = jnp.bfloat16
I32 = jnp.int32
UNIT = 128
TABLE_BLOCKS = VOCAB // UNIT
PLACE_BLOCKS = PLEN // UNIT
DENSE = PLACE_BLOCKS + (D + 4 * D + 2 * FF) // UNIT
HALF = 64
QROWS = 128
TOKENS = 2 * QROWS + 2 * PLEN
STARTS = (0, QROWS, 2 * QROWS, 2 * QROWS + PLEN)
UNITS_L = 10
L_ROWS = 4 * UNITS_L
NEVER = -1e30


def params(n_blk, small):
    return pltpu.CompilerParams(vmem_limit_bytes=(small if n_blk <= 16 else 58) << 20)


AT_POOL = PLEN
AT_Q = AT_POOL + D
AT_K = AT_Q + D
AT_V = AT_K + D
AT_O = AT_V + D
AT_UP = AT_O + D
AT_DOWN = AT_UP + FF

TAB_OWNER, TAB_RANK, TAB_SLOT, TAB_UNIT, TAB_KIND, TAB_ORDER, TAB_SORTED, TAB_ENDS, TAB_SOURCE = range(
    9
)
PIECE = 16
PIECES = 16
DENSE_CAP = 8
CLASS = DENSE // 2
HELD = DENSE_CAP // 2
AT_ASKED = DENSE_CAP // 4 * PIECE
MESSAGE_ROWS = AT_ASKED + 8

KIND_TABLE, KIND_PLACE, KIND_DENSE = 1, 2, 8

vmem = pl.BlockSpec(memory_space=pltpu.VMEM)
smem = pl.BlockSpec(memory_space=pltpu.SMEM)
hbm = pl.BlockSpec(memory_space=pl.ANY)
in_hbm = pl.BlockSpec(memory_space=pltpu.HBM)


def stay(*arrays):
    return [pltpu.with_memory_space_constraint(a, pltpu.HBM) for a in arrays]


def iota(shape, axis):
    return lax.broadcasted_iota(I32, shape, axis)


def dot_nn(a, b):
    return lax.dot_general(a, b, (((1,), (0,)), ((), ())), preferred_element_type=F32)


def dot_nt(a, b):
    return lax.dot_general(a, b, (((1,), (1,)), ((), ())), preferred_element_type=F32)


def dot_tn(a, b):
    return lax.dot_general(a, b, (((0,), (0,)), ((), ())), preferred_element_type=F32)


def split(a):
    high = a.astype(BF16)
    return high, (a - high.astype(F32)).astype(BF16)


def fine(dot, a, b):
    high, low = split(a)
    rows = a.shape[0]
    both = dot(jnp.concatenate([high, low], 0), b)
    return both[:rows] + both[rows:]


def to_column(row):
    return jnp.broadcast_to(row, (128, 128)).T[:, :1]


def token_facts(query_lengths, passage_lengths):
    lane = iota((1, TOKENS), 1)
    sequence = (
        (lane >= STARTS[1]).astype(I32)
        + (lane >= STARTS[2]).astype(I32)
        + (lane >= STARTS[3]).astype(I32)
    )
    ends = [
        STARTS[0] + query_lengths[0, 0],
        STARTS[1] + query_lengths[0, 1],
        STARTS[2] + passage_lengths[0, 0],
        STARTS[3] + passage_lengths[0, 1],
    ]
    end = jnp.where(
        sequence == 0,
        ends[0],
        jnp.where(sequence == 1, ends[1], jnp.where(sequence == 2, ends[2], ends[3])),
    )
    return sequence, lane < end


def across(values, n_blk, step):
    pairs = [(i, i // PIECES * PIECES + step(i % PIECES)) for i in range(n_blk)]
    return lax.ppermute(values, "blk", pairs)


def along_z(mine, n_blk):
    return jnp.stack(
        [mine] + [across(mine, n_blk, lambda i, k=k: (i + 4 * k) % PIECES) for k in (1, 2, 3)]
    )


def spread(first, n_blk):
    arrays = [first, lax.ppermute(first, "rep", [(0, 1), (1, 0)])]
    arrays = arrays + [across(a, n_blk, lambda i: i ^ 2) for a in arrays]
    return arrays + [across(a, n_blk, lambda i: i ^ 1) for a in arrays]


def piece_copies(me, gathered, matrices, sems):
    copies = []
    for part, array in enumerate(gathered):
        low = (me[0] % 4) ^ (part & 2) ^ (part // 4)
        odd = me[1] ^ (part % 2)
        for k in range(4):
            p = low + (me[0] % PIECES // 4 * 4 + 4 * (4 - k)) % PIECES
            row = pl.multiple_of((p % 8) * PIECE, PIECE)
            lane = pl.multiple_of((p // 8) * 128, 128)
            copies.append(
                pltpu.make_async_copy(
                    array.at[k],
                    matrices.at[:, odd, pl.ds(row, PIECE), pl.ds(lane, 128)],
                    sems.at[4 * part + k],
                )
            )
    return copies


def rows_at(matrices, tab, start, stop):
    blocks = []
    for b in range(start // UNIT, stop // UNIT):
        order = tab[b, TAB_ORDER]
        blocks.append(matrices[order // 2, order % 2])
    return jnp.concatenate(blocks, 0)


def owner_of(slot, slots, n_blk):
    owner = jnp.zeros(slot.shape, I32)
    for k in range(1, n_blk):
        owner = owner + (slot >= k * slots).astype(I32)
    return owner


def request_kernel(
    slots, n_blk, cap, take_cap, owners, me, positive, query_lengths, passage_lengths, owner_line,
    query_ids, passage_ids, weights, message, where_row, tab, ids, owner_row, asked, loaded, sems,
):
    n_rep = 2
    n_dest = n_blk * n_rep
    n_units = owners.shape[0]
    start = me[0] * slots

    def take(b, carry):
        before, have = carry
        slot = owners[n_units - DENSE + b]
        inside = slot - start
        mine = (inside >= 0) & (inside < slots)

        @pl.when(mine & (have // 2 % 2 == me[1]) & (have < DENSE_CAP))
        def _():
            spot = have // 4 * 2 + have % 2
            pltpu.make_async_copy(weights.at[inside], loaded.at[spot], sems.at[spot]).start()

        return before + (slot < start).astype(I32), have + mine.astype(I32)

    before, have = lax.fori_loop(0, DENSE, take, (0, 0))
    owner_row[...] = jnp.full(owner_row.shape, -1, I32)
    owner_row[:, :n_units] = owner_line[...].reshape(1, n_units)
    every_slot = owner_row[...]
    wide = every_slot.shape[1]
    base = n_units - DENSE
    low = base // 128 * 128
    rolled = pltpu.roll(every_slot[:, low:], wide - low - (base - low), 1)[:, :128]
    dense_owner = owner_of(rolled, slots, n_blk)
    owner_column = to_column(dense_owner)[:32]
    slot_column = to_column(rolled)[:32]
    block_row = iota((32, 128), 1)
    block_column = iota((32, 128), 0)
    same = (owner_column == dense_owner) & (block_row < block_column) & (block_row < DENSE)
    rank = jnp.sum(same.astype(I32), 1, keepdims=True)
    at = block_row * UNIT
    need = jnp.where(block_row < PLACE_BLOCKS, 0, jnp.where((at >= AT_K) & (at < AT_O), 2, 1))
    unit = jnp.sum(jnp.where(same, need, 0), 1, keepdims=True)
    lower = (dense_owner < owner_column) & (block_row < DENSE)
    order = rank + jnp.sum(lower.astype(I32), 1, keepdims=True)
    is_dense = (iota((32, 1), 0) >= PLACE_BLOCKS) & (iota((32, 1), 0) < DENSE)
    at = iota((32, 1), 0) * UNIT
    needs = jnp.where((at >= AT_K) & (at < AT_O), 2, 1)
    crowded = jnp.max(
        (
            ((rank >= DENSE_CAP) & (iota((32, 1), 0) < DENSE))
            | (is_dense & (unit + needs > UNITS_L))
        ).astype(I32)
    )
    which = iota((32, wide), 1)
    code = jnp.where(
        which < TABLE_BLOCKS,
        KIND_TABLE,
        jnp.where(
            which < TABLE_BLOCKS + PLACE_BLOCKS, KIND_PLACE + which - TABLE_BLOCKS, KIND_DENSE
        ),
    )
    here = (every_slot == me[0] * slots + iota((32, wide), 0)) & (which < n_units)
    kind = jnp.sum(jnp.where(here, code, 0), 1, keepdims=True)
    sort = jnp.where(
        kind == KIND_TABLE,
        0,
        jnp.where(kind == KIND_DENSE, 1, jnp.where(kind >= KIND_PLACE, 2, 3)),
    )
    sort = jnp.where(iota((32, 1), 0) < slots, sort, 4)

    def to_row(column):
        wide = jnp.concatenate([column, jnp.full((96, 1), 5, I32)], 0)
        return jnp.broadcast_to(wide, (128, 128)).T[:1]

    capped = jnp.minimum(rank, DENSE_CAP - 1)
    source = (2 * owner_column + capped // 2 % 2) * 2 + capped // 4
    order = jnp.minimum(order, DENSE - 1)
    by_order = jnp.sum(
        jnp.where((to_row(order) == block_column) & (block_row < DENSE), to_row(source), 0),
        1,
        keepdims=True,
    )
    sort_row = to_row(sort)
    ahead = (sort_row < sort) | ((sort_row == sort) & (block_row < block_column))
    place_row = to_row(jnp.sum(ahead.astype(I32), 1, keepdims=True))
    sorted_slot = jnp.sum(
        jnp.where((place_row == block_column) & (block_row < 32), block_row, 0), 1, keepdims=True
    )
    ends = jnp.sum((sort_row <= iota((32, 1), 0)).astype(I32), 1, keepdims=True)
    entry = block_row
    tab[...] = jnp.where(
        entry == TAB_OWNER,
        owner_column,
        jnp.where(
            entry == TAB_RANK,
            jnp.minimum(rank, DENSE_CAP - 1),
            jnp.where(
                entry == TAB_SLOT,
                slot_column - owner_column * slots,
                jnp.where(
                    entry == TAB_UNIT,
                    jnp.minimum(unit, UNITS_L - 2),
                    jnp.where(
                        entry == TAB_KIND,
                        kind,
                        jnp.where(
                            entry == TAB_ORDER,
                            order,
                            jnp.where(
                                entry == TAB_SORTED,
                                sorted_slot,
                                jnp.where(entry == TAB_ENDS, ends, by_order),
                            ),
                        ),
                    ),
                ),
            ),
        ),
    )

    ids[:, 0:QROWS] = query_ids[0:1]
    ids[:, QROWS : 2 * QROWS] = query_ids[1:2]
    ids[:, STARTS[2] : STARTS[3]] = passage_ids[0:1]
    ids[:, STARTS[3] :] = passage_ids[1:2]
    token = ids[...]
    _, live = token_facts(query_lengths, passage_lengths)
    lane = iota((1, TOKENS), 1)
    block = token // UNIT
    slot = jnp.zeros((1, TOKENS), I32)
    table_rows = -(-TABLE_BLOCKS // 128) * 128
    for at in range(0, table_rows, 128):
        column = to_column(owner_row[:, at : at + 128])
        hit = (iota((128, TOKENS), 0) + at) == block
        slot = slot + jnp.sum(jnp.where(hit, column, 0), 0, keepdims=True)
    owner = owner_of(slot, slots, n_blk)
    inside = slot - owner * slots
    row = token - block * UNIT
    upper = (row >= HALF).astype(I32)
    dest = owner * n_rep + upper
    local_row = inside * HALF + row - upper * HALF
    token = jnp.where(live, token, -1)
    first_at = []
    columns = [to_column(token[:, at : at + 128]) for at in range(0, TOKENS, 128)]
    for to_at in range(0, TOKENS, 128):
        best = jnp.full((128, 128), TOKENS, I32)
        for at in range(0, to_at + 128, 128):
            same = columns[at // 128] == token[:, to_at : to_at + 128]
            best = jnp.minimum(best, jnp.where(same, iota((128, 128), 0) + at, TOKENS))
        first_at.append(jnp.min(best, 0, keepdims=True))
    first_at = jnp.concatenate(first_at, 1)
    first = live & (first_at == lane)
    chosen = ((iota((n_dest, TOKENS), 0) == dest) & first).astype(F32)
    chosen_low = chosen.astype(BF16)
    seen = []
    for to_at in range(0, TOKENS, 256):
        above = to_at + 256
        earlier = iota((above, 256), 0) < first_at[:, to_at:above]
        seen.append(dot_nn(chosen_low[:, :above], earlier.astype(F32).astype(BF16)))
    seen = jnp.concatenate(seen, 1)
    to = iota((n_dest, TOKENS), 0)
    rank = jnp.sum(jnp.where(to == dest, seen, 0.0), 0, keepdims=True).astype(I32)
    turn = jnp.sum(jnp.where(to // n_rep == owner, seen, 0.0), 0, keepdims=True).astype(I32)
    source = owner * n_rep + me[1]
    where_row[0:1] = jnp.where(live & (turn < take_cap), owner * take_cap + turn, -1)
    where_row[1:2] = jnp.where(live & (rank < cap), dest * cap + rank, -1)
    over = jnp.max((live & ((rank >= cap) | (turn >= take_cap))).astype(I32))

    def listed(dest, spot, code):
        high = code // 32
        low = code - high * 32
        chosen = ((to == dest) & first).astype(F32)
        both = jnp.concatenate([chosen * high.astype(F32), chosen * low.astype(F32)], 0)
        spread = (iota((128, TOKENS), 0) == spot).astype(F32).astype(BF16)
        both = dot_nt(both.astype(BF16), spread)
        return both[:n_dest], both[n_dest:]

    take_high, take_low = listed(source, turn, inside * UNIT + row + 1)
    sent_high, sent_low = listed(dest, rank, local_row + 1)
    flag = jnp.maximum(over, crowded)
    column_of = iota((1, 128), 1)
    marks = jnp.where(
        column_of == 0,
        positive[0, 0],
        jnp.where(column_of == 1, positive[0, 1], jnp.where(column_of == 2, flag, 0)),
    ).astype(F32)
    asked[...] = jnp.zeros(asked.shape, F32)
    for i, part in enumerate(
        (take_high, take_low, jnp.broadcast_to(marks, (n_dest, 128)), sent_high, sent_low)
    ):
        asked[pl.ds(i, n_dest, stride=8), :] = part
    message[:, AT_ASKED:, :] = asked[: 8 * n_dest].reshape(n_dest, 8, 128).astype(BF16)
    for spot in range(HELD):
        present = spot // 2 * 4 + 2 * me[1] + spot % 2 < have

        @pl.when(present)
        def _():
            pltpu.make_async_copy(weights.at[0], loaded.at[spot], sems.at[spot]).wait()

        @pl.when(jnp.logical_not(present))
        def _():
            loaded[spot] = jnp.zeros((UNIT, D), F32)

    for odd in range(2):
        for c in range(DENSE_CAP // 4):
            whole = loaded[2 * c + (odd + before) % 2].astype(BF16)
            for s in range(n_blk):
                p = s % PIECES
                message[2 * s + odd, PIECE * c : PIECE * (c + 1)] = whole[
                    PIECE * (p % 8) : PIECE * (p % 8 + 1), 128 * (p // 8) : 128 * (p // 8 + 1)
                ]


def request(owners, me, positive, query_lengths, passage_lengths, query_ids, passage_ids, weights, n_blk, cap, take_cap):
    slots = weights.shape[0]
    n_dest = 2 * n_blk
    n_units = owners.shape[0]
    owner_row = owners
    return pl.pallas_call(
        partial(request_kernel, slots, n_blk, cap, take_cap),
        out_shape=(
            jax.ShapeDtypeStruct((n_dest, MESSAGE_ROWS, 128), BF16),
            jax.ShapeDtypeStruct((2, TOKENS), I32),
            jax.ShapeDtypeStruct((32, 128), I32),
        ),
        in_specs=[smem] * 5 + [vmem] * 3 + [in_hbm],
        out_specs=(vmem, vmem, vmem),
        scratch_shapes=[
            pltpu.VMEM((1, TOKENS), I32),
            pltpu.VMEM((1, -(-n_units // 128) * 128), I32),
            pltpu.VMEM((8 * n_dest + 8, 128), F32),
            pltpu.VMEM((HELD, UNIT, D), F32),
            pltpu.SemaphoreType.DMA((HELD,)),
        ],
        compiler_params=params(n_blk, 12),
        name="request",
    )(owners, me, positive, query_lengths, passage_lengths, owner_row, query_ids, passage_ids, *stay(weights))


def collect_kernel(tab, me, message, mine_out):
    for k in range(CLASS):
        source = tab[2 * k + me[1], TAB_SOURCE]
        spot = pl.multiple_of(source % 2 * PIECE, PIECE)
        mine_out[k] = message[source // 2, pl.ds(spot, PIECE), :]


def collect(tab, me, message):
    return pl.pallas_call(
        collect_kernel,
        out_shape=jax.ShapeDtypeStruct((CLASS, PIECE, 128), BF16),
        in_specs=[smem, smem, vmem],
        out_specs=vmem,
        compiler_params=params(message.shape[0] // 2, 2),
        name="collect",
    )(tab, me, message)


def fetch_kernel(slots, cap, take_cap, me, message, weights, rows_out, asked_out, lists, wanted, held, table, sem):
    n_dest = message.shape[0]
    copy = pltpu.make_async_copy(weights, held, sem)
    copy.start()
    n_blk = n_dest // 2
    lists[: 8 * n_dest] = message[:, AT_ASKED:, :].astype(F32).reshape(8 * n_dest, 128)
    mine = 8 * me[1]
    wanted[...] = jnp.zeros(wanted.shape, I32)
    wanted[:n_blk] = (
        lists[pl.ds(mine, n_blk, stride=16), :] * 32.0
        + lists[pl.ds(mine + 1, n_blk, stride=16), :]
        - 1.0
    ).astype(I32)
    every = [lists[pl.ds(i, n_dest, stride=8), :] for i in (2, 3, 4)]
    column_of = iota((n_dest, 128), 1)
    row = jnp.where(column_of < cap, every[1] * 32.0 + every[2] - 1.0, 0.0)
    for i in range(3):
        row = jnp.where(column_of == 124 + i, every[0][:, i : i + 1], row)
    asked_out[...] = row.astype(I32)
    wide = table.shape[0]
    columns = wanted[...].T
    copy.wait()
    table[...] = held[...].reshape(wide, D).astype(BF16)
    row_of = iota((take_cap, wide), 1)
    for at in range(0, n_dest // 2, 4):
        hot = jnp.concatenate(
            [
                (row_of == columns[:take_cap, s : s + 1]).astype(F32)
                for s in range(at, at + 4)
            ],
            0,
        ).astype(BF16)
        rows_out[at * take_cap : (at + 4) * take_cap] = dot_nn(hot, table[...]).astype(BF16)


def fetch(me, message, weights, cap, take_cap):
    slots = weights.shape[0]
    n_dest = message.shape[0]
    return pl.pallas_call(
        partial(fetch_kernel, slots, cap, take_cap),
        out_shape=(
            jax.ShapeDtypeStruct((n_dest // 2 * take_cap, D), BF16),
            jax.ShapeDtypeStruct((n_dest, 128), I32),
        ),
        in_specs=[smem, vmem, in_hbm],
        out_specs=(vmem, vmem),
        scratch_shapes=[
            pltpu.VMEM((8 * n_dest + 16, 128), F32),
            pltpu.VMEM((-(-n_dest // 256) * 128, 128), I32),
            pltpu.VMEM(weights.shape, F32),
            pltpu.VMEM((slots * UNIT, D), BF16),
            pltpu.SemaphoreType.DMA,
        ],
        compiler_params=params(n_dest // 2, 20),
        name="fetch",
    )(me, message, *stay(weights))


ST_POOLED, ST_C, ST_N2, ST_N1, ST_H, ST_O, ST_Q, ST_X0 = range(0, 64, 8)
ST_KQ, ST_B, ST_U, ST_A, ST_I1, ST_I2 = 64, 96, 128, 160, 192, 200
ST_ROWS = 208


def forward_kernel(
    tab, me, query_lengths, passage_lengths, positive, rows, where_row, vectors, g0, g1, g2, g3,
    g4, g5, g6, g7, emb_out, low_out, normed_out, scale_out, probs_out, state, matrices, embedded,
    sems,
):
    copies = piece_copies(me, (g0, g1, g2, g3, g4, g5, g6, g7), matrices, sems)
    for copy in copies:
        copy.start()
    taken = rows.shape[0]
    for at in range(0, TOKENS, 256):
        column = jnp.concatenate(
            [to_column(where_row[0:1, i : i + 128]) for i in (at, at + 128)], 0
        )
        hot = (iota((256, taken), 1) == column).astype(F32).astype(BF16)
        embedded[at : at + 256] = dot_nn(hot, rows[...])
    for copy in copies:
        copy.wait()
    shift = vectors[0:1]
    for start, length in zip(STARTS, (QROWS, QROWS, PLEN, PLEN)):
        e = embedded[start : start + length] + rows_at(matrices, tab, 0, length).astype(F32) + shift
        centred = e - jnp.mean(e, -1, keepdims=True)
        scale = lax.rsqrt(jnp.mean(centred * centred, -1, keepdims=True) + NORM_EPS)
        normed = centred * scale
        normed_out[start : start + length] = normed
        scale_out[start : start + length] = jnp.broadcast_to(scale, (length, 128))
        x = normed * vectors[1:2] + vectors[2:3]
        embedded[start : start + length] = x
        low_out[start : start + length] = x.astype(BF16)
    x0 = jnp.concatenate(
        [embedded[s : s + 1] for s in STARTS] + [jnp.zeros((4, D), F32)], 0
    )
    x0_low = x0.astype(BF16)
    q = (dot_nn(x0_low, rows_at(matrices, tab, AT_Q, AT_K)) + vectors[4:5]).astype(BF16)
    head_of = iota((8, D), 1) // HALF
    q_heads = jnp.concatenate(
        [jnp.where(head_of == h, q.astype(F32), 0.0) for h in range(HEADS)], 0
    ).astype(BF16)
    kq = dot_nt(q_heads, rows_at(matrices, tab, AT_K, AT_V)) * (D // HEADS) ** (-0.5)
    low = low_out[...]
    scores = fine(dot_nt, kq, low)
    sequence, live = token_facts(query_lengths, passage_lengths)
    valid = ((iota((32, TOKENS), 0) & 7) == sequence) & live
    scores = jnp.where(valid, scores, NEVER)
    top = jnp.max(scores, -1, keepdims=True)
    weight = jnp.where(valid, jnp.exp(scores - top), 0.0)
    total = jnp.sum(weight, -1, keepdims=True)
    probs = weight / jnp.where(total > 0.0, total, 1.0)
    probs_out[...] = probs
    mixed = dot_nn(probs.astype(BF16), low)
    valued = fine(dot_nn, mixed, rows_at(matrices, tab, AT_V, AT_O))
    blended = jnp.zeros((8, D), F32)
    for h in range(HEADS):
        blended = blended + jnp.where(head_of == h, valued[8 * h : 8 * h + 8], 0.0)
    real = iota((8, D), 0) < 4
    blended = jnp.where(real, blended + vectors[5:6], 0.0).astype(BF16)
    summed = x0 + dot_nn(blended, rows_at(matrices, tab, AT_O, AT_UP)) + vectors[6:7]
    h0, n1, i1 = norm_rows(summed, vectors[8:9], vectors[9:10])
    h_low = h0.astype(BF16)
    bias_up = jnp.concatenate([vectors[12 + i : 13 + i] for i in range(FF // D)], 1)
    u = dot_nt(h_low, rows_at(matrices, tab, AT_UP, AT_DOWN)) + bias_up
    a = (0.5 * u * (1.0 + lax.erf(u * (0.5**0.5)))).astype(BF16)
    second = h0 + dot_nn(a, rows_at(matrices, tab, AT_DOWN, DENSE * UNIT)) + vectors[7:8]
    x, n2, i2 = norm_rows(second, vectors[10:11], vectors[11:12])
    c = x.astype(BF16)
    pooled = jnp.tanh(dot_nn(c, rows_at(matrices, tab, AT_POOL, AT_Q)) + vectors[3:4])
    row8 = iota((8, 128), 0)
    sent = jnp.concatenate(
        [
            jnp.where(real, pooled, 0.0),
            jnp.where(
                row8 == 0,
                positive[0, 0].astype(F32),
                jnp.where(row8 == 1, positive[0, 1].astype(F32), -1.0),
            ),
        ],
        1,
    )
    n_blk = emb_out.shape[0] // 8
    emb_out[...] = jnp.concatenate([sent] * n_blk, 0).astype(BF16)
    state[ST_POOLED : ST_POOLED + 8] = pooled
    state[ST_C : ST_C + 8] = c.astype(F32)
    state[ST_N2 : ST_N2 + 8] = n2
    state[ST_N1 : ST_N1 + 8] = n1
    state[ST_H : ST_H + 8] = h_low.astype(F32)
    state[ST_O : ST_O + 8] = blended.astype(F32)
    state[ST_Q : ST_Q + 8] = q.astype(F32)
    state[ST_X0 : ST_X0 + 8] = x0_low.astype(F32)
    state[ST_KQ : ST_KQ + 32] = kq
    state[ST_B : ST_B + 32] = mixed
    for i in range(FF // D):
        state[ST_U + 8 * i : ST_U + 8 * i + 8] = u[:, i * D : (i + 1) * D]
        state[ST_A + 8 * i : ST_A + 8 * i + 8] = a[:, i * D : (i + 1) * D].astype(F32)
    state[ST_I1 : ST_I1 + 8] = jnp.broadcast_to(i1, (8, D))
    state[ST_I2 : ST_I2 + 8] = jnp.broadcast_to(i2, (8, D))


def forward(tab, me, query_lengths, passage_lengths, positive, rows, where_row, vectors, gathered, n_blk):
    return pl.pallas_call(
        forward_kernel,
        out_shape=(
            jax.ShapeDtypeStruct((n_blk * 8, D + 128), BF16),
            jax.ShapeDtypeStruct((TOKENS, D), BF16),
            jax.ShapeDtypeStruct((TOKENS, D), F32),
            jax.ShapeDtypeStruct((TOKENS, 128), F32),
            jax.ShapeDtypeStruct((32, TOKENS), F32),
            jax.ShapeDtypeStruct((ST_ROWS, D), F32),
            jax.ShapeDtypeStruct((CLASS, 2, UNIT, D), BF16),
        ),
        in_specs=[smem] * 5 + [vmem] * 3 + [hbm] * 8,
        out_specs=(vmem,) * 7,
        scratch_shapes=[
            pltpu.VMEM((TOKENS, D), F32),
            pltpu.SemaphoreType.DMA((2 * PIECES,)),
        ],
        compiler_params=params(n_blk, 12),
        name="forward",
    )(
        tab, me, query_lengths, passage_lengths, positive, rows, where_row, vectors,
        *stay(*gathered[:4]), *gathered[4:],
    )


def news_rows(n_dest):
    return 2 * place_rows(n_dest) + 8


def place_rows(n_dest):
    return max(PLEN // n_dest, 16)


def payload_rows(n_dest, cap):
    at_place = 2 * cap
    at_left = at_place + 2 * place_rows(n_dest)
    at_right = at_left + L_ROWS
    return at_place, at_left, at_right, at_right + 32


def backward_kernel(
    cap, tab, me, prefix_lengths, prefix_weights, emb, message, where_row, low_in, normed, scale,
    probs_in, state, vectors, matrices, payload, loss_out, count_out,
    received, grad_emb, dx, left,
):
    n_blk = emb.shape[0] // 8
    n_dest = 2 * n_blk
    for i in range(3):
        received[i * n_blk * 8 : (i + 1) * n_blk * 8] = emb[:, 128 * i : 128 * i + 128].astype(F32)

    def every(k):
        return jnp.concatenate(
            [received[pl.ds(i * n_blk * 8 + k, n_blk, stride=8), :] for i in range(3)], 1
        )

    queries = jnp.concatenate([every(0), every(1)], 0)
    passages = jnp.concatenate([every(2), every(3)], 0)[:, :D].astype(BF16)
    wanted = queries[:, D : D + 1].astype(I32)
    queries = queries[:, :D]
    size = 2 * n_blk
    counted = wanted >= 0
    counted_f = counted.astype(F32)
    column = iota((size, size), 1)
    target = (column == (wanted & 1) * n_blk + wanted // 2) & counted
    marks = message[...]
    lane = iota(marks.shape, 1)
    count = jnp.sum((((lane == 124) | (lane == 125)) & (marks >= 0)).astype(F32))
    count_out[0, 0] = count
    n_pre = prefix_lengths.shape[0]
    prefix_of = iota((n_pre * size, 1), 0) // size
    prefix = jnp.zeros((n_pre * size, 1), I32)
    share = jnp.zeros((n_pre * size, 1), F32)
    for k in range(n_pre):
        prefix = jnp.where(prefix_of == k, prefix_lengths[k], prefix)
        share = jnp.where(prefix_of == k, prefix_weights[k], share)
    temper = TEMPER * lax.rsqrt(prefix.astype(F32))
    mask = iota((n_pre * size, D), 1) < prefix
    masked = jnp.where(mask, jnp.concatenate([queries] * n_pre, 0), 0.0).astype(BF16)
    logits = dot_nt(masked, passages) * temper
    targets = jnp.concatenate([target.astype(F32)] * n_pre, 0)
    counts = jnp.concatenate([counted_f] * n_pre, 0)
    top = jnp.max(logits, -1, keepdims=True)
    weight = jnp.exp(logits - top)
    total = jnp.sum(weight, -1, keepdims=True)
    hit = jnp.sum(logits * targets, -1, keepdims=True)
    losses = share * (top + jnp.log(total) - hit) * counts
    grad = (weight / total - targets) * (counts * (share / count) * temper)
    high, lower = split(grad)
    spread_queries = jnp.where(mask, dot_nn(high, passages) + dot_nn(lower, passages), 0.0)
    d_queries = spread_queries[:size]
    for k in range(1, n_pre):
        d_queries = d_queries + spread_queries[k * size : (k + 1) * size]
    d_passages = dot_tn(high, masked) + dot_tn(lower, masked)
    loss_out[0, 0] = jnp.sum(losses)
    grad_emb[:size] = d_queries
    grad_emb[size : 2 * size] = d_passages
    grad_pooled = jnp.concatenate(
        [grad_emb[pl.ds(me[0] + i * n_blk, 1), :] for i in range(4)]
        + [jnp.zeros((4, D), F32)],
        0,
    )

    def kept_rows(at, rows=8):
        return state[at : at + rows]

    pooled = kept_rows(ST_POOLED)
    d_pre = grad_pooled * (1.0 - pooled * pooled)
    d_c = fine(dot_nt, d_pre, rows_at(matrices, tab, AT_POOL, AT_Q))
    n2 = kept_rows(ST_N2)
    d_second, d_g2, d_s2 = norm_back(d_c, n2, kept_rows(ST_I2), vectors[10:11])
    down_low = d_second.astype(BF16)
    d_a = dot_nt(down_low, rows_at(matrices, tab, AT_DOWN, DENSE * UNIT))
    u = jnp.concatenate([kept_rows(ST_U + 8 * i) for i in range(FF // D)], 1)
    slope = 0.5 * (1.0 + lax.erf(u * (0.5**0.5))) + u * jnp.exp(-0.5 * u * u) * (
        0.3989422804014327
    )
    up_low = (d_a * slope).astype(BF16)
    d_h = d_second + dot_nn(up_low, rows_at(matrices, tab, AT_UP, AT_DOWN))
    d_summed, d_g1, d_s1 = norm_back(d_h, kept_rows(ST_N1), kept_rows(ST_I1), vectors[8:9])
    branch_low = d_summed.astype(BF16)
    d_o = dot_nt(branch_low, rows_at(matrices, tab, AT_O, AT_UP)).astype(BF16)
    head_of = iota((8, D), 1) // HALF
    o_heads = jnp.concatenate(
        [jnp.where(head_of == h, d_o.astype(F32), 0.0) for h in range(HEADS)], 0
    ).astype(BF16)
    vo = dot_nt(o_heads, rows_at(matrices, tab, AT_V, AT_O))
    low = low_in[...]
    probs = probs_in[...]
    d_probs = fine(dot_nt, vo, low)
    d_scores = probs * (d_probs - jnp.sum(d_probs * probs, -1, keepdims=True))
    score_low = d_scores.astype(BF16)
    mixed_score = dot_nn(score_low, low)
    keyed = fine(dot_nn, mixed_score, rows_at(matrices, tab, AT_K, AT_V))
    d_q = jnp.zeros((8, D), F32)
    for h in range(HEADS):
        d_q = d_q + jnp.where(head_of == h, keyed[8 * h : 8 * h + 8], 0.0)
    d_q_low = (d_q * (D // HEADS) ** (-0.5)).astype(BF16)
    d_x0 = d_summed + dot_nt(d_q_low, rows_at(matrices, tab, AT_Q, AT_K))
    kq = kept_rows(ST_KQ, 32)
    vo_high, vo_low = split(vo)
    kq_high, kq_low = split(kq)
    probs_low = probs.astype(BF16)
    dx[...] = dot_tn(
        jnp.concatenate([probs_low, score_low, probs_low, score_low], 0),
        jnp.concatenate([vo_high, kq_high, vo_low, kq_low], 0),
    )
    for i, start in enumerate(STARTS):
        dx[start : start + 1] = dx[start : start + 1] + d_x0[i : i + 1]
    d_gain = jnp.zeros((1, D), F32)
    d_shift = jnp.zeros((1, D), F32)
    d_type = jnp.zeros((1, D), F32)
    for start in range(0, TOKENS, 256):
        incoming = dx[start : start + 256]
        n = normed[start : start + 256]
        d_gain = d_gain + jnp.sum(incoming * n, 0, keepdims=True)
        d_shift = d_shift + jnp.sum(incoming, 0, keepdims=True)
        dn = incoming * vectors[1:2]
        inner = (
            dn - jnp.mean(dn, -1, keepdims=True) - n * jnp.mean(dn * n, -1, keepdims=True)
        )
        de = inner * scale[start : start + 256, :1]
        d_type = d_type + jnp.sum(de, 0, keepdims=True)
        dx[start : start + 256] = de
    de_low = dx[...].astype(BF16)
    at_place, at_left, at_right, n_rows = payload_rows(n_dest, cap)
    per = 8
    step = per * cap
    for at in range(0, n_dest * cap, step):
        hot = ((iota((step, TOKENS), 0) + at) == where_row[1:2]).astype(F32).astype(BF16)
        summed = dot_nn(hot, de_low).astype(BF16)
        for i in range(per):
            d = at // cap + i
            if d < n_dest:
                payload[d, :cap] = summed[i * cap : (i + 1) * cap, :128]
                payload[d, cap : 2 * cap] = summed[i * cap : (i + 1) * cap, 128:]
    spots = dx[STARTS[2] : STARTS[3]] + dx[STARTS[3] :]
    dx[STARTS[2] : STARTS[3]] = spots
    dx[STARTS[2] : STARTS[2] + QROWS] = (
        dx[STARTS[2] : STARTS[2] + QROWS] + dx[:QROWS] + dx[QROWS : 2 * QROWS]
    )
    pr = place_rows(n_dest)
    share = PLEN // n_dest
    for d in range(n_dest):
        spot = dx[STARTS[2] + d * share : STARTS[2] + (d + 1) * share]
        if share < pr:
            spot = jnp.concatenate([spot, jnp.zeros((pr - share, D), F32)], 0)
        payload[d, at_place : at_place + pr] = spot[:, :128].astype(BF16)
        payload[d, at_place + pr : at_place + 2 * pr] = spot[:, 128:].astype(BF16)
    left[...] = jnp.zeros(left.shape, F32)
    up_f = up_low.astype(F32)

    def put(b, r, unit, values):
        spot = (tab[b, TAB_OWNER] * 2 + r) * L_ROWS + (tab[b, TAB_UNIT] + unit) * 4
        for i in range(4):
            left[pl.ds(spot + i, 1), :] = values[i : i + 1]

    for b in range(PLACE_BLOCKS, DENSE):
        at = b * UNIT
        if AT_K <= at < AT_O:
            heads = mixed_score if at < AT_V else kept_rows(ST_B, 32)
            off = (at - AT_K) % D
            for r in range(2):
                for j in range(2):
                    h = 2 * r + j
                    put(b, r, j, heads[8 * h : 8 * h + 4, off : off + UNIT])
            continue
        if at < AT_Q:
            values, off = kept_rows(ST_C), at - AT_POOL
        elif at < AT_K:
            values, off = kept_rows(ST_X0), at - AT_Q
        elif at < AT_UP:
            values, off = kept_rows(ST_O), at - AT_O
        elif at < AT_DOWN:
            values, off = up_f, at - AT_UP
        else:
            off = (at - AT_DOWN) % D
            values = kept_rows(ST_A + 8 * ((at - AT_DOWN) // D))
        for r in range(2):
            put(b, r, 0, values[:4, off : off + UNIT])
    d_vectors = jnp.concatenate(
        [
            d_type,
            d_gain,
            d_shift,
            jnp.sum(d_pre, 0, keepdims=True),
            jnp.sum(d_q_low.astype(F32), 0, keepdims=True),
            jnp.sum(d_o.astype(F32), 0, keepdims=True),
            jnp.sum(branch_low.astype(F32), 0, keepdims=True),
            jnp.sum(down_low.astype(F32), 0, keepdims=True),
            d_g1[None],
            d_s1[None],
            d_g2[None],
            d_s2[None],
        ]
        + [
            jnp.sum(up_f[:, i * D : (i + 1) * D], 0, keepdims=True) for i in range(FF // D)
        ],
        0,
    )
    scaled_q = kept_rows(ST_Q) * (D // HEADS) ** (-0.5)
    right = jnp.concatenate(
        [
            v.astype(F32)[:4]
            for v in (d_pre, d_q_low, scaled_q, d_o, branch_low, kept_rows(ST_H), down_low)
        ],
        0,
    )
    for d in range(n_dest):
        payload[d, at_left:at_right] = left[d * L_ROWS : (d + 1) * L_ROWS].astype(BF16)
        r = d % 2
        if d < 32:
            share_vec = d_vectors[d // 2 : d // 2 + 1, r * 128 : (r + 1) * 128]
        else:
            share_vec = jnp.zeros((1, 128), F32)
        payload[d, at_right:n_rows] = jnp.concatenate(
            [right[:, r * 128 : (r + 1) * 128], share_vec, jnp.zeros((3, 128), F32)], 0
        ).astype(BF16)


def backward(tab, me, prefix_lengths, prefix_weights, emb, message, where_row, low, normed, scale, probs, state, vectors, matrices, cap):
    n_dest = message.shape[0]
    n_rows = payload_rows(n_dest, cap)[-1]
    return pl.pallas_call(
        partial(backward_kernel, cap),
        out_shape=(
            jax.ShapeDtypeStruct((n_dest, n_rows, 128), BF16),
            jax.ShapeDtypeStruct((1, 1), F32),
            jax.ShapeDtypeStruct((1, 1), F32),
        ),
        in_specs=[smem] * 4 + [vmem] * 10,
        out_specs=(vmem, smem, smem),
        scratch_shapes=[
            pltpu.VMEM((emb.shape[0] * 3 + 8, 128), F32),
            pltpu.VMEM((emb.shape[0], D), F32),
            pltpu.VMEM((TOKENS, D), F32),
            pltpu.VMEM((n_dest * L_ROWS, 128), F32),
        ],
        compiler_params=params(n_dest // 2, 16),
        name="backward",
    )(tab, me, prefix_lengths, prefix_weights, emb, message, where_row, low, normed, scale, probs, state, vectors, matrices)


def reduce_kernel(slots, cap, tab, me, loss, asked, payload, reduced, news, total, row_grads, left, right):
    n_dest = payload.shape[0]
    at_place, at_left, at_right, n_rows = payload_rows(n_dest, cap)
    for d in range(n_dest):
        row_grads[d * cap : (d + 1) * cap, :128] = payload[d, :cap]
        row_grads[d * cap : (d + 1) * cap, 128:] = payload[d, cap : 2 * cap]
        left[d * L_ROWS : (d + 1) * L_ROWS] = payload[d, at_left:at_right].astype(F32)
        right[d * 32 : (d + 1) * 32] = payload[d, at_right:n_rows].astype(F32)
    grads = row_grads[...]
    filled = slots * HALF
    chunk = filled // 4
    for at in range(0, filled, chunk):
        hot = ((iota((chunk, n_dest * cap), 0) + at) == asked[...]).astype(F32).astype(BF16)
        total[at : at + chunk] = dot_nn(hot, grads)
    mine = me[0]
    odd = me[1]
    column = iota((n_dest * 4, 128), 1)

    def rows_of(ref, start, stride):
        return jnp.concatenate(
            [ref[pl.ds(start + q, n_dest, stride=stride), :] for q in range(4)], 0
        ).astype(BF16)

    for b in range(PLACE_BLOCKS, DENSE):
        at = b * UNIT
        if at < AT_Q:
            m = 0
        elif at < AT_UP:
            m = 1 + (at - AT_Q) // D
        elif at < AT_DOWN:
            m = 5
        else:
            m = 6

        @pl.when(tab[b, TAB_OWNER] == mine)
        def _():
            unit = tab[b, TAB_UNIT] * 4
            pull = rows_of(right, m * 4, 32)
            if AT_K <= at < AT_O:
                grad = dot_tn(
                    rows_of(left, unit, L_ROWS), jnp.where(column < HALF, pull, 0).astype(BF16)
                ) + dot_tn(
                    rows_of(left, unit + 4, L_ROWS),
                    jnp.where(column < HALF, 0, pull).astype(BF16),
                )
            else:
                grad = dot_tn(rows_of(left, unit, L_ROWS), pull)
            spot = pl.multiple_of(tab[b, TAB_SLOT] * HALF, HALF)
            total[pl.ds(spot, HALF), :128] = grad[:HALF]
            total[pl.ds(spot, HALF), 128:] = grad[HALF:]

    pr = place_rows(n_dest)
    spots_low = jnp.zeros((pr, 128), F32)
    spots_high = jnp.zeros((pr, 128), F32)
    for d in range(n_dest):
        spots_low = spots_low + payload[d, at_place : at_place + pr].astype(F32)
        spots_high = spots_high + payload[d, at_place + pr : at_place + 2 * pr].astype(F32)
    spots = jnp.concatenate([spots_low, spots_high], 1)
    vector = jnp.sum(right[pl.ds(28, n_dest, stride=32), :], 0, keepdims=True)
    summed = total[...]
    reduced[...] = summed.astype(BF16).reshape(reduced.shape)
    square = jnp.sum(summed * summed) + jnp.sum(spots * spots) + jnp.sum(vector * vector)
    row8 = iota((8, 128), 0)

    def parts(v):
        first = v.astype(BF16).astype(F32)
        second = (v - first).astype(BF16).astype(F32)
        return first, second, v - first - second

    extra = jnp.where(row8 == 0, vector, 0.0)
    for i, part in enumerate(
        parts(jnp.full((1, 128), square, F32)) + parts(jnp.full((1, 128), loss[0, 0], F32))
    ):
        extra = jnp.where(row8 == 1 + i, part, extra)
    block = jnp.concatenate([spots[:, :128], spots[:, 128:], extra], 0).astype(BF16)
    for d in range(n_dest):
        news[d] = block


def reduce(tab, me, loss, asked, payload, slots, cap):
    n_dest = payload.shape[0]
    pr = place_rows(n_dest)
    return pl.pallas_call(
        partial(reduce_kernel, slots, cap),
        out_shape=(
            jax.ShapeDtypeStruct((slots, HALF, D), BF16),
            jax.ShapeDtypeStruct((n_dest, news_rows(n_dest), 128), BF16),
        ),
        in_specs=[smem, smem, smem, vmem, vmem],
        out_specs=(vmem, vmem),
        scratch_shapes=[
            pltpu.VMEM((slots * HALF, D), F32),
            pltpu.VMEM((n_dest * cap, D), BF16),
            pltpu.VMEM(((n_dest + 1) * L_ROWS, 128), F32),
            pltpu.VMEM(((n_dest + 1) * 32, 128), F32),
        ],
        compiler_params=params(n_dest // 2, 16),
        name="reduce",
    )(tab, me, loss, asked, payload)


def update_slots(
    tab, half, rest, grads, places, scale, arrays, outs, held, in_sems, out_sems, wanted=None
):
    first_scale = -RATE / (1.0 - BETA_ONE**STEP)
    second_scale = 1.0 / (1.0 - BETA_TWO**STEP)
    rows = (pl.ds(pl.multiple_of(half * HALF, HALF), HALF), slice(None))
    columns = (slice(None), pl.ds(pl.multiple_of(half * 128, 128), 128))
    whole = (slice(None), slice(None))
    ends = [tab[k, TAB_ENDS] for k in range(4)]
    if wanted is not None:
        ends = [jnp.where(wanted, end, 0) for end in ends]
    spans = [(KIND_TABLE, 0, ends[0], rows), (KIND_DENSE, ends[0], ends[1], columns)]
    if rest:
        spans += [(KIND_PLACE, ends[1], ends[2], whole), (0, ends[2], ends[3], whole)]

    def loop(action):
        for case, start, stop, region in spans:

            def body(j, c):
                action(tab[j, TAB_SORTED], case, region)
                return c

            lax.fori_loop(start, stop, body, 0)

    def in_copies(i, region):
        return [
            pltpu.make_async_copy(a.at[(i,) + region], held.at[(k, i) + region], in_sems.at[k, i])
            for k, a in enumerate(arrays)
        ]

    def out_copies(i, region):
        return [
            pltpu.make_async_copy(held.at[(k, i) + region], out.at[(i,) + region], out_sems.at[k, i])
            for k, out in enumerate(outs)
        ]

    def start(i, case, region):
        for copy in in_copies(i, region):
            copy.start()

    def step(i, region, g):
        g = g * scale[: g.shape[0], : g.shape[1]]
        m1 = BETA_ONE * held[(1, i) + region] + (1.0 - BETA_ONE) * g
        m2 = BETA_TWO * held[(2, i) + region] + (1.0 - BETA_TWO) * (g * g)
        root = jnp.sqrt(m2 * second_scale) + EPSILON
        held[(0, i) + region] = (
            held[(0, i) + region] * (1.0 - RATE * DECAY) + (m1 * first_scale) / root
        )
        held[(1, i) + region] = m1
        held[(2, i) + region] = m2

    def act(i, case, region):
        for copy in in_copies(i, region):
            copy.wait()
        if case == KIND_TABLE:
            step(i, region, grads[i].astype(F32))
        elif case == KIND_DENSE:
            g = grads[i].astype(F32)
            step(i, region, jnp.concatenate([g[:, :128], g[:, 128:]], 0))
        elif case == KIND_PLACE:
            spot = pl.multiple_of((tab[i, TAB_KIND] - KIND_PLACE) * UNIT, UNIT)
            step(i, region, places[pl.ds(spot, UNIT), :])

        for copy in out_copies(i, region):
            copy.start()

    def finish(i, case, region):
        for copy in out_copies(i, region):
            copy.wait()

    loop(start)
    yield
    loop(act)
    loop(finish)
    yield


def update_kernel(
    tab, me, news, own, weight, first, second, vectors, vector_first, vector_second,
    weight_out, first_out, second_out, vectors_out, vector_first_out, vector_second_out, loss_out,
    norm_out, factor_out, places, held, in_sems, out_sems,
):
    n_dest = news.shape[0]
    pr = place_rows(n_dest)
    share = PLEN // n_dest
    scale = factor_out
    steps = update_slots(
        tab, me[1], True, own, places, scale, (weight, first, second),
        (weight_out, first_out, second_out), held, in_sems, out_sems,
    )
    next(steps)
    extras = []
    for d in range(n_dest):
        part = news[d].astype(F32)
        places[d * share : (d + 1) * share, :128] = part[:share]
        places[d * share : (d + 1) * share, 128:] = part[pr : pr + share]
        extras.append(part[2 * pr :])
    sums = extras[0]
    for extra in extras[1:]:
        sums = sums + extra
    square = sums[1:2] + sums[2:3] + sums[3:4]
    norm = jnp.sqrt(square)
    factor = CLIP_AT / jnp.maximum(norm, CLIP_AT)
    norm_out[0, 0] = norm[0, 0]
    losses = extras[0] + extras[1]
    loss = losses[4:5] + losses[5:6] + losses[6:7]
    loss_out[0, 0] = loss[0, 0]
    vector_grad = jnp.concatenate(
        [
            jnp.concatenate([extras[2 * i][0:1], extras[2 * i + 1][0:1]], 1)
            for i in range(vectors.shape[0])
        ],
        0,
    ) * jnp.concatenate([factor, factor], 1)
    v, m1, m2 = adam_step(
        vectors[...], vector_first[...], vector_second[...], vector_grad, VECTOR_RATE, 0.0
    )
    vectors_out[...] = v
    vector_first_out[...] = m1
    vector_second_out[...] = m2
    factor_out[...] = jnp.broadcast_to(jnp.concatenate([factor, factor], 1), (UNIT, D))
    next(steps)


def finish_kernel(
    full, tab, me, factor, other, weight, first, second, weight_in, first_in, second_in, weight_out,
    first_out, second_out, held, in_sems, out_sems,
):
    steps = update_slots(
        tab, 1 - me[1], False, other, None, factor, (weight, first, second),
        (weight_out, first_out, second_out), held, in_sems, out_sems, full[0] == 0,
    )
    next(steps)
    next(steps)


def update_scratch(shape):
    return [
        pltpu.VMEM((3,) + shape, F32),
        pltpu.SemaphoreType.DMA((3, shape[0])),
        pltpu.SemaphoreType.DMA((3, shape[0])),
    ]


def update(tab, me, news, own, weights, first, second, vectors, vector_first, vector_second):
    n_dest = news.shape[0]
    big = pltpu.HBM(weights.shape, F32)
    small = jax.ShapeDtypeStruct(vectors.shape, F32)
    one = jax.ShapeDtypeStruct((1, 1), F32)
    return pl.pallas_call(
        update_kernel,
        out_shape=(big, big, big, small, small, small, one, one, jax.ShapeDtypeStruct((UNIT, D), F32)),
        in_specs=[smem, smem] + [vmem] * 2 + [in_hbm] * 3 + [vmem] * 3,
        out_specs=(in_hbm, in_hbm, in_hbm, vmem, vmem, vmem, smem, smem, vmem),
        scratch_shapes=[pltpu.VMEM((PLEN, D), F32)] + update_scratch(weights.shape),
        compiler_params=params(n_dest // 2, 14),
        name="update",
    )(tab, me, news, own, *stay(weights, first, second), vectors, vector_first, vector_second)


def finish(full, tab, me, factor, other, weights, first, second, started, n_blk):
    big = pltpu.HBM(weights.shape, F32)
    return pl.pallas_call(
        finish_kernel,
        out_shape=(big, big, big),
        in_specs=[smem, smem, smem, vmem, vmem] + [in_hbm] * 6,
        out_specs=(in_hbm, in_hbm, in_hbm),
        scratch_shapes=update_scratch(weights.shape),
        input_output_aliases={8: 0, 9: 1, 10: 2},
        compiler_params=params(n_blk, 14),
        name="finish",
    )(full, tab, me, factor, other, *stay(weights, first, second, *started))


def quick(
    query_ids, passage_ids, query_lengths, passage_lengths, positive, prefix_lengths,
    prefix_weights, owners, weights, first_moments, second_moments, vectors, vector_first,
    vector_second,
):
    slots = weights.shape[0]
    n_blk = lax.axis_size("blk")
    everyone = ("blk", "rep")
    cap = 48 if n_blk <= 16 else 16
    take_cap = 80 if n_blk <= 16 else 32
    me = jnp.stack([lax.axis_index("blk"), lax.axis_index("rep")]).astype(I32)

    def exchange(a, axes):
        return lax.all_to_all(a, axes, 0, 0, tiled=True)

    message, where_row, tab = request(
        owners, me, positive, query_lengths, passage_lengths, query_ids[0], passage_ids[0],
        weights, n_blk, cap, take_cap,
    )
    message = exchange(message, everyone)
    first = along_z(collect(tab, me, message), n_blk)
    rows, message = fetch(me, message, weights, cap, take_cap)
    rows, first = lax.optimization_barrier((rows, first))
    rows = exchange(rows, "blk")
    gathered = spread(first, n_blk)
    emb, low, normed, scale, probs, state, matrices = forward(
        tab, me, query_lengths, passage_lengths, positive, rows, where_row, vectors, gathered, n_blk
    )
    emb = exchange(emb, "blk")
    payload, loss, count = backward(
        tab, me, prefix_lengths, prefix_weights, emb, message, where_row, low, normed, scale,
        probs, state, vectors, matrices, cap,
    )
    payload = exchange(payload, everyone)
    asked = message[:, :cap].reshape(1, -1)
    own, news = reduce(tab, me, loss, asked, payload, slots, cap)
    other = lax.ppermute(own, "rep", [(0, 1), (1, 0)])
    news = exchange(news, everyone)
    *outs, loss_sum, norm, factor = update(
        tab, me, news, own, weights, first_moments, second_moments, vectors, vector_first,
        vector_second,
    )
    outs = (*outs, loss_sum.reshape(()), count.reshape(()), norm.reshape(()))

    def general(carry):
        return 0, local(
            query_ids, passage_ids, query_lengths, passage_lengths, positive, prefix_lengths,
            prefix_weights, owners, weights, first_moments, second_moments, vectors, vector_first,
            vector_second,
        )

    full = jnp.max(message[:, 126])
    outs = lax.while_loop(lambda c: c[0] > 0, general, (full, outs))[1]
    finished = finish(
        full.reshape(1), tab, me, factor, other, weights, first_moments, second_moments, outs[:3],
        n_blk,
    )
    return (*finished, *outs[3:])


def solution(mesh):
    in_specs = (
        P("rep", "blk", None),
        P("rep", "blk", None),
        P("rep", "blk"),
        P("rep", "blk"),
        P("rep", "blk"),
        P(),
        P(),
        P(),
        P("blk", None, None),
        P("blk", None, None),
        P("blk", None, None),
        P(),
        P(),
        P(),
    )
    out_specs = (
        P("blk", None, None),
        P("blk", None, None),
        P("blk", None, None),
        P(),
        P(),
        P(),
        P(),
        P(),
        P(),
    )
    return jax.shard_map(quick, mesh=mesh, in_specs=in_specs, out_specs=out_specs, check_vma=False)
```

```python
from functools import partial

import jax
import jax.numpy as jnp
from jax import lax
from jax.experimental import pallas as pl
from jax.experimental.pallas import tpu as pltpu
from jax.sharding import PartitionSpec as P

D = 256
HEADS = 4
FF = 1024
VOCAB = 30592
LAYERS = 1
PLEN = 512
STEP = 7


TEMPER = 8.0
CLIP_AT = 0.01
RATE = 0.06
VECTOR_RATE = 0.8
BETA_ONE = 0.9
BETA_TWO = 0.999
DECAY = 0.01
EPSILON = 1e-08
NORM_EPS = 1e-06
HUGE = 1000000000.0
HIGHEST = lax.Precision.HIGHEST


def mult(left_op, right_op):
    return jnp.dot(left_op, right_op, preferred_element_type=jnp.float32)


def mult_tn(left_op, right_op):
    return lax.dot_general(
        left_op, right_op, (((0,), (0,)), ((), ())), preferred_element_type=jnp.float32
    )


def mult_nt(left_op, right_op):
    return lax.dot_general(
        left_op, right_op, (((1,), (1,)), ((), ())), preferred_element_type=jnp.float32
    )


def norm_rows(values_in, gain_row, shift_row):
    centred = values_in - jnp.mean(values_in, -1, keepdims=True)
    inv_scale = lax.rsqrt(jnp.mean(centred * centred, -1, keepdims=True) + NORM_EPS)
    normed = centred * inv_scale
    return (normed * gain_row + shift_row, normed, inv_scale)


def norm_back(incoming, normed, inv_scale, gain_row):
    dnormed = incoming * gain_row
    inner_part = (
        dnormed
        - jnp.mean(dnormed, -1, keepdims=True)
        - normed * jnp.mean(dnormed * normed, -1, keepdims=True)
    )
    return (inner_part * inv_scale, jnp.sum(incoming * normed, 0), jnp.sum(incoming, 0))


def layer_parts(flat_rows, vectors, layer_index):
    offset = VOCAB + PLEN + D + layer_index * (4 * D + 2 * FF)
    w_qkv = jnp.concatenate(
        [
            flat_rows[offset : offset + D],
            flat_rows[offset + D : offset + 2 * D],
            flat_rows[offset + 2 * D : offset + 3 * D],
        ],
        1,
    )
    w_out = flat_rows[offset + 3 * D : offset + 4 * D]
    w_up = flat_rows[offset + 4 * D : offset + 4 * D + FF]
    w_down = flat_rows[offset + 4 * D + FF : offset + 4 * D + 2 * FF]
    row_base = 4 + layer_index * (8 + FF // D)
    return ((w_qkv, w_out, w_up, w_down), vectors[row_base : row_base + 8 + FF // D])


def divide_into_heads(packed_buffer, column):
    return packed_buffer[:, column * D : (column + 1) * D].reshape(
        packed_buffer.shape[0], HEADS, D // HEADS
    )


def attend_probs(packed_buffer, key_keep):
    scores = jnp.einsum(
        "cnp,fnp->ncf",
        divide_into_heads(packed_buffer, 0),
        divide_into_heads(packed_buffer, 1),
        preferred_element_type=jnp.float32,
    ) * (D // HEADS) ** (-0.5)
    scores = jnp.where(key_keep[None, None, :], scores, -HUGE)
    return jax.nn.softmax(scores, -1)


def attend(pieces):
    packed_buffer, key_keep = pieces
    attn_probs = attend_probs(packed_buffer, key_keep)
    blended = jnp.einsum(
        "nbi,ins->bns",
        attn_probs.astype(jnp.bfloat16),
        divide_into_heads(packed_buffer, 2),
        preferred_element_type=jnp.float32,
    )
    return blended.reshape(packed_buffer.shape[0], D)


def attend_back(pieces):
    packed_buffer, key_keep, grad_out = pieces
    seq_len = packed_buffer.shape[0]
    head_scale = (D // HEADS) ** (-0.5)
    attn_probs = attend_probs(packed_buffer, key_keep)
    gradient_row_block = grad_out.reshape(seq_len, HEADS, D // HEADS)
    grad_values = jnp.einsum(
        "fxn,xfa->nfa",
        attn_probs.astype(jnp.bfloat16),
        gradient_row_block,
        preferred_element_type=jnp.float32,
    )
    grad_probs = jnp.einsum(
        "cnp,fnp->ncf",
        gradient_row_block,
        divide_into_heads(packed_buffer, 2),
        preferred_element_type=jnp.float32,
    )
    grad_scores = attn_probs * (grad_probs - jnp.sum(grad_probs * attn_probs, -1, keepdims=True))
    score_lowered = grad_scores.astype(jnp.bfloat16)
    grad_queries = (
        jnp.einsum(
            "nbi,ins->bns",
            score_lowered,
            divide_into_heads(packed_buffer, 1),
            preferred_element_type=jnp.float32,
        )
        * head_scale
    )
    grad_keys = (
        jnp.einsum(
            "fxn,xfa->nfa",
            score_lowered,
            divide_into_heads(packed_buffer, 0),
            preferred_element_type=jnp.float32,
        )
        * head_scale
    )
    return jnp.concatenate(
        [
            grad_queries.reshape(seq_len, D),
            grad_keys.reshape(seq_len, D),
            grad_values.reshape(seq_len, D),
        ],
        1,
    ).astype(jnp.bfloat16)


def layer_forward(hidden_in, weights_set, vec_rows, key_keep):
    w_qkv, w_out, w_up, w_down = weights_set
    groups, seq_len = key_keep.shape
    in_low = hidden_in.astype(jnp.bfloat16)
    bias_qkv = jnp.concatenate([vec_rows[0], jnp.zeros_like(vec_rows[0]), vec_rows[1]])
    packed_buffer = (mult(in_low, w_qkv) + bias_qkv).astype(jnp.bfloat16)
    blended = lax.map(attend, (packed_buffer.reshape(groups, seq_len, 3 * D), key_keep))
    blend_low = blended.reshape(groups * seq_len, D).astype(jnp.bfloat16)
    summed = hidden_in + mult(blend_low, w_out) + vec_rows[2]
    normal_one, normed_one, scale_one = norm_rows(summed, vec_rows[4], vec_rows[5])
    normal_low = normal_one.astype(jnp.bfloat16)
    up_in = mult_nt(normal_low, w_up) + vec_rows[8:].reshape(FF)
    acted = jax.nn.gelu(up_in, approximate=False).astype(jnp.bfloat16)
    second = normal_one + mult(acted, w_down) + vec_rows[3]
    result, normed_two, scale_two = norm_rows(second, vec_rows[6], vec_rows[7])
    return (
        result,
        (
            in_low,
            packed_buffer,
            blend_low,
            normed_one,
            scale_one,
            normal_low,
            up_in,
            acted,
            normed_two,
            scale_two,
        ),
    )


def layer_backward(grad_out, weights_set, vec_rows, key_keep, saved):
    w_qkv, w_out, w_up, w_down = weights_set
    (
        in_low,
        packed_buffer,
        blend_low,
        normed_one,
        scale_one,
        normal_low,
        up_in,
        acted,
        normed_two,
        scale_two,
    ) = saved
    groups, seq_len = key_keep.shape
    grad_second, grad_gain_two, grad_shift_two = norm_back(
        grad_out, normed_two, scale_two, vec_rows[6]
    )
    down_low = grad_second.astype(jnp.bfloat16)
    grad_down = mult_tn(acted, down_low)
    grad_acted = mult_nt(down_low, w_down)
    gelu_pull = jax.vjp(partial(jax.nn.gelu, approximate=False), up_in)[1]
    up_low = gelu_pull(grad_acted)[0].astype(jnp.bfloat16)
    grad_up = mult_tn(up_low, normal_low)
    grad_normal = grad_second + mult(up_low, w_up)
    grad_summed, gradient_first_gain, grad_shift_one = norm_back(
        grad_normal, normed_one, scale_one, vec_rows[4]
    )
    branch_low = grad_summed.astype(jnp.bfloat16)
    grad_wout = mult_tn(blend_low, branch_low)
    blend_grad = mult_nt(branch_low, w_out).astype(jnp.bfloat16)
    grad_packed = lax.map(
        attend_back,
        (
            packed_buffer.reshape(groups, seq_len, 3 * D),
            key_keep,
            blend_grad.reshape(groups, seq_len, D),
        ),
    ).reshape(groups * seq_len, 3 * D)
    grad_wqkv = mult_tn(in_low, grad_packed)
    grad_in = grad_summed + mult_nt(grad_packed, w_qkv)
    packed_sum = jnp.sum(grad_packed.astype(jnp.float32), 0)
    matrix_grads = jnp.concatenate(
        [
            grad_wqkv[:, :D],
            grad_wqkv[:, D : 2 * D],
            grad_wqkv[:, 2 * D :],
            grad_wout,
            grad_up,
            grad_down,
        ],
        0,
    )
    vector_grads = jnp.concatenate(
        [
            jnp.stack(
                [
                    packed_sum[:D],
                    packed_sum[2 * D :],
                    jnp.sum(branch_low.astype(jnp.float32), 0),
                    jnp.sum(down_low.astype(jnp.float32), 0),
                    gradient_first_gain,
                    grad_shift_one,
                    grad_gain_two,
                    grad_shift_two,
                ]
            ),
            jnp.sum(up_low.astype(jnp.float32), 0).reshape(FF // D, D),
        ],
        0,
    )
    return (grad_in, matrix_grads, vector_grads)


def embed_sequences(flat_rows, vectors, token_ids, lengths):
    groups, seq_len = token_ids.shape
    key_keep = jnp.arange(seq_len)[None, :] < lengths[:, None]
    table_rows = jnp.take(flat_rows, token_ids.reshape(-1), axis=0).astype(jnp.float32)
    places = flat_rows[VOCAB : VOCAB + seq_len].astype(jnp.float32)
    embedded = (table_rows.reshape(groups, seq_len, D) + places[None] + vectors[0]).reshape(
        groups * seq_len, D
    )
    hidden_now, normed_emb, scaled_embedding = norm_rows(embedded, vectors[1], vectors[2])
    weights_set, vec_rows = layer_parts(flat_rows, vectors, 0)
    hidden_now, saved = layer_forward(hidden_now, weights_set, vec_rows, key_keep)
    layer_saves = [saved]
    first_rows = hidden_now.reshape(groups, seq_len, D)[:, 0].astype(jnp.bfloat16)
    pooled = jnp.tanh(mult(first_rows, flat_rows[VOCAB + PLEN : VOCAB + PLEN + D]) + vectors[3])
    return (pooled, (normed_emb, scaled_embedding, layer_saves, first_rows))


def encode_back(grad_pooled, pooled, flat_rows, vectors, token_ids, lengths, encoder_kept):
    normed_emb, scaled_embedding, layer_saves, first_rows = encoder_kept
    groups, seq_len = token_ids.shape
    key_keep = jnp.arange(seq_len)[None, :] < lengths[:, None]
    w_pool = flat_rows[VOCAB + PLEN : VOCAB + PLEN + D].astype(jnp.float32)
    grad_pre = grad_pooled * (1.0 - pooled * pooled)
    grad_pool = jnp.dot(first_rows.astype(jnp.float32).T, grad_pre, precision=HIGHEST)
    grad_first = jnp.dot(grad_pre, w_pool.T, precision=HIGHEST)
    grad_hidden = (
        jnp.zeros((groups, seq_len, D), jnp.float32)
        .at[:, 0]
        .set(grad_first)
        .reshape(groups * seq_len, D)
    )
    matrices = []
    vector_parts = []
    for layer_index in reversed(range(LAYERS)):
        weights_set, vec_rows = layer_parts(flat_rows, vectors, layer_index)
        grad_hidden, matrix_grads, vector_grads = layer_backward(
            grad_hidden, weights_set, vec_rows, key_keep, layer_saves[layer_index]
        )
        matrices.insert(0, matrix_grads)
        vector_parts.insert(0, vector_grads)
    grad_embed, grad_gain, grad_shift = norm_back(
        grad_hidden, normed_emb, scaled_embedding, vectors[1]
    )
    grad_table = jnp.zeros((VOCAB, D), jnp.float32).at[token_ids.reshape(-1)].add(grad_embed)
    grad_places = (
        jnp.zeros((PLEN, D), jnp.float32)
        .at[:seq_len]
        .set(jnp.sum(grad_embed.reshape(groups, seq_len, D), 0))
    )
    flat_grad = jnp.concatenate([grad_table, grad_places, grad_pool] + matrices, 0)
    head_rows = jnp.stack([jnp.sum(grad_embed, 0), grad_gain, grad_shift, jnp.sum(grad_pre, 0)])
    return (flat_grad, jnp.concatenate([head_rows] + vector_parts, 0))


def adam_step(weight, moment_one, moment_two, gradient, step_rate, decay_rate):
    moment_one = BETA_ONE * moment_one + (1.0 - BETA_ONE) * gradient
    moment_two = BETA_TWO * moment_two + (1.0 - BETA_TWO) * gradient * gradient
    update = (
        moment_one
        / (1.0 - BETA_ONE**STEP)
        / (jnp.sqrt(moment_two / (1.0 - BETA_TWO**STEP)) + EPSILON)
    )
    return (weight - step_rate * (update + decay_rate * weight), moment_one, moment_two)


def gather_all(values, axes):
    count = lax.axis_size(axes)
    copies = jnp.broadcast_to(values[None], (count,) + values.shape)
    return lax.all_to_all(copies, axes, 0, 0, tiled=True).reshape((-1,) + values.shape[1:])


def sum_all(values, axes):
    count = lax.axis_size(axes)
    copies = jnp.broadcast_to(values[None], (count,) + values.shape)
    return jnp.sum(lax.all_to_all(copies, axes, 0, 0, tiled=True), 0)


def sum_share(values, axes):
    count = lax.axis_size(axes)
    parts = lax.all_to_all(values, axes, 0, 0, tiled=True)
    return jnp.sum(parts.reshape((count, -1) + values.shape[1:]), 0)


def local(
    query_ids,
    passage_ids,
    query_lengths,
    passage_lengths,
    positive,
    prefix_lengths,
    prefix_weights,
    owners,
    weights,
    first_moments,
    second_moments,
    vectors,
    vector_first,
    vector_second,
):
    slot_count, unit_rows = (weights.shape[0], weights.shape[1])
    gathered = gather_all(weights.astype(jnp.bfloat16), "blk")
    flat_rows = jnp.take(gathered, owners, axis=0).reshape(-1, D)
    query_pooled, query_kept = embed_sequences(flat_rows, vectors, query_ids[0], query_lengths[0])
    passage_pooled, passage_kept = embed_sequences(
        flat_rows, vectors, passage_ids[0], passage_lengths[0]
    )
    all_passages = gather_all(passage_pooled.astype(jnp.bfloat16), "blk")
    prefix_masks = (jnp.arange(D)[None, :] < prefix_lengths[:, None]).astype(jnp.float32)
    prefix_scale = TEMPER * lax.rsqrt(prefix_lengths.astype(jnp.float32))
    queries = query_pooled.astype(jnp.bfloat16).astype(jnp.float32)
    passages = all_passages.astype(jnp.float32)
    masked = queries[None] * prefix_masks[:, None, :]
    logits = (
        jnp.einsum("mpd,jd->mpj", masked, passages, precision=HIGHEST) * prefix_scale[:, None, None]
    )
    counted = positive[0] >= 0
    target = (jnp.arange(passages.shape[0])[None, :] == positive[0][:, None]).astype(jnp.float32)
    running_totals = jax.nn.logsumexp(logits, -1) - jnp.sum(logits * target[None], -1)
    per_query = jnp.sum(prefix_weights[:, None] * running_totals, 0)
    loss_part = jnp.sum(jnp.where(counted, per_query, 0.0))
    count_part = jnp.sum(counted.astype(jnp.float32))
    count_total, loss_total = sum_all(jnp.stack([count_part, loss_part]), ("blk", "rep"))
    row_factor = (prefix_weights * prefix_scale / count_total)[:, None, None] * counted.astype(
        jnp.float32
    )[None, :, None]
    grad_logits = (jax.nn.softmax(logits, -1) - target[None]) * row_factor
    grad_query = jnp.sum(
        jnp.einsum("mpj,jd->mpd", grad_logits, passages, precision=HIGHEST)
        * prefix_masks[:, None, :],
        0,
    )
    grad_passage = sum_share(
        jnp.einsum("mpj,mpd->jd", grad_logits, masked, precision=HIGHEST), "blk"
    )
    flat_query, vec_query = encode_back(
        grad_query, query_pooled, flat_rows, vectors, query_ids[0], query_lengths[0], query_kept
    )
    flat_pass, vec_pass = encode_back(
        grad_passage,
        passage_pooled,
        flat_rows,
        vectors,
        passage_ids[0],
        passage_lengths[0],
        passage_kept,
    )
    vec_total = sum_all(vec_query + vec_pass, ("blk", "rep"))
    buffer = (
        jnp.zeros((lax.axis_size("blk") * slot_count, unit_rows, D), jnp.float32)
        .at[owners]
        .set((flat_query + flat_pass).reshape(-1, unit_rows, D))
    )
    vec_square = jnp.sum(vec_total * vec_total)
    reduced = sum_share(buffer, "blk")
    reduced = sum_all(reduced, "rep")
    square_sum = sum_all(jnp.sum(reduced * reduced)[None], "blk")[0]
    old_weight, old_first, old_second = (weights, first_moments, second_moments)
    slot_ids = lax.axis_index("blk") * slot_count + jnp.arange(slot_count)
    owned_mask = jnp.any(slot_ids[:, None] == owners[None, :], 1)[:, None, None]
    grad_norm = jnp.sqrt(square_sum + vec_square)
    factor = CLIP_AT / jnp.maximum(grad_norm, CLIP_AT)
    new_weight, new_first, new_second = adam_step(
        old_weight, old_first, old_second, reduced * factor, RATE, DECAY
    )
    new_weight = jnp.where(owned_mask, new_weight, old_weight)
    new_first = jnp.where(owned_mask, new_first, old_first)
    new_second = jnp.where(owned_mask, new_second, old_second)
    new_vec, new_vec_first, new_vec_second = adam_step(
        vectors, vector_first, vector_second, vec_total * factor, VECTOR_RATE, 0.0
    )
    return (
        new_weight,
        new_first,
        new_second,
        new_vec,
        new_vec_first,
        new_vec_second,
        loss_total,
        count_total,
        grad_norm,
    )


F32 = jnp.float32
BF16 = jnp.bfloat16
I32 = jnp.int32
UNIT = 128
TABLE_BLOCKS = VOCAB // UNIT
PLACE_BLOCKS = PLEN // UNIT
DENSE = PLACE_BLOCKS + (D + 4 * D + 2 * FF) // UNIT
HALF = 64
QROWS = 128
TOKENS = 2 * QROWS + 2 * PLEN
STARTS = (0, QROWS, 2 * QROWS, 2 * QROWS + PLEN)
UNITS_L = 10
L_ROWS = 4 * UNITS_L
NEVER = -1e30


def params(n_blk, small):
    return pltpu.CompilerParams(vmem_limit_bytes=(small if n_blk <= 16 else 58) << 20)


AT_POOL = PLEN
AT_Q = AT_POOL + D
AT_K = AT_Q + D
AT_V = AT_K + D
AT_O = AT_V + D
AT_UP = AT_O + D
AT_DOWN = AT_UP + FF

TAB_OWNER, TAB_RANK, TAB_SLOT, TAB_UNIT, TAB_KIND, TAB_ORDER, TAB_SORTED, TAB_ENDS, TAB_SOURCE = range(
    9
)
PIECE = 16
PIECES = 16
DENSE_CAP = 8
CLASS = DENSE // 2
HELD = DENSE_CAP // 2
AT_ASKED = DENSE_CAP // 4 * PIECE
MESSAGE_ROWS = AT_ASKED + 8

KIND_TABLE, KIND_PLACE, KIND_DENSE = 1, 2, 8

vmem = pl.BlockSpec(memory_space=pltpu.VMEM)
smem = pl.BlockSpec(memory_space=pltpu.SMEM)
hbm = pl.BlockSpec(memory_space=pl.ANY)
in_hbm = pl.BlockSpec(memory_space=pltpu.HBM)


def stay(*arrays):
    return [pltpu.with_memory_space_constraint(a, pltpu.HBM) for a in arrays]


def iota(shape, axis):
    return lax.broadcasted_iota(I32, shape, axis)


def dot_nn(a, b):
    return lax.dot_general(a, b, (((1,), (0,)), ((), ())), preferred_element_type=F32)


def dot_nt(a, b):
    return lax.dot_general(a, b, (((1,), (1,)), ((), ())), preferred_element_type=F32)


def dot_tn(a, b):
    return lax.dot_general(a, b, (((0,), (0,)), ((), ())), preferred_element_type=F32)


def split(a):
    high = a.astype(BF16)
    return high, (a - high.astype(F32)).astype(BF16)


def fine(dot, a, b):
    high, low = split(a)
    rows = a.shape[0]
    both = dot(jnp.concatenate([high, low], 0), b)
    return both[:rows] + both[rows:]


def to_column(row):
    return jnp.broadcast_to(row, (128, 128)).T[:, :1]


def token_facts(query_lengths, passage_lengths):
    lane = iota((1, TOKENS), 1)
    sequence = (
        (lane >= STARTS[1]).astype(I32)
        + (lane >= STARTS[2]).astype(I32)
        + (lane >= STARTS[3]).astype(I32)
    )
    ends = [
        STARTS[0] + query_lengths[0, 0],
        STARTS[1] + query_lengths[0, 1],
        STARTS[2] + passage_lengths[0, 0],
        STARTS[3] + passage_lengths[0, 1],
    ]
    end = jnp.where(
        sequence == 0,
        ends[0],
        jnp.where(sequence == 1, ends[1], jnp.where(sequence == 2, ends[2], ends[3])),
    )
    return sequence, lane < end


def across(values, n_blk, step):
    pairs = [(i, i // PIECES * PIECES + step(i % PIECES)) for i in range(n_blk)]
    return lax.ppermute(values, "blk", pairs)


def along_z(mine, n_blk):
    return jnp.stack(
        [mine] + [across(mine, n_blk, lambda i, k=k: (i + 4 * k) % PIECES) for k in (1, 2, 3)]
    )


def spread(first, n_blk):
    arrays = [first, lax.ppermute(first, "rep", [(0, 1), (1, 0)])]
    arrays = arrays + [across(a, n_blk, lambda i: i ^ 2) for a in arrays]
    return arrays + [across(a, n_blk, lambda i: i ^ 1) for a in arrays]


def piece_copies(me, gathered, matrices, sems):
    copies = []
    for part, array in enumerate(gathered):
        low = (me[0] % 4) ^ (part & 2) ^ (part // 4)
        odd = me[1] ^ (part % 2)
        for k in range(4):
            p = low + (me[0] % PIECES // 4 * 4 + 4 * (4 - k)) % PIECES
            row = pl.multiple_of((p % 8) * PIECE, PIECE)
            lane = pl.multiple_of((p // 8) * 128, 128)
            copies.append(
                pltpu.make_async_copy(
                    array.at[k],
                    matrices.at[:, odd, pl.ds(row, PIECE), pl.ds(lane, 128)],
                    sems.at[4 * part + k],
                )
            )
    return copies


def rows_at(matrices, tab, start, stop):
    blocks = []
    for b in range(start // UNIT, stop // UNIT):
        order = tab[b, TAB_ORDER]
        blocks.append(matrices[order // 2, order % 2])
    return jnp.concatenate(blocks, 0)


def owner_of(slot, slots, n_blk):
    owner = jnp.zeros(slot.shape, I32)
    for k in range(1, n_blk):
        owner = owner + (slot >= k * slots).astype(I32)
    return owner


def request_kernel(
    slots, n_blk, cap, take_cap, owners, me, positive, query_lengths, passage_lengths, owner_line,
    query_ids, passage_ids, weights, message, where_row, tab, ids, owner_row, asked, loaded, sems,
):
    n_rep = 2
    n_dest = n_blk * n_rep
    n_units = owners.shape[0]
    start = me[0] * slots

    def take(b, carry):
        before, have = carry
        slot = owners[n_units - DENSE + b]
        inside = slot - start
        mine = (inside >= 0) & (inside < slots)

        @pl.when(mine & (have // 2 % 2 == me[1]) & (have < DENSE_CAP))
        def _():
            spot = have // 4 * 2 + have % 2
            pltpu.make_async_copy(weights.at[inside], loaded.at[spot], sems.at[spot]).start()

        return before + (slot < start).astype(I32), have + mine.astype(I32)

    before, have = lax.fori_loop(0, DENSE, take, (0, 0))
    owner_row[...] = jnp.full(owner_row.shape, -1, I32)
    owner_row[:, :n_units] = owner_line[...].reshape(1, n_units)
    every_slot = owner_row[...]
    wide = every_slot.shape[1]
    base = n_units - DENSE
    low = base // 128 * 128
    rolled = pltpu.roll(every_slot[:, low:], wide - low - (base - low), 1)[:, :128]
    dense_owner = owner_of(rolled, slots, n_blk)
    owner_column = to_column(dense_owner)[:32]
    slot_column = to_column(rolled)[:32]
    block_row = iota((32, 128), 1)
    block_column = iota((32, 128), 0)
    same = (owner_column == dense_owner) & (block_row < block_column) & (block_row < DENSE)
    rank = jnp.sum(same.astype(I32), 1, keepdims=True)
    at = block_row * UNIT
    need = jnp.where(block_row < PLACE_BLOCKS, 0, jnp.where((at >= AT_K) & (at < AT_O), 2, 1))
    unit = jnp.sum(jnp.where(same, need, 0), 1, keepdims=True)
    lower = (dense_owner < owner_column) & (block_row < DENSE)
    order = rank + jnp.sum(lower.astype(I32), 1, keepdims=True)
    is_dense = (iota((32, 1), 0) >= PLACE_BLOCKS) & (iota((32, 1), 0) < DENSE)
    at = iota((32, 1), 0) * UNIT
    needs = jnp.where((at >= AT_K) & (at < AT_O), 2, 1)
    crowded = jnp.max(
        (
            ((rank >= DENSE_CAP) & (iota((32, 1), 0) < DENSE))
            | (is_dense & (unit + needs > UNITS_L))
        ).astype(I32)
    )
    which = iota((32, wide), 1)
    code = jnp.where(
        which < TABLE_BLOCKS,
        KIND_TABLE,
        jnp.where(
            which < TABLE_BLOCKS + PLACE_BLOCKS, KIND_PLACE + which - TABLE_BLOCKS, KIND_DENSE
        ),
    )
    here = (every_slot == me[0] * slots + iota((32, wide), 0)) & (which < n_units)
    kind = jnp.sum(jnp.where(here, code, 0), 1, keepdims=True)
    sort = jnp.where(
        kind == KIND_TABLE,
        0,
        jnp.where(kind == KIND_DENSE, 1, jnp.where(kind >= KIND_PLACE, 2, 3)),
    )
    sort = jnp.where(iota((32, 1), 0) < slots, sort, 4)

    def to_row(column):
        wide = jnp.concatenate([column, jnp.full((96, 1), 5, I32)], 0)
        return jnp.broadcast_to(wide, (128, 128)).T[:1]

    capped = jnp.minimum(rank, DENSE_CAP - 1)
    source = (2 * owner_column + capped // 2 % 2) * 2 + capped // 4
    order = jnp.minimum(order, DENSE - 1)
    by_order = jnp.sum(
        jnp.where((to_row(order) == block_column) & (block_row < DENSE), to_row(source), 0),
        1,
        keepdims=True,
    )
    sort_row = to_row(sort)
    ahead = (sort_row < sort) | ((sort_row == sort) & (block_row < block_column))
    place_row = to_row(jnp.sum(ahead.astype(I32), 1, keepdims=True))
    sorted_slot = jnp.sum(
        jnp.where((place_row == block_column) & (block_row < 32), block_row, 0), 1, keepdims=True
    )
    ends = jnp.sum((sort_row <= iota((32, 1), 0)).astype(I32), 1, keepdims=True)
    entry = block_row
    tab[...] = jnp.where(
        entry == TAB_OWNER,
        owner_column,
        jnp.where(
            entry == TAB_RANK,
            jnp.minimum(rank, DENSE_CAP - 1),
            jnp.where(
                entry == TAB_SLOT,
                slot_column - owner_column * slots,
                jnp.where(
                    entry == TAB_UNIT,
                    jnp.minimum(unit, UNITS_L - 2),
                    jnp.where(
                        entry == TAB_KIND,
                        kind,
                        jnp.where(
                            entry == TAB_ORDER,
                            order,
                            jnp.where(
                                entry == TAB_SORTED,
                                sorted_slot,
                                jnp.where(entry == TAB_ENDS, ends, by_order),
                            ),
                        ),
                    ),
                ),
            ),
        ),
    )

    ids[:, 0:QROWS] = query_ids[0:1]
    ids[:, QROWS : 2 * QROWS] = query_ids[1:2]
    ids[:, STARTS[2] : STARTS[3]] = passage_ids[0:1]
    ids[:, STARTS[3] :] = passage_ids[1:2]
    token = ids[...]
    _, live = token_facts(query_lengths, passage_lengths)
    lane = iota((1, TOKENS), 1)
    block = token // UNIT
    slot = jnp.zeros((1, TOKENS), I32)
    table_rows = -(-TABLE_BLOCKS // 128) * 128
    for at in range(0, table_rows, 128):
        column = to_column(owner_row[:, at : at + 128])
        hit = (iota((128, TOKENS), 0) + at) == block
        slot = slot + jnp.sum(jnp.where(hit, column, 0), 0, keepdims=True)
    owner = owner_of(slot, slots, n_blk)
    inside = slot - owner * slots
    row = token - block * UNIT
    upper = (row >= HALF).astype(I32)
    dest = owner * n_rep + upper
    local_row = inside * HALF + row - upper * HALF
    token = jnp.where(live, token, -1)
    first_at = []
    columns = [to_column(token[:, at : at + 128]) for at in range(0, TOKENS, 128)]
    for to_at in range(0, TOKENS, 128):
        best = jnp.full((128, 128), TOKENS, I32)
        for at in range(0, to_at + 128, 128):
            same = columns[at // 128] == token[:, to_at : to_at + 128]
            best = jnp.minimum(best, jnp.where(same, iota((128, 128), 0) + at, TOKENS))
        first_at.append(jnp.min(best, 0, keepdims=True))
    first_at = jnp.concatenate(first_at, 1)
    first = live & (first_at == lane)
    chosen = ((iota((n_dest, TOKENS), 0) == dest) & first).astype(F32)
    chosen_low = chosen.astype(BF16)
    seen = []
    for to_at in range(0, TOKENS, 256):
        above = to_at + 256
        earlier = iota((above, 256), 0) < first_at[:, to_at:above]
        seen.append(dot_nn(chosen_low[:, :above], earlier.astype(F32).astype(BF16)))
    seen = jnp.concatenate(seen, 1)
    to = iota((n_dest, TOKENS), 0)
    rank = jnp.sum(jnp.where(to == dest, seen, 0.0), 0, keepdims=True).astype(I32)
    turn = jnp.sum(jnp.where(to // n_rep == owner, seen, 0.0), 0, keepdims=True).astype(I32)
    source = owner * n_rep + me[1]
    where_row[0:1] = jnp.where(live & (turn < take_cap), owner * take_cap + turn, -1)
    where_row[1:2] = jnp.where(live & (rank < cap), dest * cap + rank, -1)
    over = jnp.max((live & ((rank >= cap) | (turn >= take_cap))).astype(I32))

    def listed(dest, spot, code):
        high = code // 32
        low = code - high * 32
        chosen = ((to == dest) & first).astype(F32)
        both = jnp.concatenate([chosen * high.astype(F32), chosen * low.astype(F32)], 0)
        spread = (iota((128, TOKENS), 0) == spot).astype(F32).astype(BF16)
        both = dot_nt(both.astype(BF16), spread)
        return both[:n_dest], both[n_dest:]

    take_high, take_low = listed(source, turn, inside * UNIT + row + 1)
    sent_high, sent_low = listed(dest, rank, local_row + 1)
    flag = jnp.maximum(over, crowded)
    column_of = iota((1, 128), 1)
    marks = jnp.where(
        column_of == 0,
        positive[0, 0],
        jnp.where(column_of == 1, positive[0, 1], jnp.where(column_of == 2, flag, 0)),
    ).astype(F32)
    asked[...] = jnp.zeros(asked.shape, F32)
    for i, part in enumerate(
        (take_high, take_low, jnp.broadcast_to(marks, (n_dest, 128)), sent_high, sent_low)
    ):
        asked[pl.ds(i, n_dest, stride=8), :] = part
    message[:, AT_ASKED:, :] = asked[: 8 * n_dest].reshape(n_dest, 8, 128).astype(BF16)
    for spot in range(HELD):
        present = spot // 2 * 4 + 2 * me[1] + spot % 2 < have

        @pl.when(present)
        def _():
            pltpu.make_async_copy(weights.at[0], loaded.at[spot], sems.at[spot]).wait()

        @pl.when(jnp.logical_not(present))
        def _():
            loaded[spot] = jnp.zeros((UNIT, D), F32)

    for odd in range(2):
        for c in range(DENSE_CAP // 4):
            whole = loaded[2 * c + (odd + before) % 2].astype(BF16)
            for s in range(n_blk):
                p = s % PIECES
                message[2 * s + odd, PIECE * c : PIECE * (c + 1)] = whole[
                    PIECE * (p % 8) : PIECE * (p % 8 + 1), 128 * (p // 8) : 128 * (p // 8 + 1)
                ]


def request(owners, me, positive, query_lengths, passage_lengths, query_ids, passage_ids, weights, n_blk, cap, take_cap):
    slots = weights.shape[0]
    n_dest = 2 * n_blk
    n_units = owners.shape[0]
    owner_row = owners
    return pl.pallas_call(
        partial(request_kernel, slots, n_blk, cap, take_cap),
        out_shape=(
            jax.ShapeDtypeStruct((n_dest, MESSAGE_ROWS, 128), BF16),
            jax.ShapeDtypeStruct((2, TOKENS), I32),
            jax.ShapeDtypeStruct((32, 128), I32),
        ),
        in_specs=[smem] * 5 + [vmem] * 3 + [in_hbm],
        out_specs=(vmem, vmem, vmem),
        scratch_shapes=[
            pltpu.VMEM((1, TOKENS), I32),
            pltpu.VMEM((1, -(-n_units // 128) * 128), I32),
            pltpu.VMEM((8 * n_dest + 8, 128), F32),
            pltpu.VMEM((HELD, UNIT, D), F32),
            pltpu.SemaphoreType.DMA((HELD,)),
        ],
        compiler_params=params(n_blk, 12),
        name="request",
    )(owners, me, positive, query_lengths, passage_lengths, owner_row, query_ids, passage_ids, *stay(weights))


def collect_kernel(tab, me, message, mine_out):
    for k in range(CLASS):
        source = tab[2 * k + me[1], TAB_SOURCE]
        spot = pl.multiple_of(source % 2 * PIECE, PIECE)
        mine_out[k] = message[source // 2, pl.ds(spot, PIECE), :]


def collect(tab, me, message):
    return pl.pallas_call(
        collect_kernel,
        out_shape=jax.ShapeDtypeStruct((CLASS, PIECE, 128), BF16),
        in_specs=[smem, smem, vmem],
        out_specs=vmem,
        compiler_params=params(message.shape[0] // 2, 2),
        name="collect",
    )(tab, me, message)


def fetch_kernel(slots, cap, take_cap, me, message, weights, rows_out, asked_out, lists, wanted, held, table, sem):
    n_dest = message.shape[0]
    copy = pltpu.make_async_copy(weights, held, sem)
    copy.start()
    n_blk = n_dest // 2
    lists[: 8 * n_dest] = message[:, AT_ASKED:, :].astype(F32).reshape(8 * n_dest, 128)
    mine = 8 * me[1]
    wanted[...] = jnp.zeros(wanted.shape, I32)
    wanted[:n_blk] = (
        lists[pl.ds(mine, n_blk, stride=16), :] * 32.0
        + lists[pl.ds(mine + 1, n_blk, stride=16), :]
        - 1.0
    ).astype(I32)
    every = [lists[pl.ds(i, n_dest, stride=8), :] for i in (2, 3, 4)]
    column_of = iota((n_dest, 128), 1)
    row = jnp.where(column_of < cap, every[1] * 32.0 + every[2] - 1.0, 0.0)
    for i in range(3):
        row = jnp.where(column_of == 124 + i, every[0][:, i : i + 1], row)
    asked_out[...] = row.astype(I32)
    wide = table.shape[0]
    columns = wanted[...].T
    copy.wait()
    table[...] = held[...].reshape(wide, D).astype(BF16)
    row_of = iota((take_cap, wide), 1)
    for at in range(0, n_dest // 2, 4):
        hot = jnp.concatenate(
            [
                (row_of == columns[:take_cap, s : s + 1]).astype(F32)
                for s in range(at, at + 4)
            ],
            0,
        ).astype(BF16)
        rows_out[at * take_cap : (at + 4) * take_cap] = dot_nn(hot, table[...]).astype(BF16)


def fetch(me, message, weights, cap, take_cap):
    slots = weights.shape[0]
    n_dest = message.shape[0]
    return pl.pallas_call(
        partial(fetch_kernel, slots, cap, take_cap),
        out_shape=(
            jax.ShapeDtypeStruct((n_dest // 2 * take_cap, D), BF16),
            jax.ShapeDtypeStruct((n_dest, 128), I32),
        ),
        in_specs=[smem, vmem, in_hbm],
        out_specs=(vmem, vmem),
        scratch_shapes=[
            pltpu.VMEM((8 * n_dest + 16, 128), F32),
            pltpu.VMEM((-(-n_dest // 256) * 128, 128), I32),
            pltpu.VMEM(weights.shape, F32),
            pltpu.VMEM((slots * UNIT, D), BF16),
            pltpu.SemaphoreType.DMA,
        ],
        compiler_params=params(n_dest // 2, 20),
        name="fetch",
    )(me, message, *stay(weights))


ST_POOLED, ST_C, ST_N2, ST_N1, ST_H, ST_O, ST_Q, ST_X0 = range(0, 64, 8)
ST_KQ, ST_B, ST_U, ST_A, ST_I1, ST_I2 = 64, 96, 128, 160, 192, 200
ST_ROWS = 208


def forward_kernel(
    tab, me, query_lengths, passage_lengths, positive, rows, where_row, vectors, g0, g1, g2, g3,
    g4, g5, g6, g7, emb_out, low_out, normed_out, scale_out, probs_out, state, matrices, embedded,
    sems,
):
    copies = piece_copies(me, (g0, g1, g2, g3, g4, g5, g6, g7), matrices, sems)
    for copy in copies:
        copy.start()
    taken = rows.shape[0]
    for at in range(0, TOKENS, 256):
        column = jnp.concatenate(
            [to_column(where_row[0:1, i : i + 128]) for i in (at, at + 128)], 0
        )
        hot = (iota((256, taken), 1) == column).astype(F32).astype(BF16)
        embedded[at : at + 256] = dot_nn(hot, rows[...])
    for copy in copies:
        copy.wait()
    shift = vectors[0:1]
    for start, length in zip(STARTS, (QROWS, QROWS, PLEN, PLEN)):
        e = embedded[start : start + length] + rows_at(matrices, tab, 0, length).astype(F32) + shift
        centred = e - jnp.mean(e, -1, keepdims=True)
        scale = lax.rsqrt(jnp.mean(centred * centred, -1, keepdims=True) + NORM_EPS)
        normed = centred * scale
        normed_out[start : start + length] = normed
        scale_out[start : start + length] = jnp.broadcast_to(scale, (length, 128))
        x = normed * vectors[1:2] + vectors[2:3]
        embedded[start : start + length] = x
        low_out[start : start + length] = x.astype(BF16)
    x0 = jnp.concatenate(
        [embedded[s : s + 1] for s in STARTS] + [jnp.zeros((4, D), F32)], 0
    )
    x0_low = x0.astype(BF16)
    q = (dot_nn(x0_low, rows_at(matrices, tab, AT_Q, AT_K)) + vectors[4:5]).astype(BF16)
    head_of = iota((8, D), 1) // HALF
    q_heads = jnp.concatenate(
        [jnp.where(head_of == h, q.astype(F32), 0.0) for h in range(HEADS)], 0
    ).astype(BF16)
    kq = dot_nt(q_heads, rows_at(matrices, tab, AT_K, AT_V)) * (D // HEADS) ** (-0.5)
    low = low_out[...]
    scores = fine(dot_nt, kq, low)
    sequence, live = token_facts(query_lengths, passage_lengths)
    valid = ((iota((32, TOKENS), 0) & 7) == sequence) & live
    scores = jnp.where(valid, scores, NEVER)
    top = jnp.max(scores, -1, keepdims=True)
    weight = jnp.where(valid, jnp.exp(scores - top), 0.0)
    total = jnp.sum(weight, -1, keepdims=True)
    probs = weight / jnp.where(total > 0.0, total, 1.0)
    probs_out[...] = probs
    mixed = dot_nn(probs.astype(BF16), low)
    valued = fine(dot_nn, mixed, rows_at(matrices, tab, AT_V, AT_O))
    blended = jnp.zeros((8, D), F32)
    for h in range(HEADS):
        blended = blended + jnp.where(head_of == h, valued[8 * h : 8 * h + 8], 0.0)
    real = iota((8, D), 0) < 4
    blended = jnp.where(real, blended + vectors[5:6], 0.0).astype(BF16)
    summed = x0 + dot_nn(blended, rows_at(matrices, tab, AT_O, AT_UP)) + vectors[6:7]
    h0, n1, i1 = norm_rows(summed, vectors[8:9], vectors[9:10])
    h_low = h0.astype(BF16)
    bias_up = jnp.concatenate([vectors[12 + i : 13 + i] for i in range(FF // D)], 1)
    u = dot_nt(h_low, rows_at(matrices, tab, AT_UP, AT_DOWN)) + bias_up
    a = (0.5 * u * (1.0 + lax.erf(u * (0.5**0.5)))).astype(BF16)
    second = h0 + dot_nn(a, rows_at(matrices, tab, AT_DOWN, DENSE * UNIT)) + vectors[7:8]
    x, n2, i2 = norm_rows(second, vectors[10:11], vectors[11:12])
    c = x.astype(BF16)
    pooled = jnp.tanh(dot_nn(c, rows_at(matrices, tab, AT_POOL, AT_Q)) + vectors[3:4])
    row8 = iota((8, 128), 0)
    sent = jnp.concatenate(
        [
            jnp.where(real, pooled, 0.0),
            jnp.where(
                row8 == 0,
                positive[0, 0].astype(F32),
                jnp.where(row8 == 1, positive[0, 1].astype(F32), -1.0),
            ),
        ],
        1,
    )
    n_blk = emb_out.shape[0] // 8
    emb_out[...] = jnp.concatenate([sent] * n_blk, 0).astype(BF16)
    state[ST_POOLED : ST_POOLED + 8] = pooled
    state[ST_C : ST_C + 8] = c.astype(F32)
    state[ST_N2 : ST_N2 + 8] = n2
    state[ST_N1 : ST_N1 + 8] = n1
    state[ST_H : ST_H + 8] = h_low.astype(F32)
    state[ST_O : ST_O + 8] = blended.astype(F32)
    state[ST_Q : ST_Q + 8] = q.astype(F32)
    state[ST_X0 : ST_X0 + 8] = x0_low.astype(F32)
    state[ST_KQ : ST_KQ + 32] = kq
    state[ST_B : ST_B + 32] = mixed
    for i in range(FF // D):
        state[ST_U + 8 * i : ST_U + 8 * i + 8] = u[:, i * D : (i + 1) * D]
        state[ST_A + 8 * i : ST_A + 8 * i + 8] = a[:, i * D : (i + 1) * D].astype(F32)
    state[ST_I1 : ST_I1 + 8] = jnp.broadcast_to(i1, (8, D))
    state[ST_I2 : ST_I2 + 8] = jnp.broadcast_to(i2, (8, D))


def forward(tab, me, query_lengths, passage_lengths, positive, rows, where_row, vectors, gathered, n_blk):
    return pl.pallas_call(
        forward_kernel,
        out_shape=(
            jax.ShapeDtypeStruct((n_blk * 8, D + 128), BF16),
            jax.ShapeDtypeStruct((TOKENS, D), BF16),
            jax.ShapeDtypeStruct((TOKENS, D), F32),
            jax.ShapeDtypeStruct((TOKENS, 128), F32),
            jax.ShapeDtypeStruct((32, TOKENS), F32),
            jax.ShapeDtypeStruct((ST_ROWS, D), F32),
            jax.ShapeDtypeStruct((CLASS, 2, UNIT, D), BF16),
        ),
        in_specs=[smem] * 5 + [vmem] * 3 + [hbm] * 8,
        out_specs=(vmem,) * 7,
        scratch_shapes=[
            pltpu.VMEM((TOKENS, D), F32),
            pltpu.SemaphoreType.DMA((2 * PIECES,)),
        ],
        compiler_params=params(n_blk, 12),
        name="forward",
    )(
        tab, me, query_lengths, passage_lengths, positive, rows, where_row, vectors,
        *stay(*gathered[:4]), *gathered[4:],
    )


def news_rows(n_dest):
    return 2 * place_rows(n_dest) + 8


def place_rows(n_dest):
    return max(PLEN // n_dest, 16)


def payload_rows(n_dest, cap):
    at_place = 2 * cap
    at_left = at_place + 2 * place_rows(n_dest)
    at_right = at_left + L_ROWS
    return at_place, at_left, at_right, at_right + 32


def backward_kernel(
    cap, tab, me, prefix_lengths, prefix_weights, emb, message, where_row, low_in, normed, scale,
    probs_in, state, vectors, matrices, payload, loss_out, count_out,
    received, grad_emb, dx, left,
):
    n_blk = emb.shape[0] // 8
    n_dest = 2 * n_blk
    for i in range(3):
        received[i * n_blk * 8 : (i + 1) * n_blk * 8] = emb[:, 128 * i : 128 * i + 128].astype(F32)

    def every(k):
        return jnp.concatenate(
            [received[pl.ds(i * n_blk * 8 + k, n_blk, stride=8), :] for i in range(3)], 1
        )

    queries = jnp.concatenate([every(0), every(1)], 0)
    passages = jnp.concatenate([every(2), every(3)], 0)[:, :D].astype(BF16)
    wanted = queries[:, D : D + 1].astype(I32)
    queries = queries[:, :D]
    size = 2 * n_blk
    counted = wanted >= 0
    counted_f = counted.astype(F32)
    column = iota((size, size), 1)
    target = (column == (wanted & 1) * n_blk + wanted // 2) & counted
    marks = message[...]
    lane = iota(marks.shape, 1)
    count = jnp.sum((((lane == 124) | (lane == 125)) & (marks >= 0)).astype(F32))
    count_out[0, 0] = count
    n_pre = prefix_lengths.shape[0]
    prefix_of = iota((n_pre * size, 1), 0) // size
    prefix = jnp.zeros((n_pre * size, 1), I32)
    share = jnp.zeros((n_pre * size, 1), F32)
    for k in range(n_pre):
        prefix = jnp.where(prefix_of == k, prefix_lengths[k], prefix)
        share = jnp.where(prefix_of == k, prefix_weights[k], share)
    temper = TEMPER * lax.rsqrt(prefix.astype(F32))
    mask = iota((n_pre * size, D), 1) < prefix
    masked = jnp.where(mask, jnp.concatenate([queries] * n_pre, 0), 0.0).astype(BF16)
    logits = dot_nt(masked, passages) * temper
    targets = jnp.concatenate([target.astype(F32)] * n_pre, 0)
    counts = jnp.concatenate([counted_f] * n_pre, 0)
    top = jnp.max(logits, -1, keepdims=True)
    weight = jnp.exp(logits - top)
    total = jnp.sum(weight, -1, keepdims=True)
    hit = jnp.sum(logits * targets, -1, keepdims=True)
    losses = share * (top + jnp.log(total) - hit) * counts
    grad = (weight / total - targets) * (counts * (share / count) * temper)
    high, lower = split(grad)
    spread_queries = jnp.where(mask, dot_nn(high, passages) + dot_nn(lower, passages), 0.0)
    d_queries = spread_queries[:size]
    for k in range(1, n_pre):
        d_queries = d_queries + spread_queries[k * size : (k + 1) * size]
    d_passages = dot_tn(high, masked) + dot_tn(lower, masked)
    loss_out[0, 0] = jnp.sum(losses)
    grad_emb[:size] = d_queries
    grad_emb[size : 2 * size] = d_passages
    grad_pooled = jnp.concatenate(
        [grad_emb[pl.ds(me[0] + i * n_blk, 1), :] for i in range(4)]
        + [jnp.zeros((4, D), F32)],
        0,
    )

    def kept_rows(at, rows=8):
        return state[at : at + rows]

    pooled = kept_rows(ST_POOLED)
    d_pre = grad_pooled * (1.0 - pooled * pooled)
    d_c = fine(dot_nt, d_pre, rows_at(matrices, tab, AT_POOL, AT_Q))
    n2 = kept_rows(ST_N2)
    d_second, d_g2, d_s2 = norm_back(d_c, n2, kept_rows(ST_I2), vectors[10:11])
    down_low = d_second.astype(BF16)
    d_a = dot_nt(down_low, rows_at(matrices, tab, AT_DOWN, DENSE * UNIT))
    u = jnp.concatenate([kept_rows(ST_U + 8 * i) for i in range(FF // D)], 1)
    slope = 0.5 * (1.0 + lax.erf(u * (0.5**0.5))) + u * jnp.exp(-0.5 * u * u) * (
        0.3989422804014327
    )
    up_low = (d_a * slope).astype(BF16)
    d_h = d_second + dot_nn(up_low, rows_at(matrices, tab, AT_UP, AT_DOWN))
    d_summed, d_g1, d_s1 = norm_back(d_h, kept_rows(ST_N1), kept_rows(ST_I1), vectors[8:9])
    branch_low = d_summed.astype(BF16)
    d_o = dot_nt(branch_low, rows_at(matrices, tab, AT_O, AT_UP)).astype(BF16)
    head_of = iota((8, D), 1) // HALF
    o_heads = jnp.concatenate(
        [jnp.where(head_of == h, d_o.astype(F32), 0.0) for h in range(HEADS)], 0
    ).astype(BF16)
    vo = dot_nt(o_heads, rows_at(matrices, tab, AT_V, AT_O))
    low = low_in[...]
    probs = probs_in[...]
    d_probs = fine(dot_nt, vo, low)
    d_scores = probs * (d_probs - jnp.sum(d_probs * probs, -1, keepdims=True))
    score_low = d_scores.astype(BF16)
    mixed_score = dot_nn(score_low, low)
    keyed = fine(dot_nn, mixed_score, rows_at(matrices, tab, AT_K, AT_V))
    d_q = jnp.zeros((8, D), F32)
    for h in range(HEADS):
        d_q = d_q + jnp.where(head_of == h, keyed[8 * h : 8 * h + 8], 0.0)
    d_q_low = (d_q * (D // HEADS) ** (-0.5)).astype(BF16)
    d_x0 = d_summed + dot_nt(d_q_low, rows_at(matrices, tab, AT_Q, AT_K))
    kq = kept_rows(ST_KQ, 32)
    vo_high, vo_low = split(vo)
    kq_high, kq_low = split(kq)
    probs_low = probs.astype(BF16)
    dx[...] = dot_tn(
        jnp.concatenate([probs_low, score_low, probs_low, score_low], 0),
        jnp.concatenate([vo_high, kq_high, vo_low, kq_low], 0),
    )
    for i, start in enumerate(STARTS):
        dx[start : start + 1] = dx[start : start + 1] + d_x0[i : i + 1]
    d_gain = jnp.zeros((1, D), F32)
    d_shift = jnp.zeros((1, D), F32)
    d_type = jnp.zeros((1, D), F32)
    for start in range(0, TOKENS, 256):
        incoming = dx[start : start + 256]
        n = normed[start : start + 256]
        d_gain = d_gain + jnp.sum(incoming * n, 0, keepdims=True)
        d_shift = d_shift + jnp.sum(incoming, 0, keepdims=True)
        dn = incoming * vectors[1:2]
        inner = (
            dn - jnp.mean(dn, -1, keepdims=True) - n * jnp.mean(dn * n, -1, keepdims=True)
        )
        de = inner * scale[start : start + 256, :1]
        d_type = d_type + jnp.sum(de, 0, keepdims=True)
        dx[start : start + 256] = de
    de_low = dx[...].astype(BF16)
    at_place, at_left, at_right, n_rows = payload_rows(n_dest, cap)
    per = 8
    step = per * cap
    for at in range(0, n_dest * cap, step):
        hot = ((iota((step, TOKENS), 0) + at) == where_row[1:2]).astype(F32).astype(BF16)
        summed = dot_nn(hot, de_low).astype(BF16)
        for i in range(per):
            d = at // cap + i
            if d < n_dest:
                payload[d, :cap] = summed[i * cap : (i + 1) * cap, :128]
                payload[d, cap : 2 * cap] = summed[i * cap : (i + 1) * cap, 128:]
    spots = dx[STARTS[2] : STARTS[3]] + dx[STARTS[3] :]
    dx[STARTS[2] : STARTS[3]] = spots
    dx[STARTS[2] : STARTS[2] + QROWS] = (
        dx[STARTS[2] : STARTS[2] + QROWS] + dx[:QROWS] + dx[QROWS : 2 * QROWS]
    )
    pr = place_rows(n_dest)
    share = PLEN // n_dest
    for d in range(n_dest):
        spot = dx[STARTS[2] + d * share : STARTS[2] + (d + 1) * share]
        if share < pr:
            spot = jnp.concatenate([spot, jnp.zeros((pr - share, D), F32)], 0)
        payload[d, at_place : at_place + pr] = spot[:, :128].astype(BF16)
        payload[d, at_place + pr : at_place + 2 * pr] = spot[:, 128:].astype(BF16)
    left[...] = jnp.zeros(left.shape, F32)
    up_f = up_low.astype(F32)

    def put(b, r, unit, values):
        spot = (tab[b, TAB_OWNER] * 2 + r) * L_ROWS + (tab[b, TAB_UNIT] + unit) * 4
        for i in range(4):
            left[pl.ds(spot + i, 1), :] = values[i : i + 1]

    for b in range(PLACE_BLOCKS, DENSE):
        at = b * UNIT
        if AT_K <= at < AT_O:
            heads = mixed_score if at < AT_V else kept_rows(ST_B, 32)
            off = (at - AT_K) % D
            for r in range(2):
                for j in range(2):
                    h = 2 * r + j
                    put(b, r, j, heads[8 * h : 8 * h + 4, off : off + UNIT])
            continue
        if at < AT_Q:
            values, off = kept_rows(ST_C), at - AT_POOL
        elif at < AT_K:
            values, off = kept_rows(ST_X0), at - AT_Q
        elif at < AT_UP:
            values, off = kept_rows(ST_O), at - AT_O
        elif at < AT_DOWN:
            values, off = up_f, at - AT_UP
        else:
            off = (at - AT_DOWN) % D
            values = kept_rows(ST_A + 8 * ((at - AT_DOWN) // D))
        for r in range(2):
            put(b, r, 0, values[:4, off : off + UNIT])
    d_vectors = jnp.concatenate(
        [
            d_type,
            d_gain,
            d_shift,
            jnp.sum(d_pre, 0, keepdims=True),
            jnp.sum(d_q_low.astype(F32), 0, keepdims=True),
            jnp.sum(d_o.astype(F32), 0, keepdims=True),
            jnp.sum(branch_low.astype(F32), 0, keepdims=True),
            jnp.sum(down_low.astype(F32), 0, keepdims=True),
            d_g1[None],
            d_s1[None],
            d_g2[None],
            d_s2[None],
        ]
        + [
            jnp.sum(up_f[:, i * D : (i + 1) * D], 0, keepdims=True) for i in range(FF // D)
        ],
        0,
    )
    scaled_q = kept_rows(ST_Q) * (D // HEADS) ** (-0.5)
    right = jnp.concatenate(
        [
            v.astype(F32)[:4]
            for v in (d_pre, d_q_low, scaled_q, d_o, branch_low, kept_rows(ST_H), down_low)
        ],
        0,
    )
    for d in range(n_dest):
        payload[d, at_left:at_right] = left[d * L_ROWS : (d + 1) * L_ROWS].astype(BF16)
        r = d % 2
        if d < 32:
            share_vec = d_vectors[d // 2 : d // 2 + 1, r * 128 : (r + 1) * 128]
        else:
            share_vec = jnp.zeros((1, 128), F32)
        payload[d, at_right:n_rows] = jnp.concatenate(
            [right[:, r * 128 : (r + 1) * 128], share_vec, jnp.zeros((3, 128), F32)], 0
        ).astype(BF16)


def backward(tab, me, prefix_lengths, prefix_weights, emb, message, where_row, low, normed, scale, probs, state, vectors, matrices, cap):
    n_dest = message.shape[0]
    n_rows = payload_rows(n_dest, cap)[-1]
    return pl.pallas_call(
        partial(backward_kernel, cap),
        out_shape=(
            jax.ShapeDtypeStruct((n_dest, n_rows, 128), BF16),
            jax.ShapeDtypeStruct((1, 1), F32),
            jax.ShapeDtypeStruct((1, 1), F32),
        ),
        in_specs=[smem] * 4 + [vmem] * 10,
        out_specs=(vmem, smem, smem),
        scratch_shapes=[
            pltpu.VMEM((emb.shape[0] * 3 + 8, 128), F32),
            pltpu.VMEM((emb.shape[0], D), F32),
            pltpu.VMEM((TOKENS, D), F32),
            pltpu.VMEM((n_dest * L_ROWS, 128), F32),
        ],
        compiler_params=params(n_dest // 2, 16),
        name="backward",
    )(tab, me, prefix_lengths, prefix_weights, emb, message, where_row, low, normed, scale, probs, state, vectors, matrices)


def reduce_kernel(slots, cap, tab, me, loss, asked, payload, reduced, news, total, row_grads, left, right):
    n_dest = payload.shape[0]
    at_place, at_left, at_right, n_rows = payload_rows(n_dest, cap)
    for d in range(n_dest):
        row_grads[d * cap : (d + 1) * cap, :128] = payload[d, :cap]
        row_grads[d * cap : (d + 1) * cap, 128:] = payload[d, cap : 2 * cap]
        left[d * L_ROWS : (d + 1) * L_ROWS] = payload[d, at_left:at_right].astype(F32)
        right[d * 32 : (d + 1) * 32] = payload[d, at_right:n_rows].astype(F32)
    grads = row_grads[...]
    filled = slots * HALF
    chunk = filled // 4
    for at in range(0, filled, chunk):
        hot = ((iota((chunk, n_dest * cap), 0) + at) == asked[...]).astype(F32).astype(BF16)
        total[at : at + chunk] = dot_nn(hot, grads)
    mine = me[0]
    odd = me[1]
    column = iota((n_dest * 4, 128), 1)

    def rows_of(ref, start, stride):
        return jnp.concatenate(
            [ref[pl.ds(start + q, n_dest, stride=stride), :] for q in range(4)], 0
        ).astype(BF16)

    for b in range(PLACE_BLOCKS, DENSE):
        at = b * UNIT
        if at < AT_Q:
            m = 0
        elif at < AT_UP:
            m = 1 + (at - AT_Q) // D
        elif at < AT_DOWN:
            m = 5
        else:
            m = 6

        @pl.when(tab[b, TAB_OWNER] == mine)
        def _():
            unit = tab[b, TAB_UNIT] * 4
            pull = rows_of(right, m * 4, 32)
            if AT_K <= at < AT_O:
                grad = dot_tn(
                    rows_of(left, unit, L_ROWS), jnp.where(column < HALF, pull, 0).astype(BF16)
                ) + dot_tn(
                    rows_of(left, unit + 4, L_ROWS),
                    jnp.where(column < HALF, 0, pull).astype(BF16),
                )
            else:
                grad = dot_tn(rows_of(left, unit, L_ROWS), pull)
            spot = pl.multiple_of(tab[b, TAB_SLOT] * HALF, HALF)
            total[pl.ds(spot, HALF), :128] = grad[:HALF]
            total[pl.ds(spot, HALF), 128:] = grad[HALF:]

    pr = place_rows(n_dest)
    spots_low = jnp.zeros((pr, 128), F32)
    spots_high = jnp.zeros((pr, 128), F32)
    for d in range(n_dest):
        spots_low = spots_low + payload[d, at_place : at_place + pr].astype(F32)
        spots_high = spots_high + payload[d, at_place + pr : at_place + 2 * pr].astype(F32)
    spots = jnp.concatenate([spots_low, spots_high], 1)
    vector = jnp.sum(right[pl.ds(28, n_dest, stride=32), :], 0, keepdims=True)
    summed = total[...]
    reduced[...] = summed.astype(BF16).reshape(reduced.shape)
    square = jnp.sum(summed * summed) + jnp.sum(spots * spots) + jnp.sum(vector * vector)
    row8 = iota((8, 128), 0)

    def parts(v):
        first = v.astype(BF16).astype(F32)
        second = (v - first).astype(BF16).astype(F32)
        return first, second, v - first - second

    extra = jnp.where(row8 == 0, vector, 0.0)
    for i, part in enumerate(
        parts(jnp.full((1, 128), square, F32)) + parts(jnp.full((1, 128), loss[0, 0], F32))
    ):
        extra = jnp.where(row8 == 1 + i, part, extra)
    block = jnp.concatenate([spots[:, :128], spots[:, 128:], extra], 0).astype(BF16)
    for d in range(n_dest):
        news[d] = block


def reduce(tab, me, loss, asked, payload, slots, cap):
    n_dest = payload.shape[0]
    pr = place_rows(n_dest)
    return pl.pallas_call(
        partial(reduce_kernel, slots, cap),
        out_shape=(
            jax.ShapeDtypeStruct((slots, HALF, D), BF16),
            jax.ShapeDtypeStruct((n_dest, news_rows(n_dest), 128), BF16),
        ),
        in_specs=[smem, smem, smem, vmem, vmem],
        out_specs=(vmem, vmem),
        scratch_shapes=[
            pltpu.VMEM((slots * HALF, D), F32),
            pltpu.VMEM((n_dest * cap, D), BF16),
            pltpu.VMEM(((n_dest + 1) * L_ROWS, 128), F32),
            pltpu.VMEM(((n_dest + 1) * 32, 128), F32),
        ],
        compiler_params=params(n_dest // 2, 16),
        name="reduce",
    )(tab, me, loss, asked, payload)


def update_slots(
    tab, half, rest, grads, places, scale, arrays, outs, held, in_sems, out_sems, ready=None
):
    old = held if ready is None else ready
    first_scale = -RATE / (1.0 - BETA_ONE**STEP)
    second_scale = 1.0 / (1.0 - BETA_TWO**STEP)
    rows = (pl.ds(pl.multiple_of(half * HALF, HALF), HALF), slice(None))
    columns = (slice(None), pl.ds(pl.multiple_of(half * 128, 128), 128))
    whole = (slice(None), slice(None))
    ends = [tab[k, TAB_ENDS] for k in range(4)]
    spans = [(KIND_TABLE, 0, ends[0], rows), (KIND_DENSE, ends[0], ends[1], columns)]
    if rest:
        spans += [(KIND_PLACE, ends[1], ends[2], whole), (0, ends[2], ends[3], whole)]

    def loop(action):
        for case, start, stop, region in spans:

            def body(j, c):
                action(tab[j, TAB_SORTED], case, region)
                return c

            lax.fori_loop(start, stop, body, 0)

    def in_copies(i, region):
        return [
            pltpu.make_async_copy(a.at[(i,) + region], held.at[(k, i) + region], in_sems.at[k, i])
            for k, a in enumerate(arrays)
        ]

    def out_copies(i, region):
        return [
            pltpu.make_async_copy(held.at[(k, i) + region], out.at[(i,) + region], out_sems.at[k, i])
            for k, out in enumerate(outs)
        ]

    def start(i, case, region):
        for copy in in_copies(i, region):
            copy.start()

    def step(i, region, g):
        g = g * scale[: g.shape[0], : g.shape[1]]
        m1 = BETA_ONE * old[(1, i) + region] + (1.0 - BETA_ONE) * g
        m2 = BETA_TWO * old[(2, i) + region] + (1.0 - BETA_TWO) * (g * g)
        root = jnp.sqrt(m2 * second_scale) + EPSILON
        held[(0, i) + region] = (
            old[(0, i) + region] * (1.0 - RATE * DECAY) + (m1 * first_scale) / root
        )
        held[(1, i) + region] = m1
        held[(2, i) + region] = m2

    def act(i, case, region):
        if ready is None:
            for copy in in_copies(i, region):
                copy.wait()
        if case == KIND_TABLE:
            step(i, region, grads[i].astype(F32))
        elif case == KIND_DENSE:
            g = grads[i].astype(F32)
            step(i, region, jnp.concatenate([g[:, :128], g[:, 128:]], 0))
        elif case == KIND_PLACE:
            spot = pl.multiple_of((tab[i, TAB_KIND] - KIND_PLACE) * UNIT, UNIT)
            step(i, region, places[pl.ds(spot, UNIT), :])

        for copy in out_copies(i, region):
            copy.start()

    def finish(i, case, region):
        for copy in out_copies(i, region):
            copy.wait()

    if ready is None:
        loop(start)
    yield
    loop(act)
    loop(finish)
    yield


def ahead_copies(tab, half, arrays, ready, sems, wait):
    rows = (pl.ds(pl.multiple_of(half * HALF, HALF), HALF), slice(None))
    columns = (slice(None), pl.ds(pl.multiple_of(half * 128, 128), 128))
    ends = [tab[k, TAB_ENDS] for k in range(2)]
    for start, stop, region in ((0, ends[0], rows), (ends[0], ends[1], columns)):

        def body(j, c):
            i = tab[j, TAB_SORTED]
            for k, a in enumerate(arrays):
                copy = pltpu.make_async_copy(
                    a.at[(i,) + region], ready.at[(k, i) + region], sems.at[k, i]
                )
                copy.wait() if wait else copy.start()
            return c

        lax.fori_loop(start, stop, body, 0)


def update_kernel(
    tab, me, news, own, weight, first, second, vectors, vector_first, vector_second,
    weight_out, first_out, second_out, vectors_out, vector_first_out, vector_second_out, loss_out,
    norm_out, factor_out, ready, places, held, in_sems, out_sems, ready_sems,
):
    n_dest = news.shape[0]
    pr = place_rows(n_dest)
    share = PLEN // n_dest
    scale = factor_out
    steps = update_slots(
        tab, me[1], True, own, places, scale, (weight, first, second),
        (weight_out, first_out, second_out), held, in_sems, out_sems,
    )
    next(steps)
    ahead_copies(tab, 1 - me[1], (weight, first, second), ready, ready_sems, False)
    extras = []
    for d in range(n_dest):
        part = news[d].astype(F32)
        places[d * share : (d + 1) * share, :128] = part[:share]
        places[d * share : (d + 1) * share, 128:] = part[pr : pr + share]
        extras.append(part[2 * pr :])
    sums = extras[0]
    for extra in extras[1:]:
        sums = sums + extra
    square = sums[1:2] + sums[2:3] + sums[3:4]
    norm = jnp.sqrt(square)
    factor = CLIP_AT / jnp.maximum(norm, CLIP_AT)
    norm_out[0, 0] = norm[0, 0]
    losses = extras[0] + extras[1]
    loss = losses[4:5] + losses[5:6] + losses[6:7]
    loss_out[0, 0] = loss[0, 0]
    vector_grad = jnp.concatenate(
        [
            jnp.concatenate([extras[2 * i][0:1], extras[2 * i + 1][0:1]], 1)
            for i in range(vectors.shape[0])
        ],
        0,
    ) * jnp.concatenate([factor, factor], 1)
    v, m1, m2 = adam_step(
        vectors[...], vector_first[...], vector_second[...], vector_grad, VECTOR_RATE, 0.0
    )
    vectors_out[...] = v
    vector_first_out[...] = m1
    vector_second_out[...] = m2
    factor_out[...] = jnp.broadcast_to(jnp.concatenate([factor, factor], 1), (UNIT, D))
    next(steps)
    ahead_copies(tab, 1 - me[1], (weight, first, second), ready, ready_sems, True)


def finish_kernel(
    tab, me, factor, other, ready, weight_in, first_in, second_in, weight_out,
    first_out, second_out, held, in_sems, out_sems,
):
    steps = update_slots(
        tab, 1 - me[1], False, other, None, factor, (),
        (weight_out, first_out, second_out), held, in_sems, out_sems, ready=ready,
    )
    next(steps)
    next(steps)


def update_scratch(shape):
    return [
        pltpu.VMEM((3,) + shape, F32),
        pltpu.SemaphoreType.DMA((3, shape[0])),
        pltpu.SemaphoreType.DMA((3, shape[0])),
    ]


def update(tab, me, news, own, weights, first, second, vectors, vector_first, vector_second):
    n_dest = news.shape[0]
    big = pltpu.HBM(weights.shape, F32)
    small = jax.ShapeDtypeStruct(vectors.shape, F32)
    one = jax.ShapeDtypeStruct((1, 1), F32)
    return pl.pallas_call(
        update_kernel,
        out_shape=(big, big, big, small, small, small, one, one, jax.ShapeDtypeStruct((UNIT, D), F32),
            pltpu.VMEM((3,) + weights.shape, F32),
        ),
        in_specs=[smem, smem] + [vmem] * 2 + [in_hbm] * 3 + [vmem] * 3,
        out_specs=(in_hbm, in_hbm, in_hbm, vmem, vmem, vmem, smem, smem, vmem, vmem),
        scratch_shapes=[pltpu.VMEM((PLEN, D), F32)]
        + update_scratch(weights.shape)
        + [pltpu.SemaphoreType.DMA((3, weights.shape[0]))],
        compiler_params=params(n_dest // 2, 14),
        name="update",
    )(tab, me, news, own, *stay(weights, first, second), vectors, vector_first, vector_second)


def finish(tab, me, factor, other, ready, started, n_blk):
    shape = started[0].shape
    big = pltpu.HBM(shape, F32)
    return pl.pallas_call(
        finish_kernel,
        out_shape=(big, big, big),
        in_specs=[smem, smem, vmem, vmem, vmem] + [in_hbm] * 3,
        out_specs=(in_hbm, in_hbm, in_hbm),
        scratch_shapes=update_scratch(shape),
        input_output_aliases={5: 0, 6: 1, 7: 2},
        compiler_params=params(n_blk, 14),
        name="finish",
    )(
        tab, me, factor, other, pltpu.with_memory_space_constraint(ready, pltpu.VMEM),
        *stay(*started),
    )


def quick(
    query_ids, passage_ids, query_lengths, passage_lengths, positive, prefix_lengths,
    prefix_weights, owners, weights, first_moments, second_moments, vectors, vector_first,
    vector_second,
):
    slots = weights.shape[0]
    n_blk = lax.axis_size("blk")
    everyone = ("blk", "rep")
    cap = 48 if n_blk <= 16 else 16
    take_cap = 80 if n_blk <= 16 else 32
    me = jnp.stack([lax.axis_index("blk"), lax.axis_index("rep")]).astype(I32)

    def exchange(a, axes):
        return lax.all_to_all(a, axes, 0, 0, tiled=True)

    message, where_row, tab = request(
        owners, me, positive, query_lengths, passage_lengths, query_ids[0], passage_ids[0],
        weights, n_blk, cap, take_cap,
    )
    message = exchange(message, everyone)
    first = along_z(collect(tab, me, message), n_blk)
    rows, message = fetch(me, message, weights, cap, take_cap)
    rows, first = lax.optimization_barrier((rows, first))
    rows = exchange(rows, "blk")
    gathered = spread(first, n_blk)
    emb, low, normed, scale, probs, state, matrices = forward(
        tab, me, query_lengths, passage_lengths, positive, rows, where_row, vectors, gathered, n_blk
    )
    emb = exchange(emb, "blk")
    payload, loss, count = backward(
        tab, me, prefix_lengths, prefix_weights, emb, message, where_row, low, normed, scale,
        probs, state, vectors, matrices, cap,
    )
    payload = exchange(payload, everyone)
    asked = message[:, :cap].reshape(1, -1)
    own, news = reduce(tab, me, loss, asked, payload, slots, cap)
    other = lax.ppermute(own, "rep", [(0, 1), (1, 0)])
    news = exchange(news, everyone)
    *outs, loss_sum, norm, factor, ready = update(
        tab, me, news, own, weights, first_moments, second_moments, vectors, vector_first,
        vector_second,
    )
    outs = (*outs, loss_sum.reshape(()), count.reshape(()), norm.reshape(()))

    def general(carry):
        return 0, local(
            query_ids, passage_ids, query_lengths, passage_lengths, positive, prefix_lengths,
            prefix_weights, owners, weights, first_moments, second_moments, vectors, vector_first,
            vector_second,
        )

    full = jnp.max(message[:, 126])
    outs = (*finish(tab, me, factor, other, ready, outs[:3], n_blk), *outs[3:])
    return lax.while_loop(lambda c: c[0] > 0, general, (full, outs))[1]


def solution(mesh):
    in_specs = (
        P("rep", "blk", None),
        P("rep", "blk", None),
        P("rep", "blk"),
        P("rep", "blk"),
        P("rep", "blk"),
        P(),
        P(),
        P(),
        P("blk", None, None),
        P("blk", None, None),
        P("blk", None, None),
        P(),
        P(),
        P(),
    )
    out_specs = (
        P("blk", None, None),
        P("blk", None, None),
        P("blk", None, None),
        P(),
        P(),
        P(),
        P(),
        P(),
        P(),
    )
    return jax.shard_map(quick, mesh=mesh, in_specs=in_specs, out_specs=out_specs, check_vma=False)
```
